32 devices in a mesh: rep: 4 (over y, x), fsdp: 8 (over z, core).
Axes of the slice: x: 2, y: 2, z: 4, core: 2. Of those that a mesh axis runs over, the one named last changes fastest.
Arguments:
- content_stream: bfloat16 [16384, 768], P(('rep', 'fsdp')), may hold values from -6 to 6
- query_stream: bfloat16 [16384, 768], P(('rep', 'fsdp')), may hold values from -6 to 6
- lengths: int32 [32], P(('rep', 'fsdp')), may hold values from 128 to 512, as said below
- ranking: int32 [32, 512], P(('rep', 'fsdp')), may hold values from 0 to 511, as said below
- query_weight: bfloat16 [768, 768], P('fsdp'), may hold values from -0.21875 to 0.21875
- query_bias: bfloat16 [768], P('fsdp'), may hold values from -3 to 3
- key_weight: bfloat16 [768, 768], P('fsdp'), may hold values from -0.21875 to 0.21875
- value_weight: bfloat16 [768, 768], P('fsdp'), may hold values from -0.21875 to 0.21875
- value_bias: bfloat16 [768], P('fsdp'), may hold values from -3 to 3
- output_weight: bfloat16 [768, 768], P('fsdp'), may hold values from -0.875 to 0.875
- output_bias: bfloat16 [768], P('fsdp'), may hold values from -3 to 3
- norm_gain: bfloat16 [768], P('fsdp'), may hold values from 0.5 to 1.5
- norm_shift: bfloat16 [768], P('fsdp'), may hold values from -3 to 3
- inner_weight: bfloat16 [768, 3072], P('fsdp'), may hold values from -0.21875 to 0.21875
- inner_bias: bfloat16 [3072], P('fsdp'), may hold values from -3 to 3
- outer_weight: bfloat16 [3072, 768], P('fsdp'), may hold values from -0.109375 to 0.109375
- outer_bias: bfloat16 [768], P('fsdp'), may hold values from -3 to 3
- final_gain: bfloat16 [768], P('fsdp'), may hold values from 0.5 to 1.5
- final_shift: bfloat16 [768], P('fsdp'), may hold values from -3 to 3
- bucket_bias: bfloat16 [384], P('fsdp'), may hold values from -4 to 4
- content_cotangent: bfloat16 [16384, 768], P(('rep', 'fsdp')), may hold values from -6 to 6
- query_cotangent: bfloat16 [16384, 768], P(('rep', 'fsdp')), may hold values from -6 to 6
Outputs:
- content_out: bfloat16 [16384, 768], P(('rep', 'fsdp'))
- query_out: bfloat16 [16384, 768], P(('rep', 'fsdp'))
- content_grad: float32 [16384, 768], P(('rep', 'fsdp'))
- query_grad: float32 [16384, 768], P(('rep', 'fsdp'))
- query_weight_grad: float32 [768, 768], P('fsdp')
- query_bias_grad: float32 [768], P('fsdp')
- key_weight_grad: float32 [768, 768], P('fsdp')
- value_weight_grad: float32 [768, 768], P('fsdp')
- value_bias_grad: float32 [768], P('fsdp')
- output_weight_grad: float32 [768, 768], P('fsdp')
- output_bias_grad: float32 [768], P('fsdp')
- norm_gain_grad: float32 [768], P('fsdp')
- norm_shift_grad: float32 [768], P('fsdp')
- inner_weight_grad: float32 [768, 3072], P('fsdp')
- inner_bias_grad: float32 [3072], P('fsdp')
- outer_weight_grad: float32 [3072, 768], P('fsdp')
- outer_bias_grad: float32 [768], P('fsdp')
- final_gain_grad: float32 [768], P('fsdp')
- final_shift_grad: float32 [768], P('fsdp')
- bucket_bias_grad: float32 [384], P('fsdp')
The draws below stay inside these ranges and needn't reach their ends.
Inputs may be any that keep to these rules, and one draw needn't show every extreme that they name: `lengths`: the first sequence has all 512 slots real. `ranking`: in each sequence the slots below its length hold 0 to length - 1 once each, and the padded slots hold length to 511 once each.
All inputs are finite; a program needn't handle non-finite values.
Results may differ from the reference program's by a relative error of at most 0.019.
Values may be sent and summed in bfloat16 or wider, within the bound.
A program may use at most 256 MiB of HBM per device.

```python
import math
import jax
import jax.numpy as jnp
from jax import lax

D = 768
HEADS = 12
HEAD_DIM = 64
FF = 3072
BUCKETS = 32
SEQ = 512
SEQS = 32
TOKENS = 16384


def shared_lengths(key):
    inner_key = jax.random.fold_in(key, 101)
    drawn = jax.random.randint(inner_key, (SEQS,), SEQ // 4, SEQ + 1)
    return drawn.at[0].set(SEQ).astype(jnp.int32)


def draw_lengths(key, part):
    return shared_lengths(key)


def draw_ranking(key, part):
    lengths = shared_lengths(key)
    key = jax.random.fold_in(key, 2)
    keys = jax.random.split(key, SEQS)
    scores = jax.vmap(lambda one_key: jax.random.permutation(one_key, SEQ))(keys).astype(jnp.int32)
    places = jnp.arange(SEQ, dtype=jnp.int32)
    scores = scores + SEQ * (places[None, :] >= lengths[:, None]).astype(jnp.int32)
    placing = jnp.argsort(scores, axis=1, stable=True)
    return jnp.argsort(placing, axis=1, stable=True).astype(jnp.int32)


def spiked(values, own_key, source, target, shards_of, factor):
    owner, partner = [(jnp.arange(values.shape[axis_at]) // (values.shape[axis_at] // shards_of)).reshape([-1 if axis == axis_at else 1 for axis in range(values.ndim)]) for axis_at in (source, target)]
    chosen = jax.random.permutation(own_key, shards_of)[partner]
    strong = (owner == chosen) | (owner == (partner + shards_of // 2) % shards_of)
    return jnp.where(strong, factor * values, values)


def steps_of(rng, extent, shards, smallest, largest):
    def one(dim, shards_of):
        heights = jax.random.uniform(jax.random.fold_in(jax.random.fold_in(rng, 6), dim), (shards_of,), jnp.float32, smallest / len(shards), largest / len(shards))
        return jnp.repeat(jnp.exp(heights), extent[dim] // shards_of).reshape((-1,) + (1,) * (len(extent) - dim - 1))

    factor_of = one(*shards[0])
    for cut in shards[1:]:
        factor_of = factor_of * one(*cut)
    return factor_of


def noise(stream_key, extent, spread, bound, pieces=(), held_as=jnp.bfloat16):
    result = spread * jax.random.normal(stream_key, extent, jnp.float32)
    if pieces:
        result = result * steps_of(stream_key, extent, pieces, -0.22, 0.18)
    return jnp.clip(result, -bound, bound).astype(held_as)


def heavy_noise(stream_key, dims, deviation, most, shards, heavy, held_as=jnp.bfloat16):
    result = deviation * jax.random.normal(stream_key, dims, jnp.float32)
    if shards:
        result = result * steps_of(stream_key, dims, shards, -0.22, 0.18)
    return jnp.clip(spiked(result, jax.random.fold_in(stream_key, 3), *heavy), -most, most).astype(held_as)


def setup_inputs(seed: int = 0) -> dict:
    arg_keys = jax.random.split(jax.random.key(seed), 23)
    content_stream = heavy_noise(arg_keys[0], (TOKENS, D), 1.0, 6.0, ((0, 32),), (0, 1, 32, 2.75))
    query_stream = noise(arg_keys[1], (TOKENS, D), 1.0, 6.0, ((0, 32),))
    lengths = draw_lengths(jax.random.fold_in(arg_keys[22], 71), 0)
    ranking = draw_ranking(jax.random.fold_in(arg_keys[22], 71), 0)
    query_weight = noise(arg_keys[4], (D, D), D ** -0.5, 0.21875, ((0, 8),))
    query_bias = noise(arg_keys[5], (D,), 0.5, 3.0, ((0, 8),))
    key_weight = noise(arg_keys[6], (D, D), D ** -0.5, 0.21875, ((0, 8),))
    value_weight = noise(arg_keys[7], (D, D), D ** -0.5, 0.21875, ((0, 8),))
    value_bias = noise(arg_keys[8], (D,), 0.5, 3.0, ((0, 8),))
    output_weight = noise(arg_keys[9], (D, D), (max(D // 16, 1)) ** -0.5, 0.875, ((0, 8),))
    output_bias = noise(arg_keys[10], (D,), 0.5, 3.0, ((0, 8),))
    norm_gain = jnp.clip(1.0 + 0.1 * jax.random.normal(arg_keys[11], (D,), jnp.float32), 0.5, 1.5).astype(jnp.bfloat16)
    norm_shift = noise(arg_keys[12], (D,), 0.5, 3.0, ((0, 8),))
    inner_weight = noise(arg_keys[13], (D, FF), D ** -0.5, 0.21875, ((0, 8),))
    inner_bias = noise(arg_keys[14], (FF,), 0.5, 3.0, ((0, 8),))
    outer_weight = noise(arg_keys[15], (FF, D), FF ** -0.5, 0.109375, ((0, 8),))
    outer_bias = noise(arg_keys[16], (D,), 0.5, 3.0, ((0, 8),))
    final_gain = jnp.clip(1.0 + 0.1 * jax.random.normal(arg_keys[17], (D,), jnp.float32), 0.5, 1.5).astype(jnp.bfloat16)
    final_shift = noise(arg_keys[18], (D,), 0.5, 3.0, ((0, 8),))
    bucket_bias = noise(arg_keys[19], (HEADS * BUCKETS,), 1.0, 4.0, ((0, 8),))
    content_cotangent = noise(arg_keys[20], (TOKENS, D), 1.0, 6.0, ((0, 32),))
    query_cotangent = noise(arg_keys[21], (TOKENS, D), 1.0, 6.0, ((0, 32),))
    return {"content_stream": content_stream, "query_stream": query_stream, "lengths": lengths, "ranking": ranking, "query_weight": query_weight, "query_bias": query_bias, "key_weight": key_weight, "value_weight": value_weight, "value_bias": value_bias, "output_weight": output_weight, "output_bias": output_bias, "norm_gain": norm_gain, "norm_shift": norm_shift, "inner_weight": inner_weight, "inner_bias": inner_bias, "outer_weight": outer_weight, "outer_bias": outer_bias, "final_gain": final_gain, "final_shift": final_shift, "bucket_bias": bucket_bias, "content_cotangent": content_cotangent, "query_cotangent": query_cotangent}


@jax.custom_vjp
def low(v):
    return lax.optimization_barrier(v.astype(jnp.bfloat16)).astype(jnp.float32)

@jax.custom_vjp
def low_back(v):
    return v

def low_keep(v):
    return (low(v), None)

def low_pass(kept, grad):
    return (grad,)

def back_keep(v):
    return (v, None)

def back_low(kept, grad):
    return (low(grad),)
low.defvjp(low_keep, low_pass)
low_back.defvjp(back_keep, back_low)
EPS = 1e-05
NEG = -1e+30
HIGH = lax.Precision.HIGHEST
FAR_STEPS = (12, 16, 23, 32, 46, 64, 91)

def rounded_both(value):
    return low_back(low(value))

def matmul(left, right):
    return jnp.dot(left, right, precision=HIGH)

def bucket_index(seq_len):
    places = jnp.arange(seq_len, dtype=jnp.int32)
    offset = places[None, :] - places[:, None]
    distance = jnp.abs(offset)
    farther = jnp.full(distance.shape, 8, jnp.int32)
    for step_at in FAR_STEPS:
        farther = farther + (distance >= step_at).astype(jnp.int32)
    return jnp.where(distance < 8, distance, farther) + 16 * (offset > 0).astype(jnp.int32)

def visibility(length, order_rank):
    places = jnp.arange(order_rank.shape[0], dtype=jnp.int32)
    valid = places < length
    chosen = valid & (order_rank >= length - 3 * length // 20)
    open_key = valid & jnp.logical_not(chosen)
    earlier_same = order_rank[None, :] <= order_rank[:, None]
    earlier = order_rank[None, :] < order_rank[:, None]
    content_see = open_key[None, :] | chosen[None, :] & earlier_same
    query_see = open_key[None, :] | chosen[None, :] & earlier
    return (content_see, query_see)

def norm_rows(rows, gain, shift):
    mean_row = lax.optimization_barrier(jnp.mean(rows, axis=-1, keepdims=True))
    centred = rows - mean_row
    variance = lax.optimization_barrier(jnp.mean(centred * centred, axis=-1, keepdims=True))
    return centred * lax.rsqrt(variance + EPS) * gain + shift

def attend(queries, key_rows, value_rows, bias, visible):
    raw = jnp.einsum('qhe,khe->hqk', queries, key_rows, precision=HIGH) * HEAD_DIM ** (-0.5) + bias
    scores = jnp.where(visible[None], low_back(raw), NEG)
    probs = low(jax.nn.softmax(scores, axis=2))
    context = jnp.einsum('hqk,khe->qhe', probs, value_rows, precision=HIGH)
    return context.reshape(SEQ, HEADS * HEAD_DIM)

def stream_tail(stream, context, params):
    w_query, b_query, w_key, w_value, b_value, w_output, b_output, gain_one, shift_one, w_inner, b_inner, w_outer, b_outer, gain_two, shift_two, table = params
    attended = low_back(matmul(rounded_both(context), w_output) + b_output)
    normed = norm_rows(stream + attended, gain_one, shift_one)
    inner = low_back(matmul(low(normed), w_inner) + b_inner)
    active = low(jax.nn.gelu(inner, approximate=False))
    branch = low_back(matmul(active, w_outer) + b_outer)
    return norm_rows(normed + branch, gain_two, shift_two)

def group_forward(params, content, query, length_part, rank_part):
    w_query, b_query, w_key, w_value, b_value, w_output, b_output, gain_one, shift_one, w_inner, b_inner, w_outer, b_outer, gain_two, shift_two, table = params
    content_q = rounded_both(matmul(content, w_query) + b_query)
    query_q = rounded_both(matmul(query, w_query) + b_query)
    key_rows = rounded_both(matmul(content, w_key))
    value_rows = rounded_both(matmul(content, w_value) + b_value)
    position_bias = table.reshape(HEADS, BUCKETS)[:, bucket_index(SEQ)]
    count = length_part.shape[0]
    shape_four = (count, SEQ, HEADS, HEAD_DIM)

    def one_sequence(items):
        content_part, query_part, key_part, value_part, length, order_rank = items
        content_see, query_see = visibility(length, order_rank)
        return (attend(content_part, key_part, value_part, position_bias, content_see), attend(query_part, key_part, value_part, position_bias, query_see))
    context_c, context_g = lax.map(jax.checkpoint(one_sequence), (content_q.reshape(shape_four), query_q.reshape(shape_four), key_rows.reshape(shape_four), value_rows.reshape(shape_four), length_part, rank_part))
    out_c = stream_tail(content, context_c.reshape(count * SEQ, D), params)
    out_g = stream_tail(query, context_g.reshape(count * SEQ, D), params)
    return (out_c, out_g)

def reference(content_stream, query_stream, lengths, ranking, query_weight, query_bias, key_weight, value_weight, value_bias, output_weight, output_bias, norm_gain, norm_shift, inner_weight, inner_bias, outer_weight, outer_bias, final_gain, final_shift, bucket_bias, content_cotangent, query_cotangent):
    params = tuple((item.astype(jnp.float32) for item in (query_weight, query_bias, key_weight, value_weight, value_bias, output_weight, output_bias, norm_gain, norm_shift, inner_weight, inner_bias, outer_weight, outer_bias, final_gain, final_shift, bucket_bias)))
    group = math.gcd(SEQS, max(1, 4096 // SEQ))
    rounds = SEQS // group
    rows_group = group * SEQ

    def split_rows(array):
        return array.astype(jnp.float32).reshape(rounds, rows_group, D)
    inputs = (split_rows(content_stream), split_rows(query_stream), lengths.reshape(rounds, group), ranking.reshape(rounds, group, SEQ), split_rows(content_cotangent), split_rows(query_cotangent))

    def step(totals, items):
        content, query, length_part, rank_part, cot_content, cot_query = items

        def forward(params_in, content_in, query_in):
            return group_forward(params_in, content_in, query_in, length_part, rank_part)
        outputs, pull = jax.vjp(forward, params, content, query)
        grad_params, grad_content, grad_query = pull((cot_content, cot_query))
        totals = tuple((left + right for left, right in zip(totals, grad_params)))
        return (totals, (outputs[0].astype(jnp.bfloat16), outputs[1].astype(jnp.bfloat16), grad_content, grad_query))
    zeros = tuple((jnp.zeros_like(item) for item in params))
    totals, (out_c, out_g, grad_c, grad_g) = lax.scan(step, zeros, inputs)
    return (out_c.reshape(TOKENS, D), out_g.reshape(TOKENS, D), grad_c.reshape(TOKENS, D), grad_g.reshape(TOKENS, D), totals[0], totals[1], totals[2], totals[3], totals[4], totals[5], totals[6], totals[7], totals[8], totals[9], totals[10], totals[11], totals[12], totals[13], totals[14], totals[15])
```

```python
import functools

import jax
import jax.numpy as jnp
from jax import lax
from jax.experimental import pallas as pl
from jax.experimental.pallas import tpu as pltpu
from jax.sharding import PartitionSpec as P

HEADS = 12
HEAD_DIM = 64
PAIRS = HEADS // 2
BUCKETS = 32
SEQ = 512
ROWS = 2 * SEQ
D = 768
FF = 3072
TILE = 256
TILES = FF // TILE
EPS = 1e-05
NEG = -1e30
LOG2E = 1.4426950408889634
SCALE = HEAD_DIM**-0.5
FAR_STEPS = (12, 16, 23, 32, 46, 64, 91)
F32 = jnp.float32
BF16 = jnp.bfloat16
VMEM_LIMIT = 60 * 2**20

TAIL_P = 0.28
TAIL = (
    0.11608706693762069,
    0.07021928496801585,
    0.26212226118724974,
    -0.22858899246095166,
    0.3847049667747488,
    -0.10454457204169064,
)


def mm(a, b):
    return jnp.dot(a, b, preferred_element_type=F32)


def mm_nt(a, b):
    return lax.dot_general(a, b, (((1,), (1,)), ((), ())), preferred_element_type=F32)


def mm_tn(a, b):
    return lax.dot_general(a, b, (((0,), (0,)), ((), ())), preferred_element_type=F32)


def bucket_of(offset):
    distance = jnp.abs(offset)
    farther = jnp.full(distance.shape, 8, jnp.int32)
    for step_at in FAR_STEPS:
        farther = farther + jnp.where(distance >= step_at, 1, 0)
    return jnp.where(distance < 8, distance, farther) + jnp.where(offset > 0, 16, 0)


def normal_parts(x):
    size = jnp.abs(x)
    t = 1.0 / (1.0 + TAIL_P * size)
    poly = jnp.full(x.shape, TAIL[-1], F32)
    for c in TAIL[-2::-1]:
        poly = poly * t + c
    bell = jnp.exp2(x * x * (-0.5 * LOG2E))
    tail = poly * t * bell
    return jnp.where(x < 0, tail, 1.0 - tail), bell * 0.3989422804014327


def ds(start, size):
    return pl.ds(pl.multiple_of(start, size), size)


def build_masks(len_ref, rank_ref, mask_s):
    n = len_ref[0]
    rank = rank_ref[...]
    place = lax.broadcasted_iota(jnp.int32, (1, SEQ), 1)
    valid = place < n
    chosen = valid & (rank >= n - 3 * n // 20)
    key = jnp.where(chosen, rank, jnp.where(valid, -1, 2 * SEQ)).astype(F32)
    column = jnp.broadcast_to(rank.astype(F32), (128, SEQ)).T
    for s in range(2):
        for j in range(SEQ // 128):
            seen = jnp.broadcast_to(key[:, j * 128 : (j + 1) * 128], (SEQ, 128)) <= column - s
            mask_s[s, :, j * 128 : (j + 1) * 128] = jnp.where(seen, 0.0, NEG)


def build_strip(tab_ref, strip_s):
    offset = lax.broadcasted_iota(jnp.int32, (128, 1024), 1) - 512
    bucket = lax.broadcasted_iota(jnp.int32, (128, 1024), 0)
    onehot = jnp.where(bucket_of(offset) == bucket, 1.0, 0.0).astype(BF16)
    line = mm(tab_ref[...], onehot) * LOG2E
    for h in range(HEADS):
        wide = jnp.broadcast_to(line[h : h + 1], (128, 1024))
        strip_s[h] = pltpu.roll(wide, 0, 1, stride=1, stride_axis=0)[:, 128:]


def project(x_ref, y_ref, vec_ref, w_s, q_s, k_s, v_s):
    for pair in range(0, PAIRS, 2):
        cols = slice(pair * 128, pair * 128 + 256)
        x = x_ref[...]
        parts = (
            (q_s, 0, mm(x, w_s[0, :, cols]) + vec_ref[0:1, cols]),
            (q_s, 1, mm(y_ref[...], w_s[0, :, cols]) + vec_ref[0:1, cols]),
            (k_s, None, mm(x, w_s[1, :, cols])),
            (v_s, None, mm(x, w_s[2, :, cols]) + vec_ref[1:2, cols]),
        )
        for ref, s, value in parts:
            value = value.astype(BF16)
            for e in range(2):
                piece = value[:, e * 128 : (e + 1) * 128]
                if s is None:
                    ref[pair + e] = piece
                else:
                    ref[s, pair + e] = piece


def attend(q_s, k_s, v_s, strip_s, mask_s, p_st, ctx_s, hp, slot):
    lane = lax.broadcasted_iota(jnp.int32, (SEQ, 128), 1)
    k = k_s[hp]
    v = v_s[hp]
    for s in range(2):
        q = q_s[s, hp]
        outs = []
        for e in range(2):
            own = (lane < 64) if e == 0 else (lane >= 64)
            scores = mm_nt(jnp.where(own, q, jnp.zeros_like(q)), k)
            for i in range(SEQ // 128):
                rows = slice(i * 128, (i + 1) * 128)
                blk = (
                    scores[rows] * (SCALE * LOG2E)
                    + strip_s[2 * hp + e, :, (3 - i) * 128 : (3 - i) * 128 + SEQ]
                    + mask_s[s, rows, :]
                )
                top = jnp.max(blk, axis=1, keepdims=True)
                w = jnp.exp2(blk - top)
                w = w * (1.0 / jnp.sum(w, axis=1, keepdims=True))
                p_st[slot, e, s, rows, :] = w.astype(BF16)
            outs.append(mm(p_st[slot, e, s], v))
        ctx_s[s * SEQ : (s + 1) * SEQ, ds(hp * 128, 128)] = jnp.where(
            lane < 64, outs[0], outs[1]
        ).astype(BF16)


def norm_stats(r):
    mean = jnp.mean(r, axis=1, keepdims=True)
    centred = r - mean
    inverse = lax.rsqrt(jnp.mean(centred * centred, axis=1, keepdims=True) + EPS)
    return centred * inverse, inverse


def forward_kernel(
    x_ref, y_ref, len_ref, rank_ref, vec_ref, tab_ref, wa_h, wi_h, wo_h,
    oc_ref, oq_ref, q_h, k_h, v_h, p_h, ctx_h, n1_h, inv1_h, nl_h, act_h, slope_h, n2_h, inv2_h,
    wa_s, wi_s, wo_s, q_s, k_s, v_s, ctx_s, nl_s, n1_s, br_s, inv1_s, inv2_s, w_sem, o_sem, st_sem,
):
    loads = [pltpu.make_async_copy(wa_h.at[i], wa_s.at[i], w_sem.at[i]) for i in range(4)]
    loads.append(pltpu.make_async_copy(wi_h, wi_s, w_sem.at[4]))
    loads.append(pltpu.make_async_copy(wo_h, wo_s, w_sem.at[5]))
    for c in loads:
        c.start()
    stores = []

    def keep(src, dst):
        pltpu.make_async_copy(src, dst, o_sem.at[len(stores)]).start()
        stores.append((src, dst))

    def attention(strip_s, mask_s, p_st):
        build_masks(len_ref, rank_ref, mask_s)
        build_strip(tab_ref, strip_s)
        for c in loads[:3]:
            c.wait()
        project(x_ref, y_ref, vec_ref, wa_s, q_s, k_s, v_s)
        keep(q_s, q_h)
        keep(k_s, k_h)
        keep(v_s, v_h)

        def store(hp, slot):
            return pltpu.make_async_copy(p_st.at[slot], p_h.at[hp], st_sem.at[slot])

        def step(hp, carry):
            slot = (hp % 2)

            @pl.when(hp >= 2)
            def _():
                store(hp - 2, slot).wait()

            attend(q_s, k_s, v_s, strip_s, mask_s, p_st, ctx_s, hp, slot)
            store(hp, slot).start()
            return carry

        lax.fori_loop(0, PAIRS, step, 0)
        store(PAIRS - 2, 0).wait()
        store(PAIRS - 1, 1).wait()

    pl.run_scoped(
        attention,
        pltpu.VMEM((HEADS, 128, 896), F32),
        pltpu.VMEM((2, SEQ, SEQ), F32),
        pltpu.VMEM((2, 2, 2, SEQ, SEQ), BF16),
    )
    keep(ctx_s, ctx_h)

    loads[3].wait()
    for s, in_ref in ((0, x_ref), (1, y_ref)):
        def first(i, carry, s=s, in_ref=in_ref):
            own = ds(i * 256, 256)
            rows = ds(s * SEQ + i * 256, 256)
            r = in_ref[own, :].astype(F32) + mm(ctx_s[rows, :], wa_s[3]) + vec_ref[2:3, :]
            n, inverse = norm_stats(r)
            n1_s[rows, :] = n
            inv1_s[rows, :] = jnp.broadcast_to(inverse, (256, 128))
            nl_s[rows, :] = (n * vec_ref[3:4, :] + vec_ref[4:5, :]).astype(BF16)
            return carry

        lax.fori_loop(0, SEQ // 256, first, 0)
    keep(n1_s, n1_h)
    keep(inv1_s, inv1_h)
    keep(nl_s, nl_h)

    loads[4].wait()
    loads[5].wait()
    br_s[...] = jnp.zeros_like(br_s)

    def feed(act_st, slope_st):
        def pair(t, slot):
            return (
                pltpu.make_async_copy(act_st.at[slot], act_h.at[t], st_sem.at[slot]),
                pltpu.make_async_copy(slope_st.at[slot], slope_h.at[t], st_sem.at[2 + slot]),
            )

        def step(t, carry):
            slot = (t % 2)

            @pl.when(t >= 2)
            def _():
                for c in pair(t - 2, slot):
                    c.wait()

            cols = ds(t * TILE, TILE)
            inner = mm(nl_s[...], wi_s[:, cols]) + vec_ref[pl.ds(8 + (t // 3), 1), ds((t % 3) * TILE, TILE)]
            spread, bell = normal_parts(inner)
            act = (inner * spread).astype(BF16)
            act_st[slot] = act
            slope_st[slot] = (spread + inner * bell).astype(BF16)
            br_s[...] += mm(act, wo_s[cols, :])
            for c in pair(t, slot):
                c.start()
            return carry

        lax.fori_loop(0, TILES, step, 0)
        for t in (TILES - 2, TILES - 1):
            for c in pair(t, t % 2):
                c.wait()

    pl.run_scoped(feed, pltpu.VMEM((2, ROWS, TILE), BF16), pltpu.VMEM((2, ROWS, TILE), BF16))

    for s, o_ref in ((0, oc_ref), (1, oq_ref)):
        def last(i, carry, s=s, o_ref=o_ref):
            rows = ds(s * SEQ + i * 128, 128)
            normed = n1_s[rows, :] * vec_ref[3:4, :] + vec_ref[4:5, :]
            n, inverse = norm_stats(normed + br_s[rows, :] + vec_ref[5:6, :])
            br_s[rows, :] = n
            inv2_s[rows, :] = jnp.broadcast_to(inverse, (128, 128))
            o_ref[ds(i * 128, 128), :] = (n * vec_ref[6:7, :] + vec_ref[7:8, :]).astype(BF16)
            return carry

        lax.fori_loop(0, SEQ // 128, last, 0)
    keep(br_s, n2_h)
    keep(inv2_s, inv2_h)
    for i, (src, dst) in enumerate(stores):
        pltpu.make_async_copy(src, dst, o_sem.at[i]).wait()


def call_forward(x, y, length, rank, vecs, table, wa, wi, wo):
    hbm = pl.BlockSpec(memory_space=pl.ANY)
    vmem = pl.BlockSpec(memory_space=pltpu.VMEM)
    smem = pl.BlockSpec(memory_space=pltpu.SMEM)
    shape = jax.ShapeDtypeStruct
    outs = (
        shape((SEQ, D), BF16), shape((SEQ, D), BF16),
        shape((2, PAIRS, SEQ, 128), BF16), shape((PAIRS, SEQ, 128), BF16), shape((PAIRS, SEQ, 128), BF16),
        shape((PAIRS, 2, 2, SEQ, SEQ), BF16), shape((ROWS, D), BF16),
        shape((ROWS, D), F32), shape((ROWS, 128), F32), shape((ROWS, D), BF16),
        shape((TILES, ROWS, TILE), BF16), shape((TILES, ROWS, TILE), BF16),
        shape((ROWS, D), F32), shape((ROWS, 128), F32),
    )
    return pl.pallas_call(
        forward_kernel,
        out_shape=outs,
        in_specs=[vmem, vmem, smem, vmem, vmem, vmem, hbm, hbm, hbm],
        out_specs=[vmem, vmem] + [hbm] * 12,
        scratch_shapes=[
            pltpu.VMEM((4, D, D), BF16), pltpu.VMEM((D, FF), BF16), pltpu.VMEM((FF, D), BF16),
            pltpu.VMEM((2, PAIRS, SEQ, 128), BF16), pltpu.VMEM((PAIRS, SEQ, 128), BF16), pltpu.VMEM((PAIRS, SEQ, 128), BF16),
            pltpu.VMEM((ROWS, D), BF16), pltpu.VMEM((ROWS, D), BF16), pltpu.VMEM((ROWS, D), F32), pltpu.VMEM((ROWS, D), F32),
            pltpu.VMEM((ROWS, 128), F32), pltpu.VMEM((ROWS, 128), F32),
            pltpu.SemaphoreType.DMA((6,)), pltpu.SemaphoreType.DMA((9,)), pltpu.SemaphoreType.DMA((4,)),
        ],
        compiler_params=pltpu.CompilerParams(vmem_limit_bytes=VMEM_LIMIT),
        name="forward",
    )(x, y, length, rank, vecs, table, wa, wi, wo)


def norm_grad(u, gain, n, inverse):
    ug = u * gain
    return inverse * (
        ug - jnp.mean(ug, axis=1, keepdims=True) - n * jnp.mean(ug * n, axis=1, keepdims=True)
    )


def backward_kernel(
    x_ref, y_ref, cc_ref, cq_ref, vec_ref, wa_h, wi_h, wo_h,
    q_h, k_h, v_h, p_h, ctx_h, n1_h, inv1_h, nl_h, act_h, slope_h, n2_h, inv2_h,
    gc_ref, gq_ref, ga_h, gi_h, go_h, gvec_ref, gtab_ref,
    wa_s, ctx_s, g_s, dctx_s, tr_s, st_s, l_sem, t_sem, g_sem,
):
    wload = pltpu.make_async_copy(wa_h, wa_s, l_sem.at[0])
    cload = pltpu.make_async_copy(ctx_h, ctx_s, l_sem.at[1])
    wload.start()
    cload.start()
    gvec_ref[...] = jnp.zeros_like(gvec_ref)

    def add_vec(row, value, cols=slice(None)):
        gvec_ref[row : row + 1, cols] += jnp.sum(value, axis=0, keepdims=True)

    def tail(n_s, inv_s, nl_s, db_s, act_s, slope_s, wi_s, wo_s):
        nload = pltpu.make_async_copy(n2_h, n_s, l_sem.at[2])
        iload = pltpu.make_async_copy(inv2_h, inv_s, l_sem.at[3])
        nlload = pltpu.make_async_copy(nl_h, nl_s, l_sem.at[4])
        nload.start()
        iload.start()
        nlload.start()

        def fetch(t, slot):
            return (
                pltpu.make_async_copy(act_h.at[t], act_s.at[slot], t_sem.at[slot]),
                pltpu.make_async_copy(slope_h.at[t], slope_s.at[slot], t_sem.at[2 + slot]),
                pltpu.make_async_copy(wi_h.at[:, ds(t * TILE, TILE)], wi_s.at[slot], t_sem.at[4 + slot]),
                pltpu.make_async_copy(wo_h.at[ds(t * TILE, TILE), :], wo_s.at[slot], t_sem.at[6 + slot]),
            )

        for c in fetch(0, 0):
            c.start()
        nload.wait()
        iload.wait()
        for s, cot in ((0, cc_ref), (1, cq_ref)):
            def second(i, carry, s=s, cot=cot):
                rows = ds(s * SEQ + i * 128, 128)
                u = cot[ds(i * 128, 128), :].astype(F32)
                n = n_s[rows, :]
                g = norm_grad(u, vec_ref[6:7, :], n, inv_s[rows, 0:1])
                add_vec(6, u * n)
                add_vec(7, u)
                g_s[rows, :] = g
                low = g.astype(BF16)
                db_s[rows, :] = low
                add_vec(5, low.astype(F32))
                return carry

            lax.fori_loop(0, SEQ // 128, second, 0)
        n1load = pltpu.make_async_copy(n1_h, n_s, l_sem.at[2])
        i1load = pltpu.make_async_copy(inv1_h, inv_s, l_sem.at[3])
        n1load.start()
        i1load.start()
        nlload.wait()
        tr_s[...] = nl_s[...].T

        def out_copies(t, slot):
            return (
                pltpu.make_async_copy(st_s.at[slot], go_h.at[ds(t * TILE, TILE), :], g_sem.at[slot]),
                pltpu.make_async_copy(st_s.at[2 + slot, :, :], gi_h.at[t], g_sem.at[2 + slot]),
            )

        def step(t, carry):
            slot = (t % 2)
            for c in fetch(t, slot):
                c.wait()

            @pl.when(t + 1 < TILES)
            def _():
                for c in fetch(t + 1, 1 - slot):
                    c.start()

            @pl.when(t >= 2)
            def _():
                for c in out_copies(t - 2, slot):
                    c.wait()

            db = db_s[...]
            di = (mm_nt(db, wo_s[slot]) * slope_s[slot].astype(F32)).astype(BF16)
            row, cols = (t // 3), ds((t % 3) * TILE, TILE)
            mine = lax.broadcasted_iota(jnp.int32, (8, TILE), 0) == row
            gvec_ref[8:16, cols] += jnp.where(mine, jnp.sum(di.astype(F32), axis=0, keepdims=True), 0.0)
            st_s[slot] = mm_tn(act_s[slot], db).astype(BF16)
            gin = mm(tr_s[...], di).astype(BF16)
            for j in range(3):
                st_s[2 + slot, :, j * 256 : (j + 1) * 256] = gin[j * 256 : (j + 1) * 256, :]
            g_s[...] += mm_nt(di, wi_s[slot])
            for c in out_copies(t, slot):
                c.start()
            return carry

        lax.fori_loop(0, TILES, step, 0)
        for t in (TILES - 2, TILES - 1):
            for c in out_copies(t, t % 2):
                c.wait()

        n1load.wait()
        i1load.wait()

        def first(i, carry):
            rows = ds(i * 128, 128)
            u = g_s[rows, :]
            n = n_s[rows, :]
            g = norm_grad(u, vec_ref[3:4, :], n, inv_s[rows, 0:1])
            add_vec(3, u * n)
            add_vec(4, u)
            g_s[rows, :] = g
            low = g.astype(BF16)
            db_s[rows, :] = low
            add_vec(2, low.astype(F32))
            return carry

        lax.fori_loop(0, ROWS // 128, first, 0)
        wload.wait()
        cload.wait()
        tr_s[...] = ctx_s[...].T

        def outer(j, carry):
            cols = ds(j * 256, 256)
            st_s[0, :, cols] = mm(tr_s[ds(j * 256, 256), :], db_s[...]).astype(BF16)[:, :256]
            return carry

        del outer
        for j in range(3):
            st_s[j] = mm(tr_s[j * 256 : (j + 1) * 256, :], db_s[...]).astype(BF16)
        for j in range(4):
            dctx_s[j * 256 : (j + 1) * 256, :] = mm_nt(db_s[j * 256 : (j + 1) * 256, :], wa_s[3]).astype(BF16)
        cs = [pltpu.make_async_copy(st_s.at[j], ga_h.at[3, j * 256 : (j + 1) * 256, :], g_sem.at[j]) for j in range(3)]
        for c in cs:
            c.start()
        for c in cs:
            c.wait()

    pl.run_scoped(
        tail,
        pltpu.VMEM((ROWS, D), F32),
        pltpu.VMEM((ROWS, 128), F32),
        pltpu.VMEM((ROWS, D), BF16),
        pltpu.VMEM((ROWS, D), BF16),
        pltpu.VMEM((2, ROWS, TILE), BF16),
        pltpu.VMEM((2, ROWS, TILE), BF16),
        pltpu.VMEM((2, D, TILE), BF16),
        pltpu.VMEM((2, TILE, D), BF16),
    )

    def attention(q_s, k_s, v_s, p_s, qt_s, dt_s, dq_s, dkt_s, dvt_s, far_s, bt_s):
        cs = [pltpu.make_async_copy(a, b, l_sem.at[2 + i]) for i, (a, b) in enumerate(((q_h, q_s), (k_h, k_s), (v_h, v_s)))]
        for c in cs:
            c.start()

        def fetch(hp, slot):
            return pltpu.make_async_copy(p_h.at[hp], p_s.at[slot], t_sem.at[slot])

        fetch(0, 0).start()
        for c in cs:
            c.wait()
        dt_s[...] = dctx_s[...].T
        for s in range(2):
            for hp in range(PAIRS):
                qt_s[s, hp] = q_s[s, hp].T

        def step(hp, carry):
            slot = (hp % 2)
            fetch(hp, slot).wait()

            @pl.when(hp + 1 < PAIRS)
            def _():
                fetch(hp + 1, 1 - slot).start()

            lane = lax.broadcasted_iota(jnp.int32, (SEQ, 128), 1)
            k, v = k_s[hp], v_s[hp]
            zero = jnp.zeros((SEQ, 128), BF16)
            dq = [None, None]
            for e in range(2):
                own = (lane < 64) if e == 0 else (lane >= 64)
                both = None
                dkt = dvt = None
                for s in range(2):
                    rows = slice(s * SEQ, (s + 1) * SEQ)
                    do = jnp.where(own, dctx_s[rows, ds(hp * 128, 128)], zero)
                    weight = jnp.sum(do.astype(F32) * ctx_s[rows, ds(hp * 128, 128)].astype(F32), axis=1, keepdims=True)
                    p = p_s[slot, e, s]
                    g = p.astype(F32) * (mm_nt(do, v) - weight)
                    low = g.astype(BF16)
                    both = g if both is None else both + g
                    part = mm(low, jnp.where(own, k, zero))
                    dq[s] = part if dq[s] is None else dq[s] + part
                    half = ds(hp * 128 + e * 64, 64)
                    a = mm(dt_s[half, rows], p)
                    b = mm(qt_s[s, hp, e * 64 : (e + 1) * 64, :], low)
                    dvt = a if dvt is None else dvt + a
                    dkt = b if dkt is None else dkt + b
                dvt_s[ds(hp * 128 + e * 64, 64), :] = dvt.astype(BF16)
                dkt_s[ds(hp * 128 + e * 64, 64), :] = (dkt * SCALE).astype(BF16)
                sums = [None] * 7
                for i in range(4):
                    for j in range(4):
                        blk = both[i * 128 : (i + 1) * 128, j * 128 : (j + 1) * 128]
                        at = min(max(j - i, -2), 2) + 2
                        sums[at] = blk if sums[at] is None else sums[at] + blk
                strip = jnp.concatenate([jnp.zeros((128, 128), F32), sums[1], sums[2], sums[3]], axis=1)
                flat = strip[0:8]
                for g in range(1, 16):
                    flat = flat + pltpu.roll(strip[8 * g : 8 * g + 8], 512 - 8 * g, 1)
                row = lax.broadcasted_iota(jnp.int32, (8, 512), 0)
                for bit in (1, 2, 4):
                    flat = jnp.where((row & bit) != 0, pltpu.roll(flat, 512 - bit, 1), flat)
                h = 2 * hp + e
                for ref, cols, value in (
                    (bt_s, slice(0, 512), flat),
                    (far_s, slice(0, 128), sums[0]),
                    (far_s, slice(128, 256), sums[4]),
                ):
                    line = jnp.sum(value, axis=0, keepdims=True)
                    mine = lax.broadcasted_iota(jnp.int32, (16, line.shape[1]), 0) == h
                    ref[:, cols] = jnp.where(mine, line, ref[:, cols])
            for s in range(2):
                dq_s[s * SEQ : (s + 1) * SEQ, ds(hp * 128, 128)] = (dq[s] * SCALE).astype(BF16)
            return carry

        bt_s[...] = jnp.zeros_like(bt_s)
        far_s[...] = jnp.zeros_like(far_s)
        lax.fori_loop(0, PAIRS, step, 0)

        offset = lax.broadcasted_iota(jnp.int32, (512, 128), 0) - 256
        bucket = lax.broadcasted_iota(jnp.int32, (512, 128), 1)
        near = jnp.where(bucket_of(offset) == bucket, 1.0, 0.0)
        lane = lax.broadcasted_iota(jnp.int32, (16, 128), 1)
        gtab_ref[...] = (
            lax.dot_general(bt_s[...], near, (((1,), (0,)), ((), ())), precision=lax.Precision.HIGHEST, preferred_element_type=F32)
            + jnp.where(lane == 15, jnp.sum(far_s[:, 0:128], axis=1, keepdims=True), 0.0)
            + jnp.where(lane == 31, jnp.sum(far_s[:, 128:256], axis=1, keepdims=True), 0.0)
        )

        dk = dkt_s[...].T
        dv = dvt_s[...].T
        add_vec(0, dq_s[...].astype(F32))
        add_vec(1, dv.astype(F32))
        tr_s[:, 0:SEQ] = x_ref[...].T
        tr_s[:, SEQ:] = y_ref[...].T
        slot = 0
        cs = []
        for w, grad in ((0, dq_s[...]), (1, dk), (2, dv)):
            left = tr_s[...] if w == 0 else tr_s[:, 0:SEQ]
            for j in range(3):
                if len(cs) >= 4:
                    cs[len(cs) - 4].wait()
                st_s[slot % 4] = mm(left[j * 256 : (j + 1) * 256, :], grad).astype(BF16)
                c = pltpu.make_async_copy(st_s.at[slot % 4], ga_h.at[w, j * 256 : (j + 1) * 256, :], g_sem.at[slot % 4])
                c.start()
                cs.append(c)
                slot += 1
        gc_ref[...] = g_s[0:SEQ, :] + mm_nt(dq_s[0:SEQ, :], wa_s[0]) + mm_nt(dk, wa_s[1]) + mm_nt(dv, wa_s[2])
        gq_ref[...] = g_s[SEQ:, :] + mm_nt(dq_s[SEQ:, :], wa_s[0])
        for c in cs[-4:]:
            c.wait()

    pl.run_scoped(
        attention,
        pltpu.VMEM((2, PAIRS, SEQ, 128), BF16),
        pltpu.VMEM((PAIRS, SEQ, 128), BF16),
        pltpu.VMEM((PAIRS, SEQ, 128), BF16),
        pltpu.VMEM((2, 2, 2, SEQ, SEQ), BF16),
        pltpu.VMEM((2, PAIRS, 128, SEQ), BF16),
        pltpu.VMEM((D, ROWS), BF16),
        pltpu.VMEM((ROWS, D), BF16),
        pltpu.VMEM((D, SEQ), BF16),
        pltpu.VMEM((D, SEQ), BF16),
        pltpu.VMEM((16, 256), F32),
        pltpu.VMEM((16, 512), F32),
    )


def call_backward(x, y, cc, cq, vecs, wa, wi, wo, saved):
    hbm = pl.BlockSpec(memory_space=pl.ANY)
    vmem = pl.BlockSpec(memory_space=pltpu.VMEM)
    shape = jax.ShapeDtypeStruct
    outs = (
        shape((SEQ, D), F32), shape((SEQ, D), F32),
        shape((4, D, D), BF16), shape((TILES, TILE, D), BF16), shape((FF, D), BF16),
        shape((16, D), F32), shape((16, 128), F32),
    )
    return pl.pallas_call(
        backward_kernel,
        out_shape=outs,
        in_specs=[vmem] * 5 + [hbm] * 15,
        out_specs=[vmem, vmem, hbm, hbm, hbm, vmem, vmem],
        scratch_shapes=[
            pltpu.VMEM((4, D, D), BF16), pltpu.VMEM((ROWS, D), BF16), pltpu.VMEM((ROWS, D), F32), pltpu.VMEM((ROWS, D), BF16),
            pltpu.VMEM((D, ROWS), BF16), pltpu.VMEM((4, TILE, D), BF16),
            pltpu.SemaphoreType.DMA((5,)), pltpu.SemaphoreType.DMA((8,)), pltpu.SemaphoreType.DMA((4,)),
        ],
        compiler_params=pltpu.CompilerParams(vmem_limit_bytes=VMEM_LIMIT),
        name="backward",
    )(x, y, cc, cq, vecs, wa, wi, wo, *saved)


def shards(
    content_stream, query_stream, lengths, ranking, query_weight, query_bias, key_weight, value_weight, value_bias,
    output_weight, output_bias, norm_gain, norm_shift, inner_weight, inner_bias, outer_weight, outer_bias, final_gain,
    final_shift, bucket_bias, content_cotangent, query_cotangent,
):
    def gather(a, axis=0):
        return lax.all_gather(a, "fsdp", axis=axis, tiled=True)

    wa = gather(jnp.stack([query_weight, key_weight, value_weight, output_weight]), 1)
    wi = gather(inner_weight)
    wo = gather(outer_weight)
    small = (query_bias, value_bias, output_bias, norm_gain, norm_shift, outer_bias, final_gain, final_shift)
    width = query_bias.shape[0]
    packed = jnp.concatenate([*small, inner_bias, bucket_bias])[None, :]
    packed = gather(packed)
    cuts = [packed[:, i * width : (i + 1) * width].reshape(1, D) for i in range(8)]
    at = 8 * width
    cuts.append(packed[:, at : at + inner_bias.shape[0]].reshape(4, D))
    at += inner_bias.shape[0]
    vecs = jnp.concatenate(cuts + [jnp.zeros((4, D), BF16)]).astype(F32)
    table = jnp.pad(packed[:, at:].reshape(HEADS, BUCKETS), ((0, 4), (0, 128 - BUCKETS)))

    out_c, out_q, *saved = call_forward(
        content_stream, query_stream, lengths, ranking, vecs, table, wa, wi, wo
    )
    gc, gq, ga, gi, go, gvec, gtab = call_backward(
        content_stream, query_stream, content_cotangent, query_cotangent, vecs, wa, wi, wo, saved
    )
    gi = gi.reshape(TILES, TILE, 3, TILE).transpose(2, 1, 0, 3).reshape(D, FF)

    def reduce(a, axis=0):
        a = lax.psum_scatter(a, "fsdp", scatter_dimension=axis, tiled=True)
        return lax.psum(a.astype(BF16), "rep").astype(F32)

    ga = reduce(ga, 1)
    gi = reduce(gi)
    go = reduce(go)
    count = D // width
    flat = jnp.concatenate(
        [gvec[i].reshape(count, width) for i in range(8)]
        + [gvec[8:12].reshape(count, 4 * width), gtab[:HEADS, :BUCKETS].reshape(count, -1)],
        axis=1,
    )
    flat = lax.psum_scatter(flat, "fsdp", scatter_dimension=0, tiled=True)[0]
    flat = lax.psum(flat.astype(BF16), "rep").astype(F32)
    v = [flat[i * width : (i + 1) * width] for i in range(8)]
    return (
        out_c, out_q, gc, gq, ga[0], v[0], ga[1], ga[2], v[1], ga[3], v[2], v[3], v[4], gi,
        flat[8 * width : 12 * width], go, v[5], v[6], v[7], flat[12 * width :],
    )


def solution(mesh):
    both, fsdp = ("rep", "fsdp"), "fsdp"
    row, vec = P(fsdp, None), P(fsdp)
    tokens = P(both, None)
    in_specs = (
        tokens, tokens, P(both), tokens, row, vec, row, row, vec, row, vec, vec, vec, row, vec, row, vec, vec, vec, vec,
        tokens, tokens,
    )
    out_specs = (
        tokens, tokens, tokens, tokens, row, vec, row, row, vec, row, vec, vec, vec, row, vec, row, vec, vec, vec, vec,
    )
    return jax.shard_map(shards, mesh=mesh, in_specs=in_specs, out_specs=out_specs, check_vma=False)
```

```python
import functools

import jax
import jax.numpy as jnp
from jax import lax
from jax.experimental import pallas as pl
from jax.experimental.pallas import tpu as pltpu
from jax.sharding import PartitionSpec as P

HEADS = 12
HEAD_DIM = 64
PAIRS = HEADS // 2
BUCKETS = 32
SEQ = 512
ROWS = 2 * SEQ
D = 768
FF = 3072
TILE = 256
TILES = FF // TILE
EPS = 1e-05
NEG = -1e30
LOG2E = 1.4426950408889634
SCALE = HEAD_DIM**-0.5
FAR_STEPS = (12, 16, 23, 32, 46, 64, 91)
F32 = jnp.float32
BF16 = jnp.bfloat16
VMEM_LIMIT = 60 * 2**20

TAIL_P = 0.28
TAIL = (
    0.11608706693762069,
    0.07021928496801585,
    0.26212226118724974,
    -0.22858899246095166,
    0.3847049667747488,
    -0.10454457204169064,
)


def mm(a, b):
    return jnp.dot(a, b, preferred_element_type=F32)


def mm_nt(a, b):
    return lax.dot_general(a, b, (((1,), (1,)), ((), ())), preferred_element_type=F32)


def mm_tn(a, b):
    return lax.dot_general(a, b, (((0,), (0,)), ((), ())), preferred_element_type=F32)


def bucket_of(offset):
    distance = jnp.abs(offset)
    farther = jnp.full(distance.shape, 8, jnp.int32)
    for step_at in FAR_STEPS:
        farther = farther + jnp.where(distance >= step_at, 1, 0)
    return jnp.where(distance < 8, distance, farther) + jnp.where(offset > 0, 16, 0)


def normal_parts(x):
    size = jnp.abs(x)
    t = 1.0 / (1.0 + TAIL_P * size)
    poly = jnp.full(x.shape, TAIL[-1], F32)
    for c in TAIL[-2::-1]:
        poly = poly * t + c
    bell = jnp.exp2(x * x * (-0.5 * LOG2E))
    tail = poly * t * bell
    return jnp.where(x < 0, tail, 1.0 - tail), bell * 0.3989422804014327


def ds(start, size):
    return pl.ds(pl.multiple_of(start, size), size)


def places():
    f = lax.axis_index("fsdp")
    return lax.axis_index("rep"), f // 2, f % 2


def hop(i, k):
    if k == 0:
        return i
    if k == 1:
        return i + 1 - 2 * (i % 2)
    return (i + 2) % 4 if k == 2 else 3 - i


def remote(src, dst, send, recv, device):
    return pltpu.make_async_remote_copy(
        src_ref=src, dst_ref=dst, send_sem=send, recv_sem=recv, device_id=device, device_id_type=pl.DeviceIdType.MESH
    )


def greet(devices):
    barrier = pltpu.get_barrier_semaphore()
    for device in devices:
        pl.semaphore_signal(barrier, inc=1, device_id=device, device_id_type=pl.DeviceIdType.MESH)
    pl.semaphore_wait(barrier, len(devices))


class Gather:
    def __init__(self, refs, sems):
        self.wa, self.wi, self.wo, self.small = refs
        self.l_sem, self.zs, self.zr, self.xs, self.xr, self.cs, self.cr, self.vs, self.vr = sems
        self.r, self.z, self.c = places()

    def block(self, t, r, z, c):
        if t == 2:
            return self.wo.at[z, pl.ds(pl.multiple_of(c * 384 + r * 96, 96), 96), :]
        return (self.wa, self.wi)[t].at[r, z, ds(c * 96, 96), :]

    def slab(self, t, r, c):
        if t == 2:
            return self.wo.at[:, pl.ds(pl.multiple_of(c * 384 + r * 96, 96), 96), :]
        return (self.wa, self.wi)[t].at[r, :, ds(c * 96, 96), :]

    def own(self, shards):
        *square, inner, outer = shards
        z, c = self.z, self.c
        copies = [
            [pltpu.make_async_copy(square[m], self.block(0, m, z, c), self.l_sem.at[0, m]) for m in range(4)],
            [
                pltpu.make_async_copy(inner.at[:, m * D : (m + 1) * D], self.block(1, m, z, c), self.l_sem.at[1, m])
                for m in range(4)
            ],
            [pltpu.make_async_copy(outer, self.wo.at[z, ds(c * 384, 384), :], self.l_sem.at[2, 0])],
        ]
        return copies

    def small_copy(self, k):
        f = 2 * self.z + self.c
        return remote(
            self.small.at[f], self.small.at[f], self.vs.at[k - 1], self.vr.at[k - 1], (self.r, (f + k) % 8)
        )

    def small_come(self, k):
        f = (2 * self.z + self.c + 8 - k) % 8
        return remote(self.small.at[f], self.small.at[f], self.vs.at[k - 1], self.vr.at[k - 1], (self.r, f))

    def z_copy(self, t, k, come=False):
        far = hop(self.z, k)
        ref = self.block(t, self.r, far if come else self.z, self.c)
        return remote(ref, ref, self.zs.at[t, k - 1], self.zr.at[t, k - 1], (self.r, 2 * far + self.c))

    def x_copy(self, t, k, m, come=False):
        far = hop(self.r, m)
        ref = self.block(t, far if come else self.r, hop(self.z, k), self.c)
        at = 3 * (k - 1) + m - 1
        return remote(ref, ref, self.xs.at[t, at], self.xr.at[t, at], (far, 2 * self.z + self.c))

    def c_copy(self, t, m, come=False):
        ref = self.slab(t, hop(self.r, m), 1 - self.c if come else self.c)
        return remote(ref, ref, self.cs.at[t, m], self.cr.at[t, m], (self.r, 2 * self.z + 1 - self.c))

    def start_z(self, t):
        for k in (1, 2, 3):
            self.z_copy(t, k).start()

    def pass_on(self, t):
        for k in (1, 2, 3):
            self.z_copy(t, k, True).wait_recv()
            for m in (1, 2, 3):
                self.x_copy(t, k, m).start()

    def share(self, t):
        for m in range(4):
            if m:
                for k in (1, 2, 3):
                    self.x_copy(t, k, m, True).wait_recv()
            self.c_copy(t, m).start()

    def finish(self, t):
        for m in range(4):
            self.c_copy(t, m, True).wait_recv()

    def drain(self):
        for k in range(1, 8):
            self.small_copy(k).wait_send()
        for t in range(3):
            for k in (1, 2, 3):
                self.z_copy(t, k).wait_send()
                for m in (1, 2, 3):
                    self.x_copy(t, k, m).wait_send()
            for m in range(4):
                self.c_copy(t, m).wait_send()


def unpack_small(small_s, vec_s):
    blocks = [small_s[f] for f in range(8)]
    at = lax.broadcasted_iota(jnp.int32, (1024, D), 0)
    want = lax.broadcasted_iota(jnp.int32, (1024, D), 1)
    spread = jnp.where((at % 128 < 96) & (want == (at // 128) * 96 + at % 128), 1.0, 0.0).astype(BF16)
    vec_s[...] = mm(jnp.concatenate(blocks, axis=1), spread)
    wide = [b.astype(F32) for b in blocks]
    for m in range(4):
        for j in range(6):
            vec_s[8 + m : 9 + m, j * 128 : (j + 1) * 128] = wide[2 * m + j // 3][8 + j % 3 : 9 + j % 3]
    return [w[11:12] for w in wide]


def lines_of(rows):
    bucket = bucket_of(lax.broadcasted_iota(jnp.int32, (128, 1024), 1) - 512)
    entry = lax.broadcasted_iota(jnp.int32, (128, 1024), 0)

    def pick(first, shift):
        inside = (entry >= first) & (entry < 48)
        return jnp.where(inside & (bucket == entry + shift), 1.0, 0.0).astype(BF16)

    table = jnp.concatenate(rows, axis=0).astype(BF16)
    a0, a1, b1, b2 = (mm(table, pick(*p)) for p in ((0, 0), (32, -32), (0, 16), (16, -16)))
    lines = []
    for m in range(4):
        i, j = 2 * m, 2 * m + 1
        lines += [a0[i : i + 1], a1[i : i + 1] + b1[j : j + 1], b2[j : j + 1]]
    return [line * LOG2E for line in lines]


def build_masks(len_ref, rank_ref, mask_s):
    n = len_ref[0]
    rank = rank_ref[...]
    place = lax.broadcasted_iota(jnp.int32, (1, SEQ), 1)
    valid = place < n
    chosen = valid & (rank >= n - 3 * n // 20)
    key = jnp.where(chosen, rank, jnp.where(valid, -1, 2 * SEQ)).astype(F32)
    column = jnp.broadcast_to(rank.astype(F32), (128, SEQ)).T
    for s in range(2):
        for j in range(SEQ // 128):
            seen = jnp.broadcast_to(key[:, j * 128 : (j + 1) * 128], (SEQ, 128)) <= column - s
            mask_s[s, :, j * 128 : (j + 1) * 128] = jnp.where(seen, 0.0, NEG)


def lines_of_table(tab_ref):
    offset = lax.broadcasted_iota(jnp.int32, (128, 1024), 1) - 512
    bucket = lax.broadcasted_iota(jnp.int32, (128, 1024), 0)
    onehot = jnp.where(bucket_of(offset) == bucket, 1.0, 0.0).astype(BF16)
    line = mm(tab_ref[...], onehot) * LOG2E
    return [line[h : h + 1] for h in range(HEADS)]


def build_strip(lines, strip_s):
    for h in range(HEADS):
        wide = jnp.broadcast_to(lines[h], (128, 1024))
        strip_s[h] = pltpu.roll(wide, 0, 1, stride=1, stride_axis=0)[:, 128:]


def square(w_s, m, cols=slice(None)):
    block = w_s[m, :, :, cols]
    return block.reshape(D, block.shape[-1])


def project(x_ref, y_ref, vec_ref, w_s, q_s, k_s, v_s):
    for pair in range(0, PAIRS, 2):
        cols = slice(pair * 128, pair * 128 + 256)
        x = x_ref[...]
        parts = (
            (q_s, 0, mm(x, square(w_s, 0, cols)) + vec_ref[0:1, cols]),
            (q_s, 1, mm(y_ref[...], square(w_s, 0, cols)) + vec_ref[0:1, cols]),
            (k_s, None, mm(x, square(w_s, 1, cols))),
            (v_s, None, mm(x, square(w_s, 2, cols)) + vec_ref[1:2, cols]),
        )
        for ref, s, value in parts:
            value = value.astype(BF16)
            for e in range(2):
                piece = value[:, e * 128 : (e + 1) * 128]
                if s is None:
                    ref[pair + e] = piece
                else:
                    ref[s, pair + e] = piece


def attend(q_s, k_s, v_s, strip_s, mask_s, p_st, ctx_s, hp, slot):
    lane = lax.broadcasted_iota(jnp.int32, (SEQ, 128), 1)
    k = k_s[hp]
    v = v_s[hp]
    for s in range(2):
        q = q_s[s, hp]
        outs = []
        for e in range(2):
            own = (lane < 64) if e == 0 else (lane >= 64)
            scores = mm_nt(jnp.where(own, q, jnp.zeros_like(q)), k)
            for i in range(SEQ // 128):
                rows = slice(i * 128, (i + 1) * 128)
                blk = (
                    scores[rows] * (SCALE * LOG2E)
                    + strip_s[2 * hp + e, :, (3 - i) * 128 : (3 - i) * 128 + SEQ]
                    + mask_s[s, rows, :]
                )
                top = jnp.max(blk, axis=1, keepdims=True)
                w = jnp.exp2(blk - top)
                w = w * (1.0 / jnp.sum(w, axis=1, keepdims=True))
                p_st[slot, e, s, rows, :] = w.astype(BF16)
            outs.append(mm(p_st[slot, e, s], v))
        ctx_s[s * SEQ : (s + 1) * SEQ, ds(hp * 128, 128)] = jnp.where(
            lane < 64, outs[0], outs[1]
        ).astype(BF16)


def norm_stats(r):
    mean = jnp.mean(r, axis=1, keepdims=True)
    centred = r - mean
    inverse = lax.rsqrt(jnp.mean(centred * centred, axis=1, keepdims=True) + EPS)
    return centred * inverse, inverse


NETWORK = {
    0: (("pass_on", 1), ("start_z", 2)),
    2: (("share", 1),),
    3: (("pass_on", 2),),
    5: (("share", 2),),
}


def forward_kernel(linked, *refs):
    refs = list(refs)
    take = lambda n: [refs.pop(0) for _ in range(n)]
    x_ref, y_ref, len_ref, rank_ref = take(4)
    if linked:
        (small_ref,) = take(1)
        shards = take(6)
    else:
        vec_ref, tab_ref, *weights = take(5)
    oc_ref, oq_ref, q_h, k_h, v_h, p_h, ctx_h, n1_h, inv1_h, nl_h, act_h, slope_h, n2_h, inv2_h = take(14)
    if linked:
        vec_h, *weights = take(4)
    wa_s, wi_s, wo_s, q_s, k_s, v_s, ctx_s, nl_s, n1_s, br_s, inv1_s, inv2_s, o_sem, st_sem, w_sem = take(15)
    copies = (wa_s, wi_s, wo_s)
    if linked:
        small_s, vec_ref, *sems = take(10)
        net = Gather((wa_s, wi_s, wo_s, small_s), (w_sem, *sems))
        r, z, c = places()
        f = 2 * z + c
        own = net.own(shards)
        for batch in own:
            for copy in batch:
                copy.start()
        small_s[f] = small_ref[...]
        greet(
            [(hop(r, m), f) for m in (1, 2, 3)] + [(r, (f + k) % 8) for k in range(1, 8)]
        )
        for k in range(1, 8):
            net.small_copy(k).start()
        for copy in own[0]:
            copy.wait()
        net.start_z(0)
    else:
        loads = [pltpu.make_async_copy(src, dst, w_sem.at[i, 0]) for i, (src, dst) in enumerate(zip(weights, copies))]
        for copy in loads:
            copy.start()
    stores = []

    def keep(src, dst):
        pltpu.make_async_copy(src, dst, o_sem.at[len(stores)]).start()
        stores.append((src, dst))

    def attention(strip_s, mask_s, p_st):
        build_masks(len_ref, rank_ref, mask_s)
        if linked:
            for k in range(1, 8):
                net.small_come(k).wait_recv()
            build_strip(lines_of(unpack_small(small_s, vec_ref)), strip_s)
            net.pass_on(0)
            for copy in own[1] + own[2]:
                copy.wait()
            net.start_z(1)
            net.share(0)
            net.finish(0)
            keep(vec_ref, vec_h)
            keep(wa_s, weights[0])
        else:
            build_strip(lines_of_table(tab_ref), strip_s)
            loads[0].wait()
        project(x_ref, y_ref, vec_ref, wa_s, q_s, k_s, v_s)
        keep(q_s, q_h)
        keep(k_s, k_h)
        keep(v_s, v_h)

        def store(hp, slot):
            return pltpu.make_async_copy(p_st.at[slot], p_h.at[hp], st_sem.at[slot])

        def step(hp, carry):
            slot = (hp % 2)

            @pl.when(hp >= 2)
            def _():
                store(hp - 2, slot).wait()

            if linked:
                for at, moves in NETWORK.items():
                    @pl.when(hp == at)
                    def _(moves=moves):
                        for name, t in moves:
                            getattr(net, name)(t)

            attend(q_s, k_s, v_s, strip_s, mask_s, p_st, ctx_s, hp, slot)
            store(hp, slot).start()
            return carry

        lax.fori_loop(0, PAIRS, step, 0)
        store(PAIRS - 2, 0).wait()
        store(PAIRS - 1, 1).wait()

    pl.run_scoped(
        attention,
        pltpu.VMEM((HEADS, 128, 896), F32),
        pltpu.VMEM((2, SEQ, SEQ), F32),
        pltpu.VMEM((2, 2, 2, SEQ, SEQ), BF16),
    )
    keep(ctx_s, ctx_h)

    for s, in_ref in ((0, x_ref), (1, y_ref)):
        def first(i, carry, s=s, in_ref=in_ref):
            own = ds(i * 256, 256)
            rows = ds(s * SEQ + i * 256, 256)
            r = in_ref[own, :].astype(F32) + mm(ctx_s[rows, :], square(wa_s, 3)) + vec_ref[2:3, :]
            n, inverse = norm_stats(r)
            n1_s[rows, :] = n
            inv1_s[rows, :] = jnp.broadcast_to(inverse, (256, 128))
            nl_s[rows, :] = (n * vec_ref[3:4, :] + vec_ref[4:5, :]).astype(BF16)
            return carry

        lax.fori_loop(0, SEQ // 256, first, 0)
    keep(n1_s, n1_h)
    keep(inv1_s, inv1_h)
    keep(nl_s, nl_h)

    if linked:
        net.finish(1)
        net.finish(2)
        keep(wi_s, weights[1])
        keep(wo_s, weights[2])
    else:
        loads[1].wait()
        loads[2].wait()
    br_s[...] = jnp.zeros_like(br_s)

    def feed(act_st, slope_st):
        def pair(t, slot):
            return (
                pltpu.make_async_copy(act_st.at[slot], act_h.at[t], st_sem.at[slot]),
                pltpu.make_async_copy(slope_st.at[slot], slope_h.at[t], st_sem.at[2 + slot]),
            )

        def step(t, carry):
            slot = (t % 2)

            @pl.when(t >= 2)
            def _():
                for c in pair(t - 2, slot):
                    c.wait()

            part = ds((t % 3) * TILE, TILE)
            inner = mm(nl_s[...], square(wi_s, t // 3, part)) + vec_ref[pl.ds(8 + (t // 3), 1), ds((t % 3) * TILE, TILE)]
            spread, bell = normal_parts(inner)
            act = (inner * spread).astype(BF16)
            act_st[slot] = act
            slope_st[slot] = (spread + inner * bell).astype(BF16)
            br_s[...] += mm(act, wo_s[t // 3, part, :])
            for c in pair(t, slot):
                c.start()
            return carry

        lax.fori_loop(0, TILES, step, 0)
        for t in (TILES - 2, TILES - 1):
            for c in pair(t, t % 2):
                c.wait()

    pl.run_scoped(feed, pltpu.VMEM((2, ROWS, TILE), BF16), pltpu.VMEM((2, ROWS, TILE), BF16))

    for s, o_ref in ((0, oc_ref), (1, oq_ref)):
        def last(i, carry, s=s, o_ref=o_ref):
            rows = ds(s * SEQ + i * 128, 128)
            normed = n1_s[rows, :] * vec_ref[3:4, :] + vec_ref[4:5, :]
            n, inverse = norm_stats(normed + br_s[rows, :] + vec_ref[5:6, :])
            br_s[rows, :] = n
            inv2_s[rows, :] = jnp.broadcast_to(inverse, (128, 128))
            o_ref[ds(i * 128, 128), :] = (n * vec_ref[6:7, :] + vec_ref[7:8, :]).astype(BF16)
            return carry

        lax.fori_loop(0, SEQ // 128, last, 0)
    keep(br_s, n2_h)
    keep(inv2_s, inv2_h)
    for i, (src, dst) in enumerate(stores):
        pltpu.make_async_copy(src, dst, o_sem.at[i]).wait()
    if linked:
        net.drain()


WEIGHTS = ((4, 4, 192, D), (4, 4, 192, D), (4, D, D))


def call_forward(linked, *args):
    hbm = pl.BlockSpec(memory_space=pl.ANY)
    vmem = pl.BlockSpec(memory_space=pltpu.VMEM)
    smem = pl.BlockSpec(memory_space=pltpu.SMEM)
    dma = pltpu.SemaphoreType.DMA
    shape = jax.ShapeDtypeStruct
    outs = [
        shape((SEQ, D), BF16), shape((SEQ, D), BF16),
        shape((2, PAIRS, SEQ, 128), BF16), shape((PAIRS, SEQ, 128), BF16), shape((PAIRS, SEQ, 128), BF16),
        shape((PAIRS, 2, 2, SEQ, SEQ), BF16), shape((ROWS, D), BF16),
        shape((ROWS, D), F32), shape((ROWS, 128), F32), shape((ROWS, D), BF16),
        shape((TILES, ROWS, TILE), BF16), shape((TILES, ROWS, TILE), BF16),
        shape((ROWS, D), F32), shape((ROWS, 128), F32),
    ]
    scratch = [pltpu.VMEM(w, BF16) for w in WEIGHTS] + [
        pltpu.VMEM((2, PAIRS, SEQ, 128), BF16), pltpu.VMEM((PAIRS, SEQ, 128), BF16), pltpu.VMEM((PAIRS, SEQ, 128), BF16),
        pltpu.VMEM((ROWS, D), BF16), pltpu.VMEM((ROWS, D), BF16), pltpu.VMEM((ROWS, D), F32), pltpu.VMEM((ROWS, D), F32),
        pltpu.VMEM((ROWS, 128), F32), pltpu.VMEM((ROWS, 128), F32),
        dma((13,)), dma((4,)), dma((3, 4)),
    ]
    in_specs = [vmem, vmem, smem, vmem]
    if linked:
        in_specs += [vmem] + [hbm] * 6
        outs += [shape((16, D), F32)] + [shape(w, BF16) for w in WEIGHTS]
        scratch += [
            pltpu.VMEM((8, 16, 128), BF16), pltpu.VMEM((16, D), F32),
            dma((3, 3)), dma((3, 3)), dma((3, 9)), dma((3, 9)), dma((3, 4)), dma((3, 4)), dma((7,)), dma((7,)),
        ]
        params = pltpu.CompilerParams(vmem_limit_bytes=VMEM_LIMIT, collective_id=1, has_side_effects=True)
    else:
        in_specs += [vmem, vmem] + [hbm] * 3
        params = pltpu.CompilerParams(vmem_limit_bytes=VMEM_LIMIT)
    return pl.pallas_call(
        functools.partial(forward_kernel, linked),
        out_shape=outs,
        in_specs=in_specs,
        out_specs=[vmem, vmem] + [hbm] * (len(outs) - 2),
        scratch_shapes=scratch,
        compiler_params=params,
        name="forward",
    )(*args)


def norm_grad(u, gain, n, inverse):
    ug = u * gain
    return inverse * (
        ug - jnp.mean(ug, axis=1, keepdims=True) - n * jnp.mean(ug * n, axis=1, keepdims=True)
    )


def backward_kernel(
    x_ref, y_ref, cc_ref, cq_ref, vec_ref, wa_h, wi_h, wo_h,
    q_h, k_h, v_h, p_h, ctx_h, n1_h, inv1_h, nl_h, act_h, slope_h, n2_h, inv2_h,
    gc_ref, gq_ref, ga_h, gi_h, go_h, gvec_ref, gtab_ref,
    wa_s, ctx_s, g_s, dctx_s, tr_s, st_s, l_sem, t_sem, g_sem,
):
    wload = pltpu.make_async_copy(wa_h, wa_s, l_sem.at[0])
    cload = pltpu.make_async_copy(ctx_h, ctx_s, l_sem.at[1])
    wload.start()
    cload.start()
    gvec_ref[...] = jnp.zeros_like(gvec_ref)

    def add_vec(row, value, cols=slice(None)):
        gvec_ref[row : row + 1, cols] += jnp.sum(value, axis=0, keepdims=True)

    def tail(n_s, inv_s, nl_s, db_s, act_s, slope_s, wi_s, wo_s):
        nload = pltpu.make_async_copy(n2_h, n_s, l_sem.at[2])
        iload = pltpu.make_async_copy(inv2_h, inv_s, l_sem.at[3])
        nlload = pltpu.make_async_copy(nl_h, nl_s, l_sem.at[4])
        nload.start()
        iload.start()
        nlload.start()

        def fetch(t, slot):
            return (
                pltpu.make_async_copy(act_h.at[t], act_s.at[slot], t_sem.at[slot]),
                pltpu.make_async_copy(slope_h.at[t], slope_s.at[slot], t_sem.at[2 + slot]),
                pltpu.make_async_copy(wi_h.at[t // 3, :, :, ds((t % 3) * TILE, TILE)], wi_s.at[slot], t_sem.at[4 + slot]),
                pltpu.make_async_copy(wo_h.at[t // 3, ds((t % 3) * TILE, TILE), :], wo_s.at[slot], t_sem.at[6 + slot]),
            )

        for c in fetch(0, 0):
            c.start()
        nload.wait()
        iload.wait()
        for s, cot in ((0, cc_ref), (1, cq_ref)):
            def second(i, carry, s=s, cot=cot):
                rows = ds(s * SEQ + i * 128, 128)
                u = cot[ds(i * 128, 128), :].astype(F32)
                n = n_s[rows, :]
                g = norm_grad(u, vec_ref[6:7, :], n, inv_s[rows, 0:1])
                add_vec(6, u * n)
                add_vec(7, u)
                g_s[rows, :] = g
                low = g.astype(BF16)
                db_s[rows, :] = low
                add_vec(5, low.astype(F32))
                return carry

            lax.fori_loop(0, SEQ // 128, second, 0)
        n1load = pltpu.make_async_copy(n1_h, n_s, l_sem.at[2])
        i1load = pltpu.make_async_copy(inv1_h, inv_s, l_sem.at[3])
        n1load.start()
        i1load.start()
        nlload.wait()
        tr_s[...] = nl_s[...].T

        def out_copies(t, slot):
            return (
                pltpu.make_async_copy(st_s.at[slot], go_h.at[ds(t * TILE, TILE), :], g_sem.at[slot]),
                pltpu.make_async_copy(st_s.at[2 + slot, :, :], gi_h.at[t], g_sem.at[2 + slot]),
            )

        def step(t, carry):
            slot = (t % 2)
            for c in fetch(t, slot):
                c.wait()

            @pl.when(t + 1 < TILES)
            def _():
                for c in fetch(t + 1, 1 - slot):
                    c.start()

            @pl.when(t >= 2)
            def _():
                for c in out_copies(t - 2, slot):
                    c.wait()

            db = db_s[...]
            di = (mm_nt(db, wo_s[slot]) * slope_s[slot].astype(F32)).astype(BF16)
            row, cols = (t // 3), ds((t % 3) * TILE, TILE)
            mine = lax.broadcasted_iota(jnp.int32, (8, TILE), 0) == row
            gvec_ref[8:16, cols] += jnp.where(mine, jnp.sum(di.astype(F32), axis=0, keepdims=True), 0.0)
            st_s[slot] = mm_tn(act_s[slot], db).astype(BF16)
            gin = mm(tr_s[...], di).astype(BF16)
            for j in range(3):
                st_s[2 + slot, :, j * 256 : (j + 1) * 256] = gin[j * 256 : (j + 1) * 256, :]
            g_s[...] += mm_nt(di, wi_s[slot].reshape(D, TILE))
            for c in out_copies(t, slot):
                c.start()
            return carry

        lax.fori_loop(0, TILES, step, 0)
        for t in (TILES - 2, TILES - 1):
            for c in out_copies(t, t % 2):
                c.wait()

        n1load.wait()
        i1load.wait()

        def first(i, carry):
            rows = ds(i * 128, 128)
            u = g_s[rows, :]
            n = n_s[rows, :]
            g = norm_grad(u, vec_ref[3:4, :], n, inv_s[rows, 0:1])
            add_vec(3, u * n)
            add_vec(4, u)
            g_s[rows, :] = g
            low = g.astype(BF16)
            db_s[rows, :] = low
            add_vec(2, low.astype(F32))
            return carry

        lax.fori_loop(0, ROWS // 128, first, 0)
        wload.wait()
        cload.wait()
        tr_s[...] = ctx_s[...].T

        def outer(j, carry):
            cols = ds(j * 256, 256)
            st_s[0, :, cols] = mm(tr_s[ds(j * 256, 256), :], db_s[...]).astype(BF16)[:, :256]
            return carry

        del outer
        for j in range(3):
            st_s[j] = mm(tr_s[j * 256 : (j + 1) * 256, :], db_s[...]).astype(BF16)
        for j in range(4):
            dctx_s[j * 256 : (j + 1) * 256, :] = mm_nt(db_s[j * 256 : (j + 1) * 256, :], square(wa_s, 3)).astype(BF16)
        cs = [pltpu.make_async_copy(st_s.at[j], ga_h.at[3, j * 256 : (j + 1) * 256, :], g_sem.at[j]) for j in range(3)]
        for c in cs:
            c.start()
        for c in cs:
            c.wait()

    pl.run_scoped(
        tail,
        pltpu.VMEM((ROWS, D), F32),
        pltpu.VMEM((ROWS, 128), F32),
        pltpu.VMEM((ROWS, D), BF16),
        pltpu.VMEM((ROWS, D), BF16),
        pltpu.VMEM((2, ROWS, TILE), BF16),
        pltpu.VMEM((2, ROWS, TILE), BF16),
        pltpu.VMEM((2, 4, 192, TILE), BF16),
        pltpu.VMEM((2, TILE, D), BF16),
    )

    def attention(q_s, k_s, v_s, p_s, qt_s, dt_s, dq_s, dkt_s, dvt_s, far_s, bt_s):
        cs = [pltpu.make_async_copy(a, b, l_sem.at[2 + i]) for i, (a, b) in enumerate(((q_h, q_s), (k_h, k_s), (v_h, v_s)))]
        for c in cs:
            c.start()

        def fetch(hp, slot):
            return pltpu.make_async_copy(p_h.at[hp], p_s.at[slot], t_sem.at[slot])

        fetch(0, 0).start()
        for c in cs:
            c.wait()
        dt_s[...] = dctx_s[...].T
        for s in range(2):
            for hp in range(PAIRS):
                qt_s[s, hp] = q_s[s, hp].T

        def step(hp, carry):
            slot = (hp % 2)
            fetch(hp, slot).wait()

            @pl.when(hp + 1 < PAIRS)
            def _():
                fetch(hp + 1, 1 - slot).start()

            lane = lax.broadcasted_iota(jnp.int32, (SEQ, 128), 1)
            k, v = k_s[hp], v_s[hp]
            zero = jnp.zeros((SEQ, 128), BF16)
            dq = [None, None]
            for e in range(2):
                own = (lane < 64) if e == 0 else (lane >= 64)
                both = None
                dkt = dvt = None
                for s in range(2):
                    rows = slice(s * SEQ, (s + 1) * SEQ)
                    do = jnp.where(own, dctx_s[rows, ds(hp * 128, 128)], zero)
                    weight = jnp.sum(do.astype(F32) * ctx_s[rows, ds(hp * 128, 128)].astype(F32), axis=1, keepdims=True)
                    p = p_s[slot, e, s]
                    g = p.astype(F32) * (mm_nt(do, v) - weight)
                    low = g.astype(BF16)
                    both = g if both is None else both + g
                    part = mm(low, jnp.where(own, k, zero))
                    dq[s] = part if dq[s] is None else dq[s] + part
                    half = ds(hp * 128 + e * 64, 64)
                    a = mm(dt_s[half, rows], p)
                    b = mm(qt_s[s, hp, e * 64 : (e + 1) * 64, :], low)
                    dvt = a if dvt is None else dvt + a
                    dkt = b if dkt is None else dkt + b
                dvt_s[ds(hp * 128 + e * 64, 64), :] = dvt.astype(BF16)
                dkt_s[ds(hp * 128 + e * 64, 64), :] = (dkt * SCALE).astype(BF16)
                sums = [None] * 7
                for i in range(4):
                    for j in range(4):
                        blk = both[i * 128 : (i + 1) * 128, j * 128 : (j + 1) * 128]
                        at = min(max(j - i, -2), 2) + 2
                        sums[at] = blk if sums[at] is None else sums[at] + blk
                strip = jnp.concatenate([jnp.zeros((128, 128), F32), sums[1], sums[2], sums[3]], axis=1)
                flat = strip[0:8]
                for g in range(1, 16):
                    flat = flat + pltpu.roll(strip[8 * g : 8 * g + 8], 512 - 8 * g, 1)
                row = lax.broadcasted_iota(jnp.int32, (8, 512), 0)
                for bit in (1, 2, 4):
                    flat = jnp.where((row & bit) != 0, pltpu.roll(flat, 512 - bit, 1), flat)
                h = 2 * hp + e
                for ref, cols, value in (
                    (bt_s, slice(0, 512), flat),
                    (far_s, slice(0, 128), sums[0]),
                    (far_s, slice(128, 256), sums[4]),
                ):
                    line = jnp.sum(value, axis=0, keepdims=True)
                    mine = lax.broadcasted_iota(jnp.int32, (16, line.shape[1]), 0) == h
                    ref[:, cols] = jnp.where(mine, line, ref[:, cols])
            for s in range(2):
                dq_s[s * SEQ : (s + 1) * SEQ, ds(hp * 128, 128)] = (dq[s] * SCALE).astype(BF16)
            return carry

        bt_s[...] = jnp.zeros_like(bt_s)
        far_s[...] = jnp.zeros_like(far_s)
        lax.fori_loop(0, PAIRS, step, 0)

        offset = lax.broadcasted_iota(jnp.int32, (512, 128), 0) - 256
        bucket = lax.broadcasted_iota(jnp.int32, (512, 128), 1)
        near = jnp.where(bucket_of(offset) == bucket, 1.0, 0.0)
        lane = lax.broadcasted_iota(jnp.int32, (16, 128), 1)
        gtab_ref[...] = (
            lax.dot_general(bt_s[...], near, (((1,), (0,)), ((), ())), precision=lax.Precision.HIGHEST, preferred_element_type=F32)
            + jnp.where(lane == 15, jnp.sum(far_s[:, 0:128], axis=1, keepdims=True), 0.0)
            + jnp.where(lane == 31, jnp.sum(far_s[:, 128:256], axis=1, keepdims=True), 0.0)
        )

        dk = dkt_s[...].T
        dv = dvt_s[...].T
        add_vec(0, dq_s[...].astype(F32))
        add_vec(1, dv.astype(F32))
        tr_s[:, 0:SEQ] = x_ref[...].T
        tr_s[:, SEQ:] = y_ref[...].T
        slot = 0
        cs = []
        for w, grad in ((0, dq_s[...]), (1, dk), (2, dv)):
            left = tr_s[...] if w == 0 else tr_s[:, 0:SEQ]
            for j in range(3):
                if len(cs) >= 4:
                    cs[len(cs) - 4].wait()
                st_s[slot % 4] = mm(left[j * 256 : (j + 1) * 256, :], grad).astype(BF16)
                c = pltpu.make_async_copy(st_s.at[slot % 4], ga_h.at[w, j * 256 : (j + 1) * 256, :], g_sem.at[slot % 4])
                c.start()
                cs.append(c)
                slot += 1
        gc_ref[...] = g_s[0:SEQ, :] + mm_nt(dq_s[0:SEQ, :], square(wa_s, 0)) + mm_nt(dk, square(wa_s, 1)) + mm_nt(dv, square(wa_s, 2))
        gq_ref[...] = g_s[SEQ:, :] + mm_nt(dq_s[SEQ:, :], square(wa_s, 0))
        for c in cs[-4:]:
            c.wait()

    pl.run_scoped(
        attention,
        pltpu.VMEM((2, PAIRS, SEQ, 128), BF16),
        pltpu.VMEM((PAIRS, SEQ, 128), BF16),
        pltpu.VMEM((PAIRS, SEQ, 128), BF16),
        pltpu.VMEM((2, 2, 2, SEQ, SEQ), BF16),
        pltpu.VMEM((2, PAIRS, 128, SEQ), BF16),
        pltpu.VMEM((D, ROWS), BF16),
        pltpu.VMEM((ROWS, D), BF16),
        pltpu.VMEM((D, SEQ), BF16),
        pltpu.VMEM((D, SEQ), BF16),
        pltpu.VMEM((16, 256), F32),
        pltpu.VMEM((16, 512), F32),
    )


def call_backward(x, y, cc, cq, vecs, wa, wi, wo, saved):
    hbm = pl.BlockSpec(memory_space=pl.ANY)
    vmem = pl.BlockSpec(memory_space=pltpu.VMEM)
    shape = jax.ShapeDtypeStruct
    outs = (
        shape((SEQ, D), F32), shape((SEQ, D), F32),
        shape((4, D, D), BF16), shape((TILES, TILE, D), BF16), shape((FF, D), BF16),
        shape((16, D), F32), shape((16, 128), F32),
    )
    return pl.pallas_call(
        backward_kernel,
        out_shape=outs,
        in_specs=[vmem] * 5 + [hbm] * 15,
        out_specs=[vmem, vmem, hbm, hbm, hbm, vmem, vmem],
        scratch_shapes=[
            pltpu.VMEM(WEIGHTS[0], BF16), pltpu.VMEM((ROWS, D), BF16), pltpu.VMEM((ROWS, D), F32), pltpu.VMEM((ROWS, D), BF16),
            pltpu.VMEM((D, ROWS), BF16), pltpu.VMEM((4, TILE, D), BF16),
            pltpu.SemaphoreType.DMA((5,)), pltpu.SemaphoreType.DMA((8,)), pltpu.SemaphoreType.DMA((4,)),
        ],
        compiler_params=pltpu.CompilerParams(vmem_limit_bytes=VMEM_LIMIT),
        name="backward",
    )(x, y, cc, cq, vecs, wa, wi, wo, *saved)


def shards(
    content_stream, query_stream, lengths, ranking, query_weight, query_bias, key_weight, value_weight, value_bias,
    output_weight, output_bias, norm_gain, norm_shift, inner_weight, inner_bias, outer_weight, outer_bias, final_gain,
    final_shift, bucket_bias, content_cotangent, query_cotangent,
):
    small = (query_bias, value_bias, output_bias, norm_gain, norm_shift, outer_bias, final_gain, final_shift)
    width = query_bias.shape[0]
    linked = width * 8 == D and lax.axis_size("rep") == 4
    front = (content_stream, query_stream, lengths, ranking)
    if linked:
        rows = jnp.pad(jnp.stack(small), ((0, 0), (0, 128 - width)))
        rest = jnp.pad(bucket_bias, (0, 128 - bucket_bias.shape[0])).reshape(1, 128)
        packed = jnp.concatenate([rows, inner_bias.reshape(3, 128), rest, jnp.zeros((4, 128), BF16)])
        out_c, out_q, *saved, vecs, wa, wi, wo = call_forward(
            True, *front, packed, query_weight, key_weight, value_weight, output_weight, inner_weight, outer_weight
        )
    else:
        def gather(a, axis=0):
            return lax.all_gather(a, "fsdp", axis=axis, tiled=True)

        wa = gather(jnp.stack([query_weight, key_weight, value_weight, output_weight]), 1).reshape(WEIGHTS[0])
        wi = gather(inner_weight).reshape(D, 4, D).transpose(1, 0, 2).reshape(WEIGHTS[1])
        wo = gather(outer_weight).reshape(WEIGHTS[2])
        packed = gather(jnp.concatenate([*small, inner_bias, bucket_bias])[None, :])
        cuts = [packed[:, i * width : (i + 1) * width].reshape(1, D) for i in range(8)]
        cuts.append(packed[:, 8 * width : 12 * width].reshape(4, D))
        vecs = jnp.concatenate(cuts + [jnp.zeros((4, D), BF16)]).astype(F32)
        table = jnp.pad(packed[:, 12 * width :].reshape(HEADS, BUCKETS), ((0, 4), (0, 128 - BUCKETS)))
        out_c, out_q, *saved = call_forward(False, *front, vecs, table, wa, wi, wo)
    gc, gq, ga, gi, go, gvec, gtab = call_backward(
        content_stream, query_stream, content_cotangent, query_cotangent, vecs, wa, wi, wo, saved
    )
    gi = gi.reshape(TILES, TILE, 3, TILE).transpose(2, 1, 0, 3).reshape(D, FF)

    def reduce(a, axis=0):
        a = lax.psum_scatter(a, "fsdp", scatter_dimension=axis, tiled=True)
        return lax.psum(a.astype(BF16), "rep").astype(F32)

    ga = reduce(ga, 1)
    gi = reduce(gi)
    go = reduce(go)
    count = D // width
    flat = jnp.concatenate(
        [gvec[i].reshape(count, width) for i in range(8)]
        + [gvec[8:12].reshape(count, 4 * width), gtab[:HEADS, :BUCKETS].reshape(count, -1)],
        axis=1,
    )
    flat = lax.psum_scatter(flat, "fsdp", scatter_dimension=0, tiled=True)[0]
    flat = lax.psum(flat.astype(BF16), "rep").astype(F32)
    v = [flat[i * width : (i + 1) * width] for i in range(8)]
    return (
        out_c, out_q, gc, gq, ga[0], v[0], ga[1], ga[2], v[1], ga[3], v[2], v[3], v[4], gi,
        flat[8 * width : 12 * width], go, v[5], v[6], v[7], flat[12 * width :],
    )


def solution(mesh):
    both, fsdp = ("rep", "fsdp"), "fsdp"
    row, vec = P(fsdp, None), P(fsdp)
    tokens = P(both, None)
    in_specs = (
        tokens, tokens, P(both), tokens, row, vec, row, row, vec, row, vec, vec, vec, row, vec, row, vec, vec, vec, vec,
        tokens, tokens,
    )
    out_specs = (
        tokens, tokens, tokens, tokens, row, vec, row, row, vec, row, vec, vec, vec, row, vec, row, vec, vec, vec, vec,
    )
    return jax.shard_map(shards, mesh=mesh, in_specs=in_specs, out_specs=out_specs, check_vma=False)
```

```python
import functools

import jax
import jax.numpy as jnp
from jax import lax
from jax.experimental import pallas as pl
from jax.experimental.pallas import tpu as pltpu
from jax.sharding import PartitionSpec as P

HEADS = 12
HEAD_DIM = 64
PAIRS = HEADS // 2
BUCKETS = 32
SEQ = 512
ROWS = 2 * SEQ
D = 768
FF = 3072
TILE = 256
TILES = FF // TILE
EPS = 1e-05
NEG = -1e30
LOG2E = 1.4426950408889634
SCALE = HEAD_DIM**-0.5
FAR_STEPS = (12, 16, 23, 32, 46, 64, 91)
F32 = jnp.float32
BF16 = jnp.bfloat16
VMEM_LIMIT = 62 * 2**20

TAIL_P = 0.28
TAIL = (
    0.11608706693762069,
    0.07021928496801585,
    0.26212226118724974,
    -0.22858899246095166,
    0.3847049667747488,
    -0.10454457204169064,
)


def mm(a, b):
    return jnp.dot(a, b, preferred_element_type=F32)


def mm_nt(a, b):
    return lax.dot_general(a, b, (((1,), (1,)), ((), ())), preferred_element_type=F32)


def mm_tn(a, b):
    return lax.dot_general(a, b, (((0,), (0,)), ((), ())), preferred_element_type=F32)


def bucket_of(offset):
    distance = jnp.abs(offset)
    farther = jnp.full(distance.shape, 8, jnp.int32)
    for step_at in FAR_STEPS:
        farther = farther + jnp.where(distance >= step_at, 1, 0)
    return jnp.where(distance < 8, distance, farther) + jnp.where(offset > 0, 16, 0)


def normal_parts(x):
    size = jnp.abs(x)
    t = 1.0 / (1.0 + TAIL_P * size)
    poly = jnp.full(x.shape, TAIL[-1], F32)
    for c in TAIL[-2::-1]:
        poly = poly * t + c
    bell = jnp.exp2(x * x * (-0.5 * LOG2E))
    tail = poly * t * bell
    return jnp.where(x < 0, tail, 1.0 - tail), bell * 0.3989422804014327


def ds(start, size):
    return pl.ds(pl.multiple_of(start, size), size)


def places():
    f = lax.axis_index("fsdp")
    return lax.axis_index("rep"), f // 2, f % 2


def hop(i, k):
    if k == 0:
        return i
    if k == 1:
        return i + 1 - 2 * (i % 2)
    return (i + 2) % 4 if k == 2 else 3 - i


def remote(src, dst, send, recv, device):
    return pltpu.make_async_remote_copy(
        src_ref=src, dst_ref=dst, send_sem=send, recv_sem=recv, device_id=device, device_id_type=pl.DeviceIdType.MESH
    )


def greet(devices):
    barrier = pltpu.get_barrier_semaphore()
    for device in devices:
        pl.semaphore_signal(barrier, inc=1, device_id=device, device_id_type=pl.DeviceIdType.MESH)
    pl.semaphore_wait(barrier, len(devices))


def block_of(buffers, t, r, z, c):
    if t == 2:
        return buffers[2].at[z, pl.ds(pl.multiple_of(c * 384 + r * 96, 96), 96), :]
    return buffers[t].at[r, z, ds(c * 96, 96), :]


def slab_of(buffers, t, r, c):
    if t == 2:
        return buffers[2].at[:, pl.ds(pl.multiple_of(c * 384 + r * 96, 96), 96), :]
    return buffers[t].at[r, :, ds(c * 96, 96), :]


class Gather:
    def __init__(self, refs, sems):
        *self.w, self.small = refs
        self.l_sem, self.zs, self.zr, self.xs, self.xr, self.cs, self.cr, self.vs, self.vr = sems
        self.r, self.z, self.c = places()

    def block(self, t, r, z, c):
        return block_of(self.w, t, r, z, c)

    def slab(self, t, r, c):
        return slab_of(self.w, t, r, c)

    def own(self, shards):
        *square, inner, outer = shards
        z, c = self.z, self.c
        copies = [
            [pltpu.make_async_copy(square[m], self.block(0, m, z, c), self.l_sem.at[0, m]) for m in range(4)],
            [
                pltpu.make_async_copy(inner.at[:, m * D : (m + 1) * D], self.block(1, m, z, c), self.l_sem.at[1, m])
                for m in range(4)
            ],
            [pltpu.make_async_copy(outer, self.w[2].at[z, ds(c * 384, 384), :], self.l_sem.at[2, 0])],
        ]
        return copies

    def small_copy(self, k):
        f = 2 * self.z + self.c
        return remote(
            self.small.at[f], self.small.at[f], self.vs.at[k - 1], self.vr.at[k - 1], (self.r, (f + k) % 8)
        )

    def small_come(self, k):
        f = (2 * self.z + self.c + 8 - k) % 8
        return remote(self.small.at[f], self.small.at[f], self.vs.at[k - 1], self.vr.at[k - 1], (self.r, f))

    def z_copy(self, t, k, come=False):
        far = hop(self.z, k)
        ref = self.block(t, self.r, far if come else self.z, self.c)
        return remote(ref, ref, self.zs.at[t, k - 1], self.zr.at[t, k - 1], (self.r, 2 * far + self.c))

    def x_copy(self, t, k, m, come=False):
        far = hop(self.r, m)
        ref = self.block(t, far if come else self.r, hop(self.z, k), self.c)
        at = 3 * (k - 1) + m - 1
        return remote(ref, ref, self.xs.at[t, at], self.xr.at[t, at], (far, 2 * self.z + self.c))

    def c_copy(self, t, m, come=False):
        ref = self.slab(t, hop(self.r, m), 1 - self.c if come else self.c)
        return remote(ref, ref, self.cs.at[t, m], self.cr.at[t, m], (self.r, 2 * self.z + 1 - self.c))

    def start_z(self, t):
        for k in (1, 2, 3):
            self.z_copy(t, k).start()

    def pass_on(self, t):
        for k in (1, 2, 3):
            self.z_copy(t, k, True).wait_recv()
            for m in (1, 2, 3):
                self.x_copy(t, k, m).start()

    def share(self, t):
        for m in range(4):
            if m:
                for k in (1, 2, 3):
                    self.x_copy(t, k, m, True).wait_recv()
            self.c_copy(t, m).start()

    def finish(self, t):
        for m in range(4):
            self.c_copy(t, m, True).wait_recv()

    def drain(self):
        for k in range(1, 8):
            self.small_copy(k).wait_send()
        for t in range(3):
            for k in (1, 2, 3):
                self.z_copy(t, k).wait_send()
                for m in (1, 2, 3):
                    self.x_copy(t, k, m).wait_send()
            for m in range(4):
                self.c_copy(t, m).wait_send()


def unpack_small(small_s, vec_s):
    blocks = [small_s[f] for f in range(8)]
    at = lax.broadcasted_iota(jnp.int32, (1024, D), 0)
    want = lax.broadcasted_iota(jnp.int32, (1024, D), 1)
    spread = jnp.where((at % 128 < 96) & (want == (at // 128) * 96 + at % 128), 1.0, 0.0).astype(BF16)
    vec_s[...] = mm(jnp.concatenate(blocks, axis=1), spread)
    wide = [b.astype(F32) for b in blocks]
    for m in range(4):
        for j in range(6):
            vec_s[8 + m : 9 + m, j * 128 : (j + 1) * 128] = wide[2 * m + j // 3][8 + j % 3 : 9 + j % 3]
    return [w[11:12] for w in wide]


def lines_of(rows):
    bucket = bucket_of(lax.broadcasted_iota(jnp.int32, (128, 1024), 1) - 512)
    entry = lax.broadcasted_iota(jnp.int32, (128, 1024), 0)

    def pick(first, shift):
        inside = (entry >= first) & (entry < 48)
        return jnp.where(inside & (bucket == entry + shift), 1.0, 0.0).astype(BF16)

    table = jnp.concatenate(rows, axis=0).astype(BF16)
    a0, a1, b1, b2 = (mm(table, pick(*p)) for p in ((0, 0), (32, -32), (0, 16), (16, -16)))
    lines = []
    for m in range(4):
        i, j = 2 * m, 2 * m + 1
        lines += [a0[i : i + 1], a1[i : i + 1] + b1[j : j + 1], b2[j : j + 1]]
    return [line * LOG2E for line in lines]


def build_masks(len_ref, rank_ref, mask_s):
    n = len_ref[0]
    rank = rank_ref[...]
    place = lax.broadcasted_iota(jnp.int32, (1, SEQ), 1)
    valid = place < n
    chosen = valid & (rank >= n - 3 * n // 20)
    key = jnp.where(chosen, rank, jnp.where(valid, -1, 2 * SEQ)).astype(F32)
    column = jnp.broadcast_to(rank.astype(F32), (128, SEQ)).T
    for s in range(2):
        for j in range(SEQ // 128):
            seen = jnp.broadcast_to(key[:, j * 128 : (j + 1) * 128], (SEQ, 128)) <= column - s
            mask_s[s, :, j * 128 : (j + 1) * 128] = jnp.where(seen, 0.0, NEG)


def lines_of_table(tab_ref):
    offset = lax.broadcasted_iota(jnp.int32, (128, 1024), 1) - 512
    bucket = lax.broadcasted_iota(jnp.int32, (128, 1024), 0)
    onehot = jnp.where(bucket_of(offset) == bucket, 1.0, 0.0).astype(BF16)
    line = mm(tab_ref[...], onehot) * LOG2E
    return [line[h : h + 1] for h in range(HEADS)]


def build_strip(lines, strip_s):
    for h in range(HEADS):
        wide = jnp.broadcast_to(lines[h], (128, 1024))
        strip_s[h] = pltpu.roll(wide, 0, 1, stride=1, stride_axis=0)[:, 128:]


def square(w_s, m, cols=slice(None)):
    block = w_s[m, :, :, cols]
    return block.reshape(D, block.shape[-1])


def project(x_ref, y_ref, vec_ref, w_s, q_s, k_s, v_s):
    for pair in range(0, PAIRS, 2):
        cols = slice(pair * 128, pair * 128 + 256)
        x = x_ref[...]
        parts = (
            (q_s, 0, mm(x, square(w_s, 0, cols)) + vec_ref[0:1, cols]),
            (q_s, 1, mm(y_ref[...], square(w_s, 0, cols)) + vec_ref[0:1, cols]),
            (k_s, None, mm(x, square(w_s, 1, cols))),
            (v_s, None, mm(x, square(w_s, 2, cols)) + vec_ref[1:2, cols]),
        )
        for ref, s, value in parts:
            value = value.astype(BF16)
            for e in range(2):
                piece = value[:, e * 128 : (e + 1) * 128]
                if s is None:
                    ref[pair + e] = piece
                else:
                    ref[s, pair + e] = piece


def attend(q_s, k_s, v_s, strip_s, mask_s, p_st, ctx_s, hp, slot):
    lane = lax.broadcasted_iota(jnp.int32, (SEQ, 128), 1)
    k = k_s[hp]
    v = v_s[hp]
    for s in range(2):
        q = q_s[s, hp]
        outs = []
        for e in range(2):
            own = (lane < 64) if e == 0 else (lane >= 64)
            scores = mm_nt(jnp.where(own, q, jnp.zeros_like(q)), k)
            for i in range(SEQ // 128):
                rows = slice(i * 128, (i + 1) * 128)
                blk = (
                    scores[rows] * (SCALE * LOG2E)
                    + strip_s[2 * hp + e, :, (3 - i) * 128 : (3 - i) * 128 + SEQ]
                    + mask_s[s, rows, :]
                )
                top = jnp.max(blk, axis=1, keepdims=True)
                w = jnp.exp2(blk - top)
                w = w * (1.0 / jnp.sum(w, axis=1, keepdims=True))
                p_st[slot, e, s, rows, :] = w.astype(BF16)
            outs.append(mm(p_st[slot, e, s], v))
        ctx_s[s * SEQ : (s + 1) * SEQ, ds(hp * 128, 128)] = jnp.where(
            lane < 64, outs[0], outs[1]
        ).astype(BF16)


def norm_stats(r):
    mean = jnp.mean(r, axis=1, keepdims=True)
    centred = r - mean
    inverse = lax.rsqrt(jnp.mean(centred * centred, axis=1, keepdims=True) + EPS)
    return centred * inverse, inverse


NETWORK = {
    0: (("pass_on", 1), ("start_z", 2)),
    2: (("share", 1),),
    3: (("pass_on", 2),),
    5: (("share", 2),),
}


def forward_kernel(linked, *refs):
    refs = list(refs)
    take = lambda n: [refs.pop(0) for _ in range(n)]
    x_ref, y_ref, len_ref, rank_ref = take(4)
    if linked:
        (small_ref,) = take(1)
        shards = take(6)
    else:
        vec_ref, tab_ref, *weights = take(5)
    oc_ref, oq_ref, q_h, k_h, v_h, p_h, ctx_h, n1_h, inv1_h, nl_h, act_h, slope_h, n2_h, inv2_h = take(14)
    if linked:
        vec_h, *weights = take(4)
    wa_s, wi_s, wo_s, q_s, k_s, v_s, ctx_s, nl_s, n1_s, br_s, inv1_s, inv2_s, o_sem, st_sem, w_sem = take(15)
    copies = (wa_s, wi_s, wo_s)
    if linked:
        small_s, vec_ref, *sems = take(10)
        net = Gather((wa_s, wi_s, wo_s, small_s), (w_sem, *sems))
        r, z, c = places()
        f = 2 * z + c
        own = net.own(shards)
        for batch in own:
            for copy in batch:
                copy.start()
        small_s[f] = small_ref[...]
        greet(
            [(hop(r, m), f) for m in (1, 2, 3)] + [(r, (f + k) % 8) for k in range(1, 8)]
        )
        for k in range(1, 8):
            net.small_copy(k).start()
        for copy in own[0]:
            copy.wait()
        net.start_z(0)
    else:
        loads = [pltpu.make_async_copy(src, dst, w_sem.at[i, 0]) for i, (src, dst) in enumerate(zip(weights, copies))]
        for copy in loads:
            copy.start()
    stores = []

    def keep(src, dst):
        pltpu.make_async_copy(src, dst, o_sem.at[len(stores)]).start()
        stores.append((src, dst))

    def attention(strip_s, mask_s, p_st):
        build_masks(len_ref, rank_ref, mask_s)
        if linked:
            for k in range(1, 8):
                net.small_come(k).wait_recv()
            build_strip(lines_of(unpack_small(small_s, vec_ref)), strip_s)
            net.pass_on(0)
            for copy in own[1] + own[2]:
                copy.wait()
            net.start_z(1)
            net.share(0)
            net.finish(0)
            keep(vec_ref, vec_h)
            keep(wa_s, weights[0])
        else:
            build_strip(lines_of_table(tab_ref), strip_s)
            loads[0].wait()
        project(x_ref, y_ref, vec_ref, wa_s, q_s, k_s, v_s)
        keep(q_s, q_h)
        keep(k_s, k_h)
        keep(v_s, v_h)

        def store(hp, slot):
            return pltpu.make_async_copy(p_st.at[slot], p_h.at[hp], st_sem.at[slot])

        def step(hp, carry):
            slot = (hp % 2)

            @pl.when(hp >= 2)
            def _():
                store(hp - 2, slot).wait()

            if linked:
                for at, moves in NETWORK.items():
                    @pl.when(hp == at)
                    def _(moves=moves):
                        for name, t in moves:
                            getattr(net, name)(t)

            attend(q_s, k_s, v_s, strip_s, mask_s, p_st, ctx_s, hp, slot)
            store(hp, slot).start()
            return carry

        lax.fori_loop(0, PAIRS, step, 0)
        store(PAIRS - 2, 0).wait()
        store(PAIRS - 1, 1).wait()

    pl.run_scoped(
        attention,
        pltpu.VMEM((HEADS, 128, 896), F32),
        pltpu.VMEM((2, SEQ, SEQ), F32),
        pltpu.VMEM((2, 2, 2, SEQ, SEQ), BF16),
    )
    keep(ctx_s, ctx_h)

    for s, in_ref in ((0, x_ref), (1, y_ref)):
        def first(i, carry, s=s, in_ref=in_ref):
            own = ds(i * 256, 256)
            rows = ds(s * SEQ + i * 256, 256)
            r = in_ref[own, :].astype(F32) + mm(ctx_s[rows, :], square(wa_s, 3)) + vec_ref[2:3, :]
            n, inverse = norm_stats(r)
            n1_s[rows, :] = n
            inv1_s[rows, :] = jnp.broadcast_to(inverse, (256, 128))
            nl_s[rows, :] = (n * vec_ref[3:4, :] + vec_ref[4:5, :]).astype(BF16)
            return carry

        lax.fori_loop(0, SEQ // 256, first, 0)
    keep(n1_s, n1_h)
    keep(inv1_s, inv1_h)
    keep(nl_s, nl_h)

    if linked:
        net.finish(1)
        net.finish(2)
        keep(wi_s, weights[1])
        keep(wo_s, weights[2])
    else:
        loads[1].wait()
        loads[2].wait()
    br_s[...] = jnp.zeros_like(br_s)

    def feed(act_st, slope_st):
        def pair(t, slot):
            return (
                pltpu.make_async_copy(act_st.at[slot], act_h.at[t], st_sem.at[slot]),
                pltpu.make_async_copy(slope_st.at[slot], slope_h.at[t], st_sem.at[2 + slot]),
            )

        def step(t, carry):
            slot = (t % 2)

            @pl.when(t >= 2)
            def _():
                for c in pair(t - 2, slot):
                    c.wait()

            part = ds((t % 3) * TILE, TILE)
            inner = mm(nl_s[...], square(wi_s, t // 3, part)) + vec_ref[pl.ds(8 + (t // 3), 1), ds((t % 3) * TILE, TILE)]
            spread, bell = normal_parts(inner)
            act = (inner * spread).astype(BF16)
            act_st[slot] = act
            slope_st[slot] = (spread + inner * bell).astype(BF16)
            br_s[...] += mm(act, wo_s[t // 3, part, :])
            for c in pair(t, slot):
                c.start()
            return carry

        lax.fori_loop(0, TILES, step, 0)
        for t in (TILES - 2, TILES - 1):
            for c in pair(t, t % 2):
                c.wait()

    pl.run_scoped(feed, pltpu.VMEM((2, ROWS, TILE), BF16), pltpu.VMEM((2, ROWS, TILE), BF16))

    for s, o_ref in ((0, oc_ref), (1, oq_ref)):
        def last(i, carry, s=s, o_ref=o_ref):
            rows = ds(s * SEQ + i * 128, 128)
            normed = n1_s[rows, :] * vec_ref[3:4, :] + vec_ref[4:5, :]
            n, inverse = norm_stats(normed + br_s[rows, :] + vec_ref[5:6, :])
            br_s[rows, :] = n
            inv2_s[rows, :] = jnp.broadcast_to(inverse, (128, 128))
            o_ref[ds(i * 128, 128), :] = (n * vec_ref[6:7, :] + vec_ref[7:8, :]).astype(BF16)
            return carry

        lax.fori_loop(0, SEQ // 128, last, 0)
    keep(br_s, n2_h)
    keep(inv2_s, inv2_h)
    for i, (src, dst) in enumerate(stores):
        pltpu.make_async_copy(src, dst, o_sem.at[i]).wait()
    if linked:
        net.drain()


WEIGHTS = ((4, 4, 192, D), (4, 4, 192, D), (4, D, D))


def call_forward(linked, *args):
    hbm = pl.BlockSpec(memory_space=pl.ANY)
    vmem = pl.BlockSpec(memory_space=pltpu.VMEM)
    smem = pl.BlockSpec(memory_space=pltpu.SMEM)
    dma = pltpu.SemaphoreType.DMA
    shape = jax.ShapeDtypeStruct
    outs = [
        shape((SEQ, D), BF16), shape((SEQ, D), BF16),
        shape((2, PAIRS, SEQ, 128), BF16), shape((PAIRS, SEQ, 128), BF16), shape((PAIRS, SEQ, 128), BF16),
        shape((PAIRS, 2, 2, SEQ, SEQ), BF16), shape((ROWS, D), BF16),
        shape((ROWS, D), F32), shape((ROWS, 128), F32), shape((ROWS, D), BF16),
        shape((TILES, ROWS, TILE), BF16), shape((TILES, ROWS, TILE), BF16),
        shape((ROWS, D), F32), shape((ROWS, 128), F32),
    ]
    scratch = [pltpu.VMEM(w, BF16) for w in WEIGHTS] + [
        pltpu.VMEM((2, PAIRS, SEQ, 128), BF16), pltpu.VMEM((PAIRS, SEQ, 128), BF16), pltpu.VMEM((PAIRS, SEQ, 128), BF16),
        pltpu.VMEM((ROWS, D), BF16), pltpu.VMEM((ROWS, D), BF16), pltpu.VMEM((ROWS, D), F32), pltpu.VMEM((ROWS, D), F32),
        pltpu.VMEM((ROWS, 128), F32), pltpu.VMEM((ROWS, 128), F32),
        dma((13,)), dma((4,)), dma((3, 4)),
    ]
    in_specs = [vmem, vmem, smem, vmem]
    if linked:
        in_specs += [vmem] + [hbm] * 6
        outs += [shape((16, D), F32)] + [shape(w, BF16) for w in WEIGHTS]
        scratch += [
            pltpu.VMEM((8, 16, 128), BF16), pltpu.VMEM((16, D), F32),
            dma((3, 3)), dma((3, 3)), dma((3, 9)), dma((3, 9)), dma((3, 4)), dma((3, 4)), dma((7,)), dma((7,)),
        ]
        params = pltpu.CompilerParams(vmem_limit_bytes=VMEM_LIMIT, collective_id=1, has_side_effects=True)
    else:
        in_specs += [vmem, vmem] + [hbm] * 3
        params = pltpu.CompilerParams(vmem_limit_bytes=VMEM_LIMIT)
    return pl.pallas_call(
        functools.partial(forward_kernel, linked),
        out_shape=outs,
        in_specs=in_specs,
        out_specs=[vmem, vmem] + [hbm] * (len(outs) - 2),
        scratch_shapes=scratch,
        compiler_params=params,
        name="forward",
    )(*args)


class Reduce:
    def __init__(self, refs, sems):
        self.g, (self.cr1, self.cr2, self.xr0, self.xr, self.zr0, self.zr, self.tt, self.yr, self.res) = refs
        self.cs, self.cr, self.credit, self.xs, self.xd, self.zs, self.zd, self.ys, self.yd, self.as_, self.ad = sems
        self.r, self.z, self.c = places()
        self.f = 2 * self.z + self.c
        x, y = self.r % 2, self.r // 2
        self.keep, self.give = (x, 2 + y), (1 - x, 3 - y)

    def block(self, t, q, z):
        return block_of(self.g, t, q, z, self.c)

    def core(self, t, i):
        if t == 2:
            src, dst = self.g[2].at[i, ds((1 - self.c) * 384, 384), :], self.cr2.at[i]
        else:
            src, dst = slab_of(self.g, t, i, 1 - self.c), self.cr1.at[i]
        return remote(src, dst, self.cs.at[t, i], self.cr.at[t, i], (self.r, 2 * self.z + 1 - self.c))

    def start_core(self, t, i):
        self.core(t, i).start()

    def across(self, t, m):
        if t == 0:
            to = hop(self.r, m + 1)
            return remote(slab_of(self.g, 0, to, self.c), self.xr0.at[m], self.xs.at[0, m], self.xd.at[0, m], (to, self.f))
        src = slab_of(self.g, t, self.give[m], self.c)
        return remote(src, self.xr.at[t - 1, m], self.xs.at[t, m], self.xd.at[t, m], (hop(self.r, m + 1), self.f))

    def along(self, t, k, m):
        to = hop(self.z, k + 1)
        device = (self.r, 2 * to + self.c)
        if t == 0:
            return remote(self.block(0, self.r, to), self.zr0.at[k], self.zs.at[0, k], self.zd.at[0, k], device)
        at = 2 * k + m
        src = self.block(t, self.keep[m], to)
        return remote(src, self.zr.at[t - 1, k, m], self.zs.at[t, at], self.zd.at[t, at], device)

    def complete(self, t, m):
        src, dst = self.tt.at[t - 1, m], self.yr.at[t - 1, m]
        return remote(src, dst, self.ys.at[t - 1, m], self.yd.at[t - 1, m], (hop(self.r, 2 - m), self.f))

    def spread(self, t, m, come=False):
        far = hop(self.r, m + 1)
        if t == 0:
            ref = self.res.at[0, far if come else self.r]
        else:
            ref = self.res.at[t, self.give[m] if come else self.keep[m]]
        return remote(ref, ref, self.as_.at[t, m], self.ad.at[t, m], (far, self.f))

    def cores(self, t):
        for i in range(4):
            self.core(t, i).wait_recv()

        def add(i, carry):
            if t == 2:
                rows = ds(self.c * 384, 384)
                total = self.g[2][i, rows, :].astype(F32) + self.cr2[i].astype(F32)
                self.g[2][i, rows, :] = total.astype(BF16)
            else:
                rows = ds(self.c * 96, 96)
                total = self.g[t][i, :, rows, :].astype(F32) + self.cr1[i].astype(F32)
                self.g[t][i, :, rows, :] = total.astype(BF16)
            return carry

        lax.fori_loop(0, 4, add, 0)
        if t == 1:
            pl.semaphore_signal(
                self.credit, inc=1, device_id=(self.r, 2 * self.z + 1 - self.c), device_id_type=pl.DeviceIdType.MESH
            )
        for m in range(3 if t == 0 else 2):
            self.across(t, m).start()

    def replicas(self, t):
        for m in range(3 if t == 0 else 2):
            self.across(t, m).wait_recv()

        def add(i, carry):
            if t == 0:
                ref = self.block(0, self.r, i)
                total = ref[...].astype(F32)
                for m in range(3):
                    total = total + self.xr0[m, i].astype(F32)
                ref[...] = total.astype(BF16)
            else:
                for m in range(2):
                    ref = self.block(t, self.keep[m], i)
                    ref[...] = (ref[...].astype(F32) + self.xr[t - 1, m, i].astype(F32)).astype(BF16)
            return carry

        lax.fori_loop(0, 4, add, 0)
        for k in range(3):
            for m in range(1 if t == 0 else 2):
                self.along(t, k, m).start()

    def owners(self, t):
        for k in range(3):
            for m in range(1 if t == 0 else 2):
                self.along(t, k, m).wait_recv()
        if t == 0:
            total = self.block(0, self.r, self.z)[...].astype(F32)
            for k in range(3):
                total = total + self.zr0[k].astype(F32)
            self.res[0, self.r] = total.astype(BF16)
            for m in range(3):
                self.spread(0, m).start()
            return
        for m in range(2):
            total = self.block(t, self.keep[m], self.z)[...].astype(F32)
            for k in range(3):
                total = total + self.zr[t - 1, k, m].astype(F32)
            self.tt[t - 1, m] = total.astype(BF16)
            self.complete(t, m).start()

    def ends(self, t):
        for m in range(2):
            self.complete(t, m).wait_recv()
            total = self.tt[t - 1, m].astype(F32) + self.yr[t - 1, m].astype(F32)
            self.res[t, self.keep[m]] = total.astype(BF16)
            self.spread(t, m).start()

    def finish(self, t):
        for m in range(3 if t == 0 else 2):
            self.spread(t, m, True).wait_recv()

    def drain(self):
        for t in range(3):
            for i in range(4):
                self.core(t, i).wait_send()
            for m in range(3 if t == 0 else 2):
                self.across(t, m).wait_send()
                self.spread(t, m).wait_send()
            for k in range(3):
                for m in range(1 if t == 0 else 2):
                    self.along(t, k, m).wait_send()
            if t:
                for m in range(2):
                    self.complete(t, m).wait_send()


class SmallReduce:
    def __init__(self, refs, sems):
        self.out, self.got, self.sums = refs
        self.vs, self.vd, self.ws, self.wd = sems
        self.r, z, c = places()
        self.f = 2 * z + c

    def first(self, k):
        to = (self.f + k) % 8
        return remote(self.out.at[to], self.got.at[self.f], self.vs.at[k - 1], self.vd.at[k - 1], (self.r, to))

    def first_come(self, k):
        back = (self.f + 8 - k) % 8
        return remote(self.out.at[back], self.got.at[back], self.vs.at[k - 1], self.vd.at[k - 1], (self.r, back))

    def second(self, m, come=False):
        far = hop(self.r, m)
        ref = self.sums.at[far if come else self.r]
        return remote(ref, ref, self.ws.at[m - 1], self.wd.at[m - 1], (far, self.f))

    def start(self, vec, table):
        pack_small(vec, table, self.out)
        self.got[self.f] = self.out[self.f]
        for k in range(1, 8):
            self.first(k).start()

    def middle(self):
        for k in range(1, 8):
            self.first_come(k).wait_recv()
        total = self.got[0]
        for f in range(1, 8):
            total = total + self.got[f]
        self.sums[self.r] = total
        for m in (1, 2, 3):
            self.second(m).start()

    def finish(self):
        for m in (1, 2, 3):
            self.second(m, True).wait_recv()
        total = self.sums[0]
        for r in range(1, 4):
            total = total + self.sums[r]
        return total

    def drain(self):
        for k in range(1, 8):
            self.first(k).wait_send()
        for m in (1, 2, 3):
            self.second(m).wait_send()


def pack_small(vec_ref, table, out_ref):
    want = lax.broadcasted_iota(jnp.int32, (D, 1024), 0)
    at = lax.broadcasted_iota(jnp.int32, (D, 1024), 1)
    gathered = jnp.where((at % 128 < 96) & (want == (at // 128) * 96 + at % 128), 1.0, 0.0)
    vec = vec_ref[...]
    rows = lax.dot_general(
        vec[0:8], gathered, (((1,), (0,)), ((), ())), precision=lax.Precision.HIGHEST, preferred_element_type=F32
    )
    lane = lax.broadcasted_iota(jnp.int32, (1, 128), 1)
    for f in range(8):
        m = f // 2
        out_ref[f, 0:8, :] = rows[:, f * 128 : (f + 1) * 128]
        for j in range(3):
            col = (f % 2) * 384 + j * 128
            out_ref[f, 8 + j : 9 + j, :] = vec[8 + m : 9 + m, col : col + 128]
        head = 3 * m + f % 2
        a, b = table[head : head + 1], table[head + 1 : head + 2]
        if f % 2 == 0:
            line = jnp.where(lane < 32, a, jnp.where(lane < 48, pltpu.roll(b, 32, 1), 0.0))
        else:
            line = jnp.where(lane < 16, pltpu.roll(a, 112, 1), jnp.where(lane < 48, pltpu.roll(b, 16, 1), 0.0))
        out_ref[f, 11:12, :] = line
        out_ref[f, 12:16, :] = jnp.zeros((4, 128), F32)


def norm_grad(u, gain, n, inverse):
    ug = u * gain
    return inverse * (
        ug - jnp.mean(ug, axis=1, keepdims=True) - n * jnp.mean(ug * n, axis=1, keepdims=True)
    )


BACK_NETWORK = {
    1: (("replicas", 2),),
    3: (("replicas", 1),),
    4: (("owners", 2),),
    5: (("ends", 2),),
}


def backward_kernel(linked, *refs):
    refs = list(refs)
    take = lambda n: [refs.pop(0) for _ in range(n)]
    x_h, y_h, cc_h, cq_h, vec_ref, wa_h, wi_h, wo_h = take(8)
    q_h, k_h, v_h, p_h, ctx_h, n1_h, inv1_h, nl_h, act_h, slope_h, n2_h, inv2_h = take(12)
    gc_h, gq_h = take(2)
    if linked:
        res_ref, small_ref = take(2)
    else:
        *grads_h, gvec_ref, gtab_ref = take(5)
    ctx_s, g_s, dctx_s, tr_s, l_sem, t_sem = take(6)
    ga_s, gi_s, go_s = grads = take(3)
    if linked:
        gvec_ref, *more = take(10)
        sum_refs = take(3)
        sems = take(11)
        sum_sems = take(4)
        net = Reduce((grads, more[:9]), sems)
        sums = SmallReduce(sum_refs, sum_sems)
        r, z, c = places()
        f = 2 * z + c
        res_s = more[8]
    cload = pltpu.make_async_copy(ctx_h, ctx_s, l_sem.at[1])
    cload.start()
    gvec_ref[...] = jnp.zeros_like(gvec_ref)

    def add_vec(row, value, cols=slice(None)):
        gvec_ref[row : row + 1, cols] += jnp.sum(value, axis=0, keepdims=True)

    def tail(n_s, inv_s, nl_s, db_s, act_s, slope_s, wi_s, wo_s, cot_s, wt_s):
        wload = pltpu.make_async_copy(wa_h.at[3], wt_s, l_sem.at[0])
        wload.start()
        nload = pltpu.make_async_copy(n2_h, n_s, l_sem.at[2])
        iload = pltpu.make_async_copy(inv2_h, inv_s, l_sem.at[3])
        nlload = pltpu.make_async_copy(nl_h, nl_s, l_sem.at[4])
        cots = [pltpu.make_async_copy(ref, cot_s.at[s], l_sem.at[5 + s]) for s, ref in enumerate((cc_h, cq_h))]
        for copy in (nload, iload, *cots, nlload):
            copy.start()

        def fetch(t, slot):
            return (
                pltpu.make_async_copy(act_h.at[t], act_s.at[slot], t_sem.at[slot]),
                pltpu.make_async_copy(slope_h.at[t], slope_s.at[slot], t_sem.at[2 + slot]),
                pltpu.make_async_copy(wi_h.at[t // 3, :, :, ds((t % 3) * TILE, TILE)], wi_s.at[slot], t_sem.at[4 + slot]),
                pltpu.make_async_copy(wo_h.at[t // 3, ds((t % 3) * TILE, TILE), :], wo_s.at[slot], t_sem.at[6 + slot]),
            )

        for copy in fetch(0, 0):
            copy.start()
        if linked:
            greet([(hop(r, m), f) for m in (1, 2, 3)] + [(r, (f + k) % 8) for k in range(1, 8)])
        for copy in (nload, iload, *cots):
            copy.wait()

        def second(i, carry):
            rows = ds(i * 128, 128)
            u = cot_s[i // 4, ds((i % 4) * 128, 128), :].astype(F32)
            n = n_s[rows, :]
            g = norm_grad(u, vec_ref[6:7, :], n, inv_s[rows, 0:1])
            add_vec(6, u * n)
            add_vec(7, u)
            g_s[rows, :] = g
            low = g.astype(BF16)
            db_s[rows, :] = low
            add_vec(5, low.astype(F32))
            return carry

        lax.fori_loop(0, ROWS // 128, second, 0)
        n1load = pltpu.make_async_copy(n1_h, n_s, l_sem.at[2])
        i1load = pltpu.make_async_copy(inv1_h, inv_s, l_sem.at[3])
        n1load.start()
        i1load.start()
        nlload.wait()
        tr_s[...] = nl_s[...].T
        xyloads = [
            pltpu.make_async_copy(ref, nl_s.at[s * SEQ : (s + 1) * SEQ, :], l_sem.at[5 + s])
            for s, ref in enumerate((x_h, y_h))
        ]
        for copy in xyloads:
            copy.start()

        def step(t, carry):
            slot = t % 2
            for copy in fetch(t, slot):
                copy.wait()

            @pl.when(t + 1 < TILES)
            def _():
                for copy in fetch(t + 1, 1 - slot):
                    copy.start()

            db = db_s[...]
            di = (mm_nt(db, wo_s[slot]) * slope_s[slot].astype(F32)).astype(BF16)
            i, part = t // 3, ds((t % 3) * TILE, TILE)
            mine = lax.broadcasted_iota(jnp.int32, (8, TILE), 0) == i
            gvec_ref[8:16, part] += jnp.where(mine, jnp.sum(di.astype(F32), axis=0, keepdims=True), 0.0)
            go_s[i, part, :] = mm_tn(act_s[slot], db).astype(BF16)
            gi_s[i, :, :, part] = mm(tr_s[...], di).astype(BF16).reshape(4, 192, TILE)
            g_s[...] += mm_nt(di, wi_s[slot].reshape(D, TILE))
            if linked:
                @pl.when(t % 3 == 2)
                def _():
                    net.start_core(2, i)
                    net.start_core(1, i)

            return carry

        lax.fori_loop(0, TILES, step, 0)
        if linked:
            net.cores(2)
            net.cores(1)

        n1load.wait()
        i1load.wait()

        def first(i, carry):
            rows = ds(i * 128, 128)
            u = g_s[rows, :]
            n = n_s[rows, :]
            g = norm_grad(u, vec_ref[3:4, :], n, inv_s[rows, 0:1])
            add_vec(3, u * n)
            add_vec(4, u)
            g_s[rows, :] = g
            low = g.astype(BF16)
            db_s[rows, :] = low
            add_vec(2, low.astype(F32))
            return carry

        lax.fori_loop(0, ROWS // 128, first, 0)
        wload.wait()
        cload.wait()
        tr_s[...] = ctx_s[...].T
        ga_s[3] = mm(tr_s[...], db_s[...]).astype(BF16).reshape(4, 192, D)
        if linked:
            pl.semaphore_wait(net.credit, 1)
            net.start_core(0, 3)
        for j in range(4):
            dctx_s[j * 256 : (j + 1) * 256, :] = mm_nt(db_s[j * 256 : (j + 1) * 256, :], wt_s[...].reshape(D, D)).astype(BF16)
        for copy in xyloads:
            copy.wait()
        tr_s[...] = nl_s[...].T

    pl.run_scoped(
        tail,
        pltpu.VMEM((ROWS, D), F32),
        pltpu.VMEM((ROWS, 128), F32),
        pltpu.VMEM((ROWS, D), BF16),
        pltpu.VMEM((ROWS, D), BF16),
        pltpu.VMEM((2, ROWS, TILE), BF16),
        pltpu.VMEM((2, ROWS, TILE), BF16),
        pltpu.VMEM((2, 4, 192, TILE), BF16),
        pltpu.VMEM((2, TILE, D), BF16),
        pltpu.VMEM((2, SEQ, D), BF16),
        pltpu.VMEM(WEIGHTS[0][1:], BF16),
    )

    def attention(q_s, k_s, v_s, p_s, dq_s, dkt_s, dvt_s, far_s, bt_s, wa_s):
        wload = pltpu.make_async_copy(wa_h.at[0:3], wa_s, l_sem.at[0])
        wload.start()
        loads = [(q_h, q_s), (k_h, k_s), (v_h, v_s)]
        loads = [pltpu.make_async_copy(a, b, l_sem.at[2 + i]) for i, (a, b) in enumerate(loads)]
        for copy in loads:
            copy.start()

        def fetch(hp, slot):
            return pltpu.make_async_copy(p_h.at[hp], p_s.at[slot], t_sem.at[slot])

        fetch(0, 0).start()
        for copy in loads:
            copy.wait()

        def step(hp, carry):
            slot = hp % 2
            fetch(hp, slot).wait()

            @pl.when(hp + 1 < PAIRS)
            def _():
                fetch(hp + 1, 1 - slot).start()

            if linked:
                for at, moves in BACK_NETWORK.items():
                    @pl.when(hp == at)
                    def _(moves=moves):
                        for name, t in moves:
                            getattr(net, name)(t)

            attend_back(hp, slot)
            return carry

        def attend_back(hp, slot):
            lane = lax.broadcasted_iota(jnp.int32, (SEQ, 128), 1)
            k, v = k_s[hp], v_s[hp]
            zero = jnp.zeros((SEQ, 128), BF16)
            dq = [None, None]
            qt = [q_s[s, hp].T for s in range(2)]
            dt = [dctx_s[s * SEQ : (s + 1) * SEQ, ds(hp * 128, 128)].T for s in range(2)]
            for e in range(2):
                own = (lane < 64) if e == 0 else (lane >= 64)
                both = None
                dkt = dvt = None
                for s in range(2):
                    rows = slice(s * SEQ, (s + 1) * SEQ)
                    do = jnp.where(own, dctx_s[rows, ds(hp * 128, 128)], zero)
                    weight = jnp.sum(do.astype(F32) * ctx_s[rows, ds(hp * 128, 128)].astype(F32), axis=1, keepdims=True)
                    p = p_s[slot, e, s]
                    g = p.astype(F32) * (mm_nt(do, v) - weight)
                    low = g.astype(BF16)
                    both = g if both is None else both + g
                    part = mm(low, jnp.where(own, k, zero))
                    dq[s] = part if dq[s] is None else dq[s] + part
                    half = slice(e * 64, (e + 1) * 64)
                    a = mm(dt[s][half], p)
                    b = mm(qt[s][half], low)
                    dvt = a if dvt is None else dvt + a
                    dkt = b if dkt is None else dkt + b
                dvt_s[ds(hp * 128 + e * 64, 64), :] = dvt.astype(BF16)
                dkt_s[ds(hp * 128 + e * 64, 64), :] = (dkt * SCALE).astype(BF16)
                parts = [None] * 5
                for i in range(4):
                    for j in range(4):
                        blk = both[i * 128 : (i + 1) * 128, j * 128 : (j + 1) * 128]
                        at = min(max(j - i, -2), 2) + 2
                        parts[at] = blk if parts[at] is None else parts[at] + blk
                strip = jnp.concatenate([jnp.zeros((128, 128), F32), parts[1], parts[2], parts[3]], axis=1)
                flat = strip[0:8]
                for g in range(1, 16):
                    flat = flat + pltpu.roll(strip[8 * g : 8 * g + 8], 512 - 8 * g, 1)
                row = lax.broadcasted_iota(jnp.int32, (8, 512), 0)
                for bit in (1, 2, 4):
                    flat = jnp.where((row & bit) != 0, pltpu.roll(flat, 512 - bit, 1), flat)
                h = 2 * hp + e
                for ref, cols, value in (
                    (bt_s, slice(0, 512), flat),
                    (far_s, slice(0, 128), parts[0]),
                    (far_s, slice(128, 256), parts[4]),
                ):
                    line = jnp.sum(value, axis=0, keepdims=True)
                    mine = lax.broadcasted_iota(jnp.int32, (16, line.shape[1]), 0) == h
                    ref[:, cols] = jnp.where(mine, line, ref[:, cols])
            for s in range(2):
                dq_s[s * SEQ : (s + 1) * SEQ, ds(hp * 128, 128)] = (dq[s] * SCALE).astype(BF16)

        bt_s[...] = jnp.zeros_like(bt_s)
        far_s[...] = jnp.zeros_like(far_s)
        lax.fori_loop(0, PAIRS, step, 0)

        dk = dkt_s[...].T
        dv = dvt_s[...].T
        for w, left, grad in ((1, slice(0, SEQ), dk), (2, slice(0, SEQ), dv), (0, slice(0, ROWS), dq_s[...])):
            ga_s[w] = mm(tr_s[:, left], grad).astype(BF16).reshape(4, 192, D)
            if linked:
                net.start_core(0, w)

        offset = lax.broadcasted_iota(jnp.int32, (512, 128), 0) - 256
        bucket = lax.broadcasted_iota(jnp.int32, (512, 128), 1)
        near = jnp.where(bucket_of(offset) == bucket, 1.0, 0.0)
        lane = lax.broadcasted_iota(jnp.int32, (16, 128), 1)
        table = (
            lax.dot_general(bt_s[...], near, (((1,), (0,)), ((), ())), precision=lax.Precision.HIGHEST, preferred_element_type=F32)
            + jnp.where(lane == 15, jnp.sum(far_s[:, 0:128], axis=1, keepdims=True), 0.0)
            + jnp.where(lane == 31, jnp.sum(far_s[:, 128:256], axis=1, keepdims=True), 0.0)
        )
        add_vec(0, dq_s[...].astype(F32))
        add_vec(1, dv.astype(F32))
        if linked:
            net.cores(0)
            sums.start(gvec_ref, table)
            net.owners(1)
        else:
            gtab_ref[...] = table

        wload.wait()
        g_s[0:SEQ, :] += mm_nt(dq_s[0:SEQ, :], square(wa_s, 0)) + mm_nt(dk, square(wa_s, 1)) + mm_nt(dv, square(wa_s, 2))
        g_s[SEQ:, :] += mm_nt(dq_s[SEQ:, :], square(wa_s, 0))
        outs = [
            pltpu.make_async_copy(g_s.at[s * SEQ : (s + 1) * SEQ, :], ref, l_sem.at[2 + s])
            for s, ref in enumerate((gc_h, gq_h))
        ]
        for copy in outs:
            copy.start()
        if linked:
            sums.middle()
            net.replicas(0)
            net.ends(1)
            net.finish(2)
            net.finish(1)
            small_ref[...] = sums.finish()
            res_ref[1] = res_s[1]
            res_ref[2] = res_s[2]
            net.owners(0)
            net.finish(0)
            res_ref[0] = res_s[0]
            net.drain()
            sums.drain()
        else:
            writes = [pltpu.make_async_copy(a, b, t_sem.at[i]) for i, (a, b) in enumerate(zip(grads, grads_h))]
            for copy in writes:
                copy.start()
            for copy in writes:
                copy.wait()
        for copy in outs:
            copy.wait()

    pl.run_scoped(
        attention,
        pltpu.VMEM((2, PAIRS, SEQ, 128), BF16),
        pltpu.VMEM((PAIRS, SEQ, 128), BF16),
        pltpu.VMEM((PAIRS, SEQ, 128), BF16),
        pltpu.VMEM((2, 2, 2, SEQ, SEQ), BF16),
        pltpu.VMEM((ROWS, D), BF16),
        pltpu.VMEM((D, SEQ), BF16),
        pltpu.VMEM((D, SEQ), BF16),
        pltpu.VMEM((16, 256), F32),
        pltpu.VMEM((16, 512), F32),
        pltpu.VMEM((3, *WEIGHTS[0][1:]), BF16),
    )


def call_backward(linked, x, y, cc, cq, vecs, wa, wi, wo, saved):
    hbm = pl.BlockSpec(memory_space=pl.ANY)
    vmem = pl.BlockSpec(memory_space=pltpu.VMEM)
    dma = pltpu.SemaphoreType.DMA
    shape = jax.ShapeDtypeStruct
    outs = [shape((SEQ, D), F32), shape((SEQ, D), F32)]
    out_specs = [hbm, hbm]
    scratch = [
        pltpu.VMEM((ROWS, D), BF16), pltpu.VMEM((ROWS, D), F32), pltpu.VMEM((ROWS, D), BF16),
        pltpu.VMEM((D, ROWS), BF16), dma((7,)), dma((8,)),
    ] + [pltpu.VMEM(w, BF16) for w in WEIGHTS]
    if linked:
        outs += [shape((3, 4, 96, D), BF16), shape((16, 128), F32)]
        out_specs += [vmem, vmem]
        scratch += [pltpu.VMEM((16, D), F32)] + [
            pltpu.VMEM(s, BF16)
            for s in (
                (4, 4, 96, D), (4, 384, D), (3, 4, 96, D), (2, 2, 4, 96, D), (3, 96, D), (2, 3, 2, 96, D), (2, 2, 96, D),
                (2, 2, 96, D), (3, 4, 96, D),
            )
        ]
        scratch += [pltpu.VMEM((n, 16, 128), F32) for n in (8, 8, 4)]
        scratch += [
            dma((3, 4)), dma((3, 4)), pltpu.SemaphoreType.REGULAR, dma((3, 3)), dma((3, 3)), dma((3, 6)), dma((3, 6)),
            dma((2, 2)), dma((2, 2)), dma((3, 3)), dma((3, 3)), dma((7,)), dma((7,)), dma((3,)), dma((3,)),
        ]
        params = pltpu.CompilerParams(vmem_limit_bytes=VMEM_LIMIT, collective_id=2, has_side_effects=True)
    else:
        outs += [shape(w, BF16) for w in WEIGHTS] + [shape((16, D), F32), shape((16, 128), F32)]
        out_specs += [hbm] * 3 + [vmem, vmem]
        params = pltpu.CompilerParams(vmem_limit_bytes=VMEM_LIMIT)
    return pl.pallas_call(
        functools.partial(backward_kernel, linked),
        out_shape=outs,
        in_specs=[hbm] * 4 + [vmem] + [hbm] * 15,
        out_specs=out_specs,
        scratch_shapes=scratch,
        compiler_params=params,
        name="backward",
    )(x, y, cc, cq, vecs, wa, wi, wo, *saved)


def shards(
    content_stream, query_stream, lengths, ranking, query_weight, query_bias, key_weight, value_weight, value_bias,
    output_weight, output_bias, norm_gain, norm_shift, inner_weight, inner_bias, outer_weight, outer_bias, final_gain,
    final_shift, bucket_bias, content_cotangent, query_cotangent,
):
    small = (query_bias, value_bias, output_bias, norm_gain, norm_shift, outer_bias, final_gain, final_shift)
    width = query_bias.shape[0]
    linked = width * 8 == D and lax.axis_size("rep") == 4
    front = (content_stream, query_stream, lengths, ranking)
    if linked:
        rows = jnp.pad(jnp.stack(small), ((0, 0), (0, 128 - width)))
        rest = jnp.pad(bucket_bias, (0, 128 - bucket_bias.shape[0])).reshape(1, 128)
        packed = jnp.concatenate([rows, inner_bias.reshape(3, 128), rest, jnp.zeros((4, 128), BF16)])
        out_c, out_q, *saved, vecs, wa, wi, wo = call_forward(
            True, *front, packed, query_weight, key_weight, value_weight, output_weight, inner_weight, outer_weight
        )
    else:
        def gather(a, axis=0):
            return lax.all_gather(a, "fsdp", axis=axis, tiled=True)

        wa = gather(jnp.stack([query_weight, key_weight, value_weight, output_weight]), 1).reshape(WEIGHTS[0])
        wi = gather(inner_weight).reshape(D, 4, D).transpose(1, 0, 2).reshape(WEIGHTS[1])
        wo = gather(outer_weight).reshape(WEIGHTS[2])
        packed = gather(jnp.concatenate([*small, inner_bias, bucket_bias])[None, :])
        cuts = [packed[:, i * width : (i + 1) * width].reshape(1, D) for i in range(8)]
        cuts.append(packed[:, 8 * width : 12 * width].reshape(4, D))
        vecs = jnp.concatenate(cuts + [jnp.zeros((4, D), BF16)]).astype(F32)
        table = jnp.pad(packed[:, 12 * width :].reshape(HEADS, BUCKETS), ((0, 4), (0, 128 - BUCKETS)))
        out_c, out_q, *saved = call_forward(False, *front, vecs, table, wa, wi, wo)
    streams = (content_stream, query_stream, content_cotangent, query_cotangent)
    gc, gq, *grads = call_backward(linked, *streams, vecs, wa, wi, wo, saved)
    if linked:
        res, flat = grads
        res = res.astype(F32)
        ga, go = res[0], res[2].reshape(4 * width, D)
        gi = res[1].transpose(1, 0, 2).reshape(width, FF)
        v = [flat[i, :width] for i in range(8)]
        inner, table = flat[8:11].reshape(4 * width), flat[11, : bucket_bias.shape[0]]
    else:
        def reduce(a, axis=0):
            a = lax.psum_scatter(a, "fsdp", scatter_dimension=axis, tiled=True)
            return lax.psum(a.astype(BF16), "rep").astype(F32)

        ga, gi, go, gvec, gtab = grads
        ga = reduce(ga.reshape(4, D, D), 1)
        gi = reduce(gi.reshape(4, D, D).transpose(1, 0, 2).reshape(D, FF))
        go = reduce(go.reshape(FF, D))
        count = D // width
        flat = jnp.concatenate(
            [gvec[i].reshape(count, width) for i in range(8)]
            + [gvec[8:12].reshape(count, 4 * width), gtab[:HEADS, :BUCKETS].reshape(count, -1)],
            axis=1,
        )
        flat = lax.psum_scatter(flat, "fsdp", scatter_dimension=0, tiled=True)[0]
        flat = lax.psum(flat.astype(BF16), "rep").astype(F32)
        v = [flat[i * width : (i + 1) * width] for i in range(8)]
        inner, table = flat[8 * width : 12 * width], flat[12 * width :]
    return (
        out_c, out_q, gc, gq, ga[0], v[0], ga[1], ga[2], v[1], ga[3], v[2], v[3], v[4], gi,
        inner, go, v[5], v[6], v[7], table,
    )


def solution(mesh):
    both, fsdp = ("rep", "fsdp"), "fsdp"
    row, vec = P(fsdp, None), P(fsdp)
    tokens = P(both, None)
    in_specs = (
        tokens, tokens, P(both), tokens, row, vec, row, row, vec, row, vec, vec, vec, row, vec, row, vec, vec, vec, vec,
        tokens, tokens,
    )
    out_specs = (
        tokens, tokens, tokens, tokens, row, vec, row, row, vec, row, vec, vec, vec, row, vec, row, vec, vec, vec, vec,
    )
    return jax.shard_map(shards, mesh=mesh, in_specs=in_specs, out_specs=out_specs, check_vma=False)
```

```python
import functools

import jax
import jax.numpy as jnp
from jax import lax
from jax.experimental import pallas as pl
from jax.experimental.pallas import tpu as pltpu
from jax.sharding import PartitionSpec as P

HEADS = 12
HEAD_DIM = 64
PAIRS = HEADS // 2
BUCKETS = 32
SEQ = 512
ROWS = 2 * SEQ
D = 768
FF = 3072
TILE = 256
TILES = FF // TILE
EPS = 1e-05
NEG = -1e30
LOG2E = 1.4426950408889634
SCALE = HEAD_DIM**-0.5
FAR_STEPS = (12, 16, 23, 32, 46, 64, 91)
F32 = jnp.float32
BF16 = jnp.bfloat16
VMEM_LIMIT = 62 * 2**20

TAIL_P = 0.28
TAIL = (
    0.11608706693762069,
    0.07021928496801585,
    0.26212226118724974,
    -0.22858899246095166,
    0.3847049667747488,
    -0.10454457204169064,
)


def mm(a, b):
    return jnp.dot(a, b, preferred_element_type=F32)


def mm_nt(a, b):
    return lax.dot_general(a, b, (((1,), (1,)), ((), ())), preferred_element_type=F32)


def mm_tn(a, b):
    return lax.dot_general(a, b, (((0,), (0,)), ((), ())), preferred_element_type=F32)


def bucket_of(offset):
    distance = jnp.abs(offset)
    farther = jnp.full(distance.shape, 8, jnp.int32)
    for step_at in FAR_STEPS:
        farther = farther + jnp.where(distance >= step_at, 1, 0)
    return jnp.where(distance < 8, distance, farther) + jnp.where(offset > 0, 16, 0)


def normal_parts(x):
    size = jnp.abs(x)
    t = 1.0 / (1.0 + TAIL_P * size)
    poly = jnp.full(x.shape, TAIL[-1], F32)
    for c in TAIL[-2::-1]:
        poly = poly * t + c
    bell = jnp.exp2(x * x * (-0.5 * LOG2E))
    tail = poly * t * bell
    return jnp.where(x < 0, tail, 1.0 - tail), bell * 0.3989422804014327


def ds(start, size):
    return pl.ds(pl.multiple_of(start, size), size)


def places():
    f = lax.axis_index("fsdp")
    return lax.axis_index("rep"), f // 2, f % 2


def hop(i, k):
    if k == 0:
        return i
    if k == 1:
        return i + 1 - 2 * (i % 2)
    return (i + 2) % 4 if k == 2 else 3 - i


def remote(src, dst, send, recv, device):
    return pltpu.make_async_remote_copy(
        src_ref=src, dst_ref=dst, send_sem=send, recv_sem=recv, device_id=device, device_id_type=pl.DeviceIdType.MESH
    )


def greet(devices):
    barrier = pltpu.get_barrier_semaphore()
    for device in devices:
        pl.semaphore_signal(barrier, inc=1, device_id=device, device_id_type=pl.DeviceIdType.MESH)
    pl.semaphore_wait(barrier, len(devices))


PIECES = 3


def block_of(buffers, t, r, z, c):
    if t == 2:
        return buffers[2].at[z, pl.ds(pl.multiple_of(c * 384 + r * 96, 96), 96), :]
    return buffers[1].at[r, z, ds(c * 96, 96), :]


def quarter(u, r, c):
    rows = pl.ds(pl.multiple_of(c * 96 + (r // 2) * 48, 48), 48)
    if isinstance(u, int) and u == PIECES:
        return rows, ds((r % 2) * 384, 384)
    return rows, pl.ds(pl.multiple_of(u * 256 + (r % 2) * 128, 128), 128)


def matrices(u):
    return 3 if isinstance(u, int) and u == PIECES else slice(0, 3)


def columns(u):
    return slice(0, D) if isinstance(u, int) and u == PIECES else ds(u * 256, 256)


ALL = slice(0, 4)


class Gather:
    def __init__(self, refs, sems):
        *self.w, self.small = refs
        self.l_sem, self.zs, self.zr, self.xs, self.xr, self.cs, self.cr, self.vs, self.vr = sems
        self.r, self.z, self.c = places()

    def block(self, u, r, z, c):
        if isinstance(u, int) and u > PIECES:
            return block_of(self.w, u - PIECES, r, z, c)
        rows, cols = quarter(u, r, c)
        return self.w[0].at[matrices(u), z, rows, cols]

    def own(self, shards):
        *square, inner, outer = shards
        z, c = self.z, self.c
        rows = ds(c * 96, 96)
        copies = [
            [pltpu.make_async_copy(square[m], self.w[0].at[m, z, rows, :], self.l_sem.at[0, m]) for m in range(4)],
            [
                pltpu.make_async_copy(inner.at[:, m * D : (m + 1) * D], self.block(4, m, z, c), self.l_sem.at[1, m])
                for m in range(4)
            ],
            [pltpu.make_async_copy(outer, self.w[2].at[z, ds(c * 384, 384), :], self.l_sem.at[2, 0])],
        ]
        return copies

    def small_copy(self, k):
        f = 2 * self.z + self.c
        return remote(
            self.small.at[f], self.small.at[f], self.vs.at[k - 1], self.vr.at[k - 1], (self.r, (f + k) % 8)
        )

    def small_come(self, k):
        f = (2 * self.z + self.c + 8 - k) % 8
        return remote(self.small.at[f], self.small.at[f], self.vs.at[k - 1], self.vr.at[k - 1], (self.r, f))

    def z_copy(self, u, k, come=False):
        far = hop(self.z, k)
        ref = self.block(u, self.r, far if come else self.z, self.c)
        return remote(ref, ref, self.zs.at[u, k - 1], self.zr.at[u, k - 1], (self.r, 2 * far + self.c))

    def x_copy(self, u, k, m, come=False):
        far = hop(self.r, m)
        ref = self.block(u, far if come else self.r, hop(self.z, k), self.c)
        at = 3 * (k - 1) + m - 1
        return remote(ref, ref, self.xs.at[u, at], self.xr.at[u, at], (far, 2 * self.z + self.c))

    def c_copy(self, u, m, come=False):
        c = 1 - self.c if come else self.c
        if isinstance(u, int) and u > PIECES:
            ref = self.block(u, hop(self.r, m), ALL, c)
        else:
            ref = self.w[0].at[matrices(u), ALL, ds(c * 96, 96), columns(u)]
        return remote(ref, ref, self.cs.at[u, m], self.cr.at[u, m], (self.r, 2 * self.z + 1 - self.c))

    def parts(self, u):
        return 4 if isinstance(u, int) and u > PIECES else 1

    def start_z(self, u):
        for k in (1, 2, 3):
            self.z_copy(u, k).start()

    def pass_on(self, u):
        for k in (1, 2, 3):
            self.z_copy(u, k, True).wait_recv()
            for m in (1, 2, 3):
                self.x_copy(u, k, m).start()

    def share(self, u):
        parts = self.parts(u)
        for m in range(4):
            if m:
                for k in (1, 2, 3):
                    self.x_copy(u, k, m, True).wait_recv()
            if parts == 4:
                self.c_copy(u, m).start()
        if parts == 1:
            self.c_copy(u, 0).start()

    def finish(self, u):
        for m in range(self.parts(u)):
            self.c_copy(u, m, True).wait_recv()

    def drain(self):
        for k in range(1, 8):
            self.small_copy(k).wait_send()

        def sent(u):
            for k in (1, 2, 3):
                self.z_copy(u, k).wait_send()
                for m in (1, 2, 3):
                    self.x_copy(u, k, m).wait_send()
            for m in range(self.parts(u)):
                self.c_copy(u, m).wait_send()

        lax.fori_loop(0, PIECES, lambda u, carry: (sent(u), carry)[1], 0)
        for u in (3, 4, 5):
            sent(u)


def unpack_small(small_s, vec_s):
    blocks = [small_s[f] for f in range(8)]
    at = lax.broadcasted_iota(jnp.int32, (1024, D), 0)
    want = lax.broadcasted_iota(jnp.int32, (1024, D), 1)
    spread = jnp.where((at % 128 < 96) & (want == (at // 128) * 96 + at % 128), 1.0, 0.0).astype(BF16)
    vec_s[...] = mm(jnp.concatenate(blocks, axis=1), spread)
    wide = [b.astype(F32) for b in blocks]
    for m in range(4):
        for j in range(6):
            vec_s[8 + m : 9 + m, j * 128 : (j + 1) * 128] = wide[2 * m + j // 3][8 + j % 3 : 9 + j % 3]
    return [w[11:12] for w in wide]


def lines_of(rows):
    bucket = bucket_of(lax.broadcasted_iota(jnp.int32, (128, 1024), 1) - 512)
    entry = lax.broadcasted_iota(jnp.int32, (128, 1024), 0)

    def pick(first, shift):
        inside = (entry >= first) & (entry < 48)
        return jnp.where(inside & (bucket == entry + shift), 1.0, 0.0).astype(BF16)

    table = jnp.concatenate(rows, axis=0).astype(BF16)
    a0, a1, b1, b2 = (mm(table, pick(*p)) for p in ((0, 0), (32, -32), (0, 16), (16, -16)))
    lines = []
    for m in range(4):
        i, j = 2 * m, 2 * m + 1
        lines += [a0[i : i + 1], a1[i : i + 1] + b1[j : j + 1], b2[j : j + 1]]
    return [line * LOG2E for line in lines]


def build_masks(len_ref, rank_ref, mask_s):
    n = len_ref[0]
    rank = rank_ref[...]
    place = lax.broadcasted_iota(jnp.int32, (1, SEQ), 1)
    valid = place < n
    chosen = valid & (rank >= n - 3 * n // 20)
    key = jnp.where(chosen, rank, jnp.where(valid, -1, 2 * SEQ)).astype(F32)
    column = jnp.broadcast_to(rank.astype(F32), (128, SEQ)).T
    for s in range(2):
        for j in range(SEQ // 128):
            seen = jnp.broadcast_to(key[:, j * 128 : (j + 1) * 128], (SEQ, 128)) <= column - s
            mask_s[s, :, j * 128 : (j + 1) * 128] = jnp.where(seen, 0.0, NEG)


def lines_of_table(tab_ref):
    offset = lax.broadcasted_iota(jnp.int32, (128, 1024), 1) - 512
    bucket = lax.broadcasted_iota(jnp.int32, (128, 1024), 0)
    onehot = jnp.where(bucket_of(offset) == bucket, 1.0, 0.0).astype(BF16)
    line = mm(tab_ref[...], onehot) * LOG2E
    return [line[h : h + 1] for h in range(HEADS)]


def build_strip(lines, strip_s):
    for h in range(HEADS):
        wide = jnp.broadcast_to(lines[h], (128, 1024))
        strip_s[h] = pltpu.roll(wide, 0, 1, stride=1, stride_axis=0)[:, 128:]


def square(w_s, m, cols=slice(None)):
    block = w_s[m, :, :, cols]
    return block.reshape(D, block.shape[-1])


def project(x_ref, y_ref, vec_ref, w_s, q_s, k_s, v_s, p):
    cols = ds(p * 256, 256)
    x = x_ref[...]
    parts = (
        (q_s, 0, mm(x, square(w_s, 0, cols)) + vec_ref[0:1, cols]),
        (q_s, 1, mm(y_ref[...], square(w_s, 0, cols)) + vec_ref[0:1, cols]),
        (k_s, None, mm(x, square(w_s, 1, cols))),
        (v_s, None, mm(x, square(w_s, 2, cols)) + vec_ref[1:2, cols]),
    )
    for ref, s, value in parts:
        value = value.astype(BF16)
        for e in range(2):
            piece = value[:, e * 128 : (e + 1) * 128]
            if s is None:
                ref[2 * p + e] = piece
            else:
                ref[s, 2 * p + e] = piece


def attend(q_s, k_s, v_s, strip_s, mask_s, p_st, ctx_s, hp, slot):
    lane = lax.broadcasted_iota(jnp.int32, (SEQ, 128), 1)
    k = k_s[hp]
    v = v_s[hp]
    for s in range(2):
        q = q_s[s, hp]
        outs = []
        for e in range(2):
            own = (lane < 64) if e == 0 else (lane >= 64)
            scores = mm_nt(jnp.where(own, q, jnp.zeros_like(q)), k)
            for i in range(SEQ // 128):
                rows = slice(i * 128, (i + 1) * 128)
                blk = (
                    scores[rows] * (SCALE * LOG2E)
                    + strip_s[2 * hp + e, :, (3 - i) * 128 : (3 - i) * 128 + SEQ]
                    + mask_s[s, rows, :]
                )
                top = jnp.max(blk, axis=1, keepdims=True)
                w = jnp.exp2(blk - top)
                w = w * (1.0 / jnp.sum(w, axis=1, keepdims=True))
                p_st[slot, e, s, rows, :] = w.astype(BF16)
            outs.append(mm(p_st[slot, e, s], v))
        ctx_s[s * SEQ : (s + 1) * SEQ, ds(hp * 128, 128)] = jnp.where(
            lane < 64, outs[0], outs[1]
        ).astype(BF16)


def norm_stats(r):
    mean = jnp.mean(r, axis=1, keepdims=True)
    centred = r - mean
    inverse = lax.rsqrt(jnp.mean(centred * centred, axis=1, keepdims=True) + EPS)
    return centred * inverse, inverse


NETWORK = {
    (0, 0): (("pass_on", 2), ("start_z", 3), ("start_z", 4)),
    (0, 1): (("share", 1),),
    (1, 0): (("pass_on", 3), ("start_z", 5)),
    (1, 1): (("share", 2), ("pass_on", 4)),
    (2, 0): (("share", 3),),
    (2, 1): (("pass_on", 5),),
}


def forward_kernel(linked, *refs):
    refs = list(refs)
    take = lambda n: [refs.pop(0) for _ in range(n)]
    x_ref, y_ref, len_ref, rank_ref = take(4)
    if linked:
        (small_ref,) = take(1)
        shards = take(6)
    else:
        vec_ref, tab_ref, *weights = take(5)
    oc_ref, oq_ref, q_h, k_h, v_h, p_h, ctx_h, n1_h, inv1_h, nl_h, act_h, slope_h, n2_h, inv2_h = take(14)
    if linked:
        vec_h, *weights = take(4)
    wa_s, wi_s, wo_s, q_s, k_s, v_s, ctx_s, nl_s, n1_s, br_s, inv1_s, inv2_s, o_sem, st_sem, w_sem = take(15)
    copies = (wa_s, wi_s, wo_s)
    if linked:
        small_s, vec_ref, *sems = take(10)
        net = Gather((wa_s, wi_s, wo_s, small_s), (w_sem, *sems))
        r, z, c = places()
        f = 2 * z + c
        own = net.own(shards)
        for batch in own:
            for copy in batch:
                copy.start()
        small_s[f] = small_ref[...]
        greet(
            [(hop(r, m), f) for m in (1, 2, 3)] + [(r, (f + k) % 8) for k in range(1, 8)]
        )
        for k in range(1, 8):
            net.small_copy(k).start()
        for copy in own[0]:
            copy.wait()
        for u in range(PIECES):
            net.start_z(u)
    else:
        loads = [pltpu.make_async_copy(src, dst, w_sem.at[i, 0]) for i, (src, dst) in enumerate(zip(weights, copies))]
        for copy in loads:
            copy.start()
    stores = []

    def keep(src, dst):
        pltpu.make_async_copy(src, dst, o_sem.at[len(stores)]).start()
        stores.append((src, dst))

    def attention(strip_s, mask_s, p_st):
        build_masks(len_ref, rank_ref, mask_s)
        if linked:
            for k in range(1, 8):
                net.small_come(k).wait_recv()
            build_strip(lines_of(unpack_small(small_s, vec_ref)), strip_s)
            net.pass_on(0)
            net.pass_on(1)
            for copy in own[1] + own[2]:
                copy.wait()
            net.share(0)
            keep(vec_ref, vec_h)
        else:
            build_strip(lines_of_table(tab_ref), strip_s)
            loads[0].wait()

        def store(hp, slot):
            return pltpu.make_async_copy(p_st.at[slot], p_h.at[hp], st_sem.at[slot])

        def hooks(p, part):
            for (at, when), moves in NETWORK.items():
                if when == part:
                    @pl.when(p == at)
                    def _(moves=moves):
                        for name, u in moves:
                            getattr(net, name)(u)

        def step(p, carry):
            if linked:
                net.finish(p)
            project(x_ref, y_ref, vec_ref, wa_s, q_s, k_s, v_s, p)
            for part in range(2):
                if linked:
                    hooks(p, part)

                @pl.when(p >= 1)
                def _():
                    store(2 * p - 2 + part, part).wait()

                attend(q_s, k_s, v_s, strip_s, mask_s, p_st, ctx_s, 2 * p + part, part)
                store(2 * p + part, part).start()
            return carry

        lax.fori_loop(0, PIECES, step, 0)
        for part in range(2):
            store(PAIRS - 2 + part, part).wait()
        keep(q_s, q_h)
        keep(k_s, k_h)
        keep(v_s, v_h)

    pl.run_scoped(
        attention,
        pltpu.VMEM((HEADS, 128, 896), F32),
        pltpu.VMEM((2, SEQ, SEQ), F32),
        pltpu.VMEM((2, 2, 2, SEQ, SEQ), BF16),
    )
    keep(ctx_s, ctx_h)
    if linked:
        net.finish(3)
        keep(wa_s, weights[0])

    for s, in_ref in ((0, x_ref), (1, y_ref)):
        def first(i, carry, s=s, in_ref=in_ref):
            own = ds(i * 256, 256)
            rows = ds(s * SEQ + i * 256, 256)
            r = in_ref[own, :].astype(F32) + mm(ctx_s[rows, :], square(wa_s, 3)) + vec_ref[2:3, :]
            n, inverse = norm_stats(r)
            n1_s[rows, :] = n
            inv1_s[rows, :] = jnp.broadcast_to(inverse, (256, 128))
            nl_s[rows, :] = (n * vec_ref[3:4, :] + vec_ref[4:5, :]).astype(BF16)
            return carry

        lax.fori_loop(0, SEQ // 256, first, 0)
    keep(n1_s, n1_h)
    keep(inv1_s, inv1_h)
    keep(nl_s, nl_h)

    if linked:
        net.share(4)
        net.finish(4)
        keep(wi_s, weights[1])
    else:
        loads[1].wait()
        loads[2].wait()

    def feed(act_s, slope_st):
        def part(t):
            return ds(t * TILE, TILE)

        def pair(t, slot):
            return (
                pltpu.make_async_copy(act_s.at[:, part(t)], act_h.at[:, part(t)], st_sem.at[slot]),
                pltpu.make_async_copy(slope_st.at[slot], slope_h.at[:, part(t)], st_sem.at[2 + slot]),
            )

        def step(t, carry):
            slot = t % 2

            @pl.when(t >= 2)
            def _():
                for c in pair(t - 2, slot):
                    c.wait()

            if linked:
                @pl.when(t == 9)
                def _():
                    net.share(5)

            cols = ds((t % 3) * TILE, TILE)
            inner = mm(nl_s[...], square(wi_s, t // 3, cols)) + vec_ref[pl.ds(8 + (t // 3), 1), cols]
            spread, bell = normal_parts(inner)
            act_s[:, part(t)] = (inner * spread).astype(BF16)
            slope_st[slot] = (spread + inner * bell).astype(BF16)
            for c in pair(t, slot):
                c.start()
            return carry

        lax.fori_loop(0, TILES, step, 0)
        if linked:
            net.finish(5)
            keep(wo_s, weights[2])

        def outer(i, carry):
            rows = ds(i * 256, 256)
            br_s[rows, :] = mm(act_s[rows, :], wo_s[...].reshape(FF, D))
            return carry

        lax.fori_loop(0, ROWS // 256, outer, 0)
        for t in (TILES - 2, TILES - 1):
            for c in pair(t, t % 2):
                c.wait()

    pl.run_scoped(feed, pltpu.VMEM((ROWS, FF), BF16), pltpu.VMEM((2, ROWS, TILE), BF16))

    for s, o_ref in ((0, oc_ref), (1, oq_ref)):
        def last(i, carry, s=s, o_ref=o_ref):
            rows = ds(s * SEQ + i * 128, 128)
            normed = n1_s[rows, :] * vec_ref[3:4, :] + vec_ref[4:5, :]
            n, inverse = norm_stats(normed + br_s[rows, :] + vec_ref[5:6, :])
            br_s[rows, :] = n
            inv2_s[rows, :] = jnp.broadcast_to(inverse, (128, 128))
            o_ref[ds(i * 128, 128), :] = (n * vec_ref[6:7, :] + vec_ref[7:8, :]).astype(BF16)
            return carry

        lax.fori_loop(0, SEQ // 128, last, 0)
    keep(br_s, n2_h)
    keep(inv2_s, inv2_h)
    for i, (src, dst) in enumerate(stores):
        pltpu.make_async_copy(src, dst, o_sem.at[i]).wait()
    if linked:
        net.drain()


WEIGHTS = ((4, 4, 192, D), (4, 4, 192, D), (4, D, D))


def call_forward(linked, *args):
    hbm = pl.BlockSpec(memory_space=pl.ANY)
    vmem = pl.BlockSpec(memory_space=pltpu.VMEM)
    smem = pl.BlockSpec(memory_space=pltpu.SMEM)
    dma = pltpu.SemaphoreType.DMA
    shape = jax.ShapeDtypeStruct
    outs = [
        shape((SEQ, D), BF16), shape((SEQ, D), BF16),
        shape((2, PAIRS, SEQ, 128), BF16), shape((PAIRS, SEQ, 128), BF16), shape((PAIRS, SEQ, 128), BF16),
        shape((PAIRS, 2, 2, SEQ, SEQ), BF16), shape((ROWS, D), BF16),
        shape((ROWS, D), F32), shape((ROWS, 128), F32), shape((ROWS, D), BF16),
        shape((ROWS, FF), BF16), shape((ROWS, FF), BF16),
        shape((ROWS, D), F32), shape((ROWS, 128), F32),
    ]
    scratch = [pltpu.VMEM(w, BF16) for w in WEIGHTS] + [
        pltpu.VMEM((2, PAIRS, SEQ, 128), BF16), pltpu.VMEM((PAIRS, SEQ, 128), BF16), pltpu.VMEM((PAIRS, SEQ, 128), BF16),
        pltpu.VMEM((ROWS, D), BF16), pltpu.VMEM((ROWS, D), BF16), pltpu.VMEM((ROWS, D), F32), pltpu.VMEM((ROWS, D), F32),
        pltpu.VMEM((ROWS, 128), F32), pltpu.VMEM((ROWS, 128), F32),
        dma((13,)), dma((4,)), dma((3, 4)),
    ]
    in_specs = [vmem, vmem, smem, vmem]
    if linked:
        in_specs += [vmem] + [hbm] * 6
        outs += [shape((16, D), F32)] + [shape(w, BF16) for w in WEIGHTS]
        scratch += [
            pltpu.VMEM((8, 16, 128), BF16), pltpu.VMEM((16, D), F32),
            dma((6, 3)), dma((6, 3)), dma((6, 9)), dma((6, 9)), dma((6, 4)), dma((6, 4)), dma((7,)), dma((7,)),
        ]
        params = pltpu.CompilerParams(vmem_limit_bytes=VMEM_LIMIT, collective_id=1, has_side_effects=True)
    else:
        in_specs += [vmem, vmem] + [hbm] * 3
        params = pltpu.CompilerParams(vmem_limit_bytes=VMEM_LIMIT)
    return pl.pallas_call(
        functools.partial(forward_kernel, linked),
        out_shape=outs,
        in_specs=in_specs,
        out_specs=[vmem, vmem] + [hbm] * (len(outs) - 2),
        scratch_shapes=scratch,
        compiler_params=params,
        name="forward",
    )(*args)


class Reduce:
    def __init__(self, refs, sems):
        self.g, more = refs
        self.cr1, self.cr2, self.xr0, self.xr3, self.xr1, self.xr2, self.zr0, self.zr3, self.zr1, self.zr2 = more[:10]
        self.tt, self.yr, self.res = (more[10], more[11]), (more[12], more[13]), more[14]
        self.cs, self.cr, self.credit, self.xs, self.xd, self.zs, self.zd, self.ys, self.yd, self.as_, self.ad = sems
        self.r, self.z, self.c = places()
        self.f = 2 * self.z + self.c
        self.side = (self.r % 2, self.r // 2)


    def part(self, u, r, z):
        rows, cols = quarter(u, r, self.c)
        return self.g[0].at[matrices(u), z, rows, cols]

    def core0(self, u):
        src = self.g[0].at[matrices(u), ALL, ds((1 - self.c) * 96, 96), columns(u)]
        dst = self.cr1.at[matrices(u), ALL, :, columns(u)]
        return remote(src, dst, self.cs.at[0, u], self.cr.at[0, u], (self.r, 2 * self.z + 1 - self.c))

    def across0(self, u, m):
        to = hop(self.r, m + 1)
        dst = self.xr3.at[m] if isinstance(u, int) and u == PIECES else self.xr0.at[u, m]
        return remote(self.part(u, to, ALL), dst, self.xs.at[0, 3 * u + m], self.xd.at[0, 3 * u + m], (to, self.f))

    def along0(self, u, k):
        to = hop(self.z, k + 1)
        dst = self.zr3.at[k] if isinstance(u, int) and u == PIECES else self.zr0.at[u, k]
        device = (self.r, 2 * to + self.c)
        return remote(self.part(u, self.r, to), dst, self.zs.at[0, 3 * u + k], self.zd.at[0, 3 * u + k], device)

    def result(self, u, r):
        rows, cols = quarter(u, r, 0)
        return self.res.at[0, matrices(u), rows, cols]

    def spread0(self, u, m, come=False):
        far = hop(self.r, m + 1)
        ref = self.result(u, far if come else self.r)
        return remote(ref, ref, self.as_.at[0, 3 * u + m], self.ad.at[0, 3 * u + m], (far, self.f))

    def start0(self, u):
        self.core0(u).start()

    def cores0(self, u):
        self.core0(u).wait_recv()

        def add(i, carry):
            rows = ds(self.c * 96, 96)
            total = self.g[0][matrices(u), i, rows, columns(u)].astype(F32)
            total = total + self.cr1[matrices(u), i, :, columns(u)].astype(F32)
            self.g[0][matrices(u), i, rows, columns(u)] = total.astype(BF16)
            return carry

        lax.fori_loop(0, 4, add, 0)
        for m in range(3):
            self.across0(u, m).start()

    def replicas0(self, u):
        last = isinstance(u, int) and u == PIECES
        ref = self.part(u, self.r, ALL)
        total = ref[...].astype(F32)
        for m in range(3):
            self.across0(u, m).wait_recv()
            total = total + (self.xr3[m] if last else self.xr0[u, m]).astype(F32)
        ref[...] = total.astype(BF16)
        for k in range(3):
            self.along0(u, k).start()

    def owners0(self, u):
        last = isinstance(u, int) and u == PIECES
        total = self.part(u, self.r, self.z)[...].astype(F32)
        for k in range(3):
            self.along0(u, k).wait_recv()
            total = total + (self.zr3[k] if last else self.zr0[u, k]).astype(F32)
        self.result(u, self.r)[...] = total.astype(BF16)
        for m in range(3):
            self.spread0(u, m).start()

    def finish0(self, u):
        for m in range(3):
            self.spread0(u, m, True).wait_recv()


    def part1(self, i, m, z, give=False):
        side = 1 - self.side[m] if give else self.side[m]
        rows = pl.ds(pl.multiple_of(self.c * 96 + m * 48, 48), 48)
        return self.g[1].at[i, z, rows, ds(side * 384, 384)]

    def part2(self, m, z, give=False):
        side = 1 - self.side[m] if give else self.side[m]
        return block_of(self.g, 2, 2 * m + side, z, self.c)

    def core(self, t, i):
        if t == 2:
            src, dst = self.g[2].at[i, ds((1 - self.c) * 384, 384), :], self.cr2.at[i]
        else:
            src, dst = block_of(self.g, 1, i, ALL, 1 - self.c), self.cr1.at[i]
        return remote(src, dst, self.cs.at[t, i], self.cr.at[t, i], (self.r, 2 * self.z + 1 - self.c))

    def across(self, t, i, m):
        at, device = 2 * i + m, (hop(self.r, m + 1), self.f)
        if t == 1:
            src, dst = self.part1(i, m, ALL, True), self.xr1.at[m, i]
        else:
            src, dst = self.part2(m, i, True), self.xr2.at[m, i]
        return remote(src, dst, self.xs.at[t, at], self.xd.at[t, at], device)

    def along1(self, i, k, m, come=False):
        far = hop(self.z, k)
        src, dst = self.part1(i, m, far), self.zr1.at[k - 1, m, i]
        at = 8 * (k - 1) + 2 * i + m
        return remote(src, dst, self.zs.at[1, at], self.zd.at[1, at], (self.r, 2 * far + self.c))

    def along2(self, to, m):
        src, dst = self.part2(m, to), self.zr2.at[self.z, m]
        return remote(
            src, dst, self.zs.at[2, 2 * to + m], self.zd.at[2, 2 * self.z + m], (self.r, 2 * to + self.c)
        )

    def along2_come(self, back, m):
        src, dst = self.part2(m, back), self.zr2.at[back, m]
        return remote(src, dst, self.zs.at[2, 2 * back + m], self.zd.at[2, 2 * back + m], (self.r, 2 * back + self.c))

    def complete(self, t, m):
        src, dst = self.tt[t - 1].at[m], self.yr[t - 1].at[m]
        return remote(src, dst, self.ys.at[t - 1, m], self.yd.at[t - 1, m], (hop(self.r, 2 - m), self.f))

    def result_of(self, t, m, give=False):
        side = 1 - self.side[m] if give else self.side[m]
        if t == 1:
            return self.res.at[1, :, m * 48 : (m + 1) * 48, ds(side * 384, 384)]
        return self.res.at[2, 2 * m + side]

    def spread(self, t, m, come=False):
        ref = self.result_of(t, m, come)
        return remote(ref, ref, self.as_.at[t, m], self.ad.at[t, m], (hop(self.r, m + 1), self.f))

    def start(self, i):
        self.core(2, i).start()
        self.core(1, i).start()

    def cores(self, i):
        rows = ds(self.c * 384, 384)
        self.core(2, i).wait_recv()
        self.g[2][i, rows, :] = (self.g[2][i, rows, :].astype(F32) + self.cr2[i].astype(F32)).astype(BF16)
        for m in range(2):
            self.across(2, i, m).start()
        rows = ds(self.c * 96, 96)
        self.core(1, i).wait_recv()
        self.g[1][i, :, rows, :] = (self.g[1][i, :, rows, :].astype(F32) + self.cr1[i].astype(F32)).astype(BF16)
        for m in range(2):
            self.across(1, i, m).start()

    def allow0(self):
        pl.semaphore_signal(
            self.credit, inc=1, device_id=(self.r, 2 * self.z + 1 - self.c), device_id_type=pl.DeviceIdType.MESH
        )

    def replicas(self, i):
        for m in range(2):
            self.across(2, i, m).wait_recv()
            ref = self.part2(m, i)
            ref[...] = (ref[...].astype(F32) + self.xr2[m, i].astype(F32)).astype(BF16)

            @pl.when(self.z != i)
            def _(m=m):
                self.along2(i, m).start()

        for m in range(2):
            self.across(1, i, m).wait_recv()
            ref = self.part1(i, m, ALL)
            ref[...] = (ref[...].astype(F32) + self.xr1[m, i].astype(F32)).astype(BF16)
            for k in (1, 2, 3):
                self.along1(i, k, m).start()

    def owners(self, t):
        for m in range(2):
            if t == 1:
                for i in range(4):
                    total = self.part1(i, m, self.z)[...].astype(F32)
                    for k in (1, 2, 3):
                        self.along1(i, k, m).wait_recv()
                        total = total + self.zr1[k - 1, m, i].astype(F32)
                    self.tt[0][m, i] = total.astype(BF16)
            else:
                total = self.part2(m, self.z)[...].astype(F32)
                for k in (1, 2, 3):
                    back = hop(self.z, k)
                    self.along2_come(back, m).wait_recv()
                    total = total + self.zr2[back, m].astype(F32)
                self.tt[1][m] = total.astype(BF16)
            self.complete(t, m).start()

    def ends(self, t):
        for m in range(2):
            self.complete(t, m).wait_recv()
            total = self.tt[t - 1][m].astype(F32) + self.yr[t - 1][m].astype(F32)
            self.result_of(t, m)[...] = total.astype(BF16)
            self.spread(t, m).start()

    def finish(self, t):
        for m in range(2):
            self.spread(t, m, True).wait_recv()

    def drain(self):
        def sent(u):
            self.core0(u).wait_send()
            for m in range(3):
                self.across0(u, m).wait_send()
                self.along0(u, m).wait_send()
                self.spread0(u, m).wait_send()

        lax.fori_loop(0, PIECES, lambda u, carry: (sent(u), carry)[1], 0)
        sent(PIECES)
        for m in range(2):
            for t in (1, 2):
                for i in range(4):
                    self.across(t, i, m).wait_send()
                self.complete(t, m).wait_send()
                self.spread(t, m).wait_send()
            for k in (1, 2, 3):
                self.along2(hop(self.z, k), m).wait_send()
                for i in range(4):
                    self.along1(i, k, m).wait_send()
        for t in (1, 2):
            for i in range(4):
                self.core(t, i).wait_send()


class SmallReduce:
    def __init__(self, refs, sems):
        self.out, self.got, self.sums = refs
        self.vs, self.vd, self.ws, self.wd = sems
        self.r, z, c = places()
        self.f = 2 * z + c

    def first(self, k):
        to = (self.f + k) % 8
        return remote(self.out.at[to], self.got.at[self.f], self.vs.at[k - 1], self.vd.at[k - 1], (self.r, to))

    def first_come(self, k):
        back = (self.f + 8 - k) % 8
        return remote(self.out.at[back], self.got.at[back], self.vs.at[k - 1], self.vd.at[k - 1], (self.r, back))

    def second(self, m, come=False):
        far = hop(self.r, m)
        ref = self.sums.at[far if come else self.r]
        return remote(ref, ref, self.ws.at[m - 1], self.wd.at[m - 1], (far, self.f))

    def start(self, vec, table):
        pack_small(vec, table, self.out)
        self.got[self.f] = self.out[self.f]
        for k in range(1, 8):
            self.first(k).start()

    def middle(self):
        for k in range(1, 8):
            self.first_come(k).wait_recv()
        total = self.got[0]
        for f in range(1, 8):
            total = total + self.got[f]
        self.sums[self.r] = total
        for m in (1, 2, 3):
            self.second(m).start()

    def finish(self):
        for m in (1, 2, 3):
            self.second(m, True).wait_recv()
        total = self.sums[0]
        for r in range(1, 4):
            total = total + self.sums[r]
        return total

    def drain(self):
        for k in range(1, 8):
            self.first(k).wait_send()
        for m in (1, 2, 3):
            self.second(m).wait_send()


def pack_small(vec_ref, table, out_ref):
    want = lax.broadcasted_iota(jnp.int32, (D, 1024), 0)
    at = lax.broadcasted_iota(jnp.int32, (D, 1024), 1)
    gathered = jnp.where((at % 128 < 96) & (want == (at // 128) * 96 + at % 128), 1.0, 0.0)
    vec = vec_ref[...]
    rows = lax.dot_general(
        vec[0:8], gathered, (((1,), (0,)), ((), ())), precision=lax.Precision.HIGHEST, preferred_element_type=F32
    )
    lane = lax.broadcasted_iota(jnp.int32, (1, 128), 1)
    for f in range(8):
        m = f // 2
        out_ref[f, 0:8, :] = rows[:, f * 128 : (f + 1) * 128]
        for j in range(3):
            col = (f % 2) * 384 + j * 128
            out_ref[f, 8 + j : 9 + j, :] = vec[8 + m : 9 + m, col : col + 128]
        head = 3 * m + f % 2
        a, b = table[head : head + 1], table[head + 1 : head + 2]
        if f % 2 == 0:
            line = jnp.where(lane < 32, a, jnp.where(lane < 48, pltpu.roll(b, 32, 1), 0.0))
        else:
            line = jnp.where(lane < 16, pltpu.roll(a, 112, 1), jnp.where(lane < 48, pltpu.roll(b, 16, 1), 0.0))
        out_ref[f, 11:12, :] = line
        out_ref[f, 12:16, :] = jnp.zeros((4, 128), F32)


def norm_grad(u, gain, n, inverse):
    ug = u * gain
    return inverse * (
        ug - jnp.mean(ug, axis=1, keepdims=True) - n * jnp.mean(ug * n, axis=1, keepdims=True)
    )


BACK_NETWORK = {
    (0, 0): (("replicas", 3),),
    (0, 1): (("replicas0", 3),),
    (1, 1): (("cores0", 0), ("owners", 2)),
    (2, 0): (("replicas0", 0), ("owners0", 3)),
    (2, 1): (("cores0", 1), ("ends", 2)),
}


def backward_kernel(linked, *refs):
    refs = list(refs)
    take = lambda n: [refs.pop(0) for _ in range(n)]
    x_h, y_h, cc_h, cq_h, vec_ref, wa_h, wi_h, wo_h = take(8)
    q_h, k_h, v_h, p_h, ctx_h, n1_h, inv1_h, nl_h, act_h, slope_h, n2_h, inv2_h = take(12)
    gc_h, gq_h = take(2)
    if linked:
        res_ref, small_ref = take(2)
    else:
        *grads_h, gvec_ref, gtab_ref = take(5)
    ctx_s, g_s, dctx_s, tr_s, l_sem, t_sem = take(6)
    ga_s, gi_s, go_s = grads = take(3)
    if linked:
        gvec_ref, *more = take(16)
        sum_refs = take(3)
        sems = take(11)
        sum_sems = take(4)
        net = Reduce((grads, more), sems)
        sums = SmallReduce(sum_refs, sum_sems)
        r, z, c = places()
        f = 2 * z + c
        res_s = more[-1]
    cload = pltpu.make_async_copy(ctx_h, ctx_s, l_sem.at[1])
    cload.start()
    gvec_ref[...] = jnp.zeros_like(gvec_ref)

    def add_vec(row, value, cols=slice(None)):
        gvec_ref[row : row + 1, cols] += jnp.sum(value, axis=0, keepdims=True)

    def tail(n_s, inv_s, nl_s, db_s, act_s, slope_s, wi_s, wo_s, cot_s, wt_s):
        wload = pltpu.make_async_copy(wa_h.at[3], wt_s, l_sem.at[0])
        wload.start()
        nload = pltpu.make_async_copy(n2_h, n_s, l_sem.at[2])
        iload = pltpu.make_async_copy(inv2_h, inv_s, l_sem.at[3])
        nlload = pltpu.make_async_copy(nl_h, nl_s, l_sem.at[4])
        cots = [pltpu.make_async_copy(ref, cot_s.at[s], l_sem.at[5 + s]) for s, ref in enumerate((cc_h, cq_h))]
        for copy in (nload, iload, *cots, nlload):
            copy.start()

        def fetch(t, slot):
            return (
                pltpu.make_async_copy(act_h.at[:, ds(t * TILE, TILE)], act_s.at[slot], t_sem.at[slot]),
                pltpu.make_async_copy(slope_h.at[:, ds(t * TILE, TILE)], slope_s.at[slot], t_sem.at[2 + slot]),
                pltpu.make_async_copy(wi_h.at[t // 3, :, :, ds((t % 3) * TILE, TILE)], wi_s.at[slot], t_sem.at[4 + slot]),
                pltpu.make_async_copy(wo_h.at[t // 3, ds((t % 3) * TILE, TILE), :], wo_s.at[slot], t_sem.at[6 + slot]),
            )

        for copy in fetch(0, 0):
            copy.start()
        if linked:
            greet([(hop(r, m), f) for m in (1, 2, 3)] + [(r, (f + k) % 8) for k in range(1, 8)])
        for copy in (nload, iload, *cots):
            copy.wait()

        def second(i, carry):
            rows = ds(i * 128, 128)
            u = cot_s[i // 4, ds((i % 4) * 128, 128), :].astype(F32)
            n = n_s[rows, :]
            g = norm_grad(u, vec_ref[6:7, :], n, inv_s[rows, 0:1])
            add_vec(6, u * n)
            add_vec(7, u)
            g_s[rows, :] = g
            low = g.astype(BF16)
            db_s[rows, :] = low
            add_vec(5, low.astype(F32))
            return carry

        lax.fori_loop(0, ROWS // 128, second, 0)
        n1load = pltpu.make_async_copy(n1_h, n_s, l_sem.at[2])
        i1load = pltpu.make_async_copy(inv1_h, inv_s, l_sem.at[3])
        n1load.start()
        i1load.start()
        nlload.wait()
        tr_s[...] = nl_s[...].T
        xyloads = [
            pltpu.make_async_copy(ref, nl_s.at[s * SEQ : (s + 1) * SEQ, :], l_sem.at[5 + s])
            for s, ref in enumerate((x_h, y_h))
        ]
        for copy in xyloads:
            copy.start()

        def step(t, carry):
            slot = t % 2
            for copy in fetch(t, slot):
                copy.wait()

            @pl.when(t + 1 < TILES)
            def _():
                for copy in fetch(t + 1, 1 - slot):
                    copy.start()

            if linked:
                @pl.when((t % 3 == 1) & (t >= 4))
                def _():
                    net.cores(t // 3 - 1)

                @pl.when((t % 3 == 1) & (t >= 7))
                def _():
                    net.replicas(t // 3 - 2)

            db = db_s[...]
            di = (mm_nt(db, wo_s[slot]) * slope_s[slot].astype(F32)).astype(BF16)
            i, part = t // 3, ds((t % 3) * TILE, TILE)
            mine = lax.broadcasted_iota(jnp.int32, (8, TILE), 0) == i
            gvec_ref[8:16, part] += jnp.where(mine, jnp.sum(di.astype(F32), axis=0, keepdims=True), 0.0)
            go_s[i, part, :] = mm_tn(act_s[slot], db).astype(BF16)
            gi_s[i, :, :, part] = mm(tr_s[...], di).astype(BF16).reshape(4, 192, TILE)
            g_s[...] += mm_nt(di, wi_s[slot].reshape(D, TILE))
            if linked:
                @pl.when(t % 3 == 2)
                def _():
                    net.start(i)

            return carry

        lax.fori_loop(0, TILES, step, 0)
        n1load.wait()
        i1load.wait()

        def first(i, carry):
            rows = ds(i * 128, 128)
            u = g_s[rows, :]
            n = n_s[rows, :]
            g = norm_grad(u, vec_ref[3:4, :], n, inv_s[rows, 0:1])
            add_vec(3, u * n)
            add_vec(4, u)
            g_s[rows, :] = g
            low = g.astype(BF16)
            db_s[rows, :] = low
            add_vec(2, low.astype(F32))
            return carry

        lax.fori_loop(0, ROWS // 128, first, 0)
        wload.wait()
        cload.wait()
        if linked:
            net.cores(3)
            net.allow0()
            net.replicas(2)
        tr_s[...] = ctx_s[...].T
        ga_s[3] = mm(tr_s[...], db_s[...]).astype(BF16).reshape(4, 192, D)
        if linked:
            pl.semaphore_wait(net.credit, 1)
            net.start0(PIECES)
        for j in range(4):
            dctx_s[j * 256 : (j + 1) * 256, :] = mm_nt(db_s[j * 256 : (j + 1) * 256, :], wt_s[...].reshape(D, D)).astype(BF16)
        if linked:
            net.cores0(PIECES)
        for copy in xyloads:
            copy.wait()
        tr_s[...] = nl_s[...].T

    pl.run_scoped(
        tail,
        pltpu.VMEM((ROWS, D), F32),
        pltpu.VMEM((ROWS, 128), F32),
        pltpu.VMEM((ROWS, D), BF16),
        pltpu.VMEM((ROWS, D), BF16),
        pltpu.VMEM((2, ROWS, TILE), BF16),
        pltpu.VMEM((2, ROWS, TILE), BF16),
        pltpu.VMEM((2, 4, 192, TILE), BF16),
        pltpu.VMEM((2, TILE, D), BF16),
        pltpu.VMEM((2, SEQ, D), BF16),
        pltpu.VMEM(WEIGHTS[0][1:], BF16),
    )

    def attention(q_s, k_s, v_s, p_s, dq_s, dk_s, dv_s, dkt_s, dvt_s, far_s, bt_s, wa_s):
        wload = pltpu.make_async_copy(wa_h.at[0:3], wa_s, l_sem.at[0])
        wload.start()
        loads = [(q_h, q_s), (k_h, k_s), (v_h, v_s)]
        loads = [pltpu.make_async_copy(a, b, l_sem.at[2 + i]) for i, (a, b) in enumerate(loads)]
        for copy in loads:
            copy.start()

        def fetch(hp, slot):
            return pltpu.make_async_copy(p_h.at[hp], p_s.at[slot], t_sem.at[slot])

        fetch(0, 0).start()
        for copy in loads:
            copy.wait()

        def hooks(p, part):
            for (at, when), moves in BACK_NETWORK.items():
                if when == part:
                    @pl.when(p == at)
                    def _(moves=moves):
                        for name, u in moves:
                            getattr(net, name)(u)

        def step(p, carry):
            for part in range(2):
                hp = 2 * p + part
                if part == 0:
                    fetch(hp + 1, 1).start()
                else:
                    @pl.when(p + 1 < PIECES)
                    def _():
                        fetch(hp + 1, 0).start()

                if linked:
                    hooks(p, part)
                fetch(hp, part).wait()
                attend_back(hp, part)
            cols = ds(p * 256, 256)
            dk_s[:, cols] = dkt_s[cols, :].T
            dv_s[:, cols] = dvt_s[cols, :].T
            for w, left, grad in ((1, slice(0, SEQ), dk_s), (2, slice(0, SEQ), dv_s), (0, slice(0, ROWS), dq_s)):
                ga_s[w, :, :, cols] = mm(tr_s[:, left], grad[:, cols]).astype(BF16).reshape(4, 192, 256)
            if linked:
                net.start0(p)
            return carry

        def attend_back(hp, slot):
            lane = lax.broadcasted_iota(jnp.int32, (SEQ, 128), 1)
            k, v = k_s[hp], v_s[hp]
            zero = jnp.zeros((SEQ, 128), BF16)
            dq = [None, None]
            qt = [q_s[s, hp].T for s in range(2)]
            dt = [dctx_s[s * SEQ : (s + 1) * SEQ, ds(hp * 128, 128)].T for s in range(2)]
            for e in range(2):
                own = (lane < 64) if e == 0 else (lane >= 64)
                both = None
                dkt = dvt = None
                for s in range(2):
                    rows = slice(s * SEQ, (s + 1) * SEQ)
                    do = jnp.where(own, dctx_s[rows, ds(hp * 128, 128)], zero)
                    weight = jnp.sum(do.astype(F32) * ctx_s[rows, ds(hp * 128, 128)].astype(F32), axis=1, keepdims=True)
                    p = p_s[slot, e, s]
                    g = p.astype(F32) * (mm_nt(do, v) - weight)
                    low = g.astype(BF16)
                    both = g if both is None else both + g
                    part = mm(low, jnp.where(own, k, zero))
                    dq[s] = part if dq[s] is None else dq[s] + part
                    half = slice(e * 64, (e + 1) * 64)
                    a = mm(dt[s][half], p)
                    b = mm(qt[s][half], low)
                    dvt = a if dvt is None else dvt + a
                    dkt = b if dkt is None else dkt + b
                dvt_s[ds(hp * 128 + e * 64, 64), :] = dvt.astype(BF16)
                dkt_s[ds(hp * 128 + e * 64, 64), :] = (dkt * SCALE).astype(BF16)
                parts = [None] * 5
                for i in range(4):
                    for j in range(4):
                        blk = both[i * 128 : (i + 1) * 128, j * 128 : (j + 1) * 128]
                        at = min(max(j - i, -2), 2) + 2
                        parts[at] = blk if parts[at] is None else parts[at] + blk
                strip = jnp.concatenate([jnp.zeros((128, 128), F32), parts[1], parts[2], parts[3]], axis=1)
                flat = strip[0:8]
                for g in range(1, 16):
                    flat = flat + pltpu.roll(strip[8 * g : 8 * g + 8], 512 - 8 * g, 1)
                row = lax.broadcasted_iota(jnp.int32, (8, 512), 0)
                for bit in (1, 2, 4):
                    flat = jnp.where((row & bit) != 0, pltpu.roll(flat, 512 - bit, 1), flat)
                h = 2 * hp + e
                for ref, cols, value in (
                    (bt_s, slice(0, 512), flat),
                    (far_s, slice(0, 128), parts[0]),
                    (far_s, slice(128, 256), parts[4]),
                ):
                    line = jnp.sum(value, axis=0, keepdims=True)
                    mine = lax.broadcasted_iota(jnp.int32, (16, line.shape[1]), 0) == h
                    ref[:, cols] = jnp.where(mine, line, ref[:, cols])
            for s in range(2):
                dq_s[s * SEQ : (s + 1) * SEQ, ds(hp * 128, 128)] = (dq[s] * SCALE).astype(BF16)

        bt_s[...] = jnp.zeros_like(bt_s)
        far_s[...] = jnp.zeros_like(far_s)
        lax.fori_loop(0, PIECES, step, 0)

        offset = lax.broadcasted_iota(jnp.int32, (512, 128), 0) - 256
        bucket = lax.broadcasted_iota(jnp.int32, (512, 128), 1)
        near = jnp.where(bucket_of(offset) == bucket, 1.0, 0.0)
        lane = lax.broadcasted_iota(jnp.int32, (16, 128), 1)
        table = (
            lax.dot_general(bt_s[...], near, (((1,), (0,)), ((), ())), precision=lax.Precision.HIGHEST, preferred_element_type=F32)
            + jnp.where(lane == 15, jnp.sum(far_s[:, 0:128], axis=1, keepdims=True), 0.0)
            + jnp.where(lane == 31, jnp.sum(far_s[:, 128:256], axis=1, keepdims=True), 0.0)
        )
        add_vec(0, dq_s[...].astype(F32))
        add_vec(1, dv_s[...].astype(F32))
        if linked:
            net.cores0(2)
            sums.start(gvec_ref, table)
            net.replicas0(1)
            net.owners0(0)
        else:
            gtab_ref[...] = table

        wload.wait()
        g_s[0:SEQ, :] += mm_nt(dq_s[0:SEQ, :], square(wa_s, 0))
        g_s[0:SEQ, :] += mm_nt(dk_s[...], square(wa_s, 1))
        if linked:
            net.replicas0(2)
            net.owners0(1)
            net.owners(1)
            sums.middle()
        g_s[0:SEQ, :] += mm_nt(dv_s[...], square(wa_s, 2))
        g_s[SEQ:, :] += mm_nt(dq_s[SEQ:, :], square(wa_s, 0))
        outs = [
            pltpu.make_async_copy(g_s.at[s * SEQ : (s + 1) * SEQ, :], ref, l_sem.at[2 + s])
            for s, ref in enumerate((gc_h, gq_h))
        ]
        for copy in outs:
            copy.start()
        if linked:
            net.ends(1)
            net.owners0(2)
            net.finish(2)
            net.finish(1)
            small_ref[...] = sums.finish()
            res_ref[1] = res_s[1]
            res_ref[2] = res_s[2]
            for u in range(PIECES + 1):
                net.finish0(u)
            res_ref[0] = res_s[0]
            net.drain()
            sums.drain()
        else:
            writes = [pltpu.make_async_copy(a, b, t_sem.at[i]) for i, (a, b) in enumerate(zip(grads, grads_h))]
            for copy in writes:
                copy.start()
            for copy in writes:
                copy.wait()
        for copy in outs:
            copy.wait()

    pl.run_scoped(
        attention,
        pltpu.VMEM((2, PAIRS, SEQ, 128), BF16),
        pltpu.VMEM((PAIRS, SEQ, 128), BF16),
        pltpu.VMEM((PAIRS, SEQ, 128), BF16),
        pltpu.VMEM((2, 2, 2, SEQ, SEQ), BF16),
        pltpu.VMEM((ROWS, D), BF16),
        pltpu.VMEM((SEQ, D), BF16),
        pltpu.VMEM((SEQ, D), BF16),
        pltpu.VMEM((D, SEQ), BF16),
        pltpu.VMEM((D, SEQ), BF16),
        pltpu.VMEM((16, 256), F32),
        pltpu.VMEM((16, 512), F32),
        pltpu.VMEM((3, *WEIGHTS[0][1:]), BF16),
    )


def call_backward(linked, x, y, cc, cq, vecs, wa, wi, wo, saved):
    hbm = pl.BlockSpec(memory_space=pl.ANY)
    vmem = pl.BlockSpec(memory_space=pltpu.VMEM)
    dma = pltpu.SemaphoreType.DMA
    shape = jax.ShapeDtypeStruct
    outs = [shape((SEQ, D), F32), shape((SEQ, D), F32)]
    out_specs = [hbm, hbm]
    scratch = [
        pltpu.VMEM((ROWS, D), BF16), pltpu.VMEM((ROWS, D), F32), pltpu.VMEM((ROWS, D), BF16),
        pltpu.VMEM((D, ROWS), BF16), dma((7,)), dma((8,)),
    ] + [pltpu.VMEM(w, BF16) for w in WEIGHTS]
    if linked:
        outs += [shape((3, 4, 96, D), BF16), shape((16, 128), F32)]
        out_specs += [vmem, vmem]
        scratch += [pltpu.VMEM((16, D), F32)] + [
            pltpu.VMEM(s, BF16)
            for s in (
                (4, 4, 96, D), (4, 384, D), (3, 3, 3, 4, 48, 128), (3, 4, 48, 384), (2, 4, 4, 48, 384), (2, 4, 96, D),
                (3, 3, 3, 48, 128), (3, 48, 384), (3, 2, 4, 48, 384), (4, 2, 96, D), (2, 4, 48, 384), (2, 96, D),
                (2, 4, 48, 384), (2, 96, D), (3, 4, 96, D),
            )
        ]
        scratch += [pltpu.VMEM((n, 16, 128), F32) for n in (8, 8, 4)]
        scratch += [
            dma((3, 4)), dma((3, 4)), pltpu.SemaphoreType.REGULAR, dma((3, 12)), dma((3, 12)), dma((3, 24)), dma((3, 24)),
            dma((2, 2)), dma((2, 2)), dma((3, 12)), dma((3, 12)), dma((7,)), dma((7,)), dma((3,)), dma((3,)),
        ]
        params = pltpu.CompilerParams(vmem_limit_bytes=VMEM_LIMIT, collective_id=2, has_side_effects=True)
    else:
        outs += [shape(w, BF16) for w in WEIGHTS] + [shape((16, D), F32), shape((16, 128), F32)]
        out_specs += [hbm] * 3 + [vmem, vmem]
        params = pltpu.CompilerParams(vmem_limit_bytes=VMEM_LIMIT)
    return pl.pallas_call(
        functools.partial(backward_kernel, linked),
        out_shape=outs,
        in_specs=[hbm] * 4 + [vmem] + [hbm] * 15,
        out_specs=out_specs,
        scratch_shapes=scratch,
        compiler_params=params,
        name="backward",
    )(x, y, cc, cq, vecs, wa, wi, wo, *saved)


def shards(
    content_stream, query_stream, lengths, ranking, query_weight, query_bias, key_weight, value_weight, value_bias,
    output_weight, output_bias, norm_gain, norm_shift, inner_weight, inner_bias, outer_weight, outer_bias, final_gain,
    final_shift, bucket_bias, content_cotangent, query_cotangent,
):
    small = (query_bias, value_bias, output_bias, norm_gain, norm_shift, outer_bias, final_gain, final_shift)
    width = query_bias.shape[0]
    linked = width * 8 == D and lax.axis_size("rep") == 4
    front = (content_stream, query_stream, lengths, ranking)
    if linked:
        rows = jnp.pad(jnp.stack(small), ((0, 0), (0, 128 - width)))
        rest = jnp.pad(bucket_bias, (0, 128 - bucket_bias.shape[0])).reshape(1, 128)
        packed = jnp.concatenate([rows, inner_bias.reshape(3, 128), rest, jnp.zeros((4, 128), BF16)])
        out_c, out_q, *saved, vecs, wa, wi, wo = call_forward(
            True, *front, packed, query_weight, key_weight, value_weight, output_weight, inner_weight, outer_weight
        )
    else:
        def gather(a, axis=0):
            return lax.all_gather(a, "fsdp", axis=axis, tiled=True)

        wa = gather(jnp.stack([query_weight, key_weight, value_weight, output_weight]), 1).reshape(WEIGHTS[0])
        wi = gather(inner_weight).reshape(D, 4, D).transpose(1, 0, 2).reshape(WEIGHTS[1])
        wo = gather(outer_weight).reshape(WEIGHTS[2])
        packed = gather(jnp.concatenate([*small, inner_bias, bucket_bias])[None, :])
        cuts = [packed[:, i * width : (i + 1) * width].reshape(1, D) for i in range(8)]
        cuts.append(packed[:, 8 * width : 12 * width].reshape(4, D))
        vecs = jnp.concatenate(cuts + [jnp.zeros((4, D), BF16)]).astype(F32)
        table = jnp.pad(packed[:, 12 * width :].reshape(HEADS, BUCKETS), ((0, 4), (0, 128 - BUCKETS)))
        out_c, out_q, *saved = call_forward(False, *front, vecs, table, wa, wi, wo)
    streams = (content_stream, query_stream, content_cotangent, query_cotangent)
    gc, gq, *grads = call_backward(linked, *streams, vecs, wa, wi, wo, saved)
    if linked:
        res, flat = grads
        res = res.astype(F32)
        ga, go = res[0], res[2].reshape(4 * width, D)
        gi = res[1].transpose(1, 0, 2).reshape(width, FF)
        v = [flat[i, :width] for i in range(8)]
        inner, table = flat[8:11].reshape(4 * width), flat[11, : bucket_bias.shape[0]]
    else:
        def reduce(a, axis=0):
            a = lax.psum_scatter(a, "fsdp", scatter_dimension=axis, tiled=True)
            return lax.psum(a.astype(BF16), "rep").astype(F32)

        ga, gi, go, gvec, gtab = grads
        ga = reduce(ga.reshape(4, D, D), 1)
        gi = reduce(gi.reshape(4, D, D).transpose(1, 0, 2).reshape(D, FF))
        go = reduce(go.reshape(FF, D))
        count = D // width
        flat = jnp.concatenate(
            [gvec[i].reshape(count, width) for i in range(8)]
            + [gvec[8:12].reshape(count, 4 * width), gtab[:HEADS, :BUCKETS].reshape(count, -1)],
            axis=1,
        )
        flat = lax.psum_scatter(flat, "fsdp", scatter_dimension=0, tiled=True)[0]
        flat = lax.psum(flat.astype(BF16), "rep").astype(F32)
        v = [flat[i * width : (i + 1) * width] for i in range(8)]
        inner, table = flat[8 * width : 12 * width], flat[12 * width :]
    return (
        out_c, out_q, gc, gq, ga[0], v[0], ga[1], ga[2], v[1], ga[3], v[2], v[3], v[4], gi,
        inner, go, v[5], v[6], v[7], table,
    )


def solution(mesh):
    both, fsdp = ("rep", "fsdp"), "fsdp"
    row, vec = P(fsdp, None), P(fsdp)
    tokens = P(both, None)
    in_specs = (
        tokens, tokens, P(both), tokens, row, vec, row, row, vec, row, vec, vec, vec, row, vec, row, vec, vec, vec, vec,
        tokens, tokens,
    )
    out_specs = (
        tokens, tokens, tokens, tokens, row, vec, row, row, vec, row, vec, vec, vec, row, vec, row, vec, vec, vec, vec,
    )
    return jax.shard_map(shards, mesh=mesh, in_specs=in_specs, out_specs=out_specs, check_vma=False)
```

```python
import functools

import jax
import jax.numpy as jnp
from jax import lax
from jax.experimental import pallas as pl
from jax.experimental.pallas import tpu as pltpu
from jax.sharding import PartitionSpec as P

HEADS = 12
HEAD_DIM = 64
PAIRS = HEADS // 2
BUCKETS = 32
SEQ = 512
ROWS = 2 * SEQ
D = 768
FF = 3072
TILE = 256
TILES = FF // TILE
EPS = 1e-05
NEG = -1e30
LOG2E = 1.4426950408889634
SCALE = HEAD_DIM**-0.5
FAR_STEPS = (12, 16, 23, 32, 46, 64, 91)
F32 = jnp.float32
BF16 = jnp.bfloat16
VMEM_LIMIT = 62 * 2**20

TAIL_P = 0.28
TAIL = (
    0.11608706693762069,
    0.07021928496801585,
    0.26212226118724974,
    -0.22858899246095166,
    0.3847049667747488,
    -0.10454457204169064,
)


def mm(a, b):
    return jnp.dot(a, b, preferred_element_type=F32)


def mm_nt(a, b):
    return lax.dot_general(a, b, (((1,), (1,)), ((), ())), preferred_element_type=F32)


def mm_tn(a, b):
    return lax.dot_general(a, b, (((0,), (0,)), ((), ())), preferred_element_type=F32)


def bucket_of(offset):
    distance = jnp.abs(offset)
    farther = jnp.full(distance.shape, 8, jnp.int32)
    for step_at in FAR_STEPS:
        farther = farther + jnp.where(distance >= step_at, 1, 0)
    return jnp.where(distance < 8, distance, farther) + jnp.where(offset > 0, 16, 0)


def normal_parts(x):
    size = jnp.abs(x)
    t = 1.0 / (1.0 + TAIL_P * size)
    poly = jnp.full(x.shape, TAIL[-1], F32)
    for c in TAIL[-2::-1]:
        poly = poly * t + c
    bell = jnp.exp2(x * x * (-0.5 * LOG2E))
    tail = poly * t * bell
    return jnp.where(x < 0, tail, 1.0 - tail), bell * 0.3989422804014327


def ds(start, size):
    return pl.ds(pl.multiple_of(start, size), size)


def places():
    f = lax.axis_index("fsdp")
    return lax.axis_index("rep"), f // 2, f % 2


def hop(i, k):
    if k == 0:
        return i
    if k == 1:
        return i + 1 - 2 * (i % 2)
    return (i + 2) % 4 if k == 2 else 3 - i


def remote(src, dst, send, recv, device):
    return pltpu.make_async_remote_copy(
        src_ref=src, dst_ref=dst, send_sem=send, recv_sem=recv, device_id=device, device_id_type=pl.DeviceIdType.MESH
    )


def greet(devices):
    barrier = pltpu.get_barrier_semaphore()
    for device in devices:
        pl.semaphore_signal(barrier, inc=1, device_id=device, device_id_type=pl.DeviceIdType.MESH)
    pl.semaphore_wait(barrier, len(devices))


PIECES = 3


def block_of(buffers, t, r, z, c):
    if t == 2:
        return buffers[2].at[z, pl.ds(pl.multiple_of(c * 384 + r * 96, 96), 96), :]
    return buffers[1].at[r, z, ds(c * 96, 96), :]


def quarter(u, r, c):
    rows = pl.ds(pl.multiple_of(c * 96 + (r // 2) * 48, 48), 48)
    if isinstance(u, int) and u == PIECES:
        return rows, ds((r % 2) * 384, 384)
    return rows, pl.ds(pl.multiple_of(u * 256 + (r % 2) * 128, 128), 128)


def matrices(u):
    return 3 if isinstance(u, int) and u == PIECES else slice(0, 3)


def columns(u):
    return slice(0, D) if isinstance(u, int) and u == PIECES else ds(u * 256, 256)


ALL = slice(0, 4)


class Gather:
    def __init__(self, refs, sems):
        *self.w, self.small = refs
        self.l_sem, self.zs, self.zr, self.xs, self.xr, self.cs, self.cr, self.vs, self.vr = sems
        self.r, self.z, self.c = places()

    def block(self, u, r, z, c):
        if isinstance(u, int) and u > PIECES:
            return block_of(self.w, u - PIECES, r, z, c)
        rows, cols = quarter(u, r, c)
        return self.w[0].at[matrices(u), z, rows, cols]

    def own(self, shards):
        *square, inner, outer = shards
        z, c = self.z, self.c
        rows = ds(c * 96, 96)
        copies = [
            [pltpu.make_async_copy(square[m], self.w[0].at[m, z, rows, :], self.l_sem.at[0, m]) for m in range(4)],
            [
                pltpu.make_async_copy(inner.at[:, m * D : (m + 1) * D], self.block(4, m, z, c), self.l_sem.at[1, m])
                for m in range(4)
            ],
            [pltpu.make_async_copy(outer, self.w[2].at[z, ds(c * 384, 384), :], self.l_sem.at[2, 0])],
        ]
        return copies

    def small_copy(self, k):
        f = 2 * self.z + self.c
        return remote(
            self.small.at[f], self.small.at[f], self.vs.at[k - 1], self.vr.at[k - 1], (self.r, (f + k) % 8)
        )

    def small_come(self, k):
        f = (2 * self.z + self.c + 8 - k) % 8
        return remote(self.small.at[f], self.small.at[f], self.vs.at[k - 1], self.vr.at[k - 1], (self.r, f))

    def z_copy(self, u, k, come=False):
        far = hop(self.z, k)
        ref = self.block(u, self.r, far if come else self.z, self.c)
        return remote(ref, ref, self.zs.at[u, k - 1], self.zr.at[u, k - 1], (self.r, 2 * far + self.c))

    def x_copy(self, u, k, m, come=False):
        far = hop(self.r, m)
        ref = self.block(u, far if come else self.r, hop(self.z, k), self.c)
        at = 3 * (k - 1) + m - 1
        return remote(ref, ref, self.xs.at[u, at], self.xr.at[u, at], (far, 2 * self.z + self.c))

    def c_copy(self, u, m, come=False):
        c = 1 - self.c if come else self.c
        if isinstance(u, int) and u > PIECES:
            ref = self.block(u, hop(self.r, m), ALL, c)
        else:
            ref = self.w[0].at[matrices(u), ALL, ds(c * 96, 96), columns(u)]
        return remote(ref, ref, self.cs.at[u, m], self.cr.at[u, m], (self.r, 2 * self.z + 1 - self.c))

    def parts(self, u):
        return 4 if isinstance(u, int) and u > PIECES else 1

    def start_z(self, u):
        for k in (1, 2, 3):
            self.z_copy(u, k).start()

    def pass_on(self, u):
        for k in (1, 2, 3):
            self.z_copy(u, k, True).wait_recv()
            for m in (1, 2, 3):
                self.x_copy(u, k, m).start()

    def share(self, u):
        parts = self.parts(u)
        for m in range(4):
            if m:
                for k in (1, 2, 3):
                    self.x_copy(u, k, m, True).wait_recv()
            if parts == 4:
                self.c_copy(u, m).start()
        if parts == 1:
            self.c_copy(u, 0).start()

    def finish(self, u):
        for m in range(self.parts(u)):
            self.c_copy(u, m, True).wait_recv()

    def drain(self):
        for k in range(1, 8):
            self.small_copy(k).wait_send()

        def sent(u):
            for k in (1, 2, 3):
                self.z_copy(u, k).wait_send()
                for m in (1, 2, 3):
                    self.x_copy(u, k, m).wait_send()
            for m in range(self.parts(u)):
                self.c_copy(u, m).wait_send()

        lax.fori_loop(0, PIECES, lambda u, carry: (sent(u), carry)[1], 0)
        for u in (3, 4, 5):
            sent(u)


def unpack_small(small_s, vec_s):
    blocks = [small_s[f] for f in range(8)]
    at = lax.broadcasted_iota(jnp.int32, (1024, D), 0)
    want = lax.broadcasted_iota(jnp.int32, (1024, D), 1)
    spread = jnp.where((at % 128 < 96) & (want == (at // 128) * 96 + at % 128), 1.0, 0.0).astype(BF16)
    vec_s[...] = mm(jnp.concatenate(blocks, axis=1), spread)
    wide = [b.astype(F32) for b in blocks]
    for m in range(4):
        for j in range(6):
            vec_s[8 + m : 9 + m, j * 128 : (j + 1) * 128] = wide[2 * m + j // 3][8 + j % 3 : 9 + j % 3]
    return [w[11:12] for w in wide]


def lines_of(rows):
    bucket = bucket_of(lax.broadcasted_iota(jnp.int32, (128, 1024), 1) - 512)
    entry = lax.broadcasted_iota(jnp.int32, (128, 1024), 0)

    def pick(first, shift):
        inside = (entry >= first) & (entry < 48)
        return jnp.where(inside & (bucket == entry + shift), 1.0, 0.0).astype(BF16)

    table = jnp.concatenate(rows, axis=0).astype(BF16)
    a0, a1, b1, b2 = (mm(table, pick(*p)) for p in ((0, 0), (32, -32), (0, 16), (16, -16)))
    lines = []
    for m in range(4):
        i, j = 2 * m, 2 * m + 1
        lines += [a0[i : i + 1], a1[i : i + 1] + b1[j : j + 1], b2[j : j + 1]]
    return [line * LOG2E for line in lines]


def build_masks(len_ref, rank_ref, mask_s):
    n = len_ref[0]
    rank = rank_ref[...]
    place = lax.broadcasted_iota(jnp.int32, (1, SEQ), 1)
    valid = place < n
    chosen = valid & (rank >= n - 3 * n // 20)
    key = jnp.where(chosen, rank, jnp.where(valid, -1, 2 * SEQ)).astype(F32)
    column = jnp.broadcast_to(rank.astype(F32), (128, SEQ)).T
    for s in range(2):
        for j in range(SEQ // 128):
            seen = jnp.broadcast_to(key[:, j * 128 : (j + 1) * 128], (SEQ, 128)) <= column - s
            mask_s[s, :, j * 128 : (j + 1) * 128] = jnp.where(seen, 0.0, NEG)


def lines_of_table(tab_ref):
    offset = lax.broadcasted_iota(jnp.int32, (128, 1024), 1) - 512
    bucket = lax.broadcasted_iota(jnp.int32, (128, 1024), 0)
    onehot = jnp.where(bucket_of(offset) == bucket, 1.0, 0.0).astype(BF16)
    line = mm(tab_ref[...], onehot) * LOG2E
    return [line[h : h + 1] for h in range(HEADS)]


def build_strip(lines, strip_s):
    for h in range(HEADS):
        wide = jnp.broadcast_to(lines[h], (128, 1024))
        strip_s[h] = pltpu.roll(wide, 0, 1, stride=1, stride_axis=0)[:, 128:]


def square(w_s, m, cols=slice(None)):
    block = w_s[m, :, :, cols]
    return block.reshape(D, block.shape[-1])


def project(x_ref, y_ref, vec_ref, w_s, q_s, k_s, v_s, p):
    cols = ds(p * 256, 256)
    x = x_ref[...]
    parts = (
        (q_s, 0, mm(x, square(w_s, 0, cols)) + vec_ref[0:1, cols]),
        (q_s, 1, mm(y_ref[...], square(w_s, 0, cols)) + vec_ref[0:1, cols]),
        (k_s, None, mm(x, square(w_s, 1, cols))),
        (v_s, None, mm(x, square(w_s, 2, cols)) + vec_ref[1:2, cols]),
    )
    for ref, s, value in parts:
        value = value.astype(BF16)
        for e in range(2):
            piece = value[:, e * 128 : (e + 1) * 128]
            if s is None:
                ref[2 * p + e] = piece
            else:
                ref[s, 2 * p + e] = piece


def attend(q_s, k_s, v_s, strip_s, mask_s, p_st, ctx_s, hp, slot):
    lane = lax.broadcasted_iota(jnp.int32, (SEQ, 128), 1)
    k = k_s[hp]
    v = v_s[hp]
    for s in range(2):
        q = q_s[s, hp]
        outs = []
        for e in range(2):
            own = (lane < 64) if e == 0 else (lane >= 64)
            scores = mm_nt(jnp.where(own, q, jnp.zeros_like(q)), k)
            for i in range(SEQ // 128):
                rows = slice(i * 128, (i + 1) * 128)
                blk = (
                    scores[rows] * (SCALE * LOG2E)
                    + strip_s[2 * hp + e, :, (3 - i) * 128 : (3 - i) * 128 + SEQ]
                    + mask_s[s, rows, :]
                )
                top = jnp.max(blk, axis=1, keepdims=True)
                w = jnp.exp2(blk - top)
                w = w * (1.0 / jnp.sum(w, axis=1, keepdims=True))
                p_st[slot, e, s, rows, :] = w.astype(BF16)
            outs.append(mm(p_st[slot, e, s], v))
        ctx_s[s * SEQ : (s + 1) * SEQ, ds(hp * 128, 128)] = jnp.where(
            lane < 64, outs[0], outs[1]
        ).astype(BF16)


def norm_stats(r):
    mean = jnp.mean(r, axis=1, keepdims=True)
    centred = r - mean
    inverse = lax.rsqrt(jnp.mean(centred * centred, axis=1, keepdims=True) + EPS)
    return centred * inverse, inverse


NETWORK = {
    (0, 0): (("pass_on", 2), ("start_z", 3), ("start_z", 4)),
    (0, 1): (("share", 1),),
    (1, 0): (("pass_on", 3), ("start_z", 5)),
    (1, 1): (("share", 2), ("pass_on", 4)),
    (2, 0): (("share", 3),),
    (2, 1): (("pass_on", 5),),
}


def forward_kernel(linked, *refs):
    refs = list(refs)
    take = lambda n: [refs.pop(0) for _ in range(n)]
    x_ref, y_ref, len_ref, rank_ref = take(4)
    if linked:
        (small_ref,) = take(1)
        shards = take(6)
    else:
        vec_ref, tab_ref, *weights = take(5)
    oc_ref, oq_ref, q_h, k_h, v_h, p_h, ctx_h, n1_h, inv1_h, nl_h, act_h, slope_h, n2_h, inv2_h = take(14)
    if linked:
        vec_h, *weights = take(4)
    wa_s, wi_s, wo_s, q_s, k_s, v_s, ctx_s, nl_s, n1_s, br_s, inv1_s, inv2_s, o_sem, st_sem, w_sem = take(15)
    copies = (wa_s, wi_s, wo_s)
    if linked:
        small_s, vec_ref, *sems = take(10)
        net = Gather((wa_s, wi_s, wo_s, small_s), (w_sem, *sems))
        r, z, c = places()
        f = 2 * z + c
        own = net.own(shards)
        for batch in own:
            for copy in batch:
                copy.start()
        small_s[f] = small_ref[...]
        greet(
            [(hop(r, m), f) for m in (1, 2, 3)] + [(r, (f + k) % 8) for k in range(1, 8)]
        )
        for k in range(1, 8):
            net.small_copy(k).start()
        for copy in own[0]:
            copy.wait()
        for u in range(PIECES):
            net.start_z(u)
    else:
        loads = [pltpu.make_async_copy(src, dst, w_sem.at[i, 0]) for i, (src, dst) in enumerate(zip(weights, copies))]
        for copy in loads:
            copy.start()
    stores = []

    def keep(src, dst):
        pltpu.make_async_copy(src, dst, o_sem.at[len(stores)]).start()
        stores.append((src, dst))

    def attention(strip_s, mask_s, p_st):
        build_masks(len_ref, rank_ref, mask_s)
        if linked:
            for k in range(1, 8):
                net.small_come(k).wait_recv()
            build_strip(lines_of(unpack_small(small_s, vec_ref)), strip_s)
            net.pass_on(0)
            net.pass_on(1)
            for copy in own[1] + own[2]:
                copy.wait()
            net.share(0)
            keep(vec_ref, vec_h)
        else:
            build_strip(lines_of_table(tab_ref), strip_s)
            loads[0].wait()

        def store(hp, slot):
            return pltpu.make_async_copy(p_st.at[slot], p_h.at[hp], st_sem.at[slot])

        def hooks(p, part):
            for (at, when), moves in NETWORK.items():
                if when == part:
                    @pl.when(p == at)
                    def _(moves=moves):
                        for name, u in moves:
                            getattr(net, name)(u)

        def step(p, carry):
            if linked:
                net.finish(p)
            project(x_ref, y_ref, vec_ref, wa_s, q_s, k_s, v_s, p)
            for part in range(2):
                if linked:
                    hooks(p, part)

                @pl.when(p >= 1)
                def _():
                    store(2 * p - 2 + part, part).wait()

                attend(q_s, k_s, v_s, strip_s, mask_s, p_st, ctx_s, 2 * p + part, part)
                store(2 * p + part, part).start()
            return carry

        lax.fori_loop(0, PIECES, step, 0)
        for part in range(2):
            store(PAIRS - 2 + part, part).wait()
        keep(q_s, q_h)
        keep(k_s, k_h)
        keep(v_s, v_h)

    pl.run_scoped(
        attention,
        pltpu.VMEM((HEADS, 128, 896), F32),
        pltpu.VMEM((2, SEQ, SEQ), F32),
        pltpu.VMEM((2, 2, 2, SEQ, SEQ), BF16),
    )
    keep(ctx_s, ctx_h)
    if linked:
        net.finish(3)
        keep(wa_s, weights[0])

    for s, in_ref in ((0, x_ref), (1, y_ref)):
        def first(i, carry, s=s, in_ref=in_ref):
            own = ds(i * 256, 256)
            rows = ds(s * SEQ + i * 256, 256)
            r = in_ref[own, :].astype(F32) + mm(ctx_s[rows, :], square(wa_s, 3)) + vec_ref[2:3, :]
            n, inverse = norm_stats(r)
            n1_s[rows, :] = n
            inv1_s[rows, :] = jnp.broadcast_to(inverse, (256, 128))
            nl_s[rows, :] = (n * vec_ref[3:4, :] + vec_ref[4:5, :]).astype(BF16)
            return carry

        lax.fori_loop(0, SEQ // 256, first, 0)
    keep(n1_s, n1_h)
    keep(inv1_s, inv1_h)
    keep(nl_s, nl_h)

    if linked:
        net.share(4)
        net.finish(4)
        keep(wi_s, weights[1])
    else:
        loads[1].wait()
        loads[2].wait()

    def feed(act_s, slope_st):
        def part(t):
            return ds(t * TILE, TILE)

        def pair(t, slot):
            return (
                pltpu.make_async_copy(act_s.at[:, part(t)], act_h.at[:, part(t)], st_sem.at[slot]),
                pltpu.make_async_copy(slope_st.at[slot], slope_h.at[:, part(t)], st_sem.at[2 + slot]),
            )

        def step(t, carry):
            slot = t % 2

            @pl.when(t >= 2)
            def _():
                for c in pair(t - 2, slot):
                    c.wait()

            if linked:
                @pl.when(t == 9)
                def _():
                    net.share(5)

            cols = ds((t % 3) * TILE, TILE)
            inner = mm(nl_s[...], square(wi_s, t // 3, cols)) + vec_ref[pl.ds(8 + (t // 3), 1), cols]
            spread, bell = normal_parts(inner)
            act_s[:, part(t)] = (inner * spread).astype(BF16)
            slope_st[slot] = (spread + inner * bell).astype(BF16)
            for c in pair(t, slot):
                c.start()
            return carry

        lax.fori_loop(0, TILES, step, 0)
        if linked:
            net.finish(5)
            keep(wo_s, weights[2])

        def outer(i, carry):
            rows = ds(i * 256, 256)
            br_s[rows, :] = mm(act_s[rows, :], wo_s[...].reshape(FF, D))
            return carry

        lax.fori_loop(0, ROWS // 256, outer, 0)
        for t in (TILES - 2, TILES - 1):
            for c in pair(t, t % 2):
                c.wait()

    pl.run_scoped(feed, pltpu.VMEM((ROWS, FF), BF16), pltpu.VMEM((2, ROWS, TILE), BF16))

    for s, o_ref in ((0, oc_ref), (1, oq_ref)):
        def last(i, carry, s=s, o_ref=o_ref):
            rows = ds(s * SEQ + i * 128, 128)
            normed = n1_s[rows, :] * vec_ref[3:4, :] + vec_ref[4:5, :]
            n, inverse = norm_stats(normed + br_s[rows, :] + vec_ref[5:6, :])
            br_s[rows, :] = n
            inv2_s[rows, :] = jnp.broadcast_to(inverse, (128, 128))
            o_ref[ds(i * 128, 128), :] = (n * vec_ref[6:7, :] + vec_ref[7:8, :]).astype(BF16)
            return carry

        lax.fori_loop(0, SEQ // 128, last, 0)
    keep(br_s, n2_h)
    keep(inv2_s, inv2_h)
    for i, (src, dst) in enumerate(stores):
        pltpu.make_async_copy(src, dst, o_sem.at[i]).wait()
    if linked:
        net.drain()


WEIGHTS = ((4, 4, 192, D), (4, 4, 192, D), (4, D, D))


def call_forward(linked, *args):
    hbm = pl.BlockSpec(memory_space=pl.ANY)
    vmem = pl.BlockSpec(memory_space=pltpu.VMEM)
    smem = pl.BlockSpec(memory_space=pltpu.SMEM)
    dma = pltpu.SemaphoreType.DMA
    shape = jax.ShapeDtypeStruct
    outs = [
        shape((SEQ, D), BF16), shape((SEQ, D), BF16),
        shape((2, PAIRS, SEQ, 128), BF16), shape((PAIRS, SEQ, 128), BF16), shape((PAIRS, SEQ, 128), BF16),
        shape((PAIRS, 2, 2, SEQ, SEQ), BF16), shape((ROWS, D), BF16),
        shape((ROWS, D), F32), shape((ROWS, 128), F32), shape((ROWS, D), BF16),
        shape((ROWS, FF), BF16), shape((ROWS, FF), BF16),
        shape((ROWS, D), F32), shape((ROWS, 128), F32),
    ]
    scratch = [pltpu.VMEM(w, BF16) for w in WEIGHTS] + [
        pltpu.VMEM((2, PAIRS, SEQ, 128), BF16), pltpu.VMEM((PAIRS, SEQ, 128), BF16), pltpu.VMEM((PAIRS, SEQ, 128), BF16),
        pltpu.VMEM((ROWS, D), BF16), pltpu.VMEM((ROWS, D), BF16), pltpu.VMEM((ROWS, D), F32), pltpu.VMEM((ROWS, D), F32),
        pltpu.VMEM((ROWS, 128), F32), pltpu.VMEM((ROWS, 128), F32),
        dma((13,)), dma((4,)), dma((3, 4)),
    ]
    in_specs = [vmem, vmem, smem, vmem]
    if linked:
        in_specs += [vmem] + [hbm] * 6
        outs += [shape((16, D), F32)] + [shape(w, BF16) for w in WEIGHTS]
        scratch += [
            pltpu.VMEM((8, 16, 128), BF16), pltpu.VMEM((16, D), F32),
            dma((6, 3)), dma((6, 3)), dma((6, 9)), dma((6, 9)), dma((6, 4)), dma((6, 4)), dma((7,)), dma((7,)),
        ]
        params = pltpu.CompilerParams(vmem_limit_bytes=VMEM_LIMIT, collective_id=1, has_side_effects=True)
    else:
        in_specs += [vmem, vmem] + [hbm] * 3
        params = pltpu.CompilerParams(vmem_limit_bytes=VMEM_LIMIT)
    return pl.pallas_call(
        functools.partial(forward_kernel, linked),
        out_shape=outs,
        in_specs=in_specs,
        out_specs=[vmem, vmem] + [hbm] * (len(outs) - 2),
        scratch_shapes=scratch,
        compiler_params=params,
        name="forward",
    )(*args)


class Reduce:
    def __init__(self, refs, sems):
        self.g, more = refs
        self.cr1, self.cr2, *more, self.res = more
        self.big, self.cut, self.out = more[:5], more[5:10], more[10:]
        self.cs, self.cr, self.credit, self.xs, self.xd, self.zs, self.zd, self.ys, self.yd, self.as_, self.ad = sems
        self.r, self.z, self.c = places()
        self.f = 2 * self.z + self.c
        self.side = (self.r % 2, self.r // 2)

    def number(self, kind, i):
        return {"in": 0, "square": 4, "piece": 5, "out": 8}[kind] + i

    def columns(self, kind, i, side):
        return pl.ds(pl.multiple_of(i * 256 + side * 128, 128), 128) if kind == "piece" else ds(side * 384, 384)

    def half(self, kind, i, m, z, give=False):
        side = 1 - self.side[m] if give else self.side[m]
        if kind == "out":
            return block_of(self.g, 2, 2 * m + side, i, self.c)
        rows = pl.ds(pl.multiple_of(self.c * 96 + m * 48, 48), 48)
        cols = self.columns(kind, i, side)
        if kind == "in":
            return self.g[1].at[i, z, rows, cols]
        return self.g[0].at[3 if kind == "square" else slice(0, 3), z, rows, cols]

    def held(self, what, kind, i, m):
        if kind == "out":
            return self.out[what].at[m, i] if what == 0 else self.out[what].at[m, i // 2] if what == 1 else self.out[what].at[m]
        return self.cut[what].at[m, i] if kind == "piece" else self.big[what].at[m, 4 if kind == "square" else i]

    def mine(self, kind, i):
        rows, cols = ds(self.c * 96, 96), ds(i * 256, 256)
        if kind == "out":
            return self.g[2].at[i, ds(self.c * 384, 384), :], self.cr2.at[i]
        if kind == "in":
            return self.g[1].at[i, :, rows, :], self.cr1.at[i]
        if kind == "square":
            return self.g[0].at[3, :, rows, :], self.cr1.at[3]
        return self.g[0].at[0:3, :, rows, cols], self.cr1.at[0:3, :, :, cols]

    def core(self, kind, i):
        rows, cols = ds((1 - self.c) * 96, 96), ds(i * 256, 256)
        if kind == "out":
            src = self.g[2].at[i, ds((1 - self.c) * 384, 384), :]
        elif kind == "in":
            src = self.g[1].at[i, :, rows, :]
        elif kind == "square":
            src = self.g[0].at[3, :, rows, :]
        else:
            src = self.g[0].at[0:3, :, rows, cols]
        n = self.number(kind, i)
        return remote(src, self.mine(kind, i)[1], self.cs.at[n], self.cr.at[n], (self.r, 2 * self.z + 1 - self.c))

    def across(self, kind, i, m):
        n = 2 * self.number(kind, i) + m
        src, dst = self.half(kind, i, m, ALL, True), self.held(0, kind, i, m)
        return remote(src, dst, self.xs.at[n], self.xd.at[n], (hop(self.r, m + 1), self.f))

    def near(self, kind, i, m, j=0):
        to, n = hop(self.z, 1), 4 * self.number(kind, i) + 2 * m + j
        src, dst = self.half(kind, i, m, hop(self.z, 3) if j else to), self.held(1, kind, i, m)
        return remote(
            src, dst if kind == "out" else dst.at[j], self.zs.at[n], self.zd.at[n], (self.r, 2 * to + self.c)
        )

    def far(self, kind, i, m):
        to = hop(self.z, 2)
        if kind == "out":
            i, n = to, 64 + m
        else:
            n = 48 + 2 * self.number(kind, i) + m
        src, dst = self.half(kind, i, m, to), self.held(2, kind, i, m)
        return remote(src, dst, self.zs.at[n], self.zd.at[n], (self.r, 2 * to + self.c))

    def complete(self, kind, i, m):
        n = 2 * (8 if kind == "out" else self.number(kind, i)) + m
        src, dst = self.held(3, kind, i, m), self.held(4, kind, i, m)
        return remote(src, dst, self.ys.at[n], self.yd.at[n], (hop(self.r, 2 - m), self.f))

    def result(self, kind, i, m, give=False):
        side = 1 - self.side[m] if give else self.side[m]
        if kind == "out":
            return self.res.at[2, 2 * m + side]
        rows, cols = slice(m * 48, (m + 1) * 48), self.columns(kind, i, side)
        if kind == "in":
            return self.res.at[1, i, rows, cols]
        return self.res.at[0, 3 if kind == "square" else slice(0, 3), rows, cols]

    def spread(self, kind, i, m, come=False):
        n = 2 * (8 if kind == "out" else self.number(kind, i)) + m
        ref = self.result(kind, i, m, come)
        return remote(ref, ref, self.as_.at[n], self.ad.at[n], (hop(self.r, m + 1), self.f))

    def start(self, kind, i=0):
        self.core(kind, i).start()

    def cores(self, kind, i=0):
        self.core(kind, i).wait_recv()
        ref, come = self.mine(kind, i)
        ref[...] = (ref[...].astype(F32) + come[...].astype(F32)).astype(BF16)
        for m in range(2):
            self.across(kind, i, m).start()

    def allow(self):
        pl.semaphore_signal(
            self.credit, inc=1, device_id=(self.r, 2 * self.z + 1 - self.c), device_id_type=pl.DeviceIdType.MESH
        )

    def replicas(self, kind, i=0):
        for m in range(2):
            self.across(kind, i, m).wait_recv()
            ref = self.half(kind, i, m, ALL)
            ref[...] = (ref[...].astype(F32) + self.held(0, kind, i, m)[...].astype(F32)).astype(BF16)
            if kind == "out":
                @pl.when((self.z + i) % 2 == 1)
                def _(m=m):
                    self.near(kind, i, m).start()
            else:
                for j in range(2):
                    self.near(kind, i, m, j).start()

    def pairs(self, kind, i=0):
        if kind == "out":
            @pl.when((self.z + i) % 2 == 0)
            def _():
                for m in range(2):
                    self.near(kind, i, m).wait_recv()
                    ref = self.half(kind, i, m, None)
                    ref[...] = (ref[...].astype(F32) + self.held(1, kind, i, m)[...].astype(F32)).astype(BF16)

                    @pl.when(self.z != i)
                    def _(m=m):
                        self.far(kind, i, m).start()
            return
        for m in range(2):
            for j in (1, 0):
                self.near(kind, i, m, j).wait_recv()
                ref = self.half(kind, i, m, hop(self.z, 2 * j))
                ref[...] = (ref[...].astype(F32) + self.held(1, kind, i, m).at[j][...].astype(F32)).astype(BF16)
                if j:
                    self.far(kind, i, m).start()

    def owners(self, kind, i=0):
        for m in range(2):
            self.far(kind, i, m).wait_recv()
            total = self.half(kind, self.z if kind == "out" else i, m, self.z)[...].astype(F32)
            total = total + self.held(2, kind, i, m)[...].astype(F32)
            self.held(3, kind, i, m)[...] = total.astype(BF16)
            self.complete(kind, i, m).start()

    def ends(self, kind, i=0):
        for m in range(2):
            self.complete(kind, i, m).wait_recv()
            total = self.held(3, kind, i, m)[...].astype(F32) + self.held(4, kind, i, m)[...].astype(F32)
            self.result(kind, i, m)[...] = total.astype(BF16)
            self.spread(kind, i, m).start()

    def finish(self, kind, i=0):
        for m in range(2):
            self.spread(kind, i, m, True).wait_recv()

    def drain(self):
        def sent(kind, i):
            self.core(kind, i).wait_send()
            for m in range(2):
                self.across(kind, i, m).wait_send()
                if kind != "out":
                    for j in range(2):
                        self.near(kind, i, m, j).wait_send()
                    self.far(kind, i, m).wait_send()
                    self.complete(kind, i, m).wait_send()
                    self.spread(kind, i, m).wait_send()

        def several(kind, count):
            lax.fori_loop(0, count, lambda i, carry: (sent(kind, i), carry)[1], 0)

        several("in", 4)
        several("out", 4)
        several("piece", PIECES)
        sent("square", 0)
        for m in range(2):
            for i in (hop(self.z, 1), hop(self.z, 3)):
                self.near("out", i, m).wait_send()
            self.far("out", 0, m).wait_send()
            self.complete("out", 0, m).wait_send()
            self.spread("out", 0, m).wait_send()


class SmallReduce:
    def __init__(self, refs, sems):
        self.out, self.got, self.sums = refs
        self.vs, self.vd, self.ws, self.wd = sems
        self.r, z, c = places()
        self.f = 2 * z + c

    def first(self, k):
        to = (self.f + k) % 8
        return remote(self.out.at[to], self.got.at[self.f], self.vs.at[k - 1], self.vd.at[k - 1], (self.r, to))

    def first_come(self, k):
        back = (self.f + 8 - k) % 8
        return remote(self.out.at[back], self.got.at[back], self.vs.at[k - 1], self.vd.at[k - 1], (self.r, back))

    def second(self, m, come=False):
        far = hop(self.r, m)
        ref = self.sums.at[far if come else self.r]
        return remote(ref, ref, self.ws.at[m - 1], self.wd.at[m - 1], (far, self.f))

    def start(self, vec, table):
        pack_small(vec, table, self.out)
        self.got[self.f] = self.out[self.f]
        for k in range(1, 8):
            self.first(k).start()

    def middle(self):
        for k in range(1, 8):
            self.first_come(k).wait_recv()
        total = self.got[0]
        for f in range(1, 8):
            total = total + self.got[f]
        self.sums[self.r] = total
        for m in (1, 2, 3):
            self.second(m).start()

    def finish(self):
        for m in (1, 2, 3):
            self.second(m, True).wait_recv()
        total = self.sums[0]
        for r in range(1, 4):
            total = total + self.sums[r]
        return total

    def drain(self):
        for k in range(1, 8):
            self.first(k).wait_send()
        for m in (1, 2, 3):
            self.second(m).wait_send()


def pack_small(vec_ref, table, out_ref):
    want = lax.broadcasted_iota(jnp.int32, (D, 1024), 0)
    at = lax.broadcasted_iota(jnp.int32, (D, 1024), 1)
    gathered = jnp.where((at % 128 < 96) & (want == (at // 128) * 96 + at % 128), 1.0, 0.0)
    vec = vec_ref[...]
    rows = lax.dot_general(
        vec[0:8], gathered, (((1,), (0,)), ((), ())), precision=lax.Precision.HIGHEST, preferred_element_type=F32
    )
    lane = lax.broadcasted_iota(jnp.int32, (1, 128), 1)
    for f in range(8):
        m = f // 2
        out_ref[f, 0:8, :] = rows[:, f * 128 : (f + 1) * 128]
        for j in range(3):
            col = (f % 2) * 384 + j * 128
            out_ref[f, 8 + j : 9 + j, :] = vec[8 + m : 9 + m, col : col + 128]
        head = 3 * m + f % 2
        a, b = table[head : head + 1], table[head + 1 : head + 2]
        if f % 2 == 0:
            line = jnp.where(lane < 32, a, jnp.where(lane < 48, pltpu.roll(b, 32, 1), 0.0))
        else:
            line = jnp.where(lane < 16, pltpu.roll(a, 112, 1), jnp.where(lane < 48, pltpu.roll(b, 16, 1), 0.0))
        out_ref[f, 11:12, :] = line
        out_ref[f, 12:16, :] = jnp.zeros((4, 128), F32)


def norm_grad(u, gain, n, inverse):
    ug = u * gain
    return inverse * (
        ug - jnp.mean(ug, axis=1, keepdims=True) - n * jnp.mean(ug * n, axis=1, keepdims=True)
    )


BACK_NETWORK = {
    (0, 0): (("replicas", "out", 3), ("replicas", "in", 3), ),
    (0, 1): (("pairs", "out", 2), ("pairs", "in", 2), ("replicas", "square"), ),
    (1, 0): (),
    (1, 1): (("cores", "piece", 0), ),
    (2, 0): (("replicas", "piece", 0), ("pairs", "out", 3), ("pairs", "in", 3), ("pairs", "square"), ("owners", "in", 0), ("owners", "in", 1), ),
    (2, 1): (("cores", "piece", 1), ),
}

LAST_NETWORK = (
    (("cores", "piece", 2), ),
    (("replicas", "piece", 1), ("pairs", "piece", 0), ("owners", "out"), ),
    (("owners", "in", 2), ("owners", "square"), ("ends", "in", 0), ("ends", "in", 1), ),
    (("replicas", "piece", 2), ("pairs", "piece", 1), ("owners", "in", 3), ("sum_middle",), ),
    (("owners", "piece", 0), ("ends", "out"), ("ends", "in", 2), ("ends", "square"), ),
    (("pairs", "piece", 2), ("owners", "piece", 1), ("ends", "in", 3), ("ends", "piece", 0), ("owners", "piece", 2), ("ends", "piece", 1), ("ends", "piece", 2), ),
)


def backward_kernel(linked, *refs):
    refs = list(refs)
    take = lambda n: [refs.pop(0) for _ in range(n)]
    x_h, y_h, cc_h, cq_h, vec_ref, wa_h, wi_h, wo_h = take(8)
    q_h, k_h, v_h, p_h, ctx_h, n1_h, inv1_h, nl_h, act_h, slope_h, n2_h, inv2_h = take(12)
    gc_h, gq_h = take(2)
    if linked:
        res_ref, small_ref = take(2)
    else:
        *grads_h, gvec_ref, gtab_ref = take(5)
    ctx_s, g_s, dctx_s, tr_s, l_sem, t_sem = take(6)
    ga_s, gi_s, go_s = grads = take(3)
    if linked:
        gvec_ref, *more = take(19)
        sum_refs = take(3)
        sems = take(11)
        sum_sems = take(4)
        net = Reduce((grads, more), sems)
        sums = SmallReduce(sum_refs, sum_sems)
        r, z, c = places()
        f = 2 * z + c
        res_s = more[-1]
    cload = pltpu.make_async_copy(ctx_h, ctx_s, l_sem.at[1])
    cload.start()
    gvec_ref[...] = jnp.zeros_like(gvec_ref)

    def add_vec(row, value, cols=slice(None)):
        gvec_ref[row : row + 1, cols] += jnp.sum(value, axis=0, keepdims=True)

    def tail(n_s, inv_s, nl_s, db_s, act_s, slope_s, wi_s, wo_s, cot_s, wt_s):
        wload = pltpu.make_async_copy(wa_h.at[3], wt_s, l_sem.at[0])
        wload.start()
        nload = pltpu.make_async_copy(n2_h, n_s, l_sem.at[2])
        iload = pltpu.make_async_copy(inv2_h, inv_s, l_sem.at[3])
        nlload = pltpu.make_async_copy(nl_h, nl_s, l_sem.at[4])
        cots = [pltpu.make_async_copy(ref, cot_s.at[s], l_sem.at[5 + s]) for s, ref in enumerate((cc_h, cq_h))]
        for copy in (nload, iload, *cots, nlload):
            copy.start()

        def fetch(t, slot):
            return (
                pltpu.make_async_copy(act_h.at[:, ds(t * TILE, TILE)], act_s.at[slot], t_sem.at[slot]),
                pltpu.make_async_copy(slope_h.at[:, ds(t * TILE, TILE)], slope_s.at[slot], t_sem.at[2 + slot]),
                pltpu.make_async_copy(wi_h.at[t // 3, :, :, ds((t % 3) * TILE, TILE)], wi_s.at[slot], t_sem.at[4 + slot]),
                pltpu.make_async_copy(wo_h.at[t // 3, ds((t % 3) * TILE, TILE), :], wo_s.at[slot], t_sem.at[6 + slot]),
            )

        for copy in fetch(0, 0):
            copy.start()
        if linked:
            greet([(hop(r, m), f) for m in (1, 2, 3)] + [(r, (f + k) % 8) for k in range(1, 8)])
        for copy in (nload, iload, *cots):
            copy.wait()

        def second(i, carry):
            rows = ds(i * 128, 128)
            u = cot_s[i // 4, ds((i % 4) * 128, 128), :].astype(F32)
            n = n_s[rows, :]
            g = norm_grad(u, vec_ref[6:7, :], n, inv_s[rows, 0:1])
            add_vec(6, u * n)
            add_vec(7, u)
            g_s[rows, :] = g
            low = g.astype(BF16)
            db_s[rows, :] = low
            add_vec(5, low.astype(F32))
            return carry

        lax.fori_loop(0, ROWS // 128, second, 0)
        n1load = pltpu.make_async_copy(n1_h, n_s, l_sem.at[2])
        i1load = pltpu.make_async_copy(inv1_h, inv_s, l_sem.at[3])
        n1load.start()
        i1load.start()
        nlload.wait()
        tr_s[...] = nl_s[...].T
        xyloads = [
            pltpu.make_async_copy(ref, nl_s.at[s * SEQ : (s + 1) * SEQ, :], l_sem.at[5 + s])
            for s, ref in enumerate((x_h, y_h))
        ]
        for copy in xyloads:
            copy.start()

        def step(t, carry):
            slot = t % 2
            for copy in fetch(t, slot):
                copy.wait()

            @pl.when(t + 1 < TILES)
            def _():
                for copy in fetch(t + 1, 1 - slot):
                    copy.start()

            if linked:
                @pl.when((t % 3 == 1) & (t >= 4))
                def _():
                    for kind in ("out", "in"):
                        net.cores(kind, t // 3 - 1)

                @pl.when((t % 3 == 1) & (t >= 7))
                def _():
                    for kind in ("out", "in"):
                        net.replicas(kind, t // 3 - 2)

                @pl.when(t == 11)
                def _():
                    for kind in ("out", "in"):
                        net.pairs(kind, 0)

            db = db_s[...]
            di = (mm_nt(db, wo_s[slot]) * slope_s[slot].astype(F32)).astype(BF16)
            i, part = t // 3, ds((t % 3) * TILE, TILE)
            mine = lax.broadcasted_iota(jnp.int32, (8, TILE), 0) == i
            gvec_ref[8:16, part] += jnp.where(mine, jnp.sum(di.astype(F32), axis=0, keepdims=True), 0.0)
            go_s[i, part, :] = mm_tn(act_s[slot], db).astype(BF16)
            gi_s[i, :, :, part] = mm(tr_s[...], di).astype(BF16).reshape(4, 192, TILE)
            g_s[...] += mm_nt(di, wi_s[slot].reshape(D, TILE))
            if linked:
                @pl.when(t % 3 == 2)
                def _():
                    net.start("out", i)
                    net.start("in", i)

            return carry

        lax.fori_loop(0, TILES, step, 0)
        n1load.wait()
        i1load.wait()

        def first(i, carry):
            rows = ds(i * 128, 128)
            u = g_s[rows, :]
            n = n_s[rows, :]
            g = norm_grad(u, vec_ref[3:4, :], n, inv_s[rows, 0:1])
            add_vec(3, u * n)
            add_vec(4, u)
            g_s[rows, :] = g
            low = g.astype(BF16)
            db_s[rows, :] = low
            add_vec(2, low.astype(F32))
            return carry

        lax.fori_loop(0, ROWS // 128, first, 0)
        wload.wait()
        cload.wait()
        if linked:
            for kind in ("out", "in"):
                net.cores(kind, 3)
            net.allow()
            for kind in ("out", "in"):
                net.replicas(kind, 2)
        tr_s[...] = ctx_s[...].T
        ga_s[3] = mm(tr_s[...], db_s[...]).astype(BF16).reshape(4, 192, D)
        if linked:
            pl.semaphore_wait(net.credit, 1)
            net.start("square")
        for j in range(4):
            dctx_s[j * 256 : (j + 1) * 256, :] = mm_nt(db_s[j * 256 : (j + 1) * 256, :], wt_s[...].reshape(D, D)).astype(BF16)
        if linked:
            for kind in ("out", "in"):
                net.pairs(kind, 1)
            net.cores("square")
        for copy in xyloads:
            copy.wait()
        tr_s[...] = nl_s[...].T

    pl.run_scoped(
        tail,
        pltpu.VMEM((ROWS, D), F32),
        pltpu.VMEM((ROWS, 128), F32),
        pltpu.VMEM((ROWS, D), BF16),
        pltpu.VMEM((ROWS, D), BF16),
        pltpu.VMEM((2, ROWS, TILE), BF16),
        pltpu.VMEM((2, ROWS, TILE), BF16),
        pltpu.VMEM((2, 4, 192, TILE), BF16),
        pltpu.VMEM((2, TILE, D), BF16),
        pltpu.VMEM((2, SEQ, D), BF16),
        pltpu.VMEM(WEIGHTS[0][1:], BF16),
    )

    def attention(q_s, k_s, v_s, p_s, dq_s, dk_s, dv_s, dkt_s, dvt_s, far_s, bt_s, wa_s):
        wload = pltpu.make_async_copy(wa_h.at[0:3], wa_s, l_sem.at[0])
        wload.start()
        loads = [(q_h, q_s), (k_h, k_s), (v_h, v_s)]
        loads = [pltpu.make_async_copy(a, b, l_sem.at[2 + i]) for i, (a, b) in enumerate(loads)]
        for copy in loads:
            copy.start()

        def fetch(hp, slot):
            return pltpu.make_async_copy(p_h.at[hp], p_s.at[slot], t_sem.at[slot])

        fetch(0, 0).start()
        for copy in loads:
            copy.wait()

        def hooks(p, part):
            for (at, when), moves in BACK_NETWORK.items():
                if when == part:
                    @pl.when(p == at)
                    def _(moves=moves):
                        for name, *unit in moves:
                            getattr(net, name)(*unit)

        def step(p, carry):
            for part in range(2):
                hp = 2 * p + part
                if part == 0:
                    fetch(hp + 1, 1).start()
                else:
                    @pl.when(p + 1 < PIECES)
                    def _():
                        fetch(hp + 1, 0).start()

                if linked:
                    hooks(p, part)
                fetch(hp, part).wait()
                attend_back(hp, part)
            cols = ds(p * 256, 256)
            dk_s[:, cols] = dkt_s[cols, :].T
            dv_s[:, cols] = dvt_s[cols, :].T
            for w, left, grad in ((1, slice(0, SEQ), dk_s), (2, slice(0, SEQ), dv_s), (0, slice(0, ROWS), dq_s)):
                ga_s[w, :, :, cols] = mm(tr_s[:, left], grad[:, cols]).astype(BF16).reshape(4, 192, 256)
            if linked:
                net.start("piece", p)
            return carry

        def attend_back(hp, slot):
            lane = lax.broadcasted_iota(jnp.int32, (SEQ, 128), 1)
            k, v = k_s[hp], v_s[hp]
            zero = jnp.zeros((SEQ, 128), BF16)
            dq = [None, None]
            qt = [q_s[s, hp].T for s in range(2)]
            dt = [dctx_s[s * SEQ : (s + 1) * SEQ, ds(hp * 128, 128)].T for s in range(2)]
            for e in range(2):
                own = (lane < 64) if e == 0 else (lane >= 64)
                both = None
                dkt = dvt = None
                for s in range(2):
                    rows = slice(s * SEQ, (s + 1) * SEQ)
                    do = jnp.where(own, dctx_s[rows, ds(hp * 128, 128)], zero)
                    weight = jnp.sum(do.astype(F32) * ctx_s[rows, ds(hp * 128, 128)].astype(F32), axis=1, keepdims=True)
                    p = p_s[slot, e, s]
                    g = p.astype(F32) * (mm_nt(do, v) - weight)
                    low = g.astype(BF16)
                    both = g if both is None else both + g
                    part = mm(low, jnp.where(own, k, zero))
                    dq[s] = part if dq[s] is None else dq[s] + part
                    half = slice(e * 64, (e + 1) * 64)
                    a = mm(dt[s][half], p)
                    b = mm(qt[s][half], low)
                    dvt = a if dvt is None else dvt + a
                    dkt = b if dkt is None else dkt + b
                dvt_s[ds(hp * 128 + e * 64, 64), :] = dvt.astype(BF16)
                dkt_s[ds(hp * 128 + e * 64, 64), :] = (dkt * SCALE).astype(BF16)
                parts = [None] * 5
                for i in range(4):
                    for j in range(4):
                        blk = both[i * 128 : (i + 1) * 128, j * 128 : (j + 1) * 128]
                        at = min(max(j - i, -2), 2) + 2
                        parts[at] = blk if parts[at] is None else parts[at] + blk
                strip = jnp.concatenate([jnp.zeros((128, 128), F32), parts[1], parts[2], parts[3]], axis=1)
                flat = strip[0:8]
                for g in range(1, 16):
                    flat = flat + pltpu.roll(strip[8 * g : 8 * g + 8], 512 - 8 * g, 1)
                row = lax.broadcasted_iota(jnp.int32, (8, 512), 0)
                for bit in (1, 2, 4):
                    flat = jnp.where((row & bit) != 0, pltpu.roll(flat, 512 - bit, 1), flat)
                h = 2 * hp + e
                for ref, cols, value in (
                    (bt_s, slice(0, 512), flat),
                    (far_s, slice(0, 128), parts[0]),
                    (far_s, slice(128, 256), parts[4]),
                ):
                    line = jnp.sum(value, axis=0, keepdims=True)
                    mine = lax.broadcasted_iota(jnp.int32, (16, line.shape[1]), 0) == h
                    ref[:, cols] = jnp.where(mine, line, ref[:, cols])
            for s in range(2):
                dq_s[s * SEQ : (s + 1) * SEQ, ds(hp * 128, 128)] = (dq[s] * SCALE).astype(BF16)

        bt_s[...] = jnp.zeros_like(bt_s)
        far_s[...] = jnp.zeros_like(far_s)
        lax.fori_loop(0, PIECES, step, 0)

        offset = lax.broadcasted_iota(jnp.int32, (512, 128), 0) - 256
        bucket = lax.broadcasted_iota(jnp.int32, (512, 128), 1)
        near = jnp.where(bucket_of(offset) == bucket, 1.0, 0.0)
        lane = lax.broadcasted_iota(jnp.int32, (16, 128), 1)
        table = (
            lax.dot_general(bt_s[...], near, (((1,), (0,)), ((), ())), precision=lax.Precision.HIGHEST, preferred_element_type=F32)
            + jnp.where(lane == 15, jnp.sum(far_s[:, 0:128], axis=1, keepdims=True), 0.0)
            + jnp.where(lane == 31, jnp.sum(far_s[:, 128:256], axis=1, keepdims=True), 0.0)
        )
        add_vec(0, dq_s[...].astype(F32))
        add_vec(1, dv_s[...].astype(F32))
        def run(names):
            if linked:
                for name, *args in names:
                    (getattr(sums, name[4:]) if name.startswith("sum_") else getattr(net, name))(*args)

        run(LAST_NETWORK[0])
        if linked:
            sums.start(gvec_ref, table)
        else:
            gtab_ref[...] = table

        wload.wait()
        run(LAST_NETWORK[1])
        g_s[0:SEQ, :] += mm_nt(dq_s[0:SEQ, :], square(wa_s, 0))
        run(LAST_NETWORK[2])
        g_s[0:SEQ, :] += mm_nt(dk_s[...], square(wa_s, 1))
        run(LAST_NETWORK[3])
        g_s[0:SEQ, :] += mm_nt(dv_s[...], square(wa_s, 2))
        run(LAST_NETWORK[4])
        g_s[SEQ:, :] += mm_nt(dq_s[SEQ:, :], square(wa_s, 0))
        outs = [
            pltpu.make_async_copy(g_s.at[s * SEQ : (s + 1) * SEQ, :], ref, l_sem.at[2 + s])
            for s, ref in enumerate((gc_h, gq_h))
        ]
        for copy in outs:
            copy.start()
        run(LAST_NETWORK[5])
        if linked:
            net.finish("out")
            for i in range(4):
                net.finish("in", i)
            small_ref[...] = sums.finish()
            res_ref[1] = res_s[1]
            res_ref[2] = res_s[2]
            net.finish("square")
            for i in range(PIECES):
                net.finish("piece", i)
            res_ref[0] = res_s[0]
            net.drain()
            sums.drain()
        else:
            writes = [pltpu.make_async_copy(a, b, t_sem.at[i]) for i, (a, b) in enumerate(zip(grads, grads_h))]
            for copy in writes:
                copy.start()
            for copy in writes:
                copy.wait()
        for copy in outs:
            copy.wait()

    pl.run_scoped(
        attention,
        pltpu.VMEM((2, PAIRS, SEQ, 128), BF16),
        pltpu.VMEM((PAIRS, SEQ, 128), BF16),
        pltpu.VMEM((PAIRS, SEQ, 128), BF16),
        pltpu.VMEM((2, 2, 2, SEQ, SEQ), BF16),
        pltpu.VMEM((ROWS, D), BF16),
        pltpu.VMEM((SEQ, D), BF16),
        pltpu.VMEM((SEQ, D), BF16),
        pltpu.VMEM((D, SEQ), BF16),
        pltpu.VMEM((D, SEQ), BF16),
        pltpu.VMEM((16, 256), F32),
        pltpu.VMEM((16, 512), F32),
        pltpu.VMEM((3, *WEIGHTS[0][1:]), BF16),
    )


def call_backward(linked, x, y, cc, cq, vecs, wa, wi, wo, saved):
    hbm = pl.BlockSpec(memory_space=pl.ANY)
    vmem = pl.BlockSpec(memory_space=pltpu.VMEM)
    dma = pltpu.SemaphoreType.DMA
    shape = jax.ShapeDtypeStruct
    outs = [shape((SEQ, D), F32), shape((SEQ, D), F32)]
    out_specs = [hbm, hbm]
    scratch = [
        pltpu.VMEM((ROWS, D), BF16), pltpu.VMEM((ROWS, D), F32), pltpu.VMEM((ROWS, D), BF16),
        pltpu.VMEM((D, ROWS), BF16), dma((7,)), dma((8,)),
    ] + [pltpu.VMEM(w, BF16) for w in WEIGHTS]
    if linked:
        outs += [shape((3, 4, 96, D), BF16), shape((16, 128), F32)]
        out_specs += [vmem, vmem]
        scratch += [pltpu.VMEM((16, D), F32)] + [
            pltpu.VMEM(s, BF16)
            for s in (
                (4, 4, 96, D), (4, 384, D),
                (2, 5, 4, 48, 384), (2, 5, 2, 48, 384), (2, 5, 48, 384), (2, 5, 48, 384), (2, 5, 48, 384),
                (2, 3, 3, 4, 48, 128), (2, 3, 2, 3, 48, 128), (2, 3, 3, 48, 128), (2, 3, 3, 48, 128), (2, 3, 3, 48, 128),
                (2, 4, 96, D), (2, 2, 96, D), (2, 96, D), (2, 96, D), (2, 96, D),
                (3, 4, 96, D),
            )
        ]
        scratch += [pltpu.VMEM((n, 16, 128), F32) for n in (8, 8, 4)]
        scratch += [
            dma((12,)), dma((12,)), pltpu.SemaphoreType.REGULAR, dma((24,)), dma((24,)), dma((66,)), dma((66,)),
            dma((18,)), dma((18,)), dma((18,)), dma((18,)), dma((7,)), dma((7,)), dma((3,)), dma((3,)),
        ]
        params = pltpu.CompilerParams(vmem_limit_bytes=VMEM_LIMIT, collective_id=2, has_side_effects=True)
    else:
        outs += [shape(w, BF16) for w in WEIGHTS] + [shape((16, D), F32), shape((16, 128), F32)]
        out_specs += [hbm] * 3 + [vmem, vmem]
        params = pltpu.CompilerParams(vmem_limit_bytes=VMEM_LIMIT)
    return pl.pallas_call(
        functools.partial(backward_kernel, linked),
        out_shape=outs,
        in_specs=[hbm] * 4 + [vmem] + [hbm] * 15,
        out_specs=out_specs,
        scratch_shapes=scratch,
        compiler_params=params,
        name="backward",
    )(x, y, cc, cq, vecs, wa, wi, wo, *saved)


def finish_kernel(oc_h, oq_h, gc_h, gq_h, res_ref, small_ref, oc_o, oq_o, gc_o, gq_o, wq, wk, wv, wo, wi, wf, *rest):
    *vectors, low_s, high_s, in_sem, out_sem = rest
    moves = []
    for i, (src, dst) in enumerate(((gc_h, gc_o), (gq_h, gq_o), (oc_h, oc_o), (oq_h, oq_o))):
        held = (high_s if i < 2 else low_s).at[i % 2]
        for part in range(2):
            rows = slice(part * SEQ // 2, (part + 1) * SEQ // 2)
            n = len(moves)
            moves.append((
                pltpu.make_async_copy(src.at[rows, :], held.at[rows, :], in_sem.at[n]),
                pltpu.make_async_copy(held.at[rows, :], dst.at[rows, :], out_sem.at[n]),
            ))
    for move, _ in moves:
        move.start()
    small = small_ref[...]
    for i in range(8):
        vectors[i][...] = small[i, :96]
    for j in range(3):
        vectors[8][j * 128 : (j + 1) * 128] = small[8 + j]
    vectors[9][...] = small[11, :48]
    for q in range(4):
        (wq, wk, wv, wo)[q][...] = res_ref[0, q].astype(F32)
        wi[:, q * D : (q + 1) * D] = res_ref[1, q].astype(F32)
        wf[q * 96 : (q + 1) * 96, :] = res_ref[2, q].astype(F32)
    for move, onward in moves:
        move.wait()
        onward.start()
    for _, onward in moves:
        onward.wait()


def call_finish(oc, oq, gc, gq, res, small):
    hbm = pl.BlockSpec(memory_space=pl.ANY)
    vmem = pl.BlockSpec(memory_space=pltpu.VMEM)
    shape = jax.ShapeDtypeStruct
    outs = [shape(a.shape, a.dtype) for a in (oc, oq, gc, gq)] + [shape((96, D), F32)] * 4
    outs += [shape((96, FF), F32), shape((384, D), F32)]
    outs += [shape((96,), F32)] * 8 + [shape((384,), F32), shape((48,), F32)]
    return pl.pallas_call(
        finish_kernel,
        out_shape=outs,
        in_specs=[hbm] * 4 + [vmem] * 2,
        out_specs=[hbm] * 4 + [vmem] * 16,
        scratch_shapes=[
            pltpu.VMEM((2, SEQ, D), BF16), pltpu.VMEM((2, SEQ, D), F32),
            pltpu.SemaphoreType.DMA((8,)), pltpu.SemaphoreType.DMA((8,)),
        ],
        name="finish",
    )(oc, oq, gc, gq, res, small)


def shards(
    content_stream, query_stream, lengths, ranking, query_weight, query_bias, key_weight, value_weight, value_bias,
    output_weight, output_bias, norm_gain, norm_shift, inner_weight, inner_bias, outer_weight, outer_bias, final_gain,
    final_shift, bucket_bias, content_cotangent, query_cotangent,
):
    small = (query_bias, value_bias, output_bias, norm_gain, norm_shift, outer_bias, final_gain, final_shift)
    width = query_bias.shape[0]
    linked = width * 8 == D and lax.axis_size("rep") == 4
    front = (content_stream, query_stream, lengths, ranking)
    if linked:
        rows = jnp.pad(jnp.stack(small), ((0, 0), (0, 128 - width)))
        rest = jnp.pad(bucket_bias, (0, 128 - bucket_bias.shape[0])).reshape(1, 128)
        packed = jnp.concatenate([rows, inner_bias.reshape(3, 128), rest, jnp.zeros((4, 128), BF16)])
        out_c, out_q, *saved, vecs, wa, wi, wo = call_forward(
            True, *front, packed, query_weight, key_weight, value_weight, output_weight, inner_weight, outer_weight
        )
    else:
        def gather(a, axis=0):
            return lax.all_gather(a, "fsdp", axis=axis, tiled=True)

        wa = gather(jnp.stack([query_weight, key_weight, value_weight, output_weight]), 1).reshape(WEIGHTS[0])
        wi = gather(inner_weight).reshape(D, 4, D).transpose(1, 0, 2).reshape(WEIGHTS[1])
        wo = gather(outer_weight).reshape(WEIGHTS[2])
        packed = gather(jnp.concatenate([*small, inner_bias, bucket_bias])[None, :])
        cuts = [packed[:, i * width : (i + 1) * width].reshape(1, D) for i in range(8)]
        cuts.append(packed[:, 8 * width : 12 * width].reshape(4, D))
        vecs = jnp.concatenate(cuts + [jnp.zeros((4, D), BF16)]).astype(F32)
        table = jnp.pad(packed[:, 12 * width :].reshape(HEADS, BUCKETS), ((0, 4), (0, 128 - BUCKETS)))
        out_c, out_q, *saved = call_forward(False, *front, vecs, table, wa, wi, wo)
    streams = (content_stream, query_stream, content_cotangent, query_cotangent)
    gc, gq, *grads = call_backward(linked, *streams, vecs, wa, wi, wo, saved)
    if linked:
        out_c, out_q, gc, gq, *rest = call_finish(out_c, out_q, gc, gq, *grads)
        ga, gi, go, v, inner, table = rest[:4], rest[4], rest[5], rest[6:14], rest[14], rest[15]
    else:
        def reduce(a, axis=0):
            a = lax.psum_scatter(a, "fsdp", scatter_dimension=axis, tiled=True)
            return lax.psum(a.astype(BF16), "rep").astype(F32)

        ga, gi, go, gvec, gtab = grads
        ga = reduce(ga.reshape(4, D, D), 1)
        gi = reduce(gi.reshape(4, D, D).transpose(1, 0, 2).reshape(D, FF))
        go = reduce(go.reshape(FF, D))
        count = D // width
        flat = jnp.concatenate(
            [gvec[i].reshape(count, width) for i in range(8)]
            + [gvec[8:12].reshape(count, 4 * width), gtab[:HEADS, :BUCKETS].reshape(count, -1)],
            axis=1,
        )
        flat = lax.psum_scatter(flat, "fsdp", scatter_dimension=0, tiled=True)[0]
        flat = lax.psum(flat.astype(BF16), "rep").astype(F32)
        v = [flat[i * width : (i + 1) * width] for i in range(8)]
        inner, table = flat[8 * width : 12 * width], flat[12 * width :]
    return (
        out_c, out_q, gc, gq, ga[0], v[0], ga[1], ga[2], v[1], ga[3], v[2], v[3], v[4], gi,
        inner, go, v[5], v[6], v[7], table,
    )


def solution(mesh):
    both, fsdp = ("rep", "fsdp"), "fsdp"
    row, vec = P(fsdp, None), P(fsdp)
    tokens = P(both, None)
    in_specs = (
        tokens, tokens, P(both), tokens, row, vec, row, row, vec, row, vec, vec, vec, row, vec, row, vec, vec, vec, vec,
        tokens, tokens,
    )
    out_specs = (
        tokens, tokens, tokens, tokens, row, vec, row, row, vec, row, vec, vec, vec, row, vec, row, vec, vec, vec, vec,
    )
    return jax.shard_map(shards, mesh=mesh, in_specs=in_specs, out_specs=out_specs, check_vma=False)
```

```python
import functools

import jax
import jax.numpy as jnp
from jax import lax
from jax.experimental import pallas as pl
from jax.experimental.pallas import tpu as pltpu
from jax.sharding import PartitionSpec as P

HEADS = 12
HEAD_DIM = 64
PAIRS = HEADS // 2
BUCKETS = 32
SEQ = 512
ROWS = 2 * SEQ
D = 768
FF = 3072
TILE = 256
TILES = FF // TILE
EPS = 1e-05
NEG = -1e30
LOG2E = 1.4426950408889634
SCALE = HEAD_DIM**-0.5
FAR_STEPS = (12, 16, 23, 32, 46, 64, 91)
F32 = jnp.float32
BF16 = jnp.bfloat16
VMEM_LIMIT = 62 * 2**20

TAIL_P = 0.28
TAIL = (
    0.11608706693762069,
    0.07021928496801585,
    0.26212226118724974,
    -0.22858899246095166,
    0.3847049667747488,
    -0.10454457204169064,
)


def mm(a, b):
    return jnp.dot(a, b, preferred_element_type=F32)


def mm_nt(a, b):
    return lax.dot_general(a, b, (((1,), (1,)), ((), ())), preferred_element_type=F32)


def mm_tn(a, b):
    return lax.dot_general(a, b, (((0,), (0,)), ((), ())), preferred_element_type=F32)


def bucket_of(offset):
    distance = jnp.abs(offset)
    farther = jnp.full(distance.shape, 8, jnp.int32)
    for step_at in FAR_STEPS:
        farther = farther + jnp.where(distance >= step_at, 1, 0)
    return jnp.where(distance < 8, distance, farther) + jnp.where(offset > 0, 16, 0)


def normal_parts(x):
    size = jnp.abs(x)
    t = 1.0 / (1.0 + TAIL_P * size)
    poly = jnp.full(x.shape, TAIL[-1], F32)
    for c in TAIL[-2::-1]:
        poly = poly * t + c
    bell = jnp.exp2(x * x * (-0.5 * LOG2E))
    tail = poly * t * bell
    return jnp.where(x < 0, tail, 1.0 - tail), bell * 0.3989422804014327


def ds(start, size):
    return pl.ds(pl.multiple_of(start, size), size)


def places():
    f = lax.axis_index("fsdp")
    return lax.axis_index("rep"), f // 2, f % 2


def hop(i, k):
    if k == 0:
        return i
    if k == 1:
        return i + 1 - 2 * (i % 2)
    return (i + 2) % 4 if k == 2 else 3 - i


def remote(src, dst, send, recv, device):
    return pltpu.make_async_remote_copy(
        src_ref=src, dst_ref=dst, send_sem=send, recv_sem=recv, device_id=device, device_id_type=pl.DeviceIdType.MESH
    )


def greet(devices):
    barrier = pltpu.get_barrier_semaphore()
    for device in devices:
        pl.semaphore_signal(barrier, inc=1, device_id=device, device_id_type=pl.DeviceIdType.MESH)
    pl.semaphore_wait(barrier, len(devices))


PIECES = 3


def block_of(buffers, t, r, z, c):
    if t == 2:
        return buffers[2].at[z, pl.ds(pl.multiple_of(c * 384 + r * 96, 96), 96), :]
    return buffers[1].at[r, z, ds(c * 96, 96), :]


def quarter(u, r, c):
    rows = pl.ds(pl.multiple_of(c * 96 + (r // 2) * 48, 48), 48)
    if isinstance(u, int) and u == PIECES:
        return rows, ds((r % 2) * 384, 384)
    return rows, pl.ds(pl.multiple_of(u * 256 + (r % 2) * 128, 128), 128)


def matrices(u):
    return 3 if isinstance(u, int) and u == PIECES else slice(0, 3)


def columns(u):
    return slice(0, D) if isinstance(u, int) and u == PIECES else ds(u * 256, 256)


ALL = slice(0, 4)


class Gather:
    def __init__(self, refs, sems):
        *self.w, self.small = refs
        self.l_sem, self.zs, self.zr, self.xs, self.xr, self.cs, self.cr, self.vs, self.vr = sems
        self.r, self.z, self.c = places()

    def block(self, u, r, z, c):
        if isinstance(u, int) and u > PIECES:
            return block_of(self.w, u - PIECES, r, z, c)
        rows, cols = quarter(u, r, c)
        return self.w[0].at[matrices(u), z, rows, cols]

    def own(self, shards):
        *square, inner, outer = shards
        z, c = self.z, self.c
        rows = ds(c * 96, 96)
        copies = [
            [pltpu.make_async_copy(square[m], self.w[0].at[m, z, rows, :], self.l_sem.at[0, m]) for m in range(4)],
            [
                pltpu.make_async_copy(inner.at[:, m * D : (m + 1) * D], self.block(4, m, z, c), self.l_sem.at[1, m])
                for m in range(4)
            ],
            [pltpu.make_async_copy(outer, self.w[2].at[z, ds(c * 384, 384), :], self.l_sem.at[2, 0])],
        ]
        return copies

    def small_copy(self, k):
        f = 2 * self.z + self.c
        return remote(
            self.small.at[f], self.small.at[f], self.vs.at[k - 1], self.vr.at[k - 1], (self.r, (f + k) % 8)
        )

    def small_come(self, k):
        f = (2 * self.z + self.c + 8 - k) % 8
        return remote(self.small.at[f], self.small.at[f], self.vs.at[k - 1], self.vr.at[k - 1], (self.r, f))

    def z_half(self, u, k, m, come=False):
        q = 2 * m + (self.r % 2, self.r // 2)[m]
        ref = self.block(u, q, hop(self.z, k if come else 2 * (k == 3)), self.c)
        n = 2 * (k - 1) + m
        return remote(ref, ref, self.zs.at[u, n], self.zr.at[u, n], (self.r, 2 * hop(self.z, 1 + (k == 2)) + self.c))

    def x_half(self, u, k, m, come=False):
        side = (self.r % 2, self.r // 2)[m]
        ref = self.block(u, 2 * m + (1 - side if come else side), hop(self.z, k), self.c)
        n = 2 * (k - 1) + m
        return remote(ref, ref, self.xs.at[u, n], self.xr.at[u, n], (hop(self.r, m + 1), 2 * self.z + self.c))

    def c_inner(self, n, come=False):
        m, other = n % 2, n // 2
        side = (self.r % 2, self.r // 2)[m]
        ref = self.block(4, 2 * m + (1 - side if other else side), ALL, 1 - self.c if come else self.c)
        return remote(ref, ref, self.cs.at[4, n], self.cr.at[4, n], (self.r, 2 * self.z + 1 - self.c))

    def c_outer(self, k, come=False):
        ref = self.w[2].at[hop(self.z, k), ds((1 - self.c if come else self.c) * 384, 384), :]
        return remote(ref, ref, self.cs.at[5, k], self.cr.at[5, k], (self.r, 2 * self.z + 1 - self.c))

    def start_half(self, u):
        for k in (2, 1):
            for m in range(2):
                self.z_half(u, k, m).start()

    def pass_half(self, u, k):
        for m in range(2):
            self.z_half(u, k, m, True).wait_recv()
            if k == 2:
                self.z_half(u, 3, m).start()
            self.x_half(u, k, m).start()

    def share_inner(self, n):
        for k in (1, 2, 3) if n >= 2 else ():
            self.x_half(4, k, n % 2, True).wait_recv()
        self.c_inner(n).start()

    def finish_inner(self):
        for n in range(4):
            self.c_inner(n, True).wait_recv()

    def share_outer(self, k):
        for m in range(2 if k else 0):
            self.x_half(5, k, m, True).wait_recv()
        self.c_outer(k).start()

    def finish_outer(self, k):
        self.c_outer(k, True).wait_recv()

    def z_copy(self, u, k, come=False):
        far = hop(self.z, k)
        ref = self.block(u, self.r, far if come else self.z, self.c)
        return remote(ref, ref, self.zs.at[u, k - 1], self.zr.at[u, k - 1], (self.r, 2 * far + self.c))

    def x_copy(self, u, k, m, come=False):
        far = hop(self.r, m)
        ref = self.block(u, far if come else self.r, hop(self.z, k), self.c)
        at = 3 * (k - 1) + m - 1
        return remote(ref, ref, self.xs.at[u, at], self.xr.at[u, at], (far, 2 * self.z + self.c))

    def c_copy(self, u, come=False):
        c = 1 - self.c if come else self.c
        ref = self.w[0].at[matrices(u), ALL, ds(c * 96, 96), columns(u)]
        return remote(ref, ref, self.cs.at[u, 0], self.cr.at[u, 0], (self.r, 2 * self.z + 1 - self.c))

    def start_z(self, u):
        for k in (1, 2, 3):
            self.z_copy(u, k).start()

    def pass_on(self, u):
        for k in (1, 2, 3):
            self.z_copy(u, k, True).wait_recv()
            for m in (1, 2, 3):
                self.x_copy(u, k, m).start()

    def share(self, u):
        for m in (1, 2, 3):
            for k in (1, 2, 3):
                self.x_copy(u, k, m, True).wait_recv()
        self.c_copy(u).start()

    def finish(self, u):
        self.c_copy(u, True).wait_recv()

    def drain(self):
        for k in range(1, 8):
            self.small_copy(k).wait_send()

        def sent(u):
            for k in (1, 2, 3):
                self.z_copy(u, k).wait_send()
                for m in (1, 2, 3):
                    self.x_copy(u, k, m).wait_send()
            self.c_copy(u).wait_send()

        lax.fori_loop(0, PIECES, lambda u, carry: (sent(u), carry)[1], 0)
        sent(3)
        for k in range(4):
            self.c_inner(k).wait_send()
            self.c_outer(k).wait_send()
            for u, m in ((4, 0), (4, 1), (5, 0), (5, 1)) if k else ():
                self.z_half(u, k, m).wait_send()
                self.x_half(u, k, m).wait_send()


def unpack_small(small_s, vec_s):
    blocks = [small_s[f] for f in range(8)]
    at = lax.broadcasted_iota(jnp.int32, (128, D), 0)
    shift = jnp.where(at < 96, lax.broadcasted_iota(jnp.int32, (128, D), 1) - at, -1)
    total = None
    for f in range(8):
        part = mm(blocks[f], jnp.where(shift == 96 * f, 1.0, 0.0).astype(BF16))
        total = part if total is None else total + part
    vec_s[...] = total
    wide = [b.astype(F32) for b in blocks]
    for m in range(4):
        for j in range(6):
            vec_s[8 + m : 9 + m, j * 128 : (j + 1) * 128] = wide[2 * m + j // 3][8 + j % 3 : 9 + j % 3]
    return [w[11:12] for w in wide]


def lines_of(rows):
    bucket = jnp.broadcast_to(bucket_of(lax.broadcasted_iota(jnp.int32, (1, 1024), 1) - 512), (128, 1024))
    entry = lax.broadcasted_iota(jnp.int32, (128, 1024), 0)

    def pick(first, shift):
        inside = (entry >= first) & (entry < 48)
        return jnp.where(inside & (bucket == entry + shift), 1.0, 0.0).astype(BF16)

    table = jnp.concatenate(rows, axis=0).astype(BF16)
    a0, a1, b1, b2 = (mm(table, pick(*p)) for p in ((0, 0), (32, -32), (0, 16), (16, -16)))
    lines = []
    for m in range(4):
        i, j = 2 * m, 2 * m + 1
        lines += [a0[i : i + 1], a1[i : i + 1] + b1[j : j + 1], b2[j : j + 1]]
    return [line * LOG2E for line in lines]


def build_masks(len_ref, rank_ref, mask_s):
    n = len_ref[0]
    rank = rank_ref[...]
    place = lax.broadcasted_iota(jnp.int32, (1, SEQ), 1)
    valid = place < n
    chosen = valid & (rank >= n - 3 * n // 20)
    key = jnp.where(chosen, rank, jnp.where(valid, -1, 2 * SEQ)).astype(F32)
    column = jnp.broadcast_to(rank.astype(F32), (128, SEQ)).T
    for s in range(2):
        for j in range(SEQ // 128):
            seen = jnp.broadcast_to(key[:, j * 128 : (j + 1) * 128], (SEQ, 128)) <= column - s
            mask_s[s, :, j * 128 : (j + 1) * 128] = jnp.where(seen, 0.0, NEG)


def lines_of_table(tab_ref):
    offset = lax.broadcasted_iota(jnp.int32, (128, 1024), 1) - 512
    bucket = lax.broadcasted_iota(jnp.int32, (128, 1024), 0)
    onehot = jnp.where(bucket_of(offset) == bucket, 1.0, 0.0).astype(BF16)
    line = mm(tab_ref[...], onehot) * LOG2E
    return [line[h : h + 1] for h in range(HEADS)]


def build_strip(lines, strip_s, heads):
    for h in heads:
        line = lines[h]
        wide = jnp.broadcast_to(line[:, 256:768], (128, 512))
        strip_s[h, :, 0:256] = jnp.broadcast_to(line[:, 0:1], (128, 256))
        strip_s[h, :, 256:640] = pltpu.roll(wide, 0, 1, stride=1, stride_axis=0)[:, 128:]
        strip_s[h, :, 640:896] = jnp.broadcast_to(line[:, 1023:1024], (128, 256))


def square(w_s, m, cols=slice(None)):
    block = w_s[m, :, :, cols]
    return block.reshape(D, block.shape[-1])


def project(x_ref, y_ref, vec_ref, w_s, q_s, k_s, v_s, p):
    cols = ds(p * 256, 256)
    x = x_ref[...]
    parts = (
        (q_s, 0, mm(x, square(w_s, 0, cols)) + vec_ref[0:1, cols]),
        (q_s, 1, mm(y_ref[...], square(w_s, 0, cols)) + vec_ref[0:1, cols]),
        (k_s, None, mm(x, square(w_s, 1, cols))),
        (v_s, None, mm(x, square(w_s, 2, cols)) + vec_ref[1:2, cols]),
    )
    for ref, s, value in parts:
        value = value.astype(BF16)
        for e in range(2):
            piece = value[:, e * 128 : (e + 1) * 128]
            if s is None:
                ref[2 * p + e] = piece
            else:
                ref[s, 2 * p + e] = piece


def attend(q_s, k_s, v_s, strip_s, mask_s, p_st, ctx_s, hp, slot, ahead):
    lane = lax.broadcasted_iota(jnp.int32, (SEQ, 128), 1)
    k = k_s[hp]
    v = v_s[hp]
    for s in range(2):
        ahead(s)
        q = q_s[s, hp]
        outs = []
        for e in range(2):
            own = (lane < 64) if e == 0 else (lane >= 64)
            scores = mm_nt(jnp.where(own, q, jnp.zeros_like(q)), k)
            for i in range(SEQ // 128):
                rows = slice(i * 128, (i + 1) * 128)
                blk = (
                    scores[rows] * (SCALE * LOG2E)
                    + strip_s[2 * hp + e, :, (3 - i) * 128 : (3 - i) * 128 + SEQ]
                    + mask_s[s, rows, :]
                )
                top = jnp.max(blk, axis=1, keepdims=True)
                w = jnp.exp2(blk - top)
                w = w * (1.0 / jnp.sum(w, axis=1, keepdims=True))
                p_st[slot, e, s, rows, :] = w.astype(BF16)
            outs.append(mm(p_st[slot, e, s], v))
        ctx_s[s * SEQ : (s + 1) * SEQ, ds(hp * 128, 128)] = jnp.where(
            lane < 64, outs[0], outs[1]
        ).astype(BF16)


def norm_stats(r):
    mean = jnp.mean(r, axis=1, keepdims=True)
    centred = r - mean
    inverse = lax.rsqrt(jnp.mean(centred * centred, axis=1, keepdims=True) + EPS)
    return centred * inverse, inverse


NETWORK = {
    (0, 0): (("pass_on", 2),),
    (0, 1): (("share", 1),),
    (1, 0): (("share", 2),),
    (1, 3): (("pass_half", 4, 2), ("pass_half", 4, 1)),
    (2, 0): (("pass_on", 3), ("start_half", 5)),
}


FEED_NETWORK = {
    4: (("share_outer", 1), ("share_outer", 2)),
    6: (("pass_half", 5, 3),),
    9: (("share_outer", 3),),
}


def forward_kernel(linked, *refs):
    refs = list(refs)
    take = lambda n: [refs.pop(0) for _ in range(n)]
    x_ref, y_ref, len_ref, rank_ref = take(4)
    if linked:
        (small_ref,) = take(1)
        shards = take(6)
    else:
        vec_ref, tab_ref, *weights = take(5)
    oc_ref, oq_ref, q_h, k_h, v_h, p_h, ctx_h, n1_h, inv1_h, nl_h, act_h, slope_h, n2_h, inv2_h = take(14)
    if linked:
        vec_h, *weights = take(4)
    wa_s, wi_s, wo_s, q_s, k_s, v_s, ctx_s, nl_s, n1_s, br_s, inv1_s, inv2_s, o_sem, st_sem, w_sem = take(15)
    copies = (wa_s, wi_s, wo_s)
    if linked:
        small_s, vec_ref, *sems = take(10)
        net = Gather((wa_s, wi_s, wo_s, small_s), (w_sem, *sems))
        r, z, c = places()
        f = 2 * z + c
        own = net.own(shards)
        for batch in own:
            for copy in batch:
                copy.start()
        small_s[f] = small_ref[...]
        greet(
            [(hop(r, m), f) for m in (1, 2, 3)] + [(r, (f + k) % 8) for k in range(1, 8)]
        )
        for k in range(1, 8):
            net.small_copy(k).start()
        for copy in own[0]:
            copy.wait()
        net.start_z(0)
        net.start_z(1)
    else:
        loads = [pltpu.make_async_copy(src, dst, w_sem.at[i, 0]) for i, (src, dst) in enumerate(zip(weights, copies))]
        for copy in loads:
            copy.start()
    stores = []

    def keep(src, dst):
        pltpu.make_async_copy(src, dst, o_sem.at[len(stores)]).start()
        stores.append((src, dst))

    def attention(strip_s, mask_s, p_st):
        build_masks(len_ref, rank_ref, mask_s)
        if linked:
            net.pass_on(0)
            net.start_z(2)
            for k in range(1, 8):
                net.small_come(k).wait_recv()
            lines = lines_of(unpack_small(small_s, vec_ref))
            net.pass_on(1)
            for copy in own[1] + own[2]:
                copy.wait()
            net.start_half(4)
            net.start_z(3)
            build_strip(lines, strip_s, range(0, 4))
            net.share(0)
            net.share_outer(0)
            build_strip(lines, strip_s, range(4, HEADS))
            keep(vec_ref, vec_h)
        else:
            build_strip(lines_of_table(tab_ref), strip_s, range(HEADS))
            loads[0].wait()

        def store(hp, slot):
            return pltpu.make_async_copy(p_st.at[slot], p_h.at[hp], st_sem.at[slot])

        def hooks(p, part):
            for (at, when), moves in NETWORK.items():
                if when == part:
                    @pl.when(p == at)
                    def _(moves=moves):
                        for name, *unit in moves:
                            getattr(net, name)(*unit)

        def step(p, carry):
            if linked:
                net.finish(p)
            project(x_ref, y_ref, vec_ref, wa_s, q_s, k_s, v_s, p)
            for part in range(2):
                @pl.when(p >= 1)
                def _():
                    store(2 * p - 2 + part, part).wait()

                def ahead(s, part=part):
                    if linked:
                        hooks(p, 2 * part + s)

                attend(q_s, k_s, v_s, strip_s, mask_s, p_st, ctx_s, 2 * p + part, part, ahead)
                store(2 * p + part, part).start()
            return carry

        lax.fori_loop(0, PIECES, step, 0)
        for part in range(2):
            store(PAIRS - 2 + part, part).wait()
        keep(q_s, q_h)
        keep(k_s, k_h)
        keep(v_s, v_h)

    pl.run_scoped(
        attention,
        pltpu.VMEM((HEADS, 128, 896), F32),
        pltpu.VMEM((2, SEQ, SEQ), F32),
        pltpu.VMEM((2, 2, 2, SEQ, SEQ), BF16),
    )
    keep(ctx_s, ctx_h)
    if linked:
        net.share(3)
        net.pass_half(4, 3)
        net.share_inner(0)
        net.share_inner(1)
        net.finish(3)
        keep(wa_s, weights[0])

    for s, in_ref in ((0, x_ref), (1, y_ref)):
        def first(i, carry, s=s, in_ref=in_ref):
            own = ds(i * 256, 256)
            rows = ds(s * SEQ + i * 256, 256)
            r = in_ref[own, :].astype(F32) + mm(ctx_s[rows, :], square(wa_s, 3)) + vec_ref[2:3, :]
            n, inverse = norm_stats(r)
            n1_s[rows, :] = n
            inv1_s[rows, :] = jnp.broadcast_to(inverse, (256, 128))
            nl_s[rows, :] = (n * vec_ref[3:4, :] + vec_ref[4:5, :]).astype(BF16)
            return carry

        lax.fori_loop(0, SEQ // 256, first, 0)
    keep(n1_s, n1_h)
    keep(inv1_s, inv1_h)
    keep(nl_s, nl_h)

    if linked:
        net.share_inner(2)
        net.share_inner(3)
        net.pass_half(5, 2)
        net.pass_half(5, 1)
        net.finish_inner()
        keep(wi_s, weights[1])
    else:
        loads[1].wait()
        loads[2].wait()

    def feed(act_s, slope_st):
        def part(t):
            return ds(t * TILE, TILE)

        def pair(t, slot):
            return (
                pltpu.make_async_copy(act_s.at[:, part(t)], act_h.at[:, part(t)], st_sem.at[slot]),
                pltpu.make_async_copy(slope_st.at[slot], slope_h.at[:, part(t)], st_sem.at[2 + slot]),
            )

        def step(t, carry):
            slot = t % 2

            @pl.when(t >= 2)
            def _():
                for c in pair(t - 2, slot):
                    c.wait()

            if linked:
                for at, moves in FEED_NETWORK.items():
                    @pl.when(t == at)
                    def _(moves=moves):
                        for name, *unit in moves:
                            getattr(net, name)(*unit)

            cols = ds((t % 3) * TILE, TILE)
            inner = mm(nl_s[...], square(wi_s, t // 3, cols)) + vec_ref[pl.ds(8 + (t // 3), 1), cols]
            spread, bell = normal_parts(inner)
            act_s[:, part(t)] = (inner * spread).astype(BF16)
            slope_st[slot] = (spread + inner * bell).astype(BF16)
            for c in pair(t, slot):
                c.start()
            return carry

        lax.fori_loop(0, TILES, step, 0)
        z = places()[1] if linked else 0
        for k in range(4):
            if linked:
                net.finish_outer(k)
            far = hop(z, k)

            def outer(i, carry, k=k, far=far):
                rows = ds(i * 512, 512)
                part = mm(act_s[rows, ds(far * D, D)], wo_s[far])
                br_s[rows, :] = part + br_s[rows, :] if k else part
                return carry

            lax.fori_loop(0, ROWS // 512, outer, 0)
        if linked:
            keep(wo_s, weights[2])
        for t in (TILES - 2, TILES - 1):
            for c in pair(t, t % 2):
                c.wait()

    pl.run_scoped(feed, pltpu.VMEM((ROWS, FF), BF16), pltpu.VMEM((2, ROWS, TILE), BF16))

    for s, o_ref in ((0, oc_ref), (1, oq_ref)):
        def last(i, carry, s=s, o_ref=o_ref):
            rows = ds(s * SEQ + i * 128, 128)
            normed = n1_s[rows, :] * vec_ref[3:4, :] + vec_ref[4:5, :]
            n, inverse = norm_stats(normed + br_s[rows, :] + vec_ref[5:6, :])
            br_s[rows, :] = n
            inv2_s[rows, :] = jnp.broadcast_to(inverse, (128, 128))
            o_ref[ds(i * 128, 128), :] = (n * vec_ref[6:7, :] + vec_ref[7:8, :]).astype(BF16)
            return carry

        lax.fori_loop(0, SEQ // 128, last, 0)
    keep(br_s, n2_h)
    keep(inv2_s, inv2_h)
    for i, (src, dst) in enumerate(stores):
        pltpu.make_async_copy(src, dst, o_sem.at[i]).wait()
    if linked:
        net.drain()


WEIGHTS = ((4, 4, 192, D), (4, 4, 192, D), (4, D, D))


def call_forward(linked, *args):
    hbm = pl.BlockSpec(memory_space=pl.ANY)
    vmem = pl.BlockSpec(memory_space=pltpu.VMEM)
    smem = pl.BlockSpec(memory_space=pltpu.SMEM)
    dma = pltpu.SemaphoreType.DMA
    shape = jax.ShapeDtypeStruct
    outs = [
        shape((SEQ, D), BF16), shape((SEQ, D), BF16),
        shape((2, PAIRS, SEQ, 128), BF16), shape((PAIRS, SEQ, 128), BF16), shape((PAIRS, SEQ, 128), BF16),
        shape((PAIRS, 2, 2, SEQ, SEQ), BF16), shape((ROWS, D), BF16),
        shape((ROWS, D), F32), shape((ROWS, 128), F32), shape((ROWS, D), BF16),
        shape((ROWS, FF), BF16), shape((ROWS, FF), BF16),
        shape((ROWS, D), F32), shape((ROWS, 128), F32),
    ]
    scratch = [pltpu.VMEM(w, BF16) for w in WEIGHTS] + [
        pltpu.VMEM((2, PAIRS, SEQ, 128), BF16), pltpu.VMEM((PAIRS, SEQ, 128), BF16), pltpu.VMEM((PAIRS, SEQ, 128), BF16),
        pltpu.VMEM((ROWS, D), BF16), pltpu.VMEM((ROWS, D), BF16), pltpu.VMEM((ROWS, D), F32), pltpu.VMEM((ROWS, D), F32),
        pltpu.VMEM((ROWS, 128), F32), pltpu.VMEM((ROWS, 128), F32),
        dma((13,)), dma((4,)), dma((3, 4)),
    ]
    in_specs = [vmem, vmem, smem, vmem]
    if linked:
        in_specs += [vmem] + [hbm] * 6
        outs += [shape((16, D), F32)] + [shape(w, BF16) for w in WEIGHTS]
        scratch += [
            pltpu.VMEM((8, 16, 128), BF16), pltpu.VMEM((16, D), F32),
            dma((6, 6)), dma((6, 6)), dma((6, 9)), dma((6, 9)), dma((6, 4)), dma((6, 4)), dma((7,)), dma((7,)),
        ]
        params = pltpu.CompilerParams(vmem_limit_bytes=VMEM_LIMIT, collective_id=1, has_side_effects=True)
    else:
        in_specs += [vmem, vmem] + [hbm] * 3
        params = pltpu.CompilerParams(vmem_limit_bytes=VMEM_LIMIT)
    return pl.pallas_call(
        functools.partial(forward_kernel, linked),
        out_shape=outs,
        in_specs=in_specs,
        out_specs=[vmem, vmem] + [hbm] * (len(outs) - 2),
        scratch_shapes=scratch,
        compiler_params=params,
        name="forward",
    )(*args)


class Reduce:
    def __init__(self, refs, sems):
        self.g, more = refs
        self.cr1, self.cr2, *more, self.res = more
        self.big, self.cut, self.out = more[:5], more[5:10], more[10:]
        self.cs, self.cr, self.credit, self.xs, self.xd, self.zs, self.zd, self.ys, self.yd, self.as_, self.ad = sems
        self.r, self.z, self.c = places()
        self.f = 2 * self.z + self.c
        self.side = (self.r % 2, self.r // 2)

    def number(self, kind, i):
        return {"in": 0, "square": 4, "piece": 5, "out": 8}[kind] + i

    def columns(self, kind, i, side):
        return pl.ds(pl.multiple_of(i * 256 + side * 128, 128), 128) if kind == "piece" else ds(side * 384, 384)

    def half(self, kind, i, m, z, give=False):
        side = 1 - self.side[m] if give else self.side[m]
        if kind == "out":
            return block_of(self.g, 2, 2 * m + side, i, self.c)
        rows = pl.ds(pl.multiple_of(self.c * 96 + m * 48, 48), 48)
        cols = self.columns(kind, i, side)
        if kind == "in":
            return self.g[1].at[i, z, rows, cols]
        return self.g[0].at[3 if kind == "square" else slice(0, 3), z, rows, cols]

    def held(self, what, kind, i, m):
        if kind == "out":
            return self.out[what].at[m, i] if what == 0 else self.out[what].at[m, i // 2] if what == 1 else self.out[what].at[m]
        return self.cut[what].at[m, i] if kind == "piece" else self.big[what].at[m, 4 if kind == "square" else i]

    def mine(self, kind, i):
        rows, cols = ds(self.c * 96, 96), ds(i * 256, 256)
        if kind == "out":
            return self.g[2].at[i, ds(self.c * 384, 384), :], self.cr2.at[i]
        if kind == "in":
            return self.g[1].at[i, :, rows, :], self.cr1.at[i]
        if kind == "square":
            return self.g[0].at[3, :, rows, :], self.cr1.at[3]
        return self.g[0].at[0:3, :, rows, cols], self.cr1.at[0:3, :, :, cols]

    def core(self, kind, i):
        rows, cols = ds((1 - self.c) * 96, 96), ds(i * 256, 256)
        if kind == "out":
            src = self.g[2].at[i, ds((1 - self.c) * 384, 384), :]
        elif kind == "in":
            src = self.g[1].at[i, :, rows, :]
        elif kind == "square":
            src = self.g[0].at[3, :, rows, :]
        else:
            src = self.g[0].at[0:3, :, rows, cols]
        n = self.number(kind, i)
        return remote(src, self.mine(kind, i)[1], self.cs.at[n], self.cr.at[n], (self.r, 2 * self.z + 1 - self.c))

    def across(self, kind, i, m):
        n = 2 * self.number(kind, i) + m
        src, dst = self.half(kind, i, m, ALL, True), self.held(0, kind, i, m)
        return remote(src, dst, self.xs.at[n], self.xd.at[n], (hop(self.r, m + 1), self.f))

    def near(self, kind, i, m, j=0):
        to, n = hop(self.z, 1), 4 * self.number(kind, i) + 2 * m + j
        src, dst = self.half(kind, i, m, hop(self.z, 3) if j else to), self.held(1, kind, i, m)
        return remote(
            src, dst if kind == "out" else dst.at[j], self.zs.at[n], self.zd.at[n], (self.r, 2 * to + self.c)
        )

    def far(self, kind, i, m):
        to = hop(self.z, 2)
        if kind == "out":
            i, n = to, 64 + m
        else:
            n = 48 + 2 * self.number(kind, i) + m
        src, dst = self.half(kind, i, m, to), self.held(2, kind, i, m)
        return remote(src, dst, self.zs.at[n], self.zd.at[n], (self.r, 2 * to + self.c))

    def complete(self, kind, i, m):
        n = 2 * (8 if kind == "out" else self.number(kind, i)) + m
        src, dst = self.held(3, kind, i, m), self.held(4, kind, i, m)
        return remote(src, dst, self.ys.at[n], self.yd.at[n], (hop(self.r, 2 - m), self.f))

    def result(self, kind, i, m, give=False):
        side = 1 - self.side[m] if give else self.side[m]
        if kind == "out":
            return self.res.at[2, 2 * m + side]
        rows, cols = slice(m * 48, (m + 1) * 48), self.columns(kind, i, side)
        if kind == "in":
            return self.res.at[1, i, rows, cols]
        return self.res.at[0, 3 if kind == "square" else slice(0, 3), rows, cols]

    def spread(self, kind, i, m, come=False):
        n = 2 * (8 if kind == "out" else self.number(kind, i)) + m
        ref = self.result(kind, i, m, come)
        return remote(ref, ref, self.as_.at[n], self.ad.at[n], (hop(self.r, m + 1), self.f))

    def start(self, kind, i=0):
        self.core(kind, i).start()

    def cores(self, kind, i=0):
        self.core(kind, i).wait_recv()
        ref, come = self.mine(kind, i)
        ref[...] = ref[...] + come[...]
        for m in range(2):
            self.across(kind, i, m).start()

    def allow(self):
        pl.semaphore_signal(
            self.credit, inc=1, device_id=(self.r, 2 * self.z + 1 - self.c), device_id_type=pl.DeviceIdType.MESH
        )

    def replicas(self, kind, i=0):
        for m in range(2):
            self.across(kind, i, m).wait_recv()
            ref = self.half(kind, i, m, ALL)
            ref[...] = ref[...] + self.held(0, kind, i, m)[...]
            if kind == "out":
                @pl.when((self.z + i) % 2 == 1)
                def _(m=m):
                    self.near(kind, i, m).start()
            else:
                for j in range(2):
                    self.near(kind, i, m, j).start()

    def pairs(self, kind, i=0):
        if kind == "out":
            @pl.when((self.z + i) % 2 == 0)
            def _():
                for m in range(2):
                    self.near(kind, i, m).wait_recv()
                    ref = self.half(kind, i, m, None)
                    ref[...] = ref[...] + self.held(1, kind, i, m)[...]

                    @pl.when(self.z != i)
                    def _(m=m):
                        self.far(kind, i, m).start()
            return
        for m in range(2):
            for j in (1, 0):
                self.near(kind, i, m, j).wait_recv()
                ref = self.half(kind, i, m, hop(self.z, 2 * j))
                ref[...] = ref[...] + self.held(1, kind, i, m).at[j][...]
                if j:
                    self.far(kind, i, m).start()

    def owners(self, kind, i=0):
        for m in range(2):
            self.far(kind, i, m).wait_recv()
            total = self.half(kind, self.z if kind == "out" else i, m, self.z)[...].astype(F32)
            total = total + self.held(2, kind, i, m)[...].astype(F32)
            self.held(3, kind, i, m)[...] = total.astype(BF16)
            self.complete(kind, i, m).start()

    def ends(self, kind, i=0):
        for m in range(2):
            self.complete(kind, i, m).wait_recv()
            total = self.held(3, kind, i, m)[...].astype(F32) + self.held(4, kind, i, m)[...].astype(F32)
            self.result(kind, i, m)[...] = total.astype(BF16)
            self.spread(kind, i, m).start()

    def finish(self, kind, i=0):
        for m in range(2):
            self.spread(kind, i, m, True).wait_recv()

    def drain(self):
        def sent(kind, i):
            self.core(kind, i).wait_send()
            for m in range(2):
                self.across(kind, i, m).wait_send()
                if kind != "out":
                    for j in range(2):
                        self.near(kind, i, m, j).wait_send()
                    self.far(kind, i, m).wait_send()
                    self.complete(kind, i, m).wait_send()
                    self.spread(kind, i, m).wait_send()

        def several(kind, count):
            lax.fori_loop(0, count, lambda i, carry: (sent(kind, i), carry)[1], 0)

        several("in", 4)
        several("out", 4)
        several("piece", PIECES)
        sent("square", 0)
        for m in range(2):
            for i in (hop(self.z, 1), hop(self.z, 3)):
                self.near("out", i, m).wait_send()
            self.far("out", 0, m).wait_send()
            self.complete("out", 0, m).wait_send()
            self.spread("out", 0, m).wait_send()


class SmallReduce:
    def __init__(self, refs, sems):
        self.out, self.got, self.sums = refs
        self.vs, self.vd, self.ws, self.wd = sems
        self.r, z, c = places()
        self.f = 2 * z + c

    def first(self, k):
        to = (self.f + k) % 8
        return remote(self.out.at[to], self.got.at[self.f], self.vs.at[k - 1], self.vd.at[k - 1], (self.r, to))

    def first_come(self, k):
        back = (self.f + 8 - k) % 8
        return remote(self.out.at[back], self.got.at[back], self.vs.at[k - 1], self.vd.at[k - 1], (self.r, back))

    def second(self, m, come=False):
        far = hop(self.r, m)
        ref = self.sums.at[far if come else self.r]
        return remote(ref, ref, self.ws.at[m - 1], self.wd.at[m - 1], (far, self.f))

    def start(self, vec, table):
        pack_small(vec, table, self.out)
        self.got[self.f] = self.out[self.f]
        for k in range(1, 8):
            self.first(k).start()

    def middle(self):
        for k in range(1, 8):
            self.first_come(k).wait_recv()
        total = self.got[0]
        for f in range(1, 8):
            total = total + self.got[f]
        self.sums[self.r] = total
        for m in (1, 2, 3):
            self.second(m).start()

    def finish(self):
        for m in (1, 2, 3):
            self.second(m, True).wait_recv()
        total = self.sums[0]
        for r in range(1, 4):
            total = total + self.sums[r]
        return total

    def drain(self):
        for k in range(1, 8):
            self.first(k).wait_send()
        for m in (1, 2, 3):
            self.second(m).wait_send()


def pack_small(vec_ref, table, out_ref):
    vec = vec_ref[...]
    at = lax.broadcasted_iota(jnp.int32, (D, 128), 1)
    shift = jnp.where(at < 96, lax.broadcasted_iota(jnp.int32, (D, 128), 0) - at, -1)
    lane = lax.broadcasted_iota(jnp.int32, (1, 128), 1)
    for f in range(8):
        m = f // 2
        out_ref[f, 0:8, :] = lax.dot_general(
            vec[0:8], jnp.where(shift == 96 * f, 1.0, 0.0), (((1,), (0,)), ((), ())),
            precision=lax.Precision.HIGHEST, preferred_element_type=F32,
        )
        for j in range(3):
            col = (f % 2) * 384 + j * 128
            out_ref[f, 8 + j : 9 + j, :] = vec[8 + m : 9 + m, col : col + 128]
        head = 3 * m + f % 2
        a, b = table[head : head + 1], table[head + 1 : head + 2]
        if f % 2 == 0:
            line = jnp.where(lane < 32, a, jnp.where(lane < 48, pltpu.roll(b, 32, 1), 0.0))
        else:
            line = jnp.where(lane < 16, pltpu.roll(a, 112, 1), jnp.where(lane < 48, pltpu.roll(b, 16, 1), 0.0))
        out_ref[f, 11:12, :] = line
        out_ref[f, 12:16, :] = jnp.zeros((4, 128), F32)


def norm_grad(u, gain, n, inverse):
    ug = u * gain
    return inverse * (
        ug - jnp.mean(ug, axis=1, keepdims=True) - n * jnp.mean(ug * n, axis=1, keepdims=True)
    )


BACK_NETWORK = {
    (0, 0): (("replicas", "out", 3), ("replicas", "in", 3), ),
    (0, 1): (("pairs", "out", 2), ("pairs", "in", 2), ("replicas", "square"), ),
    (1, 1): (("cores", "piece", 0), ),
    (2, 0): (("replicas", "piece", 0), ("pairs", "out", 3), ("pairs", "in", 3), ("pairs", "square"), ("owners", "in", 0), ("owners", "in", 1), ),
    (2, 1): (("cores", "piece", 1), ),
}

LAST_NETWORK = (
    (("cores", "piece", 2), ),
    (("replicas", "piece", 1), ("pairs", "piece", 0), ("owners", "out"), ("owners", "in", 2), ),
    (("replicas", "piece", 2), ("owners", "square"), ("ends", "in", 0), ("ends", "in", 1), ),
    (("pairs", "piece", 1), ("owners", "in", 3), ("ends", "out"), ("ends", "in", 2), ("sum_middle",), ),
    (("pairs", "piece", 2), ("owners", "piece", 0), ("ends", "square"), ("ends", "in", 3), ),
    (("owners", "piece", 1), ("ends", "piece", 0), ("owners", "piece", 2), ("ends", "piece", 1), ("ends", "piece", 2), ),
)


def backward_kernel(linked, *refs):
    refs = list(refs)
    take = lambda n: [refs.pop(0) for _ in range(n)]
    x_h, y_h, cc_h, cq_h, vec_ref, wa_h, wi_h, wo_h = take(8)
    q_h, k_h, v_h, p_h, ctx_h, n1_h, inv1_h, nl_h, act_h, slope_h, n2_h, inv2_h = take(12)
    gc_h, gq_h = take(2)
    if linked:
        res_ref, small_ref = take(2)
    else:
        *grads_h, gvec_ref, gtab_ref = take(5)
    ctx_s, g_s, dctx_s, tr_s, l_sem, t_sem = take(6)
    ga_s, gi_s, go_s = grads = take(3)
    if linked:
        gvec_ref, *more = take(19)
        sum_refs = take(3)
        sems = take(11)
        sum_sems = take(4)
        net = Reduce((grads, more), sems)
        sums = SmallReduce(sum_refs, sum_sems)
        r, z, c = places()
        f = 2 * z + c
        res_s = more[-1]
    cload = pltpu.make_async_copy(ctx_h, ctx_s, l_sem.at[1])
    cload.start()
    gvec_ref[...] = jnp.zeros_like(gvec_ref)

    def add_vec(row, value, cols=slice(None)):
        gvec_ref[row : row + 1, cols] += jnp.sum(value, axis=0, keepdims=True)

    def tail(n_s, inv_s, nl_s, db_s, act_s, slope_s, wi_s, wo_s, cot_s, wt_s):
        wload = pltpu.make_async_copy(wa_h.at[3], wt_s, l_sem.at[0])
        wload.start()
        nload = pltpu.make_async_copy(n2_h, n_s, l_sem.at[2])
        iload = pltpu.make_async_copy(inv2_h, inv_s, l_sem.at[3])
        nlload = pltpu.make_async_copy(nl_h, nl_s, l_sem.at[4])
        cots = [pltpu.make_async_copy(ref, cot_s.at[s], l_sem.at[5 + s]) for s, ref in enumerate((cc_h, cq_h))]
        for copy in (nload, iload, *cots, nlload):
            copy.start()

        def fetch(t, slot):
            return (
                pltpu.make_async_copy(act_h.at[:, ds(t * TILE, TILE)], act_s.at[slot], t_sem.at[slot]),
                pltpu.make_async_copy(slope_h.at[:, ds(t * TILE, TILE)], slope_s.at[slot], t_sem.at[2 + slot]),
                pltpu.make_async_copy(wi_h.at[t // 3, :, :, ds((t % 3) * TILE, TILE)], wi_s.at[slot], t_sem.at[4 + slot]),
                pltpu.make_async_copy(wo_h.at[t // 3, ds((t % 3) * TILE, TILE), :], wo_s.at[slot], t_sem.at[6 + slot]),
            )

        for copy in fetch(0, 0):
            copy.start()
        if linked:
            greet([(hop(r, m), f) for m in (1, 2, 3)] + [(r, (f + k) % 8) for k in range(1, 8)])
        for copy in (nload, iload, *cots):
            copy.wait()

        def second(i, carry):
            rows = ds(i * 128, 128)
            u = cot_s[i // 4, ds((i % 4) * 128, 128), :].astype(F32)
            n = n_s[rows, :]
            g = norm_grad(u, vec_ref[6:7, :], n, inv_s[rows, 0:1])
            add_vec(6, u * n)
            add_vec(7, u)
            g_s[rows, :] = g
            low = g.astype(BF16)
            db_s[rows, :] = low
            add_vec(5, low.astype(F32))
            return carry

        lax.fori_loop(0, ROWS // 128, second, 0)
        n1load = pltpu.make_async_copy(n1_h, n_s, l_sem.at[2])
        i1load = pltpu.make_async_copy(inv1_h, inv_s, l_sem.at[3])
        n1load.start()
        i1load.start()
        nlload.wait()
        tr_s[...] = nl_s[...].T
        xyloads = [
            pltpu.make_async_copy(ref, nl_s.at[s * SEQ : (s + 1) * SEQ, :], l_sem.at[5 + s])
            for s, ref in enumerate((x_h, y_h))
        ]
        for copy in xyloads:
            copy.start()

        def step(t, carry):
            slot = t % 2
            for copy in fetch(t, slot):
                copy.wait()

            @pl.when(t + 1 < TILES)
            def _():
                for copy in fetch(t + 1, 1 - slot):
                    copy.start()

            if linked:
                @pl.when((t % 3 == 1) & (t >= 4))
                def _():
                    for kind in ("out", "in"):
                        net.cores(kind, t // 3 - 1)

                @pl.when((t % 3 == 1) & (t >= 7))
                def _():
                    for kind in ("out", "in"):
                        net.replicas(kind, t // 3 - 2)

                @pl.when(t == 11)
                def _():
                    for kind in ("out", "in"):
                        net.pairs(kind, 0)

            db = db_s[...]
            di = (mm_nt(db, wo_s[slot]) * slope_s[slot].astype(F32)).astype(BF16)
            i, part = t // 3, ds((t % 3) * TILE, TILE)
            mine = lax.broadcasted_iota(jnp.int32, (8, TILE), 0) == i
            gvec_ref[8:16, part] += jnp.where(mine, jnp.sum(di.astype(F32), axis=0, keepdims=True), 0.0)
            go_s[i, part, :] = mm_tn(act_s[slot], db).astype(BF16)
            gi_s[i, :, :, part] = mm(tr_s[...], di).astype(BF16).reshape(4, 192, TILE)
            g_s[...] += mm_nt(di, wi_s[slot].reshape(D, TILE))
            if linked:
                @pl.when(t % 3 == 2)
                def _():
                    net.start("out", i)
                    net.start("in", i)

            return carry

        lax.fori_loop(0, TILES, step, 0)
        n1load.wait()
        i1load.wait()

        def first(i, carry):
            rows = ds(i * 128, 128)
            u = g_s[rows, :]
            n = n_s[rows, :]
            g = norm_grad(u, vec_ref[3:4, :], n, inv_s[rows, 0:1])
            add_vec(3, u * n)
            add_vec(4, u)
            g_s[rows, :] = g
            low = g.astype(BF16)
            db_s[rows, :] = low
            add_vec(2, low.astype(F32))
            return carry

        lax.fori_loop(0, ROWS // 128, first, 0)
        wload.wait()
        cload.wait()
        if linked:
            for kind in ("out", "in"):
                net.cores(kind, 3)
            net.allow()
            for kind in ("out", "in"):
                net.replicas(kind, 2)
        tr_s[...] = ctx_s[...].T
        ga_s[3] = mm(tr_s[...], db_s[...]).astype(BF16).reshape(4, 192, D)
        if linked:
            pl.semaphore_wait(net.credit, 1)
            net.start("square")
        for j in range(4):
            dctx_s[j * 256 : (j + 1) * 256, :] = mm_nt(db_s[j * 256 : (j + 1) * 256, :], wt_s[...].reshape(D, D)).astype(BF16)
        if linked:
            for kind in ("out", "in"):
                net.pairs(kind, 1)
            net.cores("square")
        for copy in xyloads:
            copy.wait()
        tr_s[...] = nl_s[...].T

    pl.run_scoped(
        tail,
        pltpu.VMEM((ROWS, D), F32),
        pltpu.VMEM((ROWS, 128), F32),
        pltpu.VMEM((ROWS, D), BF16),
        pltpu.VMEM((ROWS, D), BF16),
        pltpu.VMEM((2, ROWS, TILE), BF16),
        pltpu.VMEM((2, ROWS, TILE), BF16),
        pltpu.VMEM((2, 4, 192, TILE), BF16),
        pltpu.VMEM((2, TILE, D), BF16),
        pltpu.VMEM((2, SEQ, D), BF16),
        pltpu.VMEM(WEIGHTS[0][1:], BF16),
    )

    def attention(q_s, k_s, v_s, p_s, dq_s, dk_s, dv_s, dkt_s, dvt_s, far_s, bt_s, wa_s):
        wload = pltpu.make_async_copy(wa_h.at[0:3], wa_s, l_sem.at[0])
        wload.start()
        loads = [(q_h, q_s), (k_h, k_s), (v_h, v_s)]
        loads = [pltpu.make_async_copy(a, b, l_sem.at[2 + i]) for i, (a, b) in enumerate(loads)]
        for copy in loads:
            copy.start()

        def fetch(hp, slot):
            return pltpu.make_async_copy(p_h.at[hp], p_s.at[slot], t_sem.at[slot])

        fetch(0, 0).start()
        for copy in loads:
            copy.wait()

        def hooks(p, part):
            for (at, when), moves in BACK_NETWORK.items():
                if when == part:
                    @pl.when(p == at)
                    def _(moves=moves):
                        for name, *unit in moves:
                            getattr(net, name)(*unit)

        def step(p, carry):
            for part in range(2):
                hp = 2 * p + part
                if part == 0:
                    fetch(hp + 1, 1).start()
                else:
                    @pl.when(p + 1 < PIECES)
                    def _():
                        fetch(hp + 1, 0).start()

                if linked:
                    hooks(p, part)
                fetch(hp, part).wait()
                attend_back(hp, part)
            cols = ds(p * 256, 256)
            dk_s[:, cols] = dkt_s[cols, :].T
            dv_s[:, cols] = dvt_s[cols, :].T
            for w, left, grad in ((1, slice(0, SEQ), dk_s), (2, slice(0, SEQ), dv_s), (0, slice(0, ROWS), dq_s)):
                ga_s[w, :, :, cols] = mm(tr_s[:, left], grad[:, cols]).astype(BF16).reshape(4, 192, 256)
            if linked:
                net.start("piece", p)
            return carry

        def attend_back(hp, slot):
            lane = lax.broadcasted_iota(jnp.int32, (SEQ, 128), 1)
            k, v = k_s[hp], v_s[hp]
            zero = jnp.zeros((SEQ, 128), BF16)
            dq = [None, None]
            qt = [q_s[s, hp].T for s in range(2)]
            dt = [dctx_s[s * SEQ : (s + 1) * SEQ, ds(hp * 128, 128)].T for s in range(2)]
            for e in range(2):
                own = (lane < 64) if e == 0 else (lane >= 64)
                both = None
                dkt = dvt = None
                for s in range(2):
                    rows = slice(s * SEQ, (s + 1) * SEQ)
                    do = jnp.where(own, dctx_s[rows, ds(hp * 128, 128)], zero)
                    weight = jnp.sum(do.astype(F32) * ctx_s[rows, ds(hp * 128, 128)].astype(F32), axis=1, keepdims=True)
                    p = p_s[slot, e, s]
                    g = p.astype(F32) * (mm_nt(do, v) - weight)
                    low = g.astype(BF16)
                    both = g if both is None else both + g
                    part = mm(low, jnp.where(own, k, zero))
                    dq[s] = part if dq[s] is None else dq[s] + part
                    half = slice(e * 64, (e + 1) * 64)
                    a = mm(dt[s][half], p)
                    b = mm(qt[s][half], low)
                    dvt = a if dvt is None else dvt + a
                    dkt = b if dkt is None else dkt + b
                dvt_s[ds(hp * 128 + e * 64, 64), :] = dvt.astype(BF16)
                dkt_s[ds(hp * 128 + e * 64, 64), :] = (dkt * SCALE).astype(BF16)
                parts = [None] * 5
                for i in range(4):
                    for j in range(4):
                        blk = both[i * 128 : (i + 1) * 128, j * 128 : (j + 1) * 128]
                        at = min(max(j - i, -2), 2) + 2
                        parts[at] = blk if parts[at] is None else parts[at] + blk
                strip = jnp.concatenate([jnp.zeros((128, 128), F32), parts[1], parts[2], parts[3]], axis=1)
                flat = strip[0:8]
                for g in range(1, 16):
                    flat = flat + pltpu.roll(strip[8 * g : 8 * g + 8], 512 - 8 * g, 1)
                row = lax.broadcasted_iota(jnp.int32, (8, 512), 0)
                for bit in (1, 2, 4):
                    flat = jnp.where((row & bit) != 0, pltpu.roll(flat, 512 - bit, 1), flat)
                h = 2 * hp + e
                for ref, cols, value in (
                    (bt_s, slice(0, 512), flat),
                    (far_s, slice(0, 128), parts[0]),
                    (far_s, slice(128, 256), parts[4]),
                ):
                    line = jnp.sum(value, axis=0, keepdims=True)
                    mine = lax.broadcasted_iota(jnp.int32, (16, line.shape[1]), 0) == h
                    ref[:, cols] = jnp.where(mine, line, ref[:, cols])
            for s in range(2):
                dq_s[s * SEQ : (s + 1) * SEQ, ds(hp * 128, 128)] = (dq[s] * SCALE).astype(BF16)

        bt_s[...] = jnp.zeros_like(bt_s)
        far_s[...] = jnp.zeros_like(far_s)
        lax.fori_loop(0, PIECES, step, 0)

        offset = lax.broadcasted_iota(jnp.int32, (512, 128), 0) - 256
        bucket = lax.broadcasted_iota(jnp.int32, (512, 128), 1)
        near = jnp.where(bucket_of(offset) == bucket, 1.0, 0.0)
        lane = lax.broadcasted_iota(jnp.int32, (16, 128), 1)
        table = (
            lax.dot_general(bt_s[...], near, (((1,), (0,)), ((), ())), precision=lax.Precision.HIGHEST, preferred_element_type=F32)
            + jnp.where(lane == 15, jnp.sum(far_s[:, 0:128], axis=1, keepdims=True), 0.0)
            + jnp.where(lane == 31, jnp.sum(far_s[:, 128:256], axis=1, keepdims=True), 0.0)
        )
        add_vec(0, dq_s[...].astype(F32))
        add_vec(1, dv_s[...].astype(F32))
        def run(names):
            if linked:
                for name, *args in names:
                    (getattr(sums, name[4:]) if name.startswith("sum_") else getattr(net, name))(*args)

        run(LAST_NETWORK[0])
        if linked:
            sums.start(gvec_ref, table)
        else:
            gtab_ref[...] = table

        wload.wait()
        run(LAST_NETWORK[1])
        g_s[0:SEQ, :] += mm_nt(dq_s[0:SEQ, :], square(wa_s, 0))
        run(LAST_NETWORK[2])
        g_s[0:SEQ, :] += mm_nt(dk_s[...], square(wa_s, 1))
        run(LAST_NETWORK[3])
        g_s[0:SEQ, :] += mm_nt(dv_s[...], square(wa_s, 2))
        run(LAST_NETWORK[4])
        g_s[SEQ:, :] += mm_nt(dq_s[SEQ:, :], square(wa_s, 0))
        outs = [
            pltpu.make_async_copy(g_s.at[s * SEQ : (s + 1) * SEQ, :], ref, l_sem.at[2 + s])
            for s, ref in enumerate((gc_h, gq_h))
        ]
        for copy in outs:
            copy.start()
        run(LAST_NETWORK[5])
        if linked:
            net.finish("out")
            for i in range(4):
                net.finish("in", i)
            small_ref[...] = sums.finish()
            res_ref[1] = res_s[1]
            res_ref[2] = res_s[2]
            net.finish("square")
            for i in range(PIECES):
                net.finish("piece", i)
            res_ref[0] = res_s[0]
            net.drain()
            sums.drain()
        else:
            writes = [pltpu.make_async_copy(a, b, t_sem.at[i]) for i, (a, b) in enumerate(zip(grads, grads_h))]
            for copy in writes:
                copy.start()
            for copy in writes:
                copy.wait()
        for copy in outs:
            copy.wait()

    pl.run_scoped(
        attention,
        pltpu.VMEM((2, PAIRS, SEQ, 128), BF16),
        pltpu.VMEM((PAIRS, SEQ, 128), BF16),
        pltpu.VMEM((PAIRS, SEQ, 128), BF16),
        pltpu.VMEM((2, 2, 2, SEQ, SEQ), BF16),
        pltpu.VMEM((ROWS, D), BF16),
        pltpu.VMEM((SEQ, D), BF16),
        pltpu.VMEM((SEQ, D), BF16),
        pltpu.VMEM((D, SEQ), BF16),
        pltpu.VMEM((D, SEQ), BF16),
        pltpu.VMEM((16, 256), F32),
        pltpu.VMEM((16, 512), F32),
        pltpu.VMEM((3, *WEIGHTS[0][1:]), BF16),
    )


def call_backward(linked, x, y, cc, cq, vecs, wa, wi, wo, saved):
    hbm = pl.BlockSpec(memory_space=pl.ANY)
    vmem = pl.BlockSpec(memory_space=pltpu.VMEM)
    dma = pltpu.SemaphoreType.DMA
    shape = jax.ShapeDtypeStruct
    outs = [shape((SEQ, D), F32), shape((SEQ, D), F32)]
    out_specs = [hbm, hbm]
    scratch = [
        pltpu.VMEM((ROWS, D), BF16), pltpu.VMEM((ROWS, D), F32), pltpu.VMEM((ROWS, D), BF16),
        pltpu.VMEM((D, ROWS), BF16), dma((7,)), dma((8,)),
    ] + [pltpu.VMEM(w, BF16) for w in WEIGHTS]
    if linked:
        outs += [shape((3, 4, 96, D), BF16), shape((16, 128), F32)]
        out_specs += [vmem, vmem]
        scratch += [pltpu.VMEM((16, D), F32)] + [
            pltpu.VMEM(s, BF16)
            for s in (
                (4, 4, 96, D), (4, 384, D),
                (2, 5, 4, 48, 384), (2, 5, 2, 48, 384), (2, 5, 48, 384), (2, 5, 48, 384), (2, 5, 48, 384),
                (2, 3, 3, 4, 48, 128), (2, 3, 2, 3, 48, 128), (2, 3, 3, 48, 128), (2, 3, 3, 48, 128), (2, 3, 3, 48, 128),
                (2, 4, 96, D), (2, 2, 96, D), (2, 96, D), (2, 96, D), (2, 96, D),
                (3, 4, 96, D),
            )
        ]
        scratch += [pltpu.VMEM((n, 16, 128), F32) for n in (8, 8, 4)]
        scratch += [
            dma((12,)), dma((12,)), pltpu.SemaphoreType.REGULAR, dma((24,)), dma((24,)), dma((66,)), dma((66,)),
            dma((18,)), dma((18,)), dma((18,)), dma((18,)), dma((7,)), dma((7,)), dma((3,)), dma((3,)),
        ]
        params = pltpu.CompilerParams(vmem_limit_bytes=VMEM_LIMIT, collective_id=2, has_side_effects=True)
    else:
        outs += [shape(w, BF16) for w in WEIGHTS] + [shape((16, D), F32), shape((16, 128), F32)]
        out_specs += [hbm] * 3 + [vmem, vmem]
        params = pltpu.CompilerParams(vmem_limit_bytes=VMEM_LIMIT)
    return pl.pallas_call(
        functools.partial(backward_kernel, linked),
        out_shape=outs,
        in_specs=[hbm] * 4 + [vmem] + [hbm] * 15,
        out_specs=out_specs,
        scratch_shapes=scratch,
        compiler_params=params,
        name="backward",
    )(x, y, cc, cq, vecs, wa, wi, wo, *saved)


def finish_kernel(oc_h, oq_h, gc_h, gq_h, res_ref, small_ref, oc_o, oq_o, gc_o, gq_o, wq, wk, wv, wo, wi, wf, *rest):
    *vectors, low_s, high_s, in_sem, out_sem = rest
    moves = []
    for i, (src, dst) in enumerate(((gc_h, gc_o), (gq_h, gq_o), (oc_h, oc_o), (oq_h, oq_o))):
        held = (high_s if i < 2 else low_s).at[i % 2]
        for part in range(2):
            rows = slice(part * SEQ // 2, (part + 1) * SEQ // 2)
            n = len(moves)
            moves.append((
                pltpu.make_async_copy(src.at[rows, :], held.at[rows, :], in_sem.at[n]),
                pltpu.make_async_copy(held.at[rows, :], dst.at[rows, :], out_sem.at[n]),
            ))
    for move, _ in moves:
        move.start()
    small = small_ref[...]
    for i in range(8):
        vectors[i][...] = small[i, :96]
    for j in range(3):
        vectors[8][j * 128 : (j + 1) * 128] = small[8 + j]
    vectors[9][...] = small[11, :48]
    for q in range(4):
        (wq, wk, wv, wo)[q][...] = res_ref[0, q].astype(F32)
        wi[:, q * D : (q + 1) * D] = res_ref[1, q].astype(F32)
        wf[q * 96 : (q + 1) * 96, :] = res_ref[2, q].astype(F32)
    for move, onward in moves:
        move.wait()
        onward.start()
    for _, onward in moves:
        onward.wait()


def call_finish(oc, oq, gc, gq, res, small):
    hbm = pl.BlockSpec(memory_space=pl.ANY)
    vmem = pl.BlockSpec(memory_space=pltpu.VMEM)
    shape = jax.ShapeDtypeStruct
    outs = [shape(a.shape, a.dtype) for a in (oc, oq, gc, gq)] + [shape((96, D), F32)] * 4
    outs += [shape((96, FF), F32), shape((384, D), F32)]
    outs += [shape((96,), F32)] * 8 + [shape((384,), F32), shape((48,), F32)]
    return pl.pallas_call(
        finish_kernel,
        out_shape=outs,
        in_specs=[hbm] * 4 + [vmem] * 2,
        out_specs=[hbm] * 4 + [vmem] * 16,
        scratch_shapes=[
            pltpu.VMEM((2, SEQ, D), BF16), pltpu.VMEM((2, SEQ, D), F32),
            pltpu.SemaphoreType.DMA((8,)), pltpu.SemaphoreType.DMA((8,)),
        ],
        name="finish",
    )(oc, oq, gc, gq, res, small)


def shards(
    content_stream, query_stream, lengths, ranking, query_weight, query_bias, key_weight, value_weight, value_bias,
    output_weight, output_bias, norm_gain, norm_shift, inner_weight, inner_bias, outer_weight, outer_bias, final_gain,
    final_shift, bucket_bias, content_cotangent, query_cotangent,
):
    small = (query_bias, value_bias, output_bias, norm_gain, norm_shift, outer_bias, final_gain, final_shift)
    width = query_bias.shape[0]
    linked = width * 8 == D and lax.axis_size("rep") == 4
    front = (content_stream, query_stream, lengths, ranking)
    if linked:
        rows = jnp.pad(jnp.stack(small), ((0, 0), (0, 128 - width)))
        rest = jnp.pad(bucket_bias, (0, 128 - bucket_bias.shape[0])).reshape(1, 128)
        packed = jnp.concatenate([rows, inner_bias.reshape(3, 128), rest, jnp.zeros((4, 128), BF16)])
        out_c, out_q, *saved, vecs, wa, wi, wo = call_forward(
            True, *front, packed, query_weight, key_weight, value_weight, output_weight, inner_weight, outer_weight
        )
    else:
        def gather(a, axis=0):
            return lax.all_gather(a, "fsdp", axis=axis, tiled=True)

        wa = gather(jnp.stack([query_weight, key_weight, value_weight, output_weight]), 1).reshape(WEIGHTS[0])
        wi = gather(inner_weight).reshape(D, 4, D).transpose(1, 0, 2).reshape(WEIGHTS[1])
        wo = gather(outer_weight).reshape(WEIGHTS[2])
        packed = gather(jnp.concatenate([*small, inner_bias, bucket_bias])[None, :])
        cuts = [packed[:, i * width : (i + 1) * width].reshape(1, D) for i in range(8)]
        cuts.append(packed[:, 8 * width : 12 * width].reshape(4, D))
        vecs = jnp.concatenate(cuts + [jnp.zeros((4, D), BF16)]).astype(F32)
        table = jnp.pad(packed[:, 12 * width :].reshape(HEADS, BUCKETS), ((0, 4), (0, 128 - BUCKETS)))
        out_c, out_q, *saved = call_forward(False, *front, vecs, table, wa, wi, wo)
    streams = (content_stream, query_stream, content_cotangent, query_cotangent)
    gc, gq, *grads = call_backward(linked, *streams, vecs, wa, wi, wo, saved)
    if linked:
        out_c, out_q, gc, gq, *rest = call_finish(out_c, out_q, gc, gq, *grads)
        ga, gi, go, v, inner, table = rest[:4], rest[4], rest[5], rest[6:14], rest[14], rest[15]
    else:
        def reduce(a, axis=0):
            a = lax.psum_scatter(a, "fsdp", scatter_dimension=axis, tiled=True)
            return lax.psum(a.astype(BF16), "rep").astype(F32)

        ga, gi, go, gvec, gtab = grads
        ga = reduce(ga.reshape(4, D, D), 1)
        gi = reduce(gi.reshape(4, D, D).transpose(1, 0, 2).reshape(D, FF))
        go = reduce(go.reshape(FF, D))
        count = D // width
        flat = jnp.concatenate(
            [gvec[i].reshape(count, width) for i in range(8)]
            + [gvec[8:12].reshape(count, 4 * width), gtab[:HEADS, :BUCKETS].reshape(count, -1)],
            axis=1,
        )
        flat = lax.psum_scatter(flat, "fsdp", scatter_dimension=0, tiled=True)[0]
        flat = lax.psum(flat.astype(BF16), "rep").astype(F32)
        v = [flat[i * width : (i + 1) * width] for i in range(8)]
        inner, table = flat[8 * width : 12 * width], flat[12 * width :]
    return (
        out_c, out_q, gc, gq, ga[0], v[0], ga[1], ga[2], v[1], ga[3], v[2], v[3], v[4], gi,
        inner, go, v[5], v[6], v[7], table,
    )


def solution(mesh):
    both, fsdp = ("rep", "fsdp"), "fsdp"
    row, vec = P(fsdp, None), P(fsdp)
    tokens = P(both, None)
    in_specs = (
        tokens, tokens, P(both), tokens, row, vec, row, row, vec, row, vec, vec, vec, row, vec, row, vec, vec, vec, vec,
        tokens, tokens,
    )
    out_specs = (
        tokens, tokens, tokens, tokens, row, vec, row, row, vec, row, vec, vec, vec, row, vec, row, vec, vec, vec, vec,
    )
    return jax.shard_map(shards, mesh=mesh, in_specs=in_specs, out_specs=out_specs, check_vma=False)
```

```python
import functools

import jax
import jax.numpy as jnp
from jax import lax
from jax.experimental import pallas as pl
from jax.experimental.pallas import tpu as pltpu
from jax.sharding import PartitionSpec as P

HEADS = 12
HEAD_DIM = 64
PAIRS = HEADS // 2
BUCKETS = 32
SEQ = 512
ROWS = 2 * SEQ
D = 768
FF = 3072
TILE = 256
TILES = FF // TILE
EPS = 1e-05
NEG = -1e30
LOG2E = 1.4426950408889634
SCALE = HEAD_DIM**-0.5
FAR_STEPS = (12, 16, 23, 32, 46, 64, 91)
F32 = jnp.float32
BF16 = jnp.bfloat16
VMEM_LIMIT = 62 * 2**20

TAIL_P = 0.28
TAIL = (
    0.11608706693762069,
    0.07021928496801585,
    0.26212226118724974,
    -0.22858899246095166,
    0.3847049667747488,
    -0.10454457204169064,
)


def mm(a, b):
    return jnp.dot(a, b, preferred_element_type=F32)


def mm_nt(a, b):
    return lax.dot_general(a, b, (((1,), (1,)), ((), ())), preferred_element_type=F32)


def mm_tn(a, b):
    return lax.dot_general(a, b, (((0,), (0,)), ((), ())), preferred_element_type=F32)


def bucket_of(offset):
    distance = jnp.abs(offset)
    farther = jnp.full(distance.shape, 8, jnp.int32)
    for step_at in FAR_STEPS:
        farther = farther + jnp.where(distance >= step_at, 1, 0)
    return jnp.where(distance < 8, distance, farther) + jnp.where(offset > 0, 16, 0)


def normal_parts(x):
    size = jnp.abs(x)
    t = 1.0 / (1.0 + TAIL_P * size)
    poly = jnp.full(x.shape, TAIL[-1], F32)
    for c in TAIL[-2::-1]:
        poly = poly * t + c
    bell = jnp.exp2(x * x * (-0.5 * LOG2E))
    tail = poly * t * bell
    return jnp.where(x < 0, tail, 1.0 - tail), bell * 0.3989422804014327


def ds(start, size):
    return pl.ds(pl.multiple_of(start, size), size)


def places():
    f = lax.axis_index("fsdp")
    return lax.axis_index("rep"), f // 2, f % 2


def hop(i, k):
    if k == 0:
        return i
    if k == 1:
        return i + 1 - 2 * (i % 2)
    return (i + 2) % 4 if k == 2 else 3 - i


def remote(src, dst, send, recv, device):
    return pltpu.make_async_remote_copy(
        src_ref=src, dst_ref=dst, send_sem=send, recv_sem=recv, device_id=device, device_id_type=pl.DeviceIdType.MESH
    )


def greet(devices):
    barrier = pltpu.get_barrier_semaphore()
    for device in devices:
        pl.semaphore_signal(barrier, inc=1, device_id=device, device_id_type=pl.DeviceIdType.MESH)
    pl.semaphore_wait(barrier, len(devices))


PIECES = 3


def block_of(buffers, t, r, z, c):
    if t == 2:
        return buffers[2].at[z, pl.ds(pl.multiple_of(c * 384 + r * 96, 96), 96), :]
    return buffers[1].at[r, z, ds(c * 96, 96), :]


def quarter(u, r, c):
    rows = pl.ds(pl.multiple_of(c * 96 + (r // 2) * 48, 48), 48)
    if isinstance(u, int) and u == PIECES:
        return rows, ds((r % 2) * 384, 384)
    return rows, pl.ds(pl.multiple_of(u * 256 + (r % 2) * 128, 128), 128)


def matrices(u):
    return 3 if isinstance(u, int) and u == PIECES else slice(0, 3)


def columns(u):
    return slice(0, D) if isinstance(u, int) and u == PIECES else ds(u * 256, 256)


ALL = slice(0, 4)


class Gather:
    def __init__(self, refs, sems):
        *self.w, self.small = refs
        self.l_sem, self.zs, self.zr, self.xs, self.xr, self.cs, self.cr, self.vs, self.vr = sems
        self.r, self.z, self.c = places()

    def block(self, u, r, z, c):
        if isinstance(u, int) and u > PIECES:
            return block_of(self.w, u - PIECES, r, z, c)
        rows, cols = quarter(u, r, c)
        return self.w[0].at[matrices(u), z, rows, cols]

    def own(self, shards):
        *square, inner, outer = shards
        z, c = self.z, self.c
        rows = ds(c * 96, 96)
        copies = [
            [pltpu.make_async_copy(square[m], self.w[0].at[m, z, rows, :], self.l_sem.at[0, m]) for m in range(4)],
            [
                pltpu.make_async_copy(inner.at[:, m * D : (m + 1) * D], self.block(4, m, z, c), self.l_sem.at[1, m])
                for m in range(4)
            ],
            [pltpu.make_async_copy(outer, self.w[2].at[z, ds(c * 384, 384), :], self.l_sem.at[2, 0])],
        ]
        return copies

    def small_copy(self, k):
        f = 2 * self.z + self.c
        return remote(
            self.small.at[f], self.small.at[f], self.vs.at[k - 1], self.vr.at[k - 1], (self.r, (f + k) % 8)
        )

    def small_come(self, k):
        f = (2 * self.z + self.c + 8 - k) % 8
        return remote(self.small.at[f], self.small.at[f], self.vs.at[k - 1], self.vr.at[k - 1], (self.r, f))

    def z_half(self, u, k, m, come=False):
        q = 2 * m + (self.r % 2, self.r // 2)[m]
        ref = self.block(u, q, hop(self.z, k if come else 2 * (k == 3)), self.c)
        n = 2 * (k - 1) + m
        return remote(ref, ref, self.zs.at[u, n], self.zr.at[u, n], (self.r, 2 * hop(self.z, 1 + (k == 2)) + self.c))

    def x_half(self, u, k, m, come=False):
        side = (self.r % 2, self.r // 2)[m]
        ref = self.block(u, 2 * m + (1 - side if come else side), hop(self.z, k), self.c)
        n = 2 * (k - 1) + m
        return remote(ref, ref, self.xs.at[u, n], self.xr.at[u, n], (hop(self.r, m + 1), 2 * self.z + self.c))

    def c_inner(self, n, come=False):
        m, other = n % 2, n // 2
        side = (self.r % 2, self.r // 2)[m]
        ref = self.block(4, 2 * m + (1 - side if other else side), ALL, 1 - self.c if come else self.c)
        return remote(ref, ref, self.cs.at[4, n], self.cr.at[4, n], (self.r, 2 * self.z + 1 - self.c))

    def c_outer(self, k, come=False):
        ref = self.w[2].at[hop(self.z, k), ds((1 - self.c if come else self.c) * 384, 384), :]
        return remote(ref, ref, self.cs.at[5, k], self.cr.at[5, k], (self.r, 2 * self.z + 1 - self.c))

    def start_half(self, u):
        for k in (2, 1):
            for m in range(2):
                self.z_half(u, k, m).start()

    def pass_half(self, u, k):
        for m in range(2):
            self.z_half(u, k, m, True).wait_recv()
            if k == 2:
                self.z_half(u, 3, m).start()
            self.x_half(u, k, m).start()

    def share_inner(self, n):
        for k in (1, 2, 3) if n >= 2 else ():
            self.x_half(4, k, n % 2, True).wait_recv()
        self.c_inner(n).start()

    def finish_inner(self):
        for n in range(4):
            self.c_inner(n, True).wait_recv()

    def share_outer(self, k):
        for m in range(2 if k else 0):
            self.x_half(5, k, m, True).wait_recv()
        self.c_outer(k).start()

    def finish_outer(self, k):
        self.c_outer(k, True).wait_recv()

    def z_copy(self, u, k, come=False):
        far = hop(self.z, k)
        ref = self.block(u, self.r, far if come else self.z, self.c)
        return remote(ref, ref, self.zs.at[u, k - 1], self.zr.at[u, k - 1], (self.r, 2 * far + self.c))

    def x_copy(self, u, k, m, come=False):
        far = hop(self.r, m)
        ref = self.block(u, far if come else self.r, hop(self.z, k), self.c)
        at = 3 * (k - 1) + m - 1
        return remote(ref, ref, self.xs.at[u, at], self.xr.at[u, at], (far, 2 * self.z + self.c))

    def c_copy(self, u, come=False):
        c = 1 - self.c if come else self.c
        ref = self.w[0].at[matrices(u), ALL, ds(c * 96, 96), columns(u)]
        return remote(ref, ref, self.cs.at[u, 0], self.cr.at[u, 0], (self.r, 2 * self.z + 1 - self.c))

    def start_z(self, u):
        for k in (1, 2, 3):
            self.z_copy(u, k).start()

    def pass_on(self, u):
        for k in (1, 2, 3):
            self.z_copy(u, k, True).wait_recv()
            for m in (1, 2, 3):
                self.x_copy(u, k, m).start()

    def share(self, u):
        for m in (1, 2, 3):
            for k in (1, 2, 3):
                self.x_copy(u, k, m, True).wait_recv()
        self.c_copy(u).start()

    def finish(self, u):
        self.c_copy(u, True).wait_recv()

    def drain(self):
        for k in range(1, 8):
            self.small_copy(k).wait_send()

        def sent(u):
            for k in (1, 2, 3):
                self.z_copy(u, k).wait_send()
                for m in (1, 2, 3):
                    self.x_copy(u, k, m).wait_send()
            self.c_copy(u).wait_send()

        lax.fori_loop(0, PIECES, lambda u, carry: (sent(u), carry)[1], 0)
        sent(3)
        for k in range(4):
            self.c_inner(k).wait_send()
            self.c_outer(k).wait_send()
            for u, m in ((4, 0), (4, 1), (5, 0), (5, 1)) if k else ():
                self.z_half(u, k, m).wait_send()
                self.x_half(u, k, m).wait_send()


def unpack_small(small_s, vec_s):
    blocks = [small_s[f] for f in range(8)]
    at = lax.broadcasted_iota(jnp.int32, (128, D), 0)
    shift = jnp.where(at < 96, lax.broadcasted_iota(jnp.int32, (128, D), 1) - at, -1)
    total = None
    for f in range(8):
        part = mm(blocks[f], jnp.where(shift == 96 * f, 1.0, 0.0).astype(BF16))
        total = part if total is None else total + part
    vec_s[...] = total
    wide = [b.astype(F32) for b in blocks]
    for m in range(4):
        for j in range(6):
            vec_s[8 + m : 9 + m, j * 128 : (j + 1) * 128] = wide[2 * m + j // 3][8 + j % 3 : 9 + j % 3]
    return [w[11:12] for w in wide]


def lines_of(rows):
    bucket = jnp.broadcast_to(bucket_of(lax.broadcasted_iota(jnp.int32, (1, 1024), 1) - 512), (128, 1024))
    entry = lax.broadcasted_iota(jnp.int32, (128, 1024), 0)

    def pick(first, shift):
        inside = (entry >= first) & (entry < 48)
        return jnp.where(inside & (bucket == entry + shift), 1.0, 0.0).astype(BF16)

    table = jnp.concatenate(rows, axis=0).astype(BF16)
    a0, a1, b1, b2 = (mm(table, pick(*p)) for p in ((0, 0), (32, -32), (0, 16), (16, -16)))
    lines = []
    for m in range(4):
        i, j = 2 * m, 2 * m + 1
        lines += [a0[i : i + 1], a1[i : i + 1] + b1[j : j + 1], b2[j : j + 1]]
    return [line * LOG2E for line in lines]


def build_masks(len_ref, rank_ref, mask_s):
    n = len_ref[0]
    rank = rank_ref[...]
    place = lax.broadcasted_iota(jnp.int32, (1, SEQ), 1)
    valid = place < n
    chosen = valid & (rank >= n - 3 * n // 20)
    key = jnp.where(chosen, rank, jnp.where(valid, -1, 2 * SEQ)).astype(F32)
    column = jnp.broadcast_to(rank.astype(F32), (128, SEQ)).T
    for s in range(2):
        for j in range(SEQ // 128):
            seen = jnp.broadcast_to(key[:, j * 128 : (j + 1) * 128], (SEQ, 128)) <= column - s
            mask_s[s, :, j * 128 : (j + 1) * 128] = jnp.where(seen, 0.0, NEG)


def lines_of_table(tab_ref):
    offset = lax.broadcasted_iota(jnp.int32, (128, 1024), 1) - 512
    bucket = lax.broadcasted_iota(jnp.int32, (128, 1024), 0)
    onehot = jnp.where(bucket_of(offset) == bucket, 1.0, 0.0).astype(BF16)
    line = mm(tab_ref[...], onehot) * LOG2E
    return [line[h : h + 1] for h in range(HEADS)]


def build_strip(lines, strip_s, heads):
    for h in heads:
        line = lines[h]
        wide = jnp.broadcast_to(line[:, 256:768], (128, 512))
        strip_s[h, :, 0:256] = jnp.broadcast_to(line[:, 0:1], (128, 256))
        strip_s[h, :, 256:640] = pltpu.roll(wide, 0, 1, stride=1, stride_axis=0)[:, 128:]
        strip_s[h, :, 640:896] = jnp.broadcast_to(line[:, 1023:1024], (128, 256))


def square(w_s, m, cols=slice(None)):
    block = w_s[m, :, :, cols]
    return block.reshape(D, block.shape[-1])


def project(x_ref, y_ref, vec_ref, w_s, q_s, k_s, v_s, p):
    cols = ds(p * 256, 256)
    x = x_ref[...]
    parts = (
        (q_s, 0, mm(x, square(w_s, 0, cols)) + vec_ref[0:1, cols]),
        (q_s, 1, mm(y_ref[...], square(w_s, 0, cols)) + vec_ref[0:1, cols]),
        (k_s, None, mm(x, square(w_s, 1, cols))),
        (v_s, None, mm(x, square(w_s, 2, cols)) + vec_ref[1:2, cols]),
    )
    for ref, s, value in parts:
        value = value.astype(BF16)
        for e in range(2):
            piece = value[:, e * 128 : (e + 1) * 128]
            if s is None:
                ref[2 * p + e] = piece
            else:
                ref[s, 2 * p + e] = piece


def attend(q_s, k_s, v_s, strip_s, mask_s, p_st, ctx_s, hp, slot, ahead):
    lane = lax.broadcasted_iota(jnp.int32, (SEQ, 128), 1)
    k = k_s[hp]
    v = v_s[hp]
    for s in range(2):
        ahead(s)
        q = q_s[s, hp]
        outs = []
        for e in range(2):
            own = (lane < 64) if e == 0 else (lane >= 64)
            scores = mm_nt(jnp.where(own, q, jnp.zeros_like(q)), k)
            for i in range(SEQ // 128):
                rows = slice(i * 128, (i + 1) * 128)
                blk = (
                    scores[rows] * (SCALE * LOG2E)
                    + strip_s[2 * hp + e, :, (3 - i) * 128 : (3 - i) * 128 + SEQ]
                    + mask_s[s, rows, :]
                )
                top = jnp.max(blk, axis=1, keepdims=True)
                w = jnp.exp2(blk - top)
                w = w * (1.0 / jnp.sum(w, axis=1, keepdims=True))
                p_st[slot, e, s, rows, :] = w.astype(BF16)
            outs.append(mm(p_st[slot, e, s], v))
        ctx_s[s * SEQ : (s + 1) * SEQ, ds(hp * 128, 128)] = jnp.where(
            lane < 64, outs[0], outs[1]
        ).astype(BF16)


def norm_stats(r):
    mean = jnp.mean(r, axis=1, keepdims=True)
    centred = r - mean
    inverse = lax.rsqrt(jnp.mean(centred * centred, axis=1, keepdims=True) + EPS)
    return centred * inverse, inverse


NETWORK = {
    (0, 0): (("pass_on", 2),),
    (0, 1): (("share", 1),),
    (1, 0): (("share", 2),),
    (1, 3): (("pass_half", 4, 2), ("pass_half", 4, 1)),
    (2, 0): (("pass_on", 3), ("start_half", 5)),
}


FEED_NETWORK = {
    5: (("share_outer", 1), ("share_outer", 2)),
    7: (("pass_half", 5, 3),),
    11: (("share_outer", 3),),
}


def forward_kernel(linked, *refs):
    refs = list(refs)
    take = lambda n: [refs.pop(0) for _ in range(n)]
    x_ref, y_ref, len_ref, rank_ref = take(4)
    if linked:
        (small_ref,) = take(1)
        shards = take(6)
    else:
        vec_ref, tab_ref, *weights = take(5)
    oc_ref, oq_ref, q_h, k_h, v_h, p_h, ctx_h, n1_h, inv1_h, nl_h, act_h, slope_h, n2_h, inv2_h = take(14)
    if linked:
        vec_h, *weights = take(4)
    wa_s, wi_s, wo_s, q_s, k_s, v_s, ctx_s, nl_s, n1_s, br_s, inv1_s, inv2_s, o_sem, st_sem, w_sem = take(15)
    copies = (wa_s, wi_s, wo_s)
    if linked:
        small_s, vec_ref, *sems = take(10)
        net = Gather((wa_s, wi_s, wo_s, small_s), (w_sem, *sems))
        r, z, c = places()
        f = 2 * z + c
        own = net.own(shards)
        for batch in own:
            for copy in batch:
                copy.start()
        small_s[f] = small_ref[...]
        greet(
            [(hop(r, m), f) for m in (1, 2, 3)] + [(r, (f + k) % 8) for k in range(1, 8)]
        )
        for k in range(1, 8):
            net.small_copy(k).start()
        for copy in own[0]:
            copy.wait()
        net.start_z(0)
        net.start_z(1)
    else:
        loads = [pltpu.make_async_copy(src, dst, w_sem.at[i, 0]) for i, (src, dst) in enumerate(zip(weights, copies))]
        for copy in loads:
            copy.start()
    stores = []

    def keep(src, dst):
        pltpu.make_async_copy(src, dst, o_sem.at[len(stores)]).start()
        stores.append((src, dst))

    def attention(strip_s, mask_s, p_st):
        build_masks(len_ref, rank_ref, mask_s)
        if linked:
            net.pass_on(0)
            net.start_z(2)
            for k in range(1, 8):
                net.small_come(k).wait_recv()
            lines = lines_of(unpack_small(small_s, vec_ref))
            net.pass_on(1)
            for copy in own[1] + own[2]:
                copy.wait()
            net.start_half(4)
            net.start_z(3)
            build_strip(lines, strip_s, range(0, 4))
            net.share(0)
            net.share_outer(0)
            build_strip(lines, strip_s, range(4, HEADS))
            keep(vec_ref, vec_h)
        else:
            build_strip(lines_of_table(tab_ref), strip_s, range(HEADS))
            loads[0].wait()

        def store(hp, slot):
            return pltpu.make_async_copy(p_st.at[slot], p_h.at[hp], st_sem.at[slot])

        def hooks(p, part):
            for (at, when), moves in NETWORK.items():
                if when == part:
                    @pl.when(p == at)
                    def _(moves=moves):
                        for name, *unit in moves:
                            getattr(net, name)(*unit)

        def step(p, carry):
            if linked:
                net.finish(p)
            project(x_ref, y_ref, vec_ref, wa_s, q_s, k_s, v_s, p)
            for part in range(2):
                @pl.when(p >= 1)
                def _():
                    store(2 * p - 2 + part, part).wait()

                def ahead(s, part=part):
                    if linked:
                        hooks(p, 2 * part + s)

                attend(q_s, k_s, v_s, strip_s, mask_s, p_st, ctx_s, 2 * p + part, part, ahead)
                store(2 * p + part, part).start()
            return carry

        lax.fori_loop(0, PIECES, step, 0)
        for part in range(2):
            store(PAIRS - 2 + part, part).wait()
        keep(q_s, q_h)
        keep(k_s, k_h)
        keep(v_s, v_h)

    pl.run_scoped(
        attention,
        pltpu.VMEM((HEADS, 128, 896), F32),
        pltpu.VMEM((2, SEQ, SEQ), F32),
        pltpu.VMEM((2, 2, 2, SEQ, SEQ), BF16),
    )
    keep(ctx_s, ctx_h)
    if linked:
        net.share(3)
        net.pass_half(4, 3)
        net.share_inner(0)
        net.share_inner(1)
        net.finish(3)
        keep(wa_s, weights[0])

    for s, in_ref in ((0, x_ref), (1, y_ref)):
        if linked and s:
            net.share_inner(2)
            net.share_inner(3)

        def first(i, carry, s=s, in_ref=in_ref):
            own = ds(i * 256, 256)
            rows = ds(s * SEQ + i * 256, 256)
            r = in_ref[own, :].astype(F32) + mm(ctx_s[rows, :], square(wa_s, 3)) + vec_ref[2:3, :]
            n, inverse = norm_stats(r)
            n1_s[rows, :] = n
            inv1_s[rows, :] = jnp.broadcast_to(inverse, (256, 128))
            nl_s[rows, :] = (n * vec_ref[3:4, :] + vec_ref[4:5, :]).astype(BF16)
            return carry

        lax.fori_loop(0, SEQ // 256, first, 0)
    keep(n1_s, n1_h)
    keep(inv1_s, inv1_h)
    keep(nl_s, nl_h)

    if linked:
        net.pass_half(5, 2)
        net.pass_half(5, 1)
        net.finish_inner()
        keep(wi_s, weights[1])
    else:
        loads[1].wait()
        loads[2].wait()

    def feed(act_s, slope_st):
        def part(t):
            return ds(t * TILE, TILE)

        def pair(t, slot):
            return (
                pltpu.make_async_copy(act_s.at[:, part(t)], act_h.at[:, part(t)], st_sem.at[slot]),
                pltpu.make_async_copy(slope_st.at[slot], slope_h.at[:, part(t)], st_sem.at[2 + slot]),
            )

        def step(t, carry):
            slot = t % 2

            @pl.when(t >= 2)
            def _():
                for c in pair(t - 2, slot):
                    c.wait()

            if linked:
                for at, moves in FEED_NETWORK.items():
                    @pl.when(t == at)
                    def _(moves=moves):
                        for name, *unit in moves:
                            getattr(net, name)(*unit)

            cols = ds((t % 3) * TILE, TILE)
            inner = mm(nl_s[...], square(wi_s, t // 3, cols)) + vec_ref[pl.ds(8 + (t // 3), 1), cols]
            spread, bell = normal_parts(inner)
            act_s[:, part(t)] = (inner * spread).astype(BF16)
            slope_st[slot] = (spread + inner * bell).astype(BF16)
            for c in pair(t, slot):
                c.start()
            return carry

        lax.fori_loop(0, TILES, step, 0)
        z = places()[1] if linked else 0
        for k in range(4):
            if linked:
                net.finish_outer(k)
            far = hop(z, k)

            def outer(i, carry, k=k, far=far):
                rows = ds(i * 512, 512)
                part = mm(act_s[rows, ds(far * D, D)], wo_s[far])
                br_s[rows, :] = part + br_s[rows, :] if k else part
                return carry

            lax.fori_loop(0, ROWS // 512, outer, 0)
        if linked:
            keep(wo_s, weights[2])
        for t in (TILES - 2, TILES - 1):
            for c in pair(t, t % 2):
                c.wait()

    pl.run_scoped(feed, pltpu.VMEM((ROWS, FF), BF16), pltpu.VMEM((2, ROWS, TILE), BF16))

    for s, o_ref in ((0, oc_ref), (1, oq_ref)):
        def last(i, carry, s=s, o_ref=o_ref):
            rows = ds(s * SEQ + i * 128, 128)
            normed = n1_s[rows, :] * vec_ref[3:4, :] + vec_ref[4:5, :]
            n, inverse = norm_stats(normed + br_s[rows, :] + vec_ref[5:6, :])
            br_s[rows, :] = n
            inv2_s[rows, :] = jnp.broadcast_to(inverse, (128, 128))
            o_ref[ds(i * 128, 128), :] = (n * vec_ref[6:7, :] + vec_ref[7:8, :]).astype(BF16)
            return carry

        lax.fori_loop(0, SEQ // 128, last, 0)
    keep(br_s, n2_h)
    keep(inv2_s, inv2_h)
    for i, (src, dst) in enumerate(stores):
        pltpu.make_async_copy(src, dst, o_sem.at[i]).wait()
    if linked:
        net.drain()


WEIGHTS = ((4, 4, 192, D), (4, 4, 192, D), (4, D, D))


def call_forward(linked, *args):
    hbm = pl.BlockSpec(memory_space=pl.ANY)
    vmem = pl.BlockSpec(memory_space=pltpu.VMEM)
    smem = pl.BlockSpec(memory_space=pltpu.SMEM)
    dma = pltpu.SemaphoreType.DMA
    shape = jax.ShapeDtypeStruct
    outs = [
        shape((SEQ, D), BF16), shape((SEQ, D), BF16),
        shape((2, PAIRS, SEQ, 128), BF16), shape((PAIRS, SEQ, 128), BF16), shape((PAIRS, SEQ, 128), BF16),
        shape((PAIRS, 2, 2, SEQ, SEQ), BF16), shape((ROWS, D), BF16),
        shape((ROWS, D), F32), shape((ROWS, 128), F32), shape((ROWS, D), BF16),
        shape((ROWS, FF), BF16), shape((ROWS, FF), BF16),
        shape((ROWS, D), F32), shape((ROWS, 128), F32),
    ]
    scratch = [pltpu.VMEM(w, BF16) for w in WEIGHTS] + [
        pltpu.VMEM((2, PAIRS, SEQ, 128), BF16), pltpu.VMEM((PAIRS, SEQ, 128), BF16), pltpu.VMEM((PAIRS, SEQ, 128), BF16),
        pltpu.VMEM((ROWS, D), BF16), pltpu.VMEM((ROWS, D), BF16), pltpu.VMEM((ROWS, D), F32), pltpu.VMEM((ROWS, D), F32),
        pltpu.VMEM((ROWS, 128), F32), pltpu.VMEM((ROWS, 128), F32),
        dma((13,)), dma((4,)), dma((3, 4)),
    ]
    in_specs = [vmem, vmem, smem, vmem]
    if linked:
        in_specs += [vmem] + [hbm] * 6
        outs += [shape((16, D), F32)] + [shape(w, BF16) for w in WEIGHTS]
        scratch += [
            pltpu.VMEM((8, 16, 128), BF16), pltpu.VMEM((16, D), F32),
            dma((6, 6)), dma((6, 6)), dma((6, 9)), dma((6, 9)), dma((6, 4)), dma((6, 4)), dma((7,)), dma((7,)),
        ]
        params = pltpu.CompilerParams(vmem_limit_bytes=VMEM_LIMIT, collective_id=1, has_side_effects=True)
    else:
        in_specs += [vmem, vmem] + [hbm] * 3
        params = pltpu.CompilerParams(vmem_limit_bytes=VMEM_LIMIT)
    return pl.pallas_call(
        functools.partial(forward_kernel, linked),
        out_shape=outs,
        in_specs=in_specs,
        out_specs=[vmem, vmem] + [hbm] * (len(outs) - 2),
        scratch_shapes=scratch,
        compiler_params=params,
        name="forward",
    )(*args)


class Reduce:
    def __init__(self, refs, sems):
        self.g, more = refs
        self.cr1, self.cr2, *more, self.res = more
        self.big, self.cut, self.out = more[:5], more[5:10], more[10:]
        self.cs, self.cr, self.credit, self.xs, self.xd, self.zs, self.zd, self.ys, self.yd, self.as_, self.ad = sems
        self.r, self.z, self.c = places()
        self.f = 2 * self.z + self.c
        self.side = (self.r % 2, self.r // 2)

    def number(self, kind, i):
        return {"in": 0, "square": 4, "piece": 5, "out": 8}[kind] + i

    def columns(self, kind, i, side):
        return pl.ds(pl.multiple_of(i * 256 + side * 128, 128), 128) if kind == "piece" else ds(side * 384, 384)

    def half(self, kind, i, m, z, give=False):
        side = 1 - self.side[m] if give else self.side[m]
        if kind == "out":
            return block_of(self.g, 2, 2 * m + side, i, self.c)
        rows = pl.ds(pl.multiple_of(self.c * 96 + m * 48, 48), 48)
        cols = self.columns(kind, i, side)
        if kind == "in":
            return self.g[1].at[i, z, rows, cols]
        return self.g[0].at[3 if kind == "square" else slice(0, 3), z, rows, cols]

    def held(self, what, kind, i, m):
        if kind == "out":
            return self.out[what].at[m, i] if what == 0 else self.out[what].at[m, i // 2] if what == 1 else self.out[what].at[m]
        return self.cut[what].at[m, i] if kind == "piece" else self.big[what].at[m, 4 if kind == "square" else i]

    def mine(self, kind, i):
        rows, cols = ds(self.c * 96, 96), ds(i * 256, 256)
        if kind == "out":
            return self.g[2].at[i, ds(self.c * 384, 384), :], self.cr2.at[i]
        if kind == "in":
            return self.g[1].at[i, :, rows, :], self.cr1.at[i]
        if kind == "square":
            return self.g[0].at[3, :, rows, :], self.cr1.at[3]
        return self.g[0].at[0:3, :, rows, cols], self.cr1.at[0:3, :, :, cols]

    def core(self, kind, i):
        rows, cols = ds((1 - self.c) * 96, 96), ds(i * 256, 256)
        if kind == "out":
            src = self.g[2].at[i, ds((1 - self.c) * 384, 384), :]
        elif kind == "in":
            src = self.g[1].at[i, :, rows, :]
        elif kind == "square":
            src = self.g[0].at[3, :, rows, :]
        else:
            src = self.g[0].at[0:3, :, rows, cols]
        n = self.number(kind, i)
        return remote(src, self.mine(kind, i)[1], self.cs.at[n], self.cr.at[n], (self.r, 2 * self.z + 1 - self.c))

    def across(self, kind, i, m):
        n = 2 * self.number(kind, i) + m
        src, dst = self.half(kind, i, m, ALL, True), self.held(0, kind, i, m)
        return remote(src, dst, self.xs.at[n], self.xd.at[n], (hop(self.r, m + 1), self.f))

    def near(self, kind, i, m, j=0):
        to, n = hop(self.z, 1), 4 * self.number(kind, i) + 2 * m + j
        src, dst = self.half(kind, i, m, hop(self.z, 3) if j else to), self.held(1, kind, i, m)
        return remote(
            src, dst if kind == "out" else dst.at[j], self.zs.at[n], self.zd.at[n], (self.r, 2 * to + self.c)
        )

    def far(self, kind, i, m):
        to = hop(self.z, 2)
        if kind == "out":
            i, n = to, 64 + m
        else:
            n = 48 + 2 * self.number(kind, i) + m
        src, dst = self.half(kind, i, m, to), self.held(2, kind, i, m)
        return remote(src, dst, self.zs.at[n], self.zd.at[n], (self.r, 2 * to + self.c))

    def complete(self, kind, i, m):
        n = 2 * (8 if kind == "out" else self.number(kind, i)) + m
        src, dst = self.held(3, kind, i, m), self.held(4, kind, i, m)
        return remote(src, dst, self.ys.at[n], self.yd.at[n], (hop(self.r, 2 - m), self.f))

    def result(self, kind, i, m, give=False):
        side = 1 - self.side[m] if give else self.side[m]
        if kind == "out":
            return self.res.at[2, 2 * m + side]
        rows, cols = slice(m * 48, (m + 1) * 48), self.columns(kind, i, side)
        if kind == "in":
            return self.res.at[1, i, rows, cols]
        return self.res.at[0, 3 if kind == "square" else slice(0, 3), rows, cols]

    def spread(self, kind, i, m, come=False):
        n = 2 * (8 if kind == "out" else self.number(kind, i)) + m
        ref = self.result(kind, i, m, come)
        return remote(ref, ref, self.as_.at[n], self.ad.at[n], (hop(self.r, m + 1), self.f))

    def start(self, kind, i=0):
        self.core(kind, i).start()

    def cores(self, kind, i=0):
        self.core(kind, i).wait_recv()
        ref, come = self.mine(kind, i)
        ref[...] = ref[...] + come[...]
        for m in range(2):
            self.across(kind, i, m).start()

    def allow(self):
        pl.semaphore_signal(
            self.credit, inc=1, device_id=(self.r, 2 * self.z + 1 - self.c), device_id_type=pl.DeviceIdType.MESH
        )

    def replicas(self, kind, i=0):
        for m in range(2):
            self.across(kind, i, m).wait_recv()
            ref = self.half(kind, i, m, ALL)
            ref[...] = ref[...] + self.held(0, kind, i, m)[...]
            if kind == "out":
                @pl.when((self.z + i) % 2 == 1)
                def _(m=m):
                    self.near(kind, i, m).start()
            else:
                for j in range(2):
                    self.near(kind, i, m, j).start()

    def pairs(self, kind, i=0):
        if kind == "out":
            @pl.when((self.z + i) % 2 == 0)
            def _():
                for m in range(2):
                    self.near(kind, i, m).wait_recv()
                    ref = self.half(kind, i, m, None)
                    ref[...] = ref[...] + self.held(1, kind, i, m)[...]

                    @pl.when(self.z != i)
                    def _(m=m):
                        self.far(kind, i, m).start()
            return
        for m in range(2):
            for j in (1, 0):
                self.near(kind, i, m, j).wait_recv()
                ref = self.half(kind, i, m, hop(self.z, 2 * j))
                ref[...] = ref[...] + self.held(1, kind, i, m).at[j][...]
                if j:
                    self.far(kind, i, m).start()

    def owners(self, kind, i=0):
        for m in range(2):
            self.far(kind, i, m).wait_recv()
            total = self.half(kind, self.z if kind == "out" else i, m, self.z)[...].astype(F32)
            total = total + self.held(2, kind, i, m)[...].astype(F32)
            self.held(3, kind, i, m)[...] = total.astype(BF16)
            self.complete(kind, i, m).start()

    def ends(self, kind, i=0):
        for m in range(2):
            self.complete(kind, i, m).wait_recv()
            total = self.held(3, kind, i, m)[...].astype(F32) + self.held(4, kind, i, m)[...].astype(F32)
            self.result(kind, i, m)[...] = total.astype(BF16)
            self.spread(kind, i, m).start()

    def finish(self, kind, i=0):
        for m in range(2):
            self.spread(kind, i, m, True).wait_recv()

    def drain(self):
        def sent(kind, i):
            self.core(kind, i).wait_send()
            for m in range(2):
                self.across(kind, i, m).wait_send()
                if kind != "out":
                    for j in range(2):
                        self.near(kind, i, m, j).wait_send()
                    self.far(kind, i, m).wait_send()
                    self.complete(kind, i, m).wait_send()
                    self.spread(kind, i, m).wait_send()

        def several(kind, count):
            lax.fori_loop(0, count, lambda i, carry: (sent(kind, i), carry)[1], 0)

        several("in", 4)
        several("out", 4)
        several("piece", PIECES)
        sent("square", 0)
        for m in range(2):
            for i in (hop(self.z, 1), hop(self.z, 3)):
                self.near("out", i, m).wait_send()
            self.far("out", 0, m).wait_send()
            self.complete("out", 0, m).wait_send()
            self.spread("out", 0, m).wait_send()


class SmallReduce:
    def __init__(self, refs, sems):
        self.out, self.got, self.sums = refs
        self.vs, self.vd, self.ws, self.wd = sems
        self.r, z, c = places()
        self.f = 2 * z + c

    def first(self, k):
        to = (self.f + k) % 8
        return remote(self.out.at[to], self.got.at[self.f], self.vs.at[k - 1], self.vd.at[k - 1], (self.r, to))

    def first_come(self, k):
        back = (self.f + 8 - k) % 8
        return remote(self.out.at[back], self.got.at[back], self.vs.at[k - 1], self.vd.at[k - 1], (self.r, back))

    def second(self, m, come=False):
        far = hop(self.r, m)
        ref = self.sums.at[far if come else self.r]
        return remote(ref, ref, self.ws.at[m - 1], self.wd.at[m - 1], (far, self.f))

    def start(self, vec, table):
        pack_small(vec, table, self.out)
        self.got[self.f] = self.out[self.f]
        for k in range(1, 8):
            self.first(k).start()

    def middle(self):
        for k in range(1, 8):
            self.first_come(k).wait_recv()
        total = self.got[0]
        for f in range(1, 8):
            total = total + self.got[f]
        self.sums[self.r] = total
        for m in (1, 2, 3):
            self.second(m).start()

    def finish(self):
        for m in (1, 2, 3):
            self.second(m, True).wait_recv()
        total = self.sums[0]
        for r in range(1, 4):
            total = total + self.sums[r]
        return total

    def drain(self):
        for k in range(1, 8):
            self.first(k).wait_send()
        for m in (1, 2, 3):
            self.second(m).wait_send()


def pack_small(vec_ref, table, out_ref):
    vec = vec_ref[...]
    at = lax.broadcasted_iota(jnp.int32, (D, 128), 1)
    shift = jnp.where(at < 96, lax.broadcasted_iota(jnp.int32, (D, 128), 0) - at, -1)
    lane = lax.broadcasted_iota(jnp.int32, (1, 128), 1)
    for f in range(8):
        m = f // 2
        out_ref[f, 0:8, :] = lax.dot_general(
            vec[0:8], jnp.where(shift == 96 * f, 1.0, 0.0), (((1,), (0,)), ((), ())),
            precision=lax.Precision.HIGHEST, preferred_element_type=F32,
        )
        for j in range(3):
            col = (f % 2) * 384 + j * 128
            out_ref[f, 8 + j : 9 + j, :] = vec[8 + m : 9 + m, col : col + 128]
        head = 3 * m + f % 2
        a, b = table[head : head + 1], table[head + 1 : head + 2]
        if f % 2 == 0:
            line = jnp.where(lane < 32, a, jnp.where(lane < 48, pltpu.roll(b, 32, 1), 0.0))
        else:
            line = jnp.where(lane < 16, pltpu.roll(a, 112, 1), jnp.where(lane < 48, pltpu.roll(b, 16, 1), 0.0))
        out_ref[f, 11:12, :] = line
        out_ref[f, 12:16, :] = jnp.zeros((4, 128), F32)


def norm_grad(u, gain, n, inverse):
    ug = u * gain
    return inverse * (
        ug - jnp.mean(ug, axis=1, keepdims=True) - n * jnp.mean(ug * n, axis=1, keepdims=True)
    )


BACK_NETWORK = {
    (0, 0): (("replicas", "out", 3), ("replicas", "in", 3), ),
    (0, 1): (("pairs", "out", 2), ("pairs", "in", 2), ("replicas", "square"), ),
    (1, 1): (("cores", "piece", 0), ),
    (2, 0): (("replicas", "piece", 0), ("pairs", "out", 3), ("pairs", "in", 3), ("pairs", "square"), ("owners", "in", 0), ("owners", "in", 1), ),
    (2, 1): (("cores", "piece", 1), ),
}

LAST_NETWORK = (
    (("cores", "piece", 2), ),
    (("replicas", "piece", 1), ("pairs", "piece", 0), ("owners", "out"), ("owners", "in", 2), ),
    (("replicas", "piece", 2), ("owners", "square"), ("ends", "in", 0), ("ends", "in", 1), ),
    (("pairs", "piece", 1), ("owners", "in", 3), ("ends", "out"), ("ends", "in", 2), ("sum_middle",), ),
    (("pairs", "piece", 2), ("owners", "piece", 0), ("ends", "square"), ("ends", "in", 3), ),
    (("owners", "piece", 1), ("ends", "piece", 0), ("owners", "piece", 2), ("ends", "piece", 1), ("ends", "piece", 2), ),
)


def backward_kernel(linked, *refs):
    refs = list(refs)
    take = lambda n: [refs.pop(0) for _ in range(n)]
    x_h, y_h, cc_h, cq_h, vec_ref, wa_h, wi_h, wo_h = take(8)
    q_h, k_h, v_h, p_h, ctx_h, n1_h, inv1_h, nl_h, act_h, slope_h, n2_h, inv2_h = take(12)
    gc_h, gq_h = take(2)
    if linked:
        res_ref, small_ref = take(2)
    else:
        *grads_h, gvec_ref, gtab_ref = take(5)
    ctx_s, g_s, dctx_s, tr_s, l_sem, t_sem = take(6)
    ga_s, gi_s, go_s = grads = take(3)
    if linked:
        gvec_ref, *more = take(19)
        sum_refs = take(3)
        sems = take(11)
        sum_sems = take(4)
        net = Reduce((grads, more), sems)
        sums = SmallReduce(sum_refs, sum_sems)
        r, z, c = places()
        f = 2 * z + c
        res_s = more[-1]
    cload = pltpu.make_async_copy(ctx_h, ctx_s, l_sem.at[1])
    cload.start()
    gvec_ref[...] = jnp.zeros_like(gvec_ref)

    def add_vec(row, value, cols=slice(None)):
        gvec_ref[row : row + 1, cols] += jnp.sum(value, axis=0, keepdims=True)

    def tail(n_s, inv_s, nl_s, db_s, act_s, slope_s, wi_s, wo_s, cot_s, wt_s):
        wload = pltpu.make_async_copy(wa_h.at[3], wt_s, l_sem.at[0])
        wload.start()
        nload = pltpu.make_async_copy(n2_h, n_s, l_sem.at[2])
        iload = pltpu.make_async_copy(inv2_h, inv_s, l_sem.at[3])
        nlload = pltpu.make_async_copy(nl_h, nl_s, l_sem.at[4])
        cots = [pltpu.make_async_copy(ref, cot_s.at[s], l_sem.at[5 + s]) for s, ref in enumerate((cc_h, cq_h))]
        for copy in (nload, iload, *cots, nlload):
            copy.start()

        def fetch(t, slot):
            return (
                pltpu.make_async_copy(act_h.at[:, ds(t * TILE, TILE)], act_s.at[slot], t_sem.at[slot]),
                pltpu.make_async_copy(slope_h.at[:, ds(t * TILE, TILE)], slope_s.at[slot], t_sem.at[2 + slot]),
                pltpu.make_async_copy(wi_h.at[t // 3, :, :, ds((t % 3) * TILE, TILE)], wi_s.at[slot], t_sem.at[4 + slot]),
                pltpu.make_async_copy(wo_h.at[t // 3, ds((t % 3) * TILE, TILE), :], wo_s.at[slot], t_sem.at[6 + slot]),
            )

        for copy in fetch(0, 0):
            copy.start()
        if linked:
            greet([(hop(r, m), f) for m in (1, 2, 3)] + [(r, (f + k) % 8) for k in range(1, 8)])
        for copy in (nload, iload, *cots):
            copy.wait()

        def second(i, carry):
            rows = ds(i * 128, 128)
            u = cot_s[i // 4, ds((i % 4) * 128, 128), :].astype(F32)
            n = n_s[rows, :]
            g = norm_grad(u, vec_ref[6:7, :], n, inv_s[rows, 0:1])
            add_vec(6, u * n)
            add_vec(7, u)
            g_s[rows, :] = g
            low = g.astype(BF16)
            db_s[rows, :] = low
            add_vec(5, low.astype(F32))
            return carry

        lax.fori_loop(0, ROWS // 128, second, 0)
        n1load = pltpu.make_async_copy(n1_h, n_s, l_sem.at[2])
        i1load = pltpu.make_async_copy(inv1_h, inv_s, l_sem.at[3])
        n1load.start()
        i1load.start()
        nlload.wait()
        tr_s[...] = nl_s[...].T
        xyloads = [
            pltpu.make_async_copy(ref, nl_s.at[s * SEQ : (s + 1) * SEQ, :], l_sem.at[5 + s])
            for s, ref in enumerate((x_h, y_h))
        ]
        for copy in xyloads:
            copy.start()

        def step(t, carry):
            slot = t % 2
            for copy in fetch(t, slot):
                copy.wait()

            @pl.when(t + 1 < TILES)
            def _():
                for copy in fetch(t + 1, 1 - slot):
                    copy.start()

            if linked:
                @pl.when((t % 3 == 1) & (t >= 4))
                def _():
                    for kind in ("out", "in"):
                        net.cores(kind, t // 3 - 1)

                @pl.when((t % 3 == 1) & (t >= 7))
                def _():
                    for kind in ("out", "in"):
                        net.replicas(kind, t // 3 - 2)

                @pl.when(t == 11)
                def _():
                    for kind in ("out", "in"):
                        net.pairs(kind, 0)

            db = db_s[...]
            di = (mm_nt(db, wo_s[slot]) * slope_s[slot].astype(F32)).astype(BF16)
            i, part = t // 3, ds((t % 3) * TILE, TILE)
            mine = lax.broadcasted_iota(jnp.int32, (8, TILE), 0) == i
            gvec_ref[8:16, part] += jnp.where(mine, jnp.sum(di.astype(F32), axis=0, keepdims=True), 0.0)
            go_s[i, part, :] = mm_tn(act_s[slot], db).astype(BF16)
            gi_s[i, :, :, part] = mm(tr_s[...], di).astype(BF16).reshape(4, 192, TILE)
            g_s[...] += mm_nt(di, wi_s[slot].reshape(D, TILE))
            if linked:
                @pl.when(t % 3 == 2)
                def _():
                    net.start("out", i)
                    net.start("in", i)

            return carry

        lax.fori_loop(0, TILES, step, 0)
        n1load.wait()
        i1load.wait()

        def first(i, carry):
            rows = ds(i * 128, 128)
            u = g_s[rows, :]
            n = n_s[rows, :]
            g = norm_grad(u, vec_ref[3:4, :], n, inv_s[rows, 0:1])
            add_vec(3, u * n)
            add_vec(4, u)
            g_s[rows, :] = g
            low = g.astype(BF16)
            db_s[rows, :] = low
            add_vec(2, low.astype(F32))
            return carry

        lax.fori_loop(0, ROWS // 128, first, 0)
        wload.wait()
        cload.wait()
        if linked:
            for kind in ("out", "in"):
                net.cores(kind, 3)
            net.allow()
            for kind in ("out", "in"):
                net.replicas(kind, 2)
        tr_s[...] = ctx_s[...].T

        def square_grad(j, carry):
            ga_s[3, j] = mm(tr_s[pl.ds(pl.multiple_of(j * 192, 192), 192), :], db_s[...]).astype(BF16)
            return carry

        lax.fori_loop(0, 4, square_grad, 0)
        if linked:
            pl.semaphore_wait(net.credit, 1)
            net.start("square")
        for j in range(4):
            dctx_s[j * 256 : (j + 1) * 256, :] = mm_nt(db_s[j * 256 : (j + 1) * 256, :], wt_s[...].reshape(D, D)).astype(BF16)
        if linked:
            for kind in ("out", "in"):
                net.pairs(kind, 1)
            net.cores("square")
        for copy in xyloads:
            copy.wait()
        tr_s[...] = nl_s[...].T

    pl.run_scoped(
        tail,
        pltpu.VMEM((ROWS, D), F32),
        pltpu.VMEM((ROWS, 128), F32),
        pltpu.VMEM((ROWS, D), BF16),
        pltpu.VMEM((ROWS, D), BF16),
        pltpu.VMEM((2, ROWS, TILE), BF16),
        pltpu.VMEM((2, ROWS, TILE), BF16),
        pltpu.VMEM((2, 4, 192, TILE), BF16),
        pltpu.VMEM((2, TILE, D), BF16),
        pltpu.VMEM((2, SEQ, D), BF16),
        pltpu.VMEM(WEIGHTS[0][1:], BF16),
    )

    def attention(q_s, k_s, v_s, p_s, dq_s, dk_s, dv_s, dkt_s, dvt_s, far_s, bt_s, wa_s):
        wload = pltpu.make_async_copy(wa_h.at[0:3], wa_s, l_sem.at[0])
        wload.start()
        loads = [(q_h, q_s), (k_h, k_s), (v_h, v_s)]
        loads = [pltpu.make_async_copy(a, b, l_sem.at[2 + i]) for i, (a, b) in enumerate(loads)]
        for copy in loads:
            copy.start()

        def fetch(hp, slot):
            return pltpu.make_async_copy(p_h.at[hp], p_s.at[slot], t_sem.at[slot])

        fetch(0, 0).start()
        for copy in loads:
            copy.wait()

        def hooks(p, part):
            for (at, when), moves in BACK_NETWORK.items():
                if when == part:
                    @pl.when(p == at)
                    def _(moves=moves):
                        for name, *unit in moves:
                            getattr(net, name)(*unit)

        def step(p, carry):
            for part in range(2):
                hp = 2 * p + part
                if part == 0:
                    fetch(hp + 1, 1).start()
                else:
                    @pl.when(p + 1 < PIECES)
                    def _():
                        fetch(hp + 1, 0).start()

                if linked:
                    hooks(p, part)
                fetch(hp, part).wait()
                attend_back(hp, part)
            cols = ds(p * 256, 256)
            dk_s[:, cols] = dkt_s[cols, :].T
            dv_s[:, cols] = dvt_s[cols, :].T
            for w, left, grad in ((1, slice(0, SEQ), dk_s), (2, slice(0, SEQ), dv_s), (0, slice(0, ROWS), dq_s)):
                ga_s[w, :, :, cols] = mm(tr_s[:, left], grad[:, cols]).astype(BF16).reshape(4, 192, 256)
            if linked:
                net.start("piece", p)
            return carry

        def attend_back(hp, slot):
            lane = lax.broadcasted_iota(jnp.int32, (SEQ, 128), 1)
            k, v = k_s[hp], v_s[hp]
            zero = jnp.zeros((SEQ, 128), BF16)
            dq = [None, None]
            qt = [q_s[s, hp].T for s in range(2)]
            dt = [dctx_s[s * SEQ : (s + 1) * SEQ, ds(hp * 128, 128)].T for s in range(2)]
            for e in range(2):
                own = (lane < 64) if e == 0 else (lane >= 64)
                both = None
                dkt = dvt = None
                for s in range(2):
                    rows = slice(s * SEQ, (s + 1) * SEQ)
                    do = jnp.where(own, dctx_s[rows, ds(hp * 128, 128)], zero)
                    weight = jnp.sum(do.astype(F32) * ctx_s[rows, ds(hp * 128, 128)].astype(F32), axis=1, keepdims=True)
                    p = p_s[slot, e, s]
                    g = p.astype(F32) * (mm_nt(do, v) - weight)
                    low = g.astype(BF16)
                    both = g if both is None else both + g
                    part = mm(low, jnp.where(own, k, zero))
                    dq[s] = part if dq[s] is None else dq[s] + part
                    half = slice(e * 64, (e + 1) * 64)
                    a = mm(dt[s][half], p)
                    b = mm(qt[s][half], low)
                    dvt = a if dvt is None else dvt + a
                    dkt = b if dkt is None else dkt + b
                dvt_s[ds(hp * 128 + e * 64, 64), :] = dvt.astype(BF16)
                dkt_s[ds(hp * 128 + e * 64, 64), :] = (dkt * SCALE).astype(BF16)
                parts = [None] * 5
                for i in range(4):
                    for j in range(4):
                        blk = both[i * 128 : (i + 1) * 128, j * 128 : (j + 1) * 128]
                        at = min(max(j - i, -2), 2) + 2
                        parts[at] = blk if parts[at] is None else parts[at] + blk
                strip = jnp.concatenate([jnp.zeros((128, 128), F32), parts[1], parts[2], parts[3]], axis=1)
                flat = strip[0:8]
                for g in range(1, 16):
                    flat = flat + pltpu.roll(strip[8 * g : 8 * g + 8], 512 - 8 * g, 1)
                row = lax.broadcasted_iota(jnp.int32, (8, 512), 0)
                for bit in (1, 2, 4):
                    flat = jnp.where((row & bit) != 0, pltpu.roll(flat, 512 - bit, 1), flat)
                h = 2 * hp + e
                for ref, cols, value in (
                    (bt_s, slice(0, 512), flat),
                    (far_s, slice(0, 128), parts[0]),
                    (far_s, slice(128, 256), parts[4]),
                ):
                    line = jnp.sum(value, axis=0, keepdims=True)
                    mine = lax.broadcasted_iota(jnp.int32, (16, line.shape[1]), 0) == h
                    ref[:, cols] = jnp.where(mine, line, ref[:, cols])
            for s in range(2):
                dq_s[s * SEQ : (s + 1) * SEQ, ds(hp * 128, 128)] = (dq[s] * SCALE).astype(BF16)

        bt_s[...] = jnp.zeros_like(bt_s)
        far_s[...] = jnp.zeros_like(far_s)
        lax.fori_loop(0, PIECES, step, 0)

        offset = lax.broadcasted_iota(jnp.int32, (512, 128), 0) - 256
        bucket = lax.broadcasted_iota(jnp.int32, (512, 128), 1)
        near = jnp.where(bucket_of(offset) == bucket, 1.0, 0.0)
        lane = lax.broadcasted_iota(jnp.int32, (16, 128), 1)
        table = (
            lax.dot_general(bt_s[...], near, (((1,), (0,)), ((), ())), precision=lax.Precision.HIGHEST, preferred_element_type=F32)
            + jnp.where(lane == 15, jnp.sum(far_s[:, 0:128], axis=1, keepdims=True), 0.0)
            + jnp.where(lane == 31, jnp.sum(far_s[:, 128:256], axis=1, keepdims=True), 0.0)
        )
        add_vec(0, dq_s[...].astype(F32))
        add_vec(1, dv_s[...].astype(F32))
        def run(names):
            if linked:
                for name, *args in names:
                    (getattr(sums, name[4:]) if name.startswith("sum_") else getattr(net, name))(*args)

        run(LAST_NETWORK[0])
        if linked:
            sums.start(gvec_ref, table)
        else:
            gtab_ref[...] = table

        wload.wait()
        run(LAST_NETWORK[1])
        g_s[0:SEQ, :] += mm_nt(dq_s[0:SEQ, :], square(wa_s, 0))
        run(LAST_NETWORK[2])
        g_s[0:SEQ, :] += mm_nt(dk_s[...], square(wa_s, 1))
        run(LAST_NETWORK[3])
        g_s[0:SEQ, :] += mm_nt(dv_s[...], square(wa_s, 2))
        run(LAST_NETWORK[4])
        g_s[SEQ:, :] += mm_nt(dq_s[SEQ:, :], square(wa_s, 0))
        outs = [
            pltpu.make_async_copy(g_s.at[s * SEQ : (s + 1) * SEQ, :], ref, l_sem.at[2 + s])
            for s, ref in enumerate((gc_h, gq_h))
        ]
        for copy in outs:
            copy.start()
        run(LAST_NETWORK[5])
        if linked:
            net.finish("out")
            for i in range(4):
                net.finish("in", i)
            small_ref[...] = sums.finish()
            res_ref[1] = res_s[1]
            res_ref[2] = res_s[2]
            net.finish("square")
            for i in range(PIECES):
                net.finish("piece", i)
            res_ref[0] = res_s[0]
            net.drain()
            sums.drain()
        else:
            writes = [pltpu.make_async_copy(a, b, t_sem.at[i]) for i, (a, b) in enumerate(zip(grads, grads_h))]
            for copy in writes:
                copy.start()
            for copy in writes:
                copy.wait()
        for copy in outs:
            copy.wait()

    pl.run_scoped(
        attention,
        pltpu.VMEM((2, PAIRS, SEQ, 128), BF16),
        pltpu.VMEM((PAIRS, SEQ, 128), BF16),
        pltpu.VMEM((PAIRS, SEQ, 128), BF16),
        pltpu.VMEM((2, 2, 2, SEQ, SEQ), BF16),
        pltpu.VMEM((ROWS, D), BF16),
        pltpu.VMEM((SEQ, D), BF16),
        pltpu.VMEM((SEQ, D), BF16),
        pltpu.VMEM((D, SEQ), BF16),
        pltpu.VMEM((D, SEQ), BF16),
        pltpu.VMEM((16, 256), F32),
        pltpu.VMEM((16, 512), F32),
        pltpu.VMEM((3, *WEIGHTS[0][1:]), BF16),
    )


def call_backward(linked, x, y, cc, cq, vecs, wa, wi, wo, saved):
    hbm = pl.BlockSpec(memory_space=pl.ANY)
    vmem = pl.BlockSpec(memory_space=pltpu.VMEM)
    dma = pltpu.SemaphoreType.DMA
    shape = jax.ShapeDtypeStruct
    outs = [shape((SEQ, D), F32), shape((SEQ, D), F32)]
    out_specs = [hbm, hbm]
    scratch = [
        pltpu.VMEM((ROWS, D), BF16), pltpu.VMEM((ROWS, D), F32), pltpu.VMEM((ROWS, D), BF16),
        pltpu.VMEM((D, ROWS), BF16), dma((7,)), dma((8,)),
    ] + [pltpu.VMEM(w, BF16) for w in WEIGHTS]
    if linked:
        outs += [shape((3, 4, 96, D), BF16), shape((16, 128), F32)]
        out_specs += [vmem, vmem]
        scratch += [pltpu.VMEM((16, D), F32)] + [
            pltpu.VMEM(s, BF16)
            for s in (
                (4, 4, 96, D), (4, 384, D),
                (2, 5, 4, 48, 384), (2, 5, 2, 48, 384), (2, 5, 48, 384), (2, 5, 48, 384), (2, 5, 48, 384),
                (2, 3, 3, 4, 48, 128), (2, 3, 2, 3, 48, 128), (2, 3, 3, 48, 128), (2, 3, 3, 48, 128), (2, 3, 3, 48, 128),
                (2, 4, 96, D), (2, 2, 96, D), (2, 96, D), (2, 96, D), (2, 96, D),
                (3, 4, 96, D),
            )
        ]
        scratch += [pltpu.VMEM((n, 16, 128), F32) for n in (8, 8, 4)]
        scratch += [
            dma((12,)), dma((12,)), pltpu.SemaphoreType.REGULAR, dma((24,)), dma((24,)), dma((66,)), dma((66,)),
            dma((18,)), dma((18,)), dma((18,)), dma((18,)), dma((7,)), dma((7,)), dma((3,)), dma((3,)),
        ]
        params = pltpu.CompilerParams(vmem_limit_bytes=VMEM_LIMIT, collective_id=2, has_side_effects=True)
    else:
        outs += [shape(w, BF16) for w in WEIGHTS] + [shape((16, D), F32), shape((16, 128), F32)]
        out_specs += [hbm] * 3 + [vmem, vmem]
        params = pltpu.CompilerParams(vmem_limit_bytes=VMEM_LIMIT)
    return pl.pallas_call(
        functools.partial(backward_kernel, linked),
        out_shape=outs,
        in_specs=[hbm] * 4 + [vmem] + [hbm] * 15,
        out_specs=out_specs,
        scratch_shapes=scratch,
        compiler_params=params,
        name="backward",
    )(x, y, cc, cq, vecs, wa, wi, wo, *saved)


def finish_kernel(oc_h, oq_h, gc_h, gq_h, res_h, small_ref, oc_o, oq_o, gc_o, gq_o, *rest):
    *weights, low_s, high_s, res_s, square_s, inner_s, outer_s, in_sem, out_sem = rest
    weights, vectors = weights[:6], weights[6:]
    held = [square_s.at[q] for q in range(4)] + [inner_s, outer_s]
    grads = [pltpu.make_async_copy(res_h.at[t], res_s.at[t], in_sem.at[8 + t]) for t in (2, 1, 0)]
    moves = []
    for i, (src, dst) in enumerate(((gc_h, gc_o), (gq_h, gq_o), (oc_h, oc_o), (oq_h, oq_o))):
        room = (high_s if i < 2 else low_s).at[i % 2]
        for part in range(2):
            rows = slice(part * SEQ // 2, (part + 1) * SEQ // 2)
            n = len(moves)
            moves.append((
                pltpu.make_async_copy(src.at[rows, :], room.at[rows, :], in_sem.at[n]),
                pltpu.make_async_copy(room.at[rows, :], dst.at[rows, :], out_sem.at[n]),
            ))
    for copy in grads:
        copy.start()
    for move, _ in moves:
        move.start()
    writes = [pltpu.make_async_copy(src, dst, out_sem.at[8 + i]) for i, (src, dst) in enumerate(zip(held, weights))]
    small = small_ref[...]
    for i in range(8):
        vectors[i][...] = small[i, :96]
    for j in range(3):
        vectors[8][j * 128 : (j + 1) * 128] = small[8 + j]
    vectors[9][...] = small[11, :48]
    grads[0].wait()
    for q in range(4):
        outer_s[q * 96 : (q + 1) * 96, :] = res_s[2, q].astype(F32)
    writes[5].start()
    grads[1].wait()
    for q in range(4):
        inner_s[:, q * D : (q + 1) * D] = res_s[1, q].astype(F32)
    writes[4].start()
    grads[2].wait()
    for q in range(4):
        square_s[q] = res_s[0, q].astype(F32)
        writes[q].start()
    for move, onward in moves:
        move.wait()
        onward.start()
    for _, onward in moves:
        onward.wait()
    for copy in writes:
        copy.wait()


def call_finish(oc, oq, gc, gq, res, small):
    hbm = pl.BlockSpec(memory_space=pl.ANY)
    vmem = pl.BlockSpec(memory_space=pltpu.VMEM)
    shape = jax.ShapeDtypeStruct
    outs = [shape(a.shape, a.dtype) for a in (oc, oq, gc, gq)] + [shape((96, D), F32)] * 4
    outs += [shape((96, FF), F32), shape((384, D), F32)]
    outs += [shape((96,), F32)] * 8 + [shape((384,), F32), shape((48,), F32)]
    return pl.pallas_call(
        finish_kernel,
        out_shape=outs,
        in_specs=[hbm] * 5 + [vmem],
        out_specs=[hbm] * 10 + [vmem] * 10,
        scratch_shapes=[
            pltpu.VMEM((2, SEQ, D), BF16), pltpu.VMEM((2, SEQ, D), F32), pltpu.VMEM((3, 4, 96, D), BF16),
            pltpu.VMEM((4, 96, D), F32), pltpu.VMEM((96, FF), F32), pltpu.VMEM((384, D), F32),
            pltpu.SemaphoreType.DMA((11,)), pltpu.SemaphoreType.DMA((14,)),
        ],
        compiler_params=pltpu.CompilerParams(vmem_limit_bytes=VMEM_LIMIT),
        name="finish",
    )(oc, oq, gc, gq, res, small)


def shards(
    content_stream, query_stream, lengths, ranking, query_weight, query_bias, key_weight, value_weight, value_bias,
    output_weight, output_bias, norm_gain, norm_shift, inner_weight, inner_bias, outer_weight, outer_bias, final_gain,
    final_shift, bucket_bias, content_cotangent, query_cotangent,
):
    small = (query_bias, value_bias, output_bias, norm_gain, norm_shift, outer_bias, final_gain, final_shift)
    width = query_bias.shape[0]
    linked = width * 8 == D and lax.axis_size("rep") == 4
    front = (content_stream, query_stream, lengths, ranking)
    if linked:
        rows = jnp.pad(jnp.stack(small), ((0, 0), (0, 128 - width)))
        rest = jnp.pad(bucket_bias, (0, 128 - bucket_bias.shape[0])).reshape(1, 128)
        packed = jnp.concatenate([rows, inner_bias.reshape(3, 128), rest, jnp.zeros((4, 128), BF16)])
        out_c, out_q, *saved, vecs, wa, wi, wo = call_forward(
            True, *front, packed, query_weight, key_weight, value_weight, output_weight, inner_weight, outer_weight
        )
    else:
        def gather(a, axis=0):
            return lax.all_gather(a, "fsdp", axis=axis, tiled=True)

        wa = gather(jnp.stack([query_weight, key_weight, value_weight, output_weight]), 1).reshape(WEIGHTS[0])
        wi = gather(inner_weight).reshape(D, 4, D).transpose(1, 0, 2).reshape(WEIGHTS[1])
        wo = gather(outer_weight).reshape(WEIGHTS[2])
        packed = gather(jnp.concatenate([*small, inner_bias, bucket_bias])[None, :])
        cuts = [packed[:, i * width : (i + 1) * width].reshape(1, D) for i in range(8)]
        cuts.append(packed[:, 8 * width : 12 * width].reshape(4, D))
        vecs = jnp.concatenate(cuts + [jnp.zeros((4, D), BF16)]).astype(F32)
        table = jnp.pad(packed[:, 12 * width :].reshape(HEADS, BUCKETS), ((0, 4), (0, 128 - BUCKETS)))
        out_c, out_q, *saved = call_forward(False, *front, vecs, table, wa, wi, wo)
    streams = (content_stream, query_stream, content_cotangent, query_cotangent)
    gc, gq, *grads = call_backward(linked, *streams, vecs, wa, wi, wo, saved)
    if linked:
        out_c, out_q, gc, gq, *rest = call_finish(out_c, out_q, gc, gq, *grads)
        ga, gi, go, v, inner, table = rest[:4], rest[4], rest[5], rest[6:14], rest[14], rest[15]
    else:
        def reduce(a, axis=0):
            a = lax.psum_scatter(a, "fsdp", scatter_dimension=axis, tiled=True)
            return lax.psum(a.astype(BF16), "rep").astype(F32)

        ga, gi, go, gvec, gtab = grads
        ga = reduce(ga.reshape(4, D, D), 1)
        gi = reduce(gi.reshape(4, D, D).transpose(1, 0, 2).reshape(D, FF))
        go = reduce(go.reshape(FF, D))
        count = D // width
        flat = jnp.concatenate(
            [gvec[i].reshape(count, width) for i in range(8)]
            + [gvec[8:12].reshape(count, 4 * width), gtab[:HEADS, :BUCKETS].reshape(count, -1)],
            axis=1,
        )
        flat = lax.psum_scatter(flat, "fsdp", scatter_dimension=0, tiled=True)[0]
        flat = lax.psum(flat.astype(BF16), "rep").astype(F32)
        v = [flat[i * width : (i + 1) * width] for i in range(8)]
        inner, table = flat[8 * width : 12 * width], flat[12 * width :]
    return (
        out_c, out_q, gc, gq, ga[0], v[0], ga[1], ga[2], v[1], ga[3], v[2], v[3], v[4], gi,
        inner, go, v[5], v[6], v[7], table,
    )


def solution(mesh):
    both, fsdp = ("rep", "fsdp"), "fsdp"
    row, vec = P(fsdp, None), P(fsdp)
    tokens = P(both, None)
    in_specs = (
        tokens, tokens, P(both), tokens, row, vec, row, row, vec, row, vec, vec, vec, row, vec, row, vec, vec, vec, vec,
        tokens, tokens,
    )
    out_specs = (
        tokens, tokens, tokens, tokens, row, vec, row, row, vec, row, vec, vec, vec, row, vec, row, vec, vec, vec, vec,
    )
    return jax.shard_map(shards, mesh=mesh, in_specs=in_specs, out_specs=out_specs, check_vma=False)
```

```python
import functools

import jax
import jax.numpy as jnp
from jax import lax
from jax.experimental import pallas as pl
from jax.experimental.pallas import tpu as pltpu
from jax.sharding import PartitionSpec as P

HEADS = 12
HEAD_DIM = 64
PAIRS = HEADS // 2
BUCKETS = 32
SEQ = 512
ROWS = 2 * SEQ
D = 768
FF = 3072
TILE = 256
TILES = FF // TILE
EPS = 1e-05
NEG = -1e30
LOG2E = 1.4426950408889634
SCALE = HEAD_DIM**-0.5
FAR_STEPS = (12, 16, 23, 32, 46, 64, 91)
F32 = jnp.float32
BF16 = jnp.bfloat16
VMEM_LIMIT = 62 * 2**20

TAIL_P = 0.28
TAIL = (
    0.11608706693762069,
    0.07021928496801585,
    0.26212226118724974,
    -0.22858899246095166,
    0.3847049667747488,
    -0.10454457204169064,
)


def mm(a, b):
    return jnp.dot(a, b, preferred_element_type=F32)


def mm_nt(a, b):
    return lax.dot_general(a, b, (((1,), (1,)), ((), ())), preferred_element_type=F32)


def mm_tn(a, b):
    return lax.dot_general(a, b, (((0,), (0,)), ((), ())), preferred_element_type=F32)


def bucket_of(offset):
    distance = jnp.abs(offset)
    farther = jnp.full(distance.shape, 8, jnp.int32)
    for step_at in FAR_STEPS:
        farther = farther + jnp.where(distance >= step_at, 1, 0)
    return jnp.where(distance < 8, distance, farther) + jnp.where(offset > 0, 16, 0)


def normal_parts(x):
    size = jnp.abs(x)
    t = 1.0 / (1.0 + TAIL_P * size)
    poly = jnp.full(x.shape, TAIL[-1], F32)
    for c in TAIL[-2::-1]:
        poly = poly * t + c
    bell = jnp.exp2(x * x * (-0.5 * LOG2E))
    tail = poly * t * bell
    return jnp.where(x < 0, tail, 1.0 - tail), bell * 0.3989422804014327


def ds(start, size):
    return pl.ds(pl.multiple_of(start, size), size)


def places():
    f = lax.axis_index("fsdp")
    return lax.axis_index("rep"), f // 2, f % 2


def hop(i, k):
    if k == 0:
        return i
    if k == 1:
        return i + 1 - 2 * (i % 2)
    return (i + 2) % 4 if k == 2 else 3 - i


def remote(src, dst, send, recv, device):
    return pltpu.make_async_remote_copy(
        src_ref=src, dst_ref=dst, send_sem=send, recv_sem=recv, device_id=device, device_id_type=pl.DeviceIdType.MESH
    )


def greet(devices):
    barrier = pltpu.get_barrier_semaphore()
    for device in devices:
        pl.semaphore_signal(barrier, inc=1, device_id=device, device_id_type=pl.DeviceIdType.MESH)
    pl.semaphore_wait(barrier, len(devices))


PIECES = 3


def block_of(buffers, t, r, z, c):
    if t == 2:
        return buffers[2].at[z, pl.ds(pl.multiple_of(c * 384 + r * 96, 96), 96), :]
    return buffers[1].at[r, z, ds(c * 96, 96), :]


def quarter(u, r, c):
    rows = pl.ds(pl.multiple_of(c * 96 + (r // 2) * 48, 48), 48)
    if isinstance(u, int) and u == PIECES:
        return rows, ds((r % 2) * 384, 384)
    return rows, pl.ds(pl.multiple_of(u * 256 + (r % 2) * 128, 128), 128)


def matrices(u):
    return 3 if isinstance(u, int) and u == PIECES else slice(0, 3)


def columns(u):
    return slice(0, D) if isinstance(u, int) and u == PIECES else ds(u * 256, 256)


ALL = slice(0, 4)


class Gather:
    def __init__(self, refs, sems):
        *self.w, self.small = refs
        self.l_sem, self.zs, self.zr, self.xs, self.xr, self.cs, self.cr, self.vs, self.vr = sems
        self.r, self.z, self.c = places()

    def block(self, u, r, z, c):
        if isinstance(u, int) and u > PIECES:
            return block_of(self.w, u - PIECES, r, z, c)
        rows, cols = quarter(u, r, c)
        return self.w[0].at[matrices(u), z, rows, cols]

    def own(self, shards):
        *square, inner, outer = shards
        z, c = self.z, self.c
        rows = ds(c * 96, 96)
        copies = [
            [pltpu.make_async_copy(square[m], self.w[0].at[m, z, rows, :], self.l_sem.at[0, m]) for m in range(4)],
            [
                pltpu.make_async_copy(inner.at[:, m * D : (m + 1) * D], self.block(4, m, z, c), self.l_sem.at[1, m])
                for m in range(4)
            ],
            [pltpu.make_async_copy(outer, self.w[2].at[z, ds(c * 384, 384), :], self.l_sem.at[2, 0])],
        ]
        return copies

    def small_copy(self, k):
        f = 2 * self.z + self.c
        return remote(
            self.small.at[f], self.small.at[f], self.vs.at[k - 1], self.vr.at[k - 1], (self.r, (f + k) % 8)
        )

    def small_come(self, k):
        f = (2 * self.z + self.c + 8 - k) % 8
        return remote(self.small.at[f], self.small.at[f], self.vs.at[k - 1], self.vr.at[k - 1], (self.r, f))

    def z_half(self, u, k, m, come=False):
        q = 2 * m + (self.r % 2, self.r // 2)[m]
        ref = self.block(u, q, hop(self.z, k if come else 2 * (k == 3)), self.c)
        n = 2 * (k - 1) + m
        return remote(ref, ref, self.zs.at[u, n], self.zr.at[u, n], (self.r, 2 * hop(self.z, 1 + (k == 2)) + self.c))

    def x_half(self, u, k, m, come=False):
        side = (self.r % 2, self.r // 2)[m]
        ref = self.block(u, 2 * m + (1 - side if come else side), hop(self.z, k), self.c)
        n = 2 * (k - 1) + m
        return remote(ref, ref, self.xs.at[u, n], self.xr.at[u, n], (hop(self.r, m + 1), 2 * self.z + self.c))

    def c_inner(self, n, come=False):
        m, other = n % 2, n // 2
        side = (self.r % 2, self.r // 2)[m]
        ref = self.block(4, 2 * m + (1 - side if other else side), ALL, 1 - self.c if come else self.c)
        return remote(ref, ref, self.cs.at[4, n], self.cr.at[4, n], (self.r, 2 * self.z + 1 - self.c))

    def c_outer(self, k, come=False):
        ref = self.w[2].at[hop(self.z, k), ds((1 - self.c if come else self.c) * 384, 384), :]
        return remote(ref, ref, self.cs.at[5, k], self.cr.at[5, k], (self.r, 2 * self.z + 1 - self.c))

    def start_half(self, u):
        for k in (2, 1):
            for m in range(2):
                self.z_half(u, k, m).start()

    def pass_half(self, u, k):
        for m in range(2):
            self.z_half(u, k, m, True).wait_recv()
            if k == 2:
                self.z_half(u, 3, m).start()
            self.x_half(u, k, m).start()

    def share_inner(self, n):
        for k in (1, 2, 3) if n >= 2 else ():
            self.x_half(4, k, n % 2, True).wait_recv()
        self.c_inner(n).start()

    def finish_inner(self):
        for n in range(4):
            self.c_inner(n, True).wait_recv()

    def share_outer(self, k):
        for m in range(2 if k else 0):
            self.x_half(5, k, m, True).wait_recv()
        self.c_outer(k).start()

    def finish_outer(self, k):
        self.c_outer(k, True).wait_recv()

    def z_copy(self, u, k, come=False):
        far = hop(self.z, k)
        ref = self.block(u, self.r, far if come else self.z, self.c)
        return remote(ref, ref, self.zs.at[u, k - 1], self.zr.at[u, k - 1], (self.r, 2 * far + self.c))

    def x_copy(self, u, k, m, come=False):
        far = hop(self.r, m)
        ref = self.block(u, far if come else self.r, hop(self.z, k), self.c)
        at = 3 * (k - 1) + m - 1
        return remote(ref, ref, self.xs.at[u, at], self.xr.at[u, at], (far, 2 * self.z + self.c))

    def c_copy(self, u, come=False):
        c = 1 - self.c if come else self.c
        ref = self.w[0].at[matrices(u), ALL, ds(c * 96, 96), columns(u)]
        return remote(ref, ref, self.cs.at[u, 0], self.cr.at[u, 0], (self.r, 2 * self.z + 1 - self.c))

    def start_z(self, u):
        for k in (1, 2, 3):
            self.z_copy(u, k).start()

    def pass_on(self, u):
        for k in (1, 2, 3):
            self.z_copy(u, k, True).wait_recv()
            for m in (1, 2, 3):
                self.x_copy(u, k, m).start()

    def share(self, u):
        for m in (1, 2, 3):
            for k in (1, 2, 3):
                self.x_copy(u, k, m, True).wait_recv()
        self.c_copy(u).start()

    def finish(self, u):
        self.c_copy(u, True).wait_recv()

    def drain(self):
        for k in range(1, 8):
            self.small_copy(k).wait_send()

        def sent(u):
            for k in (1, 2, 3):
                self.z_copy(u, k).wait_send()
                for m in (1, 2, 3):
                    self.x_copy(u, k, m).wait_send()
            self.c_copy(u).wait_send()

        lax.fori_loop(0, PIECES, lambda u, carry: (sent(u), carry)[1], 0)
        sent(3)
        for k in range(4):
            self.c_inner(k).wait_send()
            self.c_outer(k).wait_send()
            for u, m in ((4, 0), (4, 1), (5, 0), (5, 1)) if k else ():
                self.z_half(u, k, m).wait_send()
                self.x_half(u, k, m).wait_send()


def unpack_small(small_s, vec_s):
    blocks = [small_s[f] for f in range(8)]
    at = lax.broadcasted_iota(jnp.int32, (128, D), 0)
    shift = jnp.where(at < 96, lax.broadcasted_iota(jnp.int32, (128, D), 1) - at, -1)
    total = None
    for f in range(8):
        part = mm(blocks[f], jnp.where(shift == 96 * f, 1.0, 0.0).astype(BF16))
        total = part if total is None else total + part
    vec_s[...] = total
    wide = [b.astype(F32) for b in blocks]
    for m in range(4):
        for j in range(6):
            vec_s[8 + m : 9 + m, j * 128 : (j + 1) * 128] = wide[2 * m + j // 3][8 + j % 3 : 9 + j % 3]
    return [w[11:12] for w in wide]


def lines_of(rows):
    bucket = jnp.broadcast_to(bucket_of(lax.broadcasted_iota(jnp.int32, (1, 1024), 1) - 512), (128, 1024))
    entry = lax.broadcasted_iota(jnp.int32, (128, 1024), 0)

    def pick(first, shift):
        inside = (entry >= first) & (entry < 48)
        return jnp.where(inside & (bucket == entry + shift), 1.0, 0.0).astype(BF16)

    table = jnp.concatenate(rows, axis=0).astype(BF16)
    a0, a1, b1, b2 = (mm(table, pick(*p)) for p in ((0, 0), (32, -32), (0, 16), (16, -16)))
    lines = []
    for m in range(4):
        i, j = 2 * m, 2 * m + 1
        lines += [a0[i : i + 1], a1[i : i + 1] + b1[j : j + 1], b2[j : j + 1]]
    return [line * LOG2E for line in lines]


def build_masks(len_ref, rank_ref, mask_s):
    n = len_ref[0]
    rank = rank_ref[...]
    place = lax.broadcasted_iota(jnp.int32, (1, SEQ), 1)
    valid = place < n
    chosen = valid & (rank >= n - 3 * n // 20)
    key = jnp.where(chosen, rank, jnp.where(valid, -1, 2 * SEQ)).astype(F32)
    column = jnp.broadcast_to(rank.astype(F32), (128, SEQ)).T
    for s in range(2):
        for j in range(SEQ // 128):
            seen = jnp.broadcast_to(key[:, j * 128 : (j + 1) * 128], (SEQ, 128)) <= column - s
            mask_s[s, :, j * 128 : (j + 1) * 128] = jnp.where(seen, 0.0, NEG)


def lines_of_table(tab_ref):
    offset = lax.broadcasted_iota(jnp.int32, (128, 1024), 1) - 512
    bucket = lax.broadcasted_iota(jnp.int32, (128, 1024), 0)
    onehot = jnp.where(bucket_of(offset) == bucket, 1.0, 0.0).astype(BF16)
    line = mm(tab_ref[...], onehot) * LOG2E
    return [line[h : h + 1] for h in range(HEADS)]


def build_strip(lines, strip_s, heads):
    for h in heads:
        line = lines[h]
        wide = jnp.broadcast_to(line[:, 256:768], (128, 512))
        strip_s[h, :, 0:256] = jnp.broadcast_to(line[:, 0:1], (128, 256))
        strip_s[h, :, 256:640] = pltpu.roll(wide, 0, 1, stride=1, stride_axis=0)[:, 128:]
        strip_s[h, :, 640:896] = jnp.broadcast_to(line[:, 1023:1024], (128, 256))


def square(w_s, m, cols=slice(None)):
    block = w_s[m, :, :, cols]
    return block.reshape(D, block.shape[-1])


def project(x_ref, y_ref, vec_ref, w_s, q_s, k_s, v_s, p):
    cols = ds(p * 256, 256)
    x = x_ref[...]
    parts = (
        (q_s, 0, mm(x, square(w_s, 0, cols)) + vec_ref[0:1, cols]),
        (q_s, 1, mm(y_ref[...], square(w_s, 0, cols)) + vec_ref[0:1, cols]),
        (k_s, None, mm(x, square(w_s, 1, cols))),
        (v_s, None, mm(x, square(w_s, 2, cols)) + vec_ref[1:2, cols]),
    )
    for ref, s, value in parts:
        value = value.astype(BF16)
        for e in range(2):
            piece = value[:, e * 128 : (e + 1) * 128]
            if s is None:
                ref[2 * p + e] = piece
            else:
                ref[s, 2 * p + e] = piece


def attend(q_s, k_s, v_s, strip_s, mask_s, p_st, ctx_s, hp, slot, ahead):
    lane = lax.broadcasted_iota(jnp.int32, (SEQ, 128), 1)
    k = k_s[hp]
    v = v_s[hp]
    for s in range(2):
        ahead(s)
        q = q_s[s, hp]
        outs = []
        for e in range(2):
            own = (lane < 64) if e == 0 else (lane >= 64)
            scores = mm_nt(jnp.where(own, q, jnp.zeros_like(q)), k)
            for i in range(SEQ // 128):
                rows = slice(i * 128, (i + 1) * 128)
                blk = (
                    scores[rows] * (SCALE * LOG2E)
                    + strip_s[2 * hp + e, :, (3 - i) * 128 : (3 - i) * 128 + SEQ]
                    + mask_s[s, rows, :]
                )
                top = jnp.max(blk, axis=1, keepdims=True)
                w = jnp.exp2(blk - top)
                w = w * (1.0 / jnp.sum(w, axis=1, keepdims=True))
                p_st[slot, e, s, rows, :] = w.astype(BF16)
            outs.append(mm(p_st[slot, e, s], v))
        ctx_s[s * SEQ : (s + 1) * SEQ, ds(hp * 128, 128)] = jnp.where(
            lane < 64, outs[0], outs[1]
        ).astype(BF16)


def norm_stats(r):
    mean = jnp.mean(r, axis=1, keepdims=True)
    centred = r - mean
    inverse = lax.rsqrt(jnp.mean(centred * centred, axis=1, keepdims=True) + EPS)
    return centred * inverse, inverse


NETWORK = {
    (0, 0): (("pass_on", 2),),
    (0, 1): (("share", 1),),
    (1, 0): (("share", 2),),
    (1, 3): (("pass_half", 4, 2), ("pass_half", 4, 1)),
    (2, 0): (("pass_on", 3), ("start_half", 5)),
}


FEED_NETWORK = {
    5: (("share_outer", 1), ("share_outer", 2)),
    7: (("pass_half", 5, 3),),
    11: (("share_outer", 3),),
}


def forward_kernel(linked, *refs):
    refs = list(refs)
    take = lambda n: [refs.pop(0) for _ in range(n)]
    x_ref, y_ref, len_ref, rank_ref = take(4)
    if linked:
        rows_ref, inner_ref, table_ref = take(3)
        shards = take(6)
    else:
        vec_ref, tab_ref, *weights = take(5)
    oc_ref, oq_ref, q_h, k_h, v_h, p_h, ctx_h, n1_h, inv1_h, nl_h, act_h, slope_h, n2_h, inv2_h = take(14)
    if linked:
        vec_h, *weights = take(4)
    wa_s, wi_s, wo_s, q_s, k_s, v_s, ctx_s, nl_s, n1_s, br_s, inv1_s, inv2_s, o_sem, st_sem, w_sem = take(15)
    copies = (wa_s, wi_s, wo_s)
    if linked:
        small_s, vec_ref, *sems = take(10)
        net = Gather((wa_s, wi_s, wo_s, small_s), (w_sem, *sems))
        r, z, c = places()
        f = 2 * z + c
        own = net.own(shards)
        for batch in own:
            for copy in batch:
                copy.start()
        vec_ref[:, 0:128] = jnp.zeros((16, 128), F32)
        vec_ref[0:8, 0:96] = rows_ref[...].astype(F32)
        vec_ref[8:11, 0:128] = inner_ref[...].astype(F32)
        vec_ref[11:12, 0:48] = table_ref[...].astype(F32)
        small_s[f] = vec_ref[:, 0:128].astype(BF16)
        greet(
            [(hop(r, m), f) for m in (1, 2, 3)] + [(r, (f + k) % 8) for k in range(1, 8)]
        )
        for k in range(1, 8):
            net.small_copy(k).start()
        for copy in own[0]:
            copy.wait()
        net.start_z(0)
        net.start_z(1)
    else:
        loads = [pltpu.make_async_copy(src, dst, w_sem.at[i, 0]) for i, (src, dst) in enumerate(zip(weights, copies))]
        for copy in loads:
            copy.start()
    stores = []

    def keep(src, dst):
        pltpu.make_async_copy(src, dst, o_sem.at[len(stores)]).start()
        stores.append((src, dst))

    def attention(strip_s, mask_s, p_st):
        build_masks(len_ref, rank_ref, mask_s)
        if linked:
            net.pass_on(0)
            net.start_z(2)
            for k in range(1, 8):
                net.small_come(k).wait_recv()
            lines = lines_of(unpack_small(small_s, vec_ref))
            net.pass_on(1)
            for copy in own[1] + own[2]:
                copy.wait()
            net.start_half(4)
            net.start_z(3)
            build_strip(lines, strip_s, range(0, 4))
            net.share(0)
            net.share_outer(0)
            build_strip(lines, strip_s, range(4, HEADS))
            keep(vec_ref, vec_h)
        else:
            build_strip(lines_of_table(tab_ref), strip_s, range(HEADS))
            loads[0].wait()

        def store(hp, slot):
            return pltpu.make_async_copy(p_st.at[slot], p_h.at[hp], st_sem.at[slot])

        def hooks(p, part):
            for (at, when), moves in NETWORK.items():
                if when == part:
                    @pl.when(p == at)
                    def _(moves=moves):
                        for name, *unit in moves:
                            getattr(net, name)(*unit)

        def step(p, carry):
            if linked:
                net.finish(p)
            project(x_ref, y_ref, vec_ref, wa_s, q_s, k_s, v_s, p)
            for part in range(2):
                @pl.when(p >= 1)
                def _():
                    store(2 * p - 2 + part, part).wait()

                def ahead(s, part=part):
                    if linked:
                        hooks(p, 2 * part + s)

                attend(q_s, k_s, v_s, strip_s, mask_s, p_st, ctx_s, 2 * p + part, part, ahead)
                store(2 * p + part, part).start()
            return carry

        lax.fori_loop(0, PIECES, step, 0)
        for part in range(2):
            store(PAIRS - 2 + part, part).wait()
        keep(q_s, q_h)
        keep(k_s, k_h)
        keep(v_s, v_h)

    pl.run_scoped(
        attention,
        pltpu.VMEM((HEADS, 128, 896), F32),
        pltpu.VMEM((2, SEQ, SEQ), F32),
        pltpu.VMEM((2, 2, 2, SEQ, SEQ), BF16),
    )
    keep(ctx_s, ctx_h)
    if linked:
        net.share(3)
        net.pass_half(4, 3)
        net.share_inner(0)
        net.share_inner(1)
        net.finish(3)
        keep(wa_s, weights[0])

    for s, in_ref in ((0, x_ref), (1, y_ref)):
        if linked and s:
            net.share_inner(2)
            net.share_inner(3)

        def first(i, carry, s=s, in_ref=in_ref):
            own = ds(i * 256, 256)
            rows = ds(s * SEQ + i * 256, 256)
            r = in_ref[own, :].astype(F32) + mm(ctx_s[rows, :], square(wa_s, 3)) + vec_ref[2:3, :]
            n, inverse = norm_stats(r)
            n1_s[rows, :] = n
            inv1_s[rows, :] = jnp.broadcast_to(inverse, (256, 128))
            nl_s[rows, :] = (n * vec_ref[3:4, :] + vec_ref[4:5, :]).astype(BF16)
            return carry

        lax.fori_loop(0, SEQ // 256, first, 0)
    keep(n1_s, n1_h)
    keep(inv1_s, inv1_h)
    keep(nl_s, nl_h)

    if linked:
        net.pass_half(5, 2)
        net.pass_half(5, 1)
        net.finish_inner()
        keep(wi_s, weights[1])
    else:
        loads[1].wait()
        loads[2].wait()

    def feed(act_s, slope_st):
        def part(t):
            return ds(t * TILE, TILE)

        def pair(t, slot):
            return (
                pltpu.make_async_copy(act_s.at[:, part(t)], act_h.at[:, part(t)], st_sem.at[slot]),
                pltpu.make_async_copy(slope_st.at[slot], slope_h.at[:, part(t)], st_sem.at[2 + slot]),
            )

        def step(t, carry):
            slot = t % 2

            @pl.when(t >= 2)
            def _():
                for c in pair(t - 2, slot):
                    c.wait()

            if linked:
                for at, moves in FEED_NETWORK.items():
                    @pl.when(t == at)
                    def _(moves=moves):
                        for name, *unit in moves:
                            getattr(net, name)(*unit)

            cols = ds((t % 3) * TILE, TILE)
            inner = mm(nl_s[...], square(wi_s, t // 3, cols)) + vec_ref[pl.ds(8 + (t // 3), 1), cols]
            spread, bell = normal_parts(inner)
            act_s[:, part(t)] = (inner * spread).astype(BF16)
            slope_st[slot] = (spread + inner * bell).astype(BF16)
            for c in pair(t, slot):
                c.start()
            return carry

        lax.fori_loop(0, TILES, step, 0)
        z = places()[1] if linked else 0
        for k in range(4):
            if linked:
                net.finish_outer(k)
            far = hop(z, k)

            def outer(i, carry, k=k, far=far):
                rows = ds(i * 512, 512)
                part = mm(act_s[rows, ds(far * D, D)], wo_s[far])
                br_s[rows, :] = part + br_s[rows, :] if k else part
                return carry

            lax.fori_loop(0, ROWS // 512, outer, 0)
        if linked:
            keep(wo_s, weights[2])
        for t in (TILES - 2, TILES - 1):
            for c in pair(t, t % 2):
                c.wait()

    pl.run_scoped(feed, pltpu.VMEM((ROWS, FF), BF16), pltpu.VMEM((2, ROWS, TILE), BF16))

    for s, o_ref in ((0, oc_ref), (1, oq_ref)):
        def last(i, carry, s=s, o_ref=o_ref):
            rows = ds(s * SEQ + i * 128, 128)
            normed = n1_s[rows, :] * vec_ref[3:4, :] + vec_ref[4:5, :]
            n, inverse = norm_stats(normed + br_s[rows, :] + vec_ref[5:6, :])
            br_s[rows, :] = n
            inv2_s[rows, :] = jnp.broadcast_to(inverse, (128, 128))
            o_ref[ds(i * 128, 128), :] = (n * vec_ref[6:7, :] + vec_ref[7:8, :]).astype(BF16)
            return carry

        lax.fori_loop(0, SEQ // 128, last, 0)
    keep(br_s, n2_h)
    keep(inv2_s, inv2_h)
    for i, (src, dst) in enumerate(stores):
        pltpu.make_async_copy(src, dst, o_sem.at[i]).wait()
    if linked:
        net.drain()


WEIGHTS = ((4, 4, 192, D), (4, 4, 192, D), (4, D, D))


def call_forward(linked, *args):
    hbm = pl.BlockSpec(memory_space=pl.ANY)
    vmem = pl.BlockSpec(memory_space=pltpu.VMEM)
    smem = pl.BlockSpec(memory_space=pltpu.SMEM)
    dma = pltpu.SemaphoreType.DMA
    shape = jax.ShapeDtypeStruct
    outs = [
        shape((SEQ, D), BF16), shape((SEQ, D), BF16),
        shape((2, PAIRS, SEQ, 128), BF16), shape((PAIRS, SEQ, 128), BF16), shape((PAIRS, SEQ, 128), BF16),
        shape((PAIRS, 2, 2, SEQ, SEQ), BF16), shape((ROWS, D), BF16),
        shape((ROWS, D), F32), shape((ROWS, 128), F32), shape((ROWS, D), BF16),
        shape((ROWS, FF), BF16), shape((ROWS, FF), BF16),
        shape((ROWS, D), F32), shape((ROWS, 128), F32),
    ]
    scratch = [pltpu.VMEM(w, BF16) for w in WEIGHTS] + [
        pltpu.VMEM((2, PAIRS, SEQ, 128), BF16), pltpu.VMEM((PAIRS, SEQ, 128), BF16), pltpu.VMEM((PAIRS, SEQ, 128), BF16),
        pltpu.VMEM((ROWS, D), BF16), pltpu.VMEM((ROWS, D), BF16), pltpu.VMEM((ROWS, D), F32), pltpu.VMEM((ROWS, D), F32),
        pltpu.VMEM((ROWS, 128), F32), pltpu.VMEM((ROWS, 128), F32),
        dma((13,)), dma((4,)), dma((3, 4)),
    ]
    in_specs = [vmem, vmem, smem, vmem]
    if linked:
        in_specs += [vmem] * 3 + [hbm] * 6
        outs += [shape((16, D), F32)] + [shape(w, BF16) for w in WEIGHTS]
        scratch += [
            pltpu.VMEM((8, 16, 128), BF16), pltpu.VMEM((16, D), F32),
            dma((6, 6)), dma((6, 6)), dma((6, 9)), dma((6, 9)), dma((6, 4)), dma((6, 4)), dma((7,)), dma((7,)),
        ]
        params = pltpu.CompilerParams(vmem_limit_bytes=VMEM_LIMIT, collective_id=1, has_side_effects=True)
    else:
        in_specs += [vmem, vmem] + [hbm] * 3
        params = pltpu.CompilerParams(vmem_limit_bytes=VMEM_LIMIT)
    return pl.pallas_call(
        functools.partial(forward_kernel, linked),
        out_shape=outs,
        in_specs=in_specs,
        out_specs=[vmem, vmem] + [hbm] * (len(outs) - 2),
        scratch_shapes=scratch,
        compiler_params=params,
        name="forward",
    )(*args)


class Reduce:
    def __init__(self, refs, sems):
        self.g, more = refs
        self.cr1, self.cr2, *more, self.res = more
        self.big, self.cut, self.out = more[:5], more[5:10], more[10:]
        self.cs, self.cr, self.credit, self.xs, self.xd, self.zs, self.zd, self.ys, self.yd, self.as_, self.ad = sems
        self.r, self.z, self.c = places()
        self.f = 2 * self.z + self.c
        self.side = (self.r % 2, self.r // 2)

    def number(self, kind, i):
        return {"in": 0, "square": 4, "piece": 5, "out": 8}[kind] + i

    def columns(self, kind, i, side):
        return pl.ds(pl.multiple_of(i * 256 + side * 128, 128), 128) if kind == "piece" else ds(side * 384, 384)

    def half(self, kind, i, m, z, give=False):
        side = 1 - self.side[m] if give else self.side[m]
        if kind == "out":
            return block_of(self.g, 2, 2 * m + side, i, self.c)
        rows = pl.ds(pl.multiple_of(self.c * 96 + m * 48, 48), 48)
        cols = self.columns(kind, i, side)
        if kind == "in":
            return self.g[1].at[i, z, rows, cols]
        return self.g[0].at[3 if kind == "square" else slice(0, 3), z, rows, cols]

    def held(self, what, kind, i, m):
        if kind == "out":
            return self.out[what].at[m, i] if what == 0 else self.out[what].at[m, i // 2] if what == 1 else self.out[what].at[m]
        return self.cut[what].at[m, i] if kind == "piece" else self.big[what].at[m, 4 if kind == "square" else i]

    def mine(self, kind, i):
        rows, cols = ds(self.c * 96, 96), ds(i * 256, 256)
        if kind == "out":
            return self.g[2].at[i, ds(self.c * 384, 384), :], self.cr2.at[i]
        if kind == "in":
            return self.g[1].at[i, :, rows, :], self.cr1.at[i]
        if kind == "square":
            return self.g[0].at[3, :, rows, :], self.cr1.at[3]
        return self.g[0].at[0:3, :, rows, cols], self.cr1.at[0:3, :, :, cols]

    def core(self, kind, i):
        rows, cols = ds((1 - self.c) * 96, 96), ds(i * 256, 256)
        if kind == "out":
            src = self.g[2].at[i, ds((1 - self.c) * 384, 384), :]
        elif kind == "in":
            src = self.g[1].at[i, :, rows, :]
        elif kind == "square":
            src = self.g[0].at[3, :, rows, :]
        else:
            src = self.g[0].at[0:3, :, rows, cols]
        n = self.number(kind, i)
        return remote(src, self.mine(kind, i)[1], self.cs.at[n], self.cr.at[n], (self.r, 2 * self.z + 1 - self.c))

    def across(self, kind, i, m):
        n = 2 * self.number(kind, i) + m
        src, dst = self.half(kind, i, m, ALL, True), self.held(0, kind, i, m)
        return remote(src, dst, self.xs.at[n], self.xd.at[n], (hop(self.r, m + 1), self.f))

    def near(self, kind, i, m, j=0):
        to, n = hop(self.z, 1), 4 * self.number(kind, i) + 2 * m + j
        src, dst = self.half(kind, i, m, hop(self.z, 3) if j else to), self.held(1, kind, i, m)
        return remote(
            src, dst if kind == "out" else dst.at[j], self.zs.at[n], self.zd.at[n], (self.r, 2 * to + self.c)
        )

    def far(self, kind, i, m):
        to = hop(self.z, 2)
        if kind == "out":
            i, n = to, 64 + m
        else:
            n = 48 + 2 * self.number(kind, i) + m
        src, dst = self.half(kind, i, m, to), self.held(2, kind, i, m)
        return remote(src, dst, self.zs.at[n], self.zd.at[n], (self.r, 2 * to + self.c))

    def complete(self, kind, i, m):
        n = 2 * (8 if kind == "out" else self.number(kind, i)) + m
        src, dst = self.held(3, kind, i, m), self.held(4, kind, i, m)
        return remote(src, dst, self.ys.at[n], self.yd.at[n], (hop(self.r, 2 - m), self.f))

    def result(self, kind, i, m, give=False):
        side = 1 - self.side[m] if give else self.side[m]
        if kind == "out":
            return self.res.at[2, 2 * m + side]
        rows, cols = slice(m * 48, (m + 1) * 48), self.columns(kind, i, side)
        if kind == "in":
            return self.res.at[1, i, rows, cols]
        return self.res.at[0, 3 if kind == "square" else slice(0, 3), rows, cols]

    def spread(self, kind, i, m, come=False):
        n = 2 * (8 if kind == "out" else self.number(kind, i)) + m
        ref = self.result(kind, i, m, come)
        return remote(ref, ref, self.as_.at[n], self.ad.at[n], (hop(self.r, m + 1), self.f))

    def start(self, kind, i=0):
        self.core(kind, i).start()

    def cores(self, kind, i=0):
        self.core(kind, i).wait_recv()
        ref, come = self.mine(kind, i)
        ref[...] = ref[...] + come[...]
        for m in range(2):
            self.across(kind, i, m).start()

    def allow(self):
        pl.semaphore_signal(
            self.credit, inc=1, device_id=(self.r, 2 * self.z + 1 - self.c), device_id_type=pl.DeviceIdType.MESH
        )

    def replicas(self, kind, i=0):
        for m in range(2):
            self.across(kind, i, m).wait_recv()
            ref = self.half(kind, i, m, ALL)
            ref[...] = ref[...] + self.held(0, kind, i, m)[...]
            if kind == "out":
                @pl.when((self.z + i) % 2 == 1)
                def _(m=m):
                    self.near(kind, i, m).start()
            else:
                for j in range(2):
                    self.near(kind, i, m, j).start()

    def pairs(self, kind, i=0):
        if kind == "out":
            @pl.when((self.z + i) % 2 == 0)
            def _():
                for m in range(2):
                    self.near(kind, i, m).wait_recv()
                    ref = self.half(kind, i, m, None)
                    ref[...] = ref[...] + self.held(1, kind, i, m)[...]

                    @pl.when(self.z != i)
                    def _(m=m):
                        self.far(kind, i, m).start()
            return
        for m in range(2):
            for j in (1, 0):
                self.near(kind, i, m, j).wait_recv()
                ref = self.half(kind, i, m, hop(self.z, 2 * j))
                ref[...] = ref[...] + self.held(1, kind, i, m).at[j][...]
                if j:
                    self.far(kind, i, m).start()

    def owners(self, kind, i=0):
        for m in range(2):
            self.far(kind, i, m).wait_recv()
            total = self.half(kind, self.z if kind == "out" else i, m, self.z)[...].astype(F32)
            total = total + self.held(2, kind, i, m)[...].astype(F32)
            self.held(3, kind, i, m)[...] = total.astype(BF16)
            self.complete(kind, i, m).start()

    def ends(self, kind, i=0):
        for m in range(2):
            self.complete(kind, i, m).wait_recv()
            total = self.held(3, kind, i, m)[...].astype(F32) + self.held(4, kind, i, m)[...].astype(F32)
            self.result(kind, i, m)[...] = total.astype(BF16)
            self.spread(kind, i, m).start()

    def finish(self, kind, i=0):
        for m in range(2):
            self.spread(kind, i, m, True).wait_recv()

    def drain(self):
        def sent(kind, i):
            self.core(kind, i).wait_send()
            for m in range(2):
                self.across(kind, i, m).wait_send()
                if kind != "out":
                    for j in range(2):
                        self.near(kind, i, m, j).wait_send()
                    self.far(kind, i, m).wait_send()
                    self.complete(kind, i, m).wait_send()
                    self.spread(kind, i, m).wait_send()

        def several(kind, count):
            lax.fori_loop(0, count, lambda i, carry: (sent(kind, i), carry)[1], 0)

        several("in", 4)
        several("out", 4)
        several("piece", PIECES)
        sent("square", 0)
        for m in range(2):
            for i in (hop(self.z, 1), hop(self.z, 3)):
                self.near("out", i, m).wait_send()
            self.far("out", 0, m).wait_send()
            self.complete("out", 0, m).wait_send()
            self.spread("out", 0, m).wait_send()


class SmallReduce:
    def __init__(self, refs, sems):
        self.out, self.got, self.sums = refs
        self.vs, self.vd, self.ws, self.wd = sems
        self.r, z, c = places()
        self.f = 2 * z + c

    def first(self, k):
        to = (self.f + k) % 8
        return remote(self.out.at[to], self.got.at[self.f], self.vs.at[k - 1], self.vd.at[k - 1], (self.r, to))

    def first_come(self, k):
        back = (self.f + 8 - k) % 8
        return remote(self.out.at[back], self.got.at[back], self.vs.at[k - 1], self.vd.at[k - 1], (self.r, back))

    def second(self, m, come=False):
        far = hop(self.r, m)
        ref = self.sums.at[far if come else self.r]
        return remote(ref, ref, self.ws.at[m - 1], self.wd.at[m - 1], (far, self.f))

    def start(self, vec, table):
        pack_small(vec, table, self.out)
        self.got[self.f] = self.out[self.f]
        for k in range(1, 8):
            self.first(k).start()

    def middle(self):
        for k in range(1, 8):
            self.first_come(k).wait_recv()
        total = self.got[0]
        for f in range(1, 8):
            total = total + self.got[f]
        self.sums[self.r] = total
        for m in (1, 2, 3):
            self.second(m).start()

    def finish(self):
        for m in (1, 2, 3):
            self.second(m, True).wait_recv()
        total = self.sums[0]
        for r in range(1, 4):
            total = total + self.sums[r]
        return total

    def drain(self):
        for k in range(1, 8):
            self.first(k).wait_send()
        for m in (1, 2, 3):
            self.second(m).wait_send()


def pack_small(vec_ref, table, out_ref):
    vec = vec_ref[...]
    at = lax.broadcasted_iota(jnp.int32, (D, 128), 1)
    shift = jnp.where(at < 96, lax.broadcasted_iota(jnp.int32, (D, 128), 0) - at, -1)
    lane = lax.broadcasted_iota(jnp.int32, (1, 128), 1)
    for f in range(8):
        m = f // 2
        out_ref[f, 0:8, :] = lax.dot_general(
            vec[0:8], jnp.where(shift == 96 * f, 1.0, 0.0), (((1,), (0,)), ((), ())),
            precision=lax.Precision.HIGHEST, preferred_element_type=F32,
        )
        for j in range(3):
            col = (f % 2) * 384 + j * 128
            out_ref[f, 8 + j : 9 + j, :] = vec[8 + m : 9 + m, col : col + 128]
        head = 3 * m + f % 2
        a, b = table[head : head + 1], table[head + 1 : head + 2]
        if f % 2 == 0:
            line = jnp.where(lane < 32, a, jnp.where(lane < 48, pltpu.roll(b, 32, 1), 0.0))
        else:
            line = jnp.where(lane < 16, pltpu.roll(a, 112, 1), jnp.where(lane < 48, pltpu.roll(b, 16, 1), 0.0))
        out_ref[f, 11:12, :] = line
        out_ref[f, 12:16, :] = jnp.zeros((4, 128), F32)


def norm_grad(u, gain, n, inverse):
    ug = u * gain
    return inverse * (
        ug - jnp.mean(ug, axis=1, keepdims=True) - n * jnp.mean(ug * n, axis=1, keepdims=True)
    )


BACK_NETWORK = {
    (0, 0): (("replicas", "out", 3), ("replicas", "in", 3), ),
    (0, 1): (("pairs", "out", 2), ("pairs", "in", 2), ("replicas", "square"), ),
    (1, 1): (("cores", "piece", 0), ),
    (2, 0): (("replicas", "piece", 0), ("pairs", "out", 3), ("pairs", "in", 3), ("pairs", "square"), ("owners", "in", 0), ("owners", "in", 1), ),
    (2, 1): (("cores", "piece", 1), ),
}

LAST_NETWORK = (
    (("cores", "piece", 2), ),
    (("replicas", "piece", 1), ("pairs", "piece", 0), ("owners", "out"), ("owners", "in", 2), ),
    (("replicas", "piece", 2), ("owners", "square"), ("ends", "in", 0), ("ends", "in", 1), ),
    (("pairs", "piece", 1), ("owners", "in", 3), ("ends", "out"), ("ends", "in", 2), ("sum_middle",), ),
    (("pairs", "piece", 2), ("owners", "piece", 0), ("ends", "square"), ("ends", "in", 3), ),
    (("owners", "piece", 1), ("ends", "piece", 0), ("owners", "piece", 2), ("ends", "piece", 1), ("ends", "piece", 2), ),
)


def backward_kernel(linked, *refs):
    refs = list(refs)
    take = lambda n: [refs.pop(0) for _ in range(n)]
    x_h, y_h, cc_h, cq_h, vec_ref, wa_h, wi_h, wo_h = take(8)
    q_h, k_h, v_h, p_h, ctx_h, n1_h, inv1_h, nl_h, act_h, slope_h, n2_h, inv2_h = take(12)
    gc_h, gq_h = take(2)
    if linked:
        res_ref, small_ref = take(2)
    else:
        *grads_h, gvec_ref, gtab_ref = take(5)
    ctx_s, g_s, dctx_s, tr_s, l_sem, t_sem = take(6)
    ga_s, gi_s, go_s = grads = take(3)
    if linked:
        gvec_ref, *more = take(19)
        sum_refs = take(3)
        sems = take(11)
        sum_sems = take(4)
        net = Reduce((grads, more), sems)
        sums = SmallReduce(sum_refs, sum_sems)
        r, z, c = places()
        f = 2 * z + c
        res_s = more[-1]
    cload = pltpu.make_async_copy(ctx_h, ctx_s, l_sem.at[1])
    cload.start()
    gvec_ref[...] = jnp.zeros_like(gvec_ref)

    def add_vec(row, value, cols=slice(None)):
        gvec_ref[row : row + 1, cols] += jnp.sum(value, axis=0, keepdims=True)

    def tail(n_s, inv_s, nl_s, db_s, act_s, slope_s, wi_s, wo_s, cot_s, wt_s):
        wload = pltpu.make_async_copy(wa_h.at[3], wt_s, l_sem.at[0])
        wload.start()
        nload = pltpu.make_async_copy(n2_h, n_s, l_sem.at[2])
        iload = pltpu.make_async_copy(inv2_h, inv_s, l_sem.at[3])
        nlload = pltpu.make_async_copy(nl_h, nl_s, l_sem.at[4])
        cots = [pltpu.make_async_copy(ref, cot_s.at[s], l_sem.at[5 + s]) for s, ref in enumerate((cc_h, cq_h))]
        for copy in (nload, iload, *cots, nlload):
            copy.start()

        def fetch(t, slot):
            return (
                pltpu.make_async_copy(act_h.at[:, ds(t * TILE, TILE)], act_s.at[slot], t_sem.at[slot]),
                pltpu.make_async_copy(slope_h.at[:, ds(t * TILE, TILE)], slope_s.at[slot], t_sem.at[2 + slot]),
                pltpu.make_async_copy(wi_h.at[t // 3, :, :, ds((t % 3) * TILE, TILE)], wi_s.at[slot], t_sem.at[4 + slot]),
                pltpu.make_async_copy(wo_h.at[t // 3, ds((t % 3) * TILE, TILE), :], wo_s.at[slot], t_sem.at[6 + slot]),
            )

        for copy in fetch(0, 0):
            copy.start()
        if linked:
            greet([(hop(r, m), f) for m in (1, 2, 3)] + [(r, (f + k) % 8) for k in range(1, 8)])
        for copy in (nload, iload, *cots):
            copy.wait()

        def second(i, carry):
            rows = ds(i * 128, 128)
            u = cot_s[i // 4, ds((i % 4) * 128, 128), :].astype(F32)
            n = n_s[rows, :]
            g = norm_grad(u, vec_ref[6:7, :], n, inv_s[rows, 0:1])
            add_vec(6, u * n)
            add_vec(7, u)
            g_s[rows, :] = g
            low = g.astype(BF16)
            db_s[rows, :] = low
            add_vec(5, low.astype(F32))
            return carry

        lax.fori_loop(0, ROWS // 128, second, 0)
        n1load = pltpu.make_async_copy(n1_h, n_s, l_sem.at[2])
        i1load = pltpu.make_async_copy(inv1_h, inv_s, l_sem.at[3])
        n1load.start()
        i1load.start()
        nlload.wait()
        tr_s[...] = nl_s[...].T
        xyloads = [
            pltpu.make_async_copy(ref, nl_s.at[s * SEQ : (s + 1) * SEQ, :], l_sem.at[5 + s])
            for s, ref in enumerate((x_h, y_h))
        ]
        for copy in xyloads:
            copy.start()

        def step(t, carry):
            slot = t % 2
            for copy in fetch(t, slot):
                copy.wait()

            @pl.when(t + 1 < TILES)
            def _():
                for copy in fetch(t + 1, 1 - slot):
                    copy.start()

            if linked:
                @pl.when((t % 3 == 1) & (t >= 4))
                def _():
                    for kind in ("out", "in"):
                        net.cores(kind, t // 3 - 1)

                @pl.when((t % 3 == 1) & (t >= 7))
                def _():
                    for kind in ("out", "in"):
                        net.replicas(kind, t // 3 - 2)

                @pl.when(t == 11)
                def _():
                    for kind in ("out", "in"):
                        net.pairs(kind, 0)

            db = db_s[...]
            di = (mm_nt(db, wo_s[slot]) * slope_s[slot].astype(F32)).astype(BF16)
            i, part = t // 3, ds((t % 3) * TILE, TILE)
            mine = lax.broadcasted_iota(jnp.int32, (8, TILE), 0) == i
            gvec_ref[8:16, part] += jnp.where(mine, jnp.sum(di.astype(F32), axis=0, keepdims=True), 0.0)
            go_s[i, part, :] = mm_tn(act_s[slot], db).astype(BF16)
            gi_s[i, :, :, part] = mm(tr_s[...], di).astype(BF16).reshape(4, 192, TILE)
            g_s[...] += mm_nt(di, wi_s[slot].reshape(D, TILE))
            if linked:
                @pl.when(t % 3 == 2)
                def _():
                    net.start("out", i)
                    net.start("in", i)

            return carry

        lax.fori_loop(0, TILES, step, 0)
        n1load.wait()
        i1load.wait()

        def first(i, carry):
            rows = ds(i * 128, 128)
            u = g_s[rows, :]
            n = n_s[rows, :]
            g = norm_grad(u, vec_ref[3:4, :], n, inv_s[rows, 0:1])
            add_vec(3, u * n)
            add_vec(4, u)
            g_s[rows, :] = g
            low = g.astype(BF16)
            db_s[rows, :] = low
            add_vec(2, low.astype(F32))
            return carry

        lax.fori_loop(0, ROWS // 128, first, 0)
        wload.wait()
        cload.wait()
        if linked:
            for kind in ("out", "in"):
                net.cores(kind, 3)
            net.allow()
            for kind in ("out", "in"):
                net.replicas(kind, 2)
        tr_s[...] = ctx_s[...].T

        def square_grad(j, carry):
            ga_s[3, j] = mm(tr_s[pl.ds(pl.multiple_of(j * 192, 192), 192), :], db_s[...]).astype(BF16)
            return carry

        lax.fori_loop(0, 4, square_grad, 0)
        if linked:
            pl.semaphore_wait(net.credit, 1)
            net.start("square")
        for j in range(4):
            dctx_s[j * 256 : (j + 1) * 256, :] = mm_nt(db_s[j * 256 : (j + 1) * 256, :], wt_s[...].reshape(D, D)).astype(BF16)
        if linked:
            for kind in ("out", "in"):
                net.pairs(kind, 1)
            net.cores("square")
        for copy in xyloads:
            copy.wait()
        tr_s[...] = nl_s[...].T

    pl.run_scoped(
        tail,
        pltpu.VMEM((ROWS, D), F32),
        pltpu.VMEM((ROWS, 128), F32),
        pltpu.VMEM((ROWS, D), BF16),
        pltpu.VMEM((ROWS, D), BF16),
        pltpu.VMEM((2, ROWS, TILE), BF16),
        pltpu.VMEM((2, ROWS, TILE), BF16),
        pltpu.VMEM((2, 4, 192, TILE), BF16),
        pltpu.VMEM((2, TILE, D), BF16),
        pltpu.VMEM((2, SEQ, D), BF16),
        pltpu.VMEM(WEIGHTS[0][1:], BF16),
    )

    def attention(q_s, k_s, v_s, p_s, dq_s, dk_s, dv_s, dkt_s, dvt_s, far_s, bt_s, wa_s):
        wload = pltpu.make_async_copy(wa_h.at[0:3], wa_s, l_sem.at[0])
        wload.start()
        loads = [(q_h, q_s), (k_h, k_s), (v_h, v_s)]
        loads = [pltpu.make_async_copy(a, b, l_sem.at[2 + i]) for i, (a, b) in enumerate(loads)]
        for copy in loads:
            copy.start()

        def fetch(hp, slot):
            return pltpu.make_async_copy(p_h.at[hp], p_s.at[slot], t_sem.at[slot])

        fetch(0, 0).start()
        for copy in loads:
            copy.wait()

        def hooks(p, part):
            for (at, when), moves in BACK_NETWORK.items():
                if when == part:
                    @pl.when(p == at)
                    def _(moves=moves):
                        for name, *unit in moves:
                            getattr(net, name)(*unit)

        def step(p, carry):
            for part in range(2):
                hp = 2 * p + part
                if part == 0:
                    fetch(hp + 1, 1).start()
                else:
                    @pl.when(p + 1 < PIECES)
                    def _():
                        fetch(hp + 1, 0).start()

                if linked:
                    hooks(p, part)
                fetch(hp, part).wait()
                attend_back(hp, part)
            cols = ds(p * 256, 256)
            dk_s[:, cols] = dkt_s[cols, :].T
            dv_s[:, cols] = dvt_s[cols, :].T
            for w, left, grad in ((1, slice(0, SEQ), dk_s), (2, slice(0, SEQ), dv_s), (0, slice(0, ROWS), dq_s)):
                ga_s[w, :, :, cols] = mm(tr_s[:, left], grad[:, cols]).astype(BF16).reshape(4, 192, 256)
            if linked:
                net.start("piece", p)
            return carry

        def attend_back(hp, slot):
            lane = lax.broadcasted_iota(jnp.int32, (SEQ, 128), 1)
            k, v = k_s[hp], v_s[hp]
            zero = jnp.zeros((SEQ, 128), BF16)
            dq = [None, None]
            qt = [q_s[s, hp].T for s in range(2)]
            dt = [dctx_s[s * SEQ : (s + 1) * SEQ, ds(hp * 128, 128)].T for s in range(2)]
            for e in range(2):
                own = (lane < 64) if e == 0 else (lane >= 64)
                both = None
                dkt = dvt = None
                for s in range(2):
                    rows = slice(s * SEQ, (s + 1) * SEQ)
                    do = jnp.where(own, dctx_s[rows, ds(hp * 128, 128)], zero)
                    weight = jnp.sum(do.astype(F32) * ctx_s[rows, ds(hp * 128, 128)].astype(F32), axis=1, keepdims=True)
                    p = p_s[slot, e, s]
                    g = p.astype(F32) * (mm_nt(do, v) - weight)
                    low = g.astype(BF16)
                    both = g if both is None else both + g
                    part = mm(low, jnp.where(own, k, zero))
                    dq[s] = part if dq[s] is None else dq[s] + part
                    half = slice(e * 64, (e + 1) * 64)
                    a = mm(dt[s][half], p)
                    b = mm(qt[s][half], low)
                    dvt = a if dvt is None else dvt + a
                    dkt = b if dkt is None else dkt + b
                dvt_s[ds(hp * 128 + e * 64, 64), :] = dvt.astype(BF16)
                dkt_s[ds(hp * 128 + e * 64, 64), :] = (dkt * SCALE).astype(BF16)
                parts = [None] * 5
                for i in range(4):
                    for j in range(4):
                        blk = both[i * 128 : (i + 1) * 128, j * 128 : (j + 1) * 128]
                        at = min(max(j - i, -2), 2) + 2
                        parts[at] = blk if parts[at] is None else parts[at] + blk
                strip = jnp.concatenate([jnp.zeros((128, 128), F32), parts[1], parts[2], parts[3]], axis=1)
                flat = strip[0:8]
                for g in range(1, 16):
                    flat = flat + pltpu.roll(strip[8 * g : 8 * g + 8], 512 - 8 * g, 1)
                row = lax.broadcasted_iota(jnp.int32, (8, 512), 0)
                for bit in (1, 2, 4):
                    flat = jnp.where((row & bit) != 0, pltpu.roll(flat, 512 - bit, 1), flat)
                h = 2 * hp + e
                for ref, cols, value in (
                    (bt_s, slice(0, 512), flat),
                    (far_s, slice(0, 128), parts[0]),
                    (far_s, slice(128, 256), parts[4]),
                ):
                    line = jnp.sum(value, axis=0, keepdims=True)
                    mine = lax.broadcasted_iota(jnp.int32, (16, line.shape[1]), 0) == h
                    ref[:, cols] = jnp.where(mine, line, ref[:, cols])
            for s in range(2):
                dq_s[s * SEQ : (s + 1) * SEQ, ds(hp * 128, 128)] = (dq[s] * SCALE).astype(BF16)

        bt_s[...] = jnp.zeros_like(bt_s)
        far_s[...] = jnp.zeros_like(far_s)
        lax.fori_loop(0, PIECES, step, 0)

        offset = lax.broadcasted_iota(jnp.int32, (512, 128), 0) - 256
        bucket = lax.broadcasted_iota(jnp.int32, (512, 128), 1)
        near = jnp.where(bucket_of(offset) == bucket, 1.0, 0.0)
        lane = lax.broadcasted_iota(jnp.int32, (16, 128), 1)
        table = (
            lax.dot_general(bt_s[...], near, (((1,), (0,)), ((), ())), precision=lax.Precision.HIGHEST, preferred_element_type=F32)
            + jnp.where(lane == 15, jnp.sum(far_s[:, 0:128], axis=1, keepdims=True), 0.0)
            + jnp.where(lane == 31, jnp.sum(far_s[:, 128:256], axis=1, keepdims=True), 0.0)
        )
        add_vec(0, dq_s[...].astype(F32))
        add_vec(1, dv_s[...].astype(F32))
        def run(names):
            if linked:
                for name, *args in names:
                    (getattr(sums, name[4:]) if name.startswith("sum_") else getattr(net, name))(*args)

        run(LAST_NETWORK[0])
        if linked:
            sums.start(gvec_ref, table)
        else:
            gtab_ref[...] = table

        wload.wait()
        run(LAST_NETWORK[1])
        g_s[0:SEQ, :] += mm_nt(dq_s[0:SEQ, :], square(wa_s, 0))
        run(LAST_NETWORK[2])
        g_s[0:SEQ, :] += mm_nt(dk_s[...], square(wa_s, 1))
        run(LAST_NETWORK[3])
        g_s[0:SEQ, :] += mm_nt(dv_s[...], square(wa_s, 2))
        run(LAST_NETWORK[4])
        g_s[SEQ:, :] += mm_nt(dq_s[SEQ:, :], square(wa_s, 0))
        outs = [
            pltpu.make_async_copy(g_s.at[s * SEQ : (s + 1) * SEQ, :], ref, l_sem.at[2 + s])
            for s, ref in enumerate((gc_h, gq_h))
        ]
        for copy in outs:
            copy.start()
        run(LAST_NETWORK[5])
        if linked:
            net.finish("out")
            for i in range(4):
                net.finish("in", i)
            small_ref[...] = sums.finish()
            res_ref[1] = res_s[1]
            res_ref[2] = res_s[2]
            net.finish("square")
            for i in range(PIECES):
                net.finish("piece", i)
            res_ref[0] = res_s[0]
            net.drain()
            sums.drain()
        else:
            writes = [pltpu.make_async_copy(a, b, t_sem.at[i]) for i, (a, b) in enumerate(zip(grads, grads_h))]
            for copy in writes:
                copy.start()
            for copy in writes:
                copy.wait()
        for copy in outs:
            copy.wait()

    pl.run_scoped(
        attention,
        pltpu.VMEM((2, PAIRS, SEQ, 128), BF16),
        pltpu.VMEM((PAIRS, SEQ, 128), BF16),
        pltpu.VMEM((PAIRS, SEQ, 128), BF16),
        pltpu.VMEM((2, 2, 2, SEQ, SEQ), BF16),
        pltpu.VMEM((ROWS, D), BF16),
        pltpu.VMEM((SEQ, D), BF16),
        pltpu.VMEM((SEQ, D), BF16),
        pltpu.VMEM((D, SEQ), BF16),
        pltpu.VMEM((D, SEQ), BF16),
        pltpu.VMEM((16, 256), F32),
        pltpu.VMEM((16, 512), F32),
        pltpu.VMEM((3, *WEIGHTS[0][1:]), BF16),
    )


def call_backward(linked, x, y, cc, cq, vecs, wa, wi, wo, saved):
    hbm = pl.BlockSpec(memory_space=pl.ANY)
    vmem = pl.BlockSpec(memory_space=pltpu.VMEM)
    dma = pltpu.SemaphoreType.DMA
    shape = jax.ShapeDtypeStruct
    outs = [shape((SEQ, D), F32), shape((SEQ, D), F32)]
    out_specs = [hbm, hbm]
    scratch = [
        pltpu.VMEM((ROWS, D), BF16), pltpu.VMEM((ROWS, D), F32), pltpu.VMEM((ROWS, D), BF16),
        pltpu.VMEM((D, ROWS), BF16), dma((7,)), dma((8,)),
    ] + [pltpu.VMEM(w, BF16) for w in WEIGHTS]
    if linked:
        outs += [shape((3, 4, 96, D), BF16), shape((16, 128), F32)]
        out_specs += [vmem, vmem]
        scratch += [pltpu.VMEM((16, D), F32)] + [
            pltpu.VMEM(s, BF16)
            for s in (
                (4, 4, 96, D), (4, 384, D),
                (2, 5, 4, 48, 384), (2, 5, 2, 48, 384), (2, 5, 48, 384), (2, 5, 48, 384), (2, 5, 48, 384),
                (2, 3, 3, 4, 48, 128), (2, 3, 2, 3, 48, 128), (2, 3, 3, 48, 128), (2, 3, 3, 48, 128), (2, 3, 3, 48, 128),
                (2, 4, 96, D), (2, 2, 96, D), (2, 96, D), (2, 96, D), (2, 96, D),
                (3, 4, 96, D),
            )
        ]
        scratch += [pltpu.VMEM((n, 16, 128), F32) for n in (8, 8, 4)]
        scratch += [
            dma((12,)), dma((12,)), pltpu.SemaphoreType.REGULAR, dma((24,)), dma((24,)), dma((66,)), dma((66,)),
            dma((18,)), dma((18,)), dma((18,)), dma((18,)), dma((7,)), dma((7,)), dma((3,)), dma((3,)),
        ]
        params = pltpu.CompilerParams(vmem_limit_bytes=VMEM_LIMIT, collective_id=2, has_side_effects=True)
    else:
        outs += [shape(w, BF16) for w in WEIGHTS] + [shape((16, D), F32), shape((16, 128), F32)]
        out_specs += [hbm] * 3 + [vmem, vmem]
        params = pltpu.CompilerParams(vmem_limit_bytes=VMEM_LIMIT)
    return pl.pallas_call(
        functools.partial(backward_kernel, linked),
        out_shape=outs,
        in_specs=[hbm] * 4 + [vmem] + [hbm] * 15,
        out_specs=out_specs,
        scratch_shapes=scratch,
        compiler_params=params,
        name="backward",
    )(x, y, cc, cq, vecs, wa, wi, wo, *saved)


def finish_kernel(oc_h, oq_h, gc_h, gq_h, res_h, small_ref, oc_o, oq_o, gc_o, gq_o, *rest):
    *weights, low_s, high_s, res_s, square_s, inner_s, outer_s, in_sem, out_sem = rest
    weights, vectors = weights[:6], weights[6:]
    held = [square_s.at[q] for q in range(4)] + [inner_s, outer_s]
    grads = [pltpu.make_async_copy(res_h.at[t], res_s.at[t], in_sem.at[8 + t]) for t in (2, 1, 0)]
    moves = []
    for i, (src, dst) in enumerate(((gc_h, gc_o), (gq_h, gq_o), (oc_h, oc_o), (oq_h, oq_o))):
        room = (high_s if i < 2 else low_s).at[i % 2]
        for part in range(2):
            rows = slice(part * SEQ // 2, (part + 1) * SEQ // 2)
            n = len(moves)
            moves.append((
                pltpu.make_async_copy(src.at[rows, :], room.at[rows, :], in_sem.at[n]),
                pltpu.make_async_copy(room.at[rows, :], dst.at[rows, :], out_sem.at[n]),
            ))
    for copy in grads:
        copy.start()
    for move, _ in moves:
        move.start()
    writes = [pltpu.make_async_copy(src, dst, out_sem.at[8 + i]) for i, (src, dst) in enumerate(zip(held, weights))]
    small = small_ref[...]
    for i in range(8):
        vectors[i][...] = small[i, :96]
    for j in range(3):
        vectors[8][j * 128 : (j + 1) * 128] = small[8 + j]
    vectors[9][...] = small[11, :48]
    grads[0].wait()
    for q in range(4):
        outer_s[q * 96 : (q + 1) * 96, :] = res_s[2, q].astype(F32)
    writes[5].start()
    grads[1].wait()
    for q in range(4):
        inner_s[:, q * D : (q + 1) * D] = res_s[1, q].astype(F32)
    writes[4].start()
    grads[2].wait()
    for q in range(4):
        square_s[q] = res_s[0, q].astype(F32)
        writes[q].start()
    for move, onward in moves:
        move.wait()
        onward.start()
    for _, onward in moves:
        onward.wait()
    for copy in writes:
        copy.wait()


def call_finish(oc, oq, gc, gq, res, small):
    hbm = pl.BlockSpec(memory_space=pl.ANY)
    vmem = pl.BlockSpec(memory_space=pltpu.VMEM)
    shape = jax.ShapeDtypeStruct
    outs = [shape(a.shape, a.dtype) for a in (oc, oq, gc, gq)] + [shape((96, D), F32)] * 4
    outs += [shape((96, FF), F32), shape((384, D), F32)]
    outs += [shape((96,), F32)] * 8 + [shape((384,), F32), shape((48,), F32)]
    return pl.pallas_call(
        finish_kernel,
        out_shape=outs,
        in_specs=[hbm] * 5 + [vmem],
        out_specs=[hbm] * 10 + [vmem] * 10,
        scratch_shapes=[
            pltpu.VMEM((2, SEQ, D), BF16), pltpu.VMEM((2, SEQ, D), F32), pltpu.VMEM((3, 4, 96, D), BF16),
            pltpu.VMEM((4, 96, D), F32), pltpu.VMEM((96, FF), F32), pltpu.VMEM((384, D), F32),
            pltpu.SemaphoreType.DMA((11,)), pltpu.SemaphoreType.DMA((14,)),
        ],
        compiler_params=pltpu.CompilerParams(vmem_limit_bytes=VMEM_LIMIT),
        name="finish",
    )(oc, oq, gc, gq, res, small)


def shards(
    content_stream, query_stream, lengths, ranking, query_weight, query_bias, key_weight, value_weight, value_bias,
    output_weight, output_bias, norm_gain, norm_shift, inner_weight, inner_bias, outer_weight, outer_bias, final_gain,
    final_shift, bucket_bias, content_cotangent, query_cotangent,
):
    small = (query_bias, value_bias, output_bias, norm_gain, norm_shift, outer_bias, final_gain, final_shift)
    width = query_bias.shape[0]
    linked = width * 8 == D and lax.axis_size("rep") == 4
    front = (content_stream, query_stream, lengths, ranking)
    if linked:
        packed = (jnp.stack(small), inner_bias.reshape(3, 128), bucket_bias.reshape(1, -1))
        out_c, out_q, *saved, vecs, wa, wi, wo = call_forward(
            True, *front, *packed, query_weight, key_weight, value_weight, output_weight, inner_weight, outer_weight
        )
    else:
        def gather(a, axis=0):
            return lax.all_gather(a, "fsdp", axis=axis, tiled=True)

        wa = gather(jnp.stack([query_weight, key_weight, value_weight, output_weight]), 1).reshape(WEIGHTS[0])
        wi = gather(inner_weight).reshape(D, 4, D).transpose(1, 0, 2).reshape(WEIGHTS[1])
        wo = gather(outer_weight).reshape(WEIGHTS[2])
        packed = gather(jnp.concatenate([*small, inner_bias, bucket_bias])[None, :])
        cuts = [packed[:, i * width : (i + 1) * width].reshape(1, D) for i in range(8)]
        cuts.append(packed[:, 8 * width : 12 * width].reshape(4, D))
        vecs = jnp.concatenate(cuts + [jnp.zeros((4, D), BF16)]).astype(F32)
        table = jnp.pad(packed[:, 12 * width :].reshape(HEADS, BUCKETS), ((0, 4), (0, 128 - BUCKETS)))
        out_c, out_q, *saved = call_forward(False, *front, vecs, table, wa, wi, wo)
    streams = (content_stream, query_stream, content_cotangent, query_cotangent)
    gc, gq, *grads = call_backward(linked, *streams, vecs, wa, wi, wo, saved)
    if linked:
        out_c, out_q, gc, gq, *rest = call_finish(out_c, out_q, gc, gq, *grads)
        ga, gi, go, v, inner, table = rest[:4], rest[4], rest[5], rest[6:14], rest[14], rest[15]
    else:
        def reduce(a, axis=0):
            a = lax.psum_scatter(a, "fsdp", scatter_dimension=axis, tiled=True)
            return lax.psum(a.astype(BF16), "rep").astype(F32)

        ga, gi, go, gvec, gtab = grads
        ga = reduce(ga.reshape(4, D, D), 1)
        gi = reduce(gi.reshape(4, D, D).transpose(1, 0, 2).reshape(D, FF))
        go = reduce(go.reshape(FF, D))
        count = D // width
        flat = jnp.concatenate(
            [gvec[i].reshape(count, width) for i in range(8)]
            + [gvec[8:12].reshape(count, 4 * width), gtab[:HEADS, :BUCKETS].reshape(count, -1)],
            axis=1,
        )
        flat = lax.psum_scatter(flat, "fsdp", scatter_dimension=0, tiled=True)[0]
        flat = lax.psum(flat.astype(BF16), "rep").astype(F32)
        v = [flat[i * width : (i + 1) * width] for i in range(8)]
        inner, table = flat[8 * width : 12 * width], flat[12 * width :]
    return (
        out_c, out_q, gc, gq, ga[0], v[0], ga[1], ga[2], v[1], ga[3], v[2], v[3], v[4], gi,
        inner, go, v[5], v[6], v[7], table,
    )


def solution(mesh):
    both, fsdp = ("rep", "fsdp"), "fsdp"
    row, vec = P(fsdp, None), P(fsdp)
    tokens = P(both, None)
    in_specs = (
        tokens, tokens, P(both), tokens, row, vec, row, row, vec, row, vec, vec, vec, row, vec, row, vec, vec, vec, vec,
        tokens, tokens,
    )
    out_specs = (
        tokens, tokens, tokens, tokens, row, vec, row, row, vec, row, vec, vec, vec, row, vec, row, vec, vec, vec, vec,
    )
    return jax.shard_map(shards, mesh=mesh, in_specs=in_specs, out_specs=out_specs, check_vma=False)
```
